32 devices in a mesh: dp: 4 (over x, core), fsdp: 8 (over z, y).
Axes of the slice: x: 2, y: 2, z: 4, core: 2. Of those that a mesh axis runs over, the one named last changes fastest.
Arguments:
- tokens: bfloat16 [32768, 768], P(('dp', 'fsdp')), may hold values from -6 to 6
- lengths: int32 [64], P(('dp', 'fsdp')), may hold values from 16 to 512, as said below
- labels: int32 [64], P(('dp', 'fsdp')), may hold values from 0 to 2
- cotangent: bfloat16 [32768, 768], P(('dp', 'fsdp')), may hold values from -6 to 6
- qkv_weight: bfloat16 [768, 2304], P('fsdp'), may hold values from -0.21875 to 0.21875
- query_bias: bfloat16 [768], P('fsdp'), may hold values from -1.1953125 to 1.1953125
- value_bias: bfloat16 [768], P('fsdp'), may hold values from -1.1953125 to 1.1953125
- out_weight: bfloat16 [768, 768], P('fsdp'), may hold values from -1.75 to 1.75
- out_bias: bfloat16 [768], P('fsdp'), may hold values from -1.1953125 to 1.1953125
- first_gain: bfloat16 [768], P('fsdp'), may hold values from 0.5 to 1.5
- first_shift: bfloat16 [768], P('fsdp'), may hold values from -1.1953125 to 1.1953125
- inner_weight: bfloat16 [768, 3072], P('fsdp'), may hold values from -0.21875 to 0.21875
- inner_bias: bfloat16 [3072], P('fsdp'), may hold values from -1.1953125 to 1.1953125
- outer_weight: bfloat16 [3072, 768], P('fsdp'), may hold values from -0.15625 to 0.15625
- outer_bias: bfloat16 [768], P('fsdp'), may hold values from -1.1953125 to 1.1953125
- second_gain: bfloat16 [768], P('fsdp'), may hold values from 0.5 to 1.5
- second_shift: bfloat16 [768], P('fsdp'), may hold values from -1.1953125 to 1.1953125
- pool_weight: bfloat16 [768, 768], P('fsdp'), may hold values from -0.21875 to 0.21875
- pool_bias: bfloat16 [768], P('fsdp'), may hold values from -1.1953125 to 1.1953125
- class_weight: bfloat16 [768, 3], P('fsdp'), may hold values from -0.21875 to 0.21875
- class_bias: bfloat16 [3], replicated, may hold values from -2 to 2
Outputs:
- output: bfloat16 [32768, 768], P(('dp', 'fsdp'))
- exit_loss: float32 [64], P(('dp', 'fsdp'))
- tokens_grad: bfloat16 [32768, 768], P(('dp', 'fsdp'))
- qkv_weight_grad: float32 [768, 2304], P('fsdp')
- query_bias_grad: float32 [768], P('fsdp')
- value_bias_grad: float32 [768], P('fsdp')
- out_weight_grad: float32 [768, 768], P('fsdp')
- out_bias_grad: float32 [768], P('fsdp')
- first_gain_grad: float32 [768], P('fsdp')
- first_shift_grad: float32 [768], P('fsdp')
- inner_weight_grad: float32 [768, 3072], P('fsdp')
- inner_bias_grad: float32 [3072], P('fsdp')
- outer_weight_grad: float32 [3072, 768], P('fsdp')
- outer_bias_grad: float32 [768], P('fsdp')
- second_gain_grad: float32 [768], P('fsdp')
- second_shift_grad: float32 [768], P('fsdp')
- pool_weight_grad: float32 [768, 768], P('fsdp')
- pool_bias_grad: float32 [768], P('fsdp')
- class_weight_grad: float32 [768, 3], P('fsdp')
- class_bias_grad: float32 [3], replicated
The draws below stay inside these ranges and needn't reach their ends.
Inputs may be any that keep to these rules, and one draw needn't show every extreme that they name: `lengths`: true tokens of each sequence; some sequence has exactly 512 and another exactly 16.
All inputs are finite; a program needn't handle non-finite values.
Results may differ from the reference program's by a relative error of at most 0.015.
Values may be sent and summed in bfloat16 or wider, within the bound.
A program may use at most 192 MiB of HBM per device.

```python
import jax
import jax.numpy as jnp
from jax import lax

D = 768
HEADS = 12
FF = 3072
CLASSES = 3
LMAX = 512
MIN_LEN = 16
SEQS = 64
TOKENS = 32768


def draw_lengths(key, part):
    key = jax.random.fold_in(key, 11)
    first, second, third = jax.random.split(key, 3)
    values = jax.random.randint(first, (SEQS,), MIN_LEN, LMAX + 1)
    longest = jax.random.randint(second, (), 0, SEQS)
    shortest = (longest + 1 + jax.random.randint(third, (), 0, SEQS - 1)) % SEQS
    values = values.at[longest].set(LMAX)
    values = values.at[shortest].set(MIN_LEN)
    return values.astype(jnp.int32)


def with_ends(entries, key, least, top_value):
    extent = entries.shape
    spot = [jax.random.randint(jax.random.fold_in(key, axis), (), 0, extent[axis]) for axis in range(len(extent))]
    entries = entries.at[tuple(spot)].set(least)
    longest = extent.index(max(extent))
    spot[longest] = (spot[longest] + 1) % extent[longest]
    return entries.at[tuple(spot)].set(top_value)


def levels(stream_key, dims, cuts, least, largest):
    def one(position, shards_of):
        steps = jax.random.uniform(jax.random.fold_in(jax.random.fold_in(stream_key, 6), position), (shards_of,), jnp.float32, least / len(cuts), largest / len(cuts))
        return jnp.repeat(jnp.exp(steps), dims[position] // shards_of).reshape((-1,) + (1,) * (len(dims) - position - 1))

    factor_of = one(*cuts[0])
    for cut in cuts[1:]:
        factor_of = factor_of * one(*cut)
    return factor_of


def normal_values(stream_key, dims, scale, reach, pieces=(), kind=jnp.bfloat16):
    loudness = levels(stream_key, dims, pieces, -0.22, 0.18) if pieces else 1.0
    values = jax.random.normal(stream_key, dims, jnp.float32) * scale * loudness
    return jnp.minimum(jnp.maximum(values, -reach), reach).astype(kind)


def setup_inputs(seed: int = 0) -> dict:
    arg_keys = jax.random.split(jax.random.key(seed), 22)
    return {
        "tokens": normal_values(arg_keys[0], (TOKENS, D), 1.0, 6.0, ((0, 32),)),
        "lengths": draw_lengths(jax.random.fold_in(arg_keys[21], 71), 0),
        "labels": with_ends(jax.random.randint(arg_keys[2], (SEQS,), 0, CLASSES), jax.random.fold_in(arg_keys[2], 1), 0, CLASSES - 1).astype(jnp.int32),
        "cotangent": normal_values(arg_keys[3], (TOKENS, D), 1.0, 6.0, ((0, 32),)),
        "qkv_weight": normal_values(arg_keys[4], (D, 3 * D), D ** -0.5, 0.21875, ((0, 8),)),
        "query_bias": normal_values(arg_keys[5], (D,), 0.3, 1.1953125, ((0, 8),)),
        "value_bias": normal_values(arg_keys[6], (D,), 0.3, 1.1953125, ((0, 8),)),
        "out_weight": normal_values(arg_keys[7], (D, D), (D // 64) ** -0.5, 1.75, ((0, 8),)),
        "out_bias": normal_values(arg_keys[8], (D,), 0.3, 1.1953125, ((0, 8),)),
        "first_gain": jnp.clip(1.0 + 0.1 * jax.random.normal(arg_keys[9], (D,), jnp.float32), 0.5, 1.5).astype(jnp.bfloat16),
        "first_shift": normal_values(arg_keys[10], (D,), 0.3, 1.1953125, ((0, 8),)),
        "inner_weight": normal_values(arg_keys[11], (D, FF), D ** -0.5, 0.21875, ((0, 8),)),
        "inner_bias": normal_values(arg_keys[12], (FF,), 0.3, 1.1953125, ((0, 8),)),
        "outer_weight": normal_values(arg_keys[13], (FF, D), (FF // 2) ** -0.5, 0.15625, ((0, 8),)),
        "outer_bias": normal_values(arg_keys[14], (D,), 0.3, 1.1953125, ((0, 8),)),
        "second_gain": jnp.clip(1.0 + 0.1 * jax.random.normal(arg_keys[15], (D,), jnp.float32), 0.5, 1.5).astype(jnp.bfloat16),
        "second_shift": normal_values(arg_keys[16], (D,), 0.3, 1.1953125, ((0, 8),)),
        "pool_weight": normal_values(arg_keys[17], (D, D), D ** -0.5, 0.21875, ((0, 8),)),
        "pool_bias": normal_values(arg_keys[18], (D,), 0.3, 1.1953125, ((0, 8),)),
        "class_weight": normal_values(arg_keys[19], (D, CLASSES), D ** -0.5, 0.21875, ((0, 8),)),
        "class_bias": normal_values(arg_keys[20], (CLASSES,), 0.5, 2.0),
    }


@jax.custom_vjp
def low(v):
    return lax.optimization_barrier(v.astype(jnp.bfloat16)).astype(jnp.float32)

@jax.custom_vjp
def low_back(v):
    return v

def low_keep(v):
    return (low(v), None)

def low_pass(kept, grad):
    return (grad,)

def back_keep(v):
    return (v, None)

def back_low(kept, grad):
    return (low(grad),)
low.defvjp(low_keep, low_pass)
low_back.defvjp(back_keep, back_low)
EPS = 1e-12
NEG = -1000000000.0

def layer_norm(value, gain, shift):
    mean = lax.optimization_barrier(jnp.mean(value, axis=-1, keepdims=True))
    centred = value - mean
    return centred * lax.rsqrt(lax.optimization_barrier(jnp.mean(centred * centred, axis=-1, keepdims=True)) + EPS) * gain + shift

def forward_sequence(params, tokens, length, label):
    qkv_weight, query_bias, value_bias, out_weight, out_bias, first_gain, first_shift, inner_weight, inner_bias, outer_weight, outer_bias, second_gain, second_shift, pool_weight, pool_bias, class_weight, class_bias = params
    highest = lax.Precision.HIGHEST
    span, width = tokens.shape
    size = width // HEADS
    keep = jnp.arange(span, dtype=jnp.int32) < length
    valid = keep.astype(tokens.dtype)
    bias_all = jnp.concatenate([query_bias, jnp.zeros_like(query_bias), value_bias])
    qkv = low_back(low(jnp.dot(tokens, qkv_weight, precision=highest) + bias_all))
    query = qkv[:, :width].reshape(span, HEADS, size)
    key = qkv[:, width:2 * width].reshape(span, HEADS, size)
    value = qkv[:, 2 * width:].reshape(span, HEADS, size)
    scores = jnp.einsum('qhd,khd->hqk', query, key, precision=highest) * size ** (-0.5)
    scores = low_back(jnp.where(keep[None, None, :], scores, NEG))
    top = lax.optimization_barrier(jnp.max(scores, axis=-1, keepdims=True))
    expo = jnp.exp(scores - top)
    probs = low(expo / lax.optimization_barrier(jnp.sum(expo, axis=-1, keepdims=True)))
    context = jnp.einsum('hqk,khd->qhd', probs, value, precision=highest).reshape(span, width)
    context = low_back(low(context))
    attended = low_back(jnp.dot(context, out_weight, precision=highest) + out_bias)
    hidden = layer_norm(tokens + attended, first_gain, first_shift)
    inner = low_back(jnp.dot(low(hidden), inner_weight, precision=highest) + inner_bias)
    act = low(jax.nn.gelu(inner, approximate=False))
    ffn = low_back(jnp.dot(act, outer_weight, precision=highest) + outer_bias)
    layer = layer_norm(hidden + ffn, second_gain, second_shift)
    masked = layer * valid[:, None]
    first = low(layer[0:1])
    pooled = jnp.tanh(low_back(jnp.dot(first, pool_weight, precision=highest) + pool_bias))
    logits = low_back(jnp.dot(low(pooled), class_weight, precision=highest) + class_bias)[0]
    peak = jnp.max(logits)
    total = peak + jnp.log(jnp.sum(jnp.exp(logits - peak)))
    picked = jnp.sum(jnp.where(jnp.arange(logits.shape[0], dtype=jnp.int32) == label, logits, 0.0))
    return (masked, total - picked)

def reference(tokens, lengths, labels, cotangent, qkv_weight, query_bias, value_bias, out_weight, out_bias, first_gain, first_shift, inner_weight, inner_bias, outer_weight, outer_bias, second_gain, second_shift, pool_weight, pool_bias, class_weight, class_bias):
    params = tuple((p.astype(jnp.float32) for p in (qkv_weight, query_bias, value_bias, out_weight, out_bias, first_gain, first_shift, inner_weight, inner_bias, outer_weight, outer_bias, second_gain, second_shift, pool_weight, pool_bias, class_weight, class_bias)))
    seqs = lengths.shape[0]
    width = tokens.shape[1]
    token_blocks = tokens.astype(jnp.float32).reshape(seqs, -1, width)
    cot_blocks = cotangent.astype(jnp.float32).reshape(seqs, -1, width)

    def step(carry, block):
        inputs, length, label, cot = block

        def objective(weights, rows):
            return forward_sequence(weights, rows, length, label)
        (masked, loss), pull = jax.vjp(objective, params, inputs)
        grads, grad_rows = pull((cot, jnp.ones_like(loss)))
        carry = jax.tree.map(jnp.add, carry, grads)
        return (carry, (masked.astype(jnp.bfloat16), loss, grad_rows.astype(jnp.bfloat16)))
    zeros = jax.tree.map(jnp.zeros_like, params)
    totals, (outputs, losses, grad_tokens) = lax.scan(step, zeros, (token_blocks, lengths, labels, cot_blocks))
    output = outputs.reshape(-1, width)
    tokens_grad = grad_tokens.reshape(-1, width)
    return (output, losses, tokens_grad, totals[0], totals[1], totals[2], totals[3], totals[4], totals[5], totals[6], totals[7], totals[8], totals[9], totals[10], totals[11], totals[12], totals[13], totals[14], totals[15], totals[16])
```

```python
import functools
import math

import jax
import jax.numpy as jnp
from jax import lax
from jax.experimental import pallas as pl
from jax.experimental.pallas import tpu as pltpu
from jax.sharding import PartitionSpec as P

HEADS = 12
EPS = 1e-12
NEG = -1000000000.0
F32 = jnp.float32
BF16 = jnp.bfloat16
MESH = pl.DeviceIdType.MESH
LOG2E = math.log2(math.e)


def nn(left, right):
    return jnp.dot(left, right, preferred_element_type=F32)


def nt(left, right):
    return lax.dot_general(left, right, (((1,), (1,)), ((), ())), preferred_element_type=F32)


def tn(left, right):
    return lax.dot_general(left, right, (((0,), (0,)), ((), ())), preferred_element_type=F32)


def rowmean(value):
    return jnp.sum(value, axis=-1, keepdims=True) * (1.0 / value.shape[-1])


def here():
    d, f = lax.axis_index("dp"), lax.axis_index("fsdp")
    return d // 2, d % 2, f // 2, f % 2


def at(x, c, z, y):
    return (x * 2 + c, z * 2 + y)


def attend_forward(qkv, ctx, lse, lengths, i, span, width, size):
    pairs = width // (2 * size)
    wide = 2 * size
    s, hp = i // pairs, i % pairs
    rows = pl.ds(pl.multiple_of(s * span, span), span)

    def part(p):
        return qkv[rows, pl.ds(pl.multiple_of(p * width + hp * wide, wide), wide)]

    q, k, v = part(0), part(1), part(2)
    lane = lax.broadcasted_iota(jnp.int32, (span, wide), 1)
    slot = lax.broadcasted_iota(jnp.int32, (span, wide), 0)
    fill = jnp.where(slot < lengths[s], 0.0, NEG).astype(BF16)
    vt = v.T
    vrow = lax.broadcasted_iota(jnp.int32, (wide, span), 0)
    factor = size ** (-0.5) * LOG2E
    halves, sums = [], []
    for h in range(2):
        mine = lane < size if h == 0 else lane >= size
        other = (1 - h) * size
        qh = jnp.where(mine, q, jnp.where(lane == other, 1.0, 0.0).astype(BF16))
        kh = jnp.where(mine, k, fill)
        scores = nt(kh, qh)
        top = jnp.max(scores, axis=0, keepdims=True)
        e = jnp.exp2((scores - top) * factor).astype(BF16)
        vmine = vrow < size if h == 0 else vrow >= size
        vh = jnp.where(vmine, vt, jnp.ones_like(vt))
        o = nn(vh, e)
        total = o[other : other + 1, :]
        halves.append(o[h * size : (h + 1) * size, :] / total)
        sums.append(top * factor + jnp.log2(total))
    ct = jnp.concatenate(halves, axis=0)
    ctx[rows, pl.ds(pl.multiple_of(hp * wide, wide), wide)] = ct.T.astype(BF16)
    lse[i] = jnp.concatenate(sums + [jnp.zeros((6, span), F32)], axis=0)


class Gather:
    def __init__(self, buf, send, recv, split):
        self.buf, self.send, self.recv = buf, send, recv
        self.nz, _, self.r, self.cols = buf.shape
        self.x, self.c, self.z, self.y = here()
        self.half = self.cols // 2
        self.split = split
        self.base = {"z": 0}
        total = 0
        for kind, count in (("z", self.nz), ("xo", self.nz), ("ya1", self.nz), ("ya2", self.nz), ("xa", self.nz), ("co", self.nz), ("cx", self.nz)):
            self.base[kind] = total
            total += count

    def region(self, kind, k, sender):
        x, c, z, y = sender
        zk = lax.rem(self.z + self.nz - k, self.nz)
        if kind == "z":
            zk = z
        row = pl.ds(pl.multiple_of(x * (self.r // 2), 16), self.r // 2)
        every = pl.ds(0, self.r)
        c0 = c * self.half
        first = pl.ds(pl.multiple_of(c0, 128), self.split)
        second = pl.ds(pl.multiple_of(c0 + self.split, 128), self.half - self.split)
        both = pl.ds(pl.multiple_of(c0, 128), self.half)
        yy, rr, cc = {
            "z": (y, row, both),
            "xo": (y, row, both),
            "ya1": (y, every, first),
            "ya2": (y, row, second),
            "xa": (1 - y, row, second),
            "co": (y, every, both),
            "cx": (1 - y, every, both),
        }[kind]
        return self.buf.at[zk, yy, rr, cc]

    def peer(self, kind, k):
        x, c, z, y = self.x, self.c, self.z, self.y
        if kind == "z":
            return x, c, lax.rem(z + k, self.nz), y
        if kind in ("xo", "xa"):
            return 1 - x, c, z, y
        if kind in ("ya1", "ya2"):
            return x, c, z, 1 - y
        return x, 1 - c, z, y

    def copy(self, kind, k, incoming):
        me = (self.x, self.c, self.z, self.y)
        peer = self.peer(kind, k)
        sender = me
        if incoming:
            sender = (self.x, self.c, lax.rem(self.z + self.nz - k, self.nz), self.y) if kind == "z" else peer
        ref = self.region(kind, k, sender)
        n = self.base[kind] + k
        return pltpu.make_async_remote_copy(
            src_ref=ref, dst_ref=ref, send_sem=self.send.at[n], recv_sem=self.recv.at[n], device_id=at(*peer), device_id_type=MESH
        )

    def go(self, kind, k):
        self.copy(kind, k, False).start()

    def got(self, kind, k):
        self.copy(kind, k, True).wait_recv()

    def start_z(self):
        for k in range(1, self.nz):
            self.go("z", k)

    def steps(self):
        out = []
        ks = range(1, self.nz)

        def s0():
            self.go("ya1", 0)
            self.go("ya2", 0)

        out.append(s0)

        def s1(k):
            self.got("z", k)
            self.go("xo", k)
            self.go("ya2", k)

        for k in ks:
            out.append(functools.partial(s1, k))

        def s2():
            self.got("ya2", 0)
            self.go("xa", 0)

        out.append(s2)

        def s3(k):
            self.got("xo", k)
            self.go("ya1", k)
            self.go("co", k)
            self.got("ya2", k)
            self.go("xa", k)

        for k in ks:
            out.append(functools.partial(s3, k))

        def s4(k):
            self.got("ya1", k)
            self.got("xa", k)
            self.go("cx", k)

        for k in range(self.nz):
            out.append(functools.partial(s4, k))
        return out

    def finish(self):
        for k in range(1, self.nz):
            self.got("co", k)
        for k in range(self.nz):
            self.got("cx", k)

    def drain(self):
        for kind in ("z", "xo", "ya1", "ya2", "xa", "co", "cx"):
            for k in range(self.nz):
                if k == 0 and kind in ("z", "xo", "co"):
                    continue
                self.copy(kind, k, False).wait_send()


def gelu_both(value):
    cdf = 0.5 + 0.5 * lax.erf(value * (0.5**0.5))
    bell = jnp.exp2(value * value * (-0.5 * LOG2E)) * (1.0 / math.sqrt(2.0 * math.pi))
    return value * cdf, cdf + value * bell


def place(sm, f, part, width):
    row = lax.broadcasted_iota(jnp.int32, (128, width), 0)
    col = lax.broadcasted_iota(jnp.int32, (128, width), 1)
    return jnp.where((col == row + f * part) & (row < part), 1.0, 0.0).astype(BF16)


def forward_kernel(comm, tokens_h, lengths, wqkv_h, wout_h, winner_h, wouter_h, wpool_h, smalls_h,
                   out_h, w1_h, w2_h, w3_h, vec_o, ib_o, qkv_h, ctx_h, lse_o, hid_h, u1_h, act_h, dg_h, u2_h, inv_o, first_o,
                   tokens, w1, w2, w3, sm, qkv, ctx, hid, hidlow, u1, act, dg, u2, outv,
                   loc, s_sm, r_sm, s1, r1, s2, r2, s3, r3):
    x, c, z, y = here() if comm else (0, 0, 0, 0)
    nz = w1.shape[0]
    rows, width = tokens.shape
    span = rows // lengths.shape[0]
    ff = act.shape[1]
    size = width // HEADS
    pairs = HEADS // 2
    d3 = 3 * width
    fr = wouter_h.shape[0] if comm else w3.shape[2] - w1.shape[2]

    if comm:
        barrier = pltpu.get_barrier_semaphore()
        peers = [(x, c, lax.rem(z + k, nz), yy) for k in range(1, nz) for yy in (y, 1 - y)]
        peers += [(x, c, z, 1 - y), (1 - x, c, z, y), (x, 1 - c, z, y)]
        local = []

        def bring(n, src, dst):
            copy = pltpu.make_async_copy(src, dst, loc.at[n])
            copy.start()
            local.append(copy)

        f_me = z * 2 + y
        bring(0, wqkv_h, w1.at[z, y])
        bring(1, smalls_h, sm.at[f_me])
        bring(2, wout_h, w2.at[z, y, :, pl.ds(0, width)])
        bring(3, winner_h, w2.at[z, y, :, pl.ds(width, ff)])
        bring(4, wouter_h, w3.at[z, y, pl.ds(0, fr)])
        bring(5, wpool_h, w3.at[z, y, pl.ds(fr, wpool_h.shape[0])])
        bring(6, tokens_h, tokens)
        for p in peers:
            pl.semaphore_signal(barrier, inc=1, device_id=at(*p), device_id_type=MESH)
        pl.semaphore_wait(barrier, len(peers))
        g1 = Gather(w1, s1, r1, 512)
        g2 = Gather(w2, s2, r2, 640)
        g3 = Gather(w3, s3, r3, 128)
        local[0].wait()
        g1.start_z()
        local[1].wait()
        others = [p for p in peers[:-2]]

        def small(n, slot):
            px, pc, pz, py = others[n]
            return pltpu.make_async_remote_copy(
                src_ref=sm.at[slot], dst_ref=sm.at[slot], send_sem=s_sm.at[n], recv_sem=r_sm.at[n], device_id=at(px, pc, pz, py), device_id_type=MESH
            )

        for n in range(len(others)):
            small(n, f_me).start()
        todo = g1.steps()
        for n, step in enumerate(todo):
            step()
            if n == 4:
                local[2].wait()
                local[3].wait()
                g2.start_z()
        local[4].wait()
        local[5].wait()
        g3.start_z()
        for n in range(len(others)):
            if n < 2 * (nz - 1):
                k, same = n // 2 + 1, n % 2 == 0
                slot = lax.rem(z + nz - k, nz) * 2 + (y if same else 1 - y)
            else:
                slot = z * 2 + 1 - y
            small(n, slot).wait_recv()
        local[6].wait()
        g1.finish()
        steps2, steps3 = g2.steps(), g3.steps()
    else:
        steps2, steps3 = [], []
        for n, (a, b) in enumerate(((tokens_h, tokens), (w1_h, w1), (w2_h, w2), (w3_h, w3), (smalls_h, sm))):
            cp = pltpu.make_async_copy(a, b, loc.at[n])
            cp.start()
            cp.wait()

    nf = nz * 2
    part = width // nf
    vec = jnp.zeros((sm.shape[1], width), F32)
    for f in range(nf):
        vec += nn(sm[f], place(None, f, part, width))
    vec_o[...] = vec
    ibs = []
    for f in range(nf):
        piece = sm[f].astype(F32)
        for j in range(ff // nf // 128):
            ibs.append(piece[12 + j : 13 + j, :])
    ib_o[...] = jnp.broadcast_to(jnp.concatenate(ibs, axis=1), ib_o.shape)

    out_copies = []

    def save(src, dst):
        cp = pltpu.make_async_copy(src, dst, loc.at[8 + len(out_copies)])
        cp.start()
        out_copies.append(cp)

    if comm:
        save(w1, w1_h)

    tile = 256
    zero_row = jnp.zeros((1, width), F32)
    biases = (vec_o[0:1, :], zero_row, vec_o[1:2, :])

    def project(i, _):
        r = pl.ds(pl.multiple_of(i * tile, tile), tile)
        t = tokens[r, :]
        for p in range(3):
            w = w1[:, :, :, p * width : (p + 1) * width].reshape(width, width)
            qkv[r, p * width : (p + 1) * width] = (nn(t, w) + biases[p]).astype(BF16)
        for n, step in enumerate(steps2[:4]):
            pl.when(i == n)(step)
        return 0

    lax.fori_loop(0, rows // tile, project, 0)
    save(qkv, qkv_h)

    def attention(i, _):
        attend_forward(qkv, ctx, lse_o, lengths, i, span, width, size)
        for n, step in enumerate(steps2[4:]):
            pl.when(i == n)(step)
        for n, step in enumerate(steps3[:4]):
            pl.when(i == n + 8)(step)
        return 0

    lax.fori_loop(0, (rows // span) * pairs, attention, 0)
    save(ctx, ctx_h)
    if comm:
        g2.finish()
        save(w2, w2_h)

    b_out, g_first, s_first, b_outer, g_second, s_second = (vec_o[n : n + 1, :] for n in range(2, 8))

    def stage_one(i, _):
        r = pl.ds(pl.multiple_of(i * tile, tile), tile)
        w = w2[:, :, :, :width].reshape(width, width)
        resid = tokens[r, :].astype(F32) + (nn(ctx[r, :], w) + b_out)
        centred = resid - rowmean(resid)
        inv = lax.rsqrt(rowmean(centred * centred) + EPS)
        unit = centred * inv
        u1[r, :] = unit.astype(BF16)
        inv_o[0, r, :] = jnp.broadcast_to(inv, (tile, 128))
        h = unit * g_first + s_first
        hid[r, :] = h
        low = h.astype(BF16)
        hidlow[r, :] = low
        for b in range(ff // width):
            cols = pl.ds(b * width, width)
            w = w2[:, :, :, (b + 1) * width : (b + 2) * width].reshape(width, width)
            a, g = gelu_both(nn(low, w) + ib_o[0:1, b * width : (b + 1) * width])
            act[r, cols] = a.astype(BF16)
            dg[r, cols] = g.astype(BF16)
        for n in range(rows // tile):
            for step in steps3[4 + 2 * n : 6 + 2 * n]:
                pl.when(i == n)(step)
        return 0

    lax.fori_loop(0, rows // tile, stage_one, 0)
    save(u1, u1_h)
    save(hidlow, hid_h)
    save(act, act_h)
    save(dg, dg_h)
    if comm:
        g3.finish()
        save(w3, w3_h)

    def stage_two(i, _):
        r = pl.ds(pl.multiple_of(i * tile, tile), tile)
        w = w3[:, :, :fr, :].reshape(ff, width)
        resid = hid[r, :] + (nn(act[r, :], w) + b_outer)
        centred = resid - rowmean(resid)
        inv = lax.rsqrt(rowmean(centred * centred) + EPS)
        unit = centred * inv
        u2[r, :] = unit.astype(BF16)
        inv_o[1, r, :] = jnp.broadcast_to(inv, (tile, 128))
        layer = unit * g_second + s_second
        each = span // tile
        s, j = i // each, i % each

        @pl.when(j == 0)
        def _():
            first_o[pl.ds(pl.multiple_of(s * 8, 8), 8), :] = layer[0:8, :]

        slot = lax.broadcasted_iota(jnp.int32, (tile, width), 0) + j * tile
        outv[r, :] = jnp.where(slot < lengths[s], layer, 0.0).astype(BF16)
        return 0

    lax.fori_loop(0, rows // tile, stage_two, 0)
    save(u2, u2_h)
    save(outv, out_h)
    for cp in out_copies:
        cp.wait()
    if comm:
        for n in range(len(others)):
            small(n, f_me).wait_send()
        for g in (g1, g2, g3):
            g.drain()


def forward(tokens, lengths, wqkv, wout, winner, wouter, wpool, smalls, nz, gathered=None):
    rows, width = tokens.shape
    comm = gathered is None
    span = rows // lengths.shape[0]
    nf = nz * 2
    ff = winner.shape[1] if comm else gathered[1].shape[3] - width
    part = width // nf
    fpart = ff // nf
    any_, vm, smem = (pl.BlockSpec(memory_space=m) for m in (pl.ANY, pltpu.VMEM, pltpu.SMEM))
    S = jax.ShapeDtypeStruct
    pairs = HEADS // 2
    outs = [
        (S((rows, width), BF16), any_),
        (S((nz, 2, part, 3 * width), BF16), any_),
        (S((nz, 2, part, width + ff), BF16), any_),
        (S((nz, 2, fpart + part, width), BF16), any_),
        (S((16, width), F32), vm),
        (S((8, ff), F32), vm),
        (S((rows, 3 * width), BF16), any_),
        (S((rows, width), BF16), any_),
        (S(((rows // span) * pairs, 8, span), F32), vm),
        (S((rows, width), BF16), any_),
        (S((rows, width), BF16), any_),
        (S((rows, ff), BF16), any_),
        (S((rows, ff), BF16), any_),
        (S((rows, width), BF16), any_),
        (S((2, rows, 128), F32), vm),
        (S((8 * (rows // span), width), F32), vm),
    ]
    V = pltpu.VMEM
    D = pltpu.SemaphoreType.DMA
    scratch = [
        V((rows, width), BF16),
        V((nz, 2, part, 3 * width), BF16),
        V((nz, 2, part, width + ff), BF16),
        V((nz, 2, fpart + part, width), BF16),
        V((nf, 16, 128), BF16),
        V((rows, 3 * width), BF16),
        V((rows, width), BF16),
        V((rows, width), F32),
        V((rows, width), BF16),
        V((rows, width), BF16),
        V((rows, ff), BF16),
        V((rows, ff), BF16),
        V((rows, width), BF16),
        V((rows, width), BF16),
        D((24,)), D((nf,)), D((nf,)),
        D((7 * nz,)), D((7 * nz,)), D((7 * nz,)), D((7 * nz,)), D((7 * nz,)), D((7 * nz,)),
    ]
    kern = functools.partial(forward_kernel, comm)
    params = pltpu.CompilerParams(vmem_limit_bytes=60 * 2**20, has_side_effects=True, **({"collective_id": 0} if comm else {}))
    flops = 2 * rows * width * (4 * width + 2 * ff)
    cost = pl.CostEstimate(flops=flops, bytes_accessed=10**7, transcendentals=0)
    if comm:
        args = (tokens, lengths, wqkv, wout, winner, wouter, wpool, smalls)
        return pl.pallas_call(kern, out_shape=[o[0] for o in outs], out_specs=[o[1] for o in outs],
                              in_specs=[any_, smem] + [any_] * 6, scratch_shapes=scratch, compiler_params=params, cost_estimate=cost)(*args)

    def solo(tokens_h, lengths, w1_h, w2_h, w3_h, smalls_h, *rest):
        o = rest[: len(outs)]
        forward_kernel(False, tokens_h, lengths, None, None, None, None, None, smalls_h, o[0], w1_h, w2_h, w3_h, *o[4:], *rest[len(outs):])

    return pl.pallas_call(solo, out_shape=[o[0] for o in outs], out_specs=[o[1] for o in outs],
                          in_specs=[any_, smem] + [any_] * 4, scratch_shapes=scratch, compiler_params=params, cost_estimate=cost)(
        tokens, lengths, *gathered, smalls)


def normalize(value, gain, shift):
    mean = jnp.mean(value, axis=-1, keepdims=True)
    centred = value - mean
    inverse = lax.rsqrt(jnp.mean(centred * centred, axis=-1, keepdims=True) + EPS)
    unit = centred * inverse
    return (unit * gain + shift, unit, inverse)


def norm_back(grad, unit, inverse, gain):
    scaled = grad * gain
    inner = (
        scaled
        - jnp.mean(scaled, axis=-1, keepdims=True)
        - unit * jnp.mean(scaled * unit, axis=-1, keepdims=True)
    )
    return (inner * inverse, jnp.sum(grad * unit, axis=0), jnp.sum(grad, axis=0))


def matmul(left, right):
    return nn(left, right)


def transposed_left(left, right):
    return lax.dot_general(
        left, right, (((0,), (0,)), ((), ())), preferred_element_type=jnp.float32
    )


def transposed_right(left, right):
    return lax.dot_general(
        left, right, (((1,), (1,)), ((), ())), preferred_element_type=jnp.float32
    )


def column_sum(values):
    return jnp.sum(values.astype(jnp.float32), axis=0)


def attend(block):
    query, key, value, keep = block
    scale = query.shape[-1] ** (-0.5)
    scores = jnp.einsum("qhd,khd->hqk", query, key, preferred_element_type=jnp.float32) * scale
    scores = jnp.where(keep[None, None, :], scores, NEG)
    top = jnp.max(scores, axis=-1, keepdims=True)
    total = jnp.sum(jnp.exp(scores - top), axis=-1, keepdims=True)
    logsum = top + jnp.log(total)
    probs = jnp.exp(scores - logsum).astype(jnp.bfloat16)
    context = jnp.einsum("hqk,khd->qhd", probs, value, preferred_element_type=jnp.float32)
    return (context.astype(jnp.bfloat16), logsum[:, :, 0])


def attend_back(block):
    query, key, value, keep, logsum, grad_context = block
    scale = query.shape[-1] ** (-0.5)
    scores = jnp.einsum("qhd,khd->hqk", query, key, preferred_element_type=jnp.float32) * scale
    scores = jnp.where(keep[None, None, :], scores, NEG)
    probs = jnp.exp(scores - logsum[:, :, None])
    grad_value = jnp.einsum(
        "hqk,qhd->khd", probs.astype(jnp.bfloat16), grad_context, preferred_element_type=jnp.float32
    )
    grad_probs = jnp.einsum("qhd,khd->hqk", grad_context, value, preferred_element_type=jnp.float32)
    delta = jnp.sum(grad_probs * probs, axis=-1, keepdims=True)
    grad_scores = (probs * (grad_probs - delta)).astype(jnp.bfloat16)
    grad_query = (
        jnp.einsum("hqk,khd->qhd", grad_scores, key, preferred_element_type=jnp.float32) * scale
    )
    grad_key = (
        jnp.einsum("hqk,qhd->khd", grad_scores, query, preferred_element_type=jnp.float32) * scale
    )
    return (
        grad_query.astype(jnp.bfloat16),
        grad_key.astype(jnp.bfloat16),
        grad_value.astype(jnp.bfloat16),
    )


def per_device_any(
    tokens,
    lengths,
    labels,
    cotangent,
    qkv_weight,
    query_bias,
    value_bias,
    out_weight,
    out_bias,
    first_gain,
    first_shift,
    inner_weight,
    inner_bias,
    outer_weight,
    outer_bias,
    second_gain,
    second_shift,
    pool_weight,
    pool_bias,
    class_weight,
    class_bias,
):
    full = (
        lax.all_gather(qkv_weight, "fsdp", axis=0, tiled=True),
        lax.all_gather(query_bias, "fsdp", axis=0, tiled=True),
        lax.all_gather(value_bias, "fsdp", axis=0, tiled=True),
        lax.all_gather(out_weight, "fsdp", axis=0, tiled=True),
        lax.all_gather(out_bias, "fsdp", axis=0, tiled=True),
        lax.all_gather(first_gain, "fsdp", axis=0, tiled=True),
        lax.all_gather(first_shift, "fsdp", axis=0, tiled=True),
        lax.all_gather(inner_weight, "fsdp", axis=0, tiled=True),
        lax.all_gather(inner_bias, "fsdp", axis=0, tiled=True),
        lax.all_gather(outer_weight, "fsdp", axis=0, tiled=True),
        lax.all_gather(outer_bias, "fsdp", axis=0, tiled=True),
        lax.all_gather(second_gain, "fsdp", axis=0, tiled=True),
        lax.all_gather(second_shift, "fsdp", axis=0, tiled=True),
        lax.all_gather(pool_weight, "fsdp", axis=0, tiled=True),
        lax.all_gather(pool_bias, "fsdp", axis=0, tiled=True),
        lax.all_gather(class_weight, "fsdp", axis=0, tiled=True),
    )
    (
        w_qkv,
        b_query,
        b_value,
        w_out,
        b_out,
        g_first,
        s_first,
        w_inner,
        b_inner,
        w_outer,
        b_outer,
        g_second,
        s_second,
        w_pool,
        b_pool,
        w_class,
    ) = full
    b_query = b_query.astype(jnp.float32)
    b_value = b_value.astype(jnp.float32)
    b_out = b_out.astype(jnp.float32)
    g_first = g_first.astype(jnp.float32)
    s_first = s_first.astype(jnp.float32)
    b_inner = b_inner.astype(jnp.float32)
    b_outer = b_outer.astype(jnp.float32)
    g_second = g_second.astype(jnp.float32)
    s_second = s_second.astype(jnp.float32)
    b_pool = b_pool.astype(jnp.float32)
    b_class = class_bias.astype(jnp.float32)
    seqs = lengths.shape[0]
    rows, width = tokens.shape
    span = rows // seqs
    size = width // HEADS
    classes = class_bias.shape[0]
    position = lax.broadcasted_iota(jnp.int32, (seqs, span), 1)
    keep = position < lengths[:, None]
    valid = keep.reshape(rows, 1).astype(jnp.float32)
    bias_all = jnp.concatenate([b_query, jnp.zeros_like(b_query), b_value])
    qkv = (matmul(tokens, w_qkv) + bias_all).astype(jnp.bfloat16)
    query = qkv[:, :width].reshape(seqs, span, HEADS, size)
    key = qkv[:, width : 2 * width].reshape(seqs, span, HEADS, size)
    value = qkv[:, 2 * width :].reshape(seqs, span, HEADS, size)
    context, logsum = lax.map(attend, (query, key, value, keep))
    context = context.reshape(rows, width)
    attended = matmul(context, w_out) + b_out
    hidden, unit_first, inverse_first = normalize(
        tokens.astype(jnp.float32) + attended, g_first, s_first
    )
    hidden_low = hidden.astype(jnp.bfloat16)
    inner = matmul(hidden_low, w_inner) + b_inner
    act = jax.nn.gelu(inner, approximate=False).astype(jnp.bfloat16)
    ffn = matmul(act, w_outer) + b_outer
    layer, unit_second, inverse_second = normalize(hidden + ffn, g_second, s_second)
    output = (layer * valid).astype(jnp.bfloat16)
    first = layer.reshape(seqs, span, width)[:, 0].astype(jnp.bfloat16)
    pooled = jnp.tanh(matmul(first, w_pool) + b_pool)
    pooled_low = pooled.astype(jnp.bfloat16)
    logits = matmul(pooled_low, w_class) + b_class
    peak = jnp.max(logits, axis=-1, keepdims=True)
    logsum_class = peak + jnp.log(jnp.sum(jnp.exp(logits - peak), axis=-1, keepdims=True))
    onehot = (labels[:, None] == lax.broadcasted_iota(jnp.int32, (seqs, classes), 1)).astype(
        jnp.float32
    )
    exit_loss = logsum_class[:, 0] - jnp.sum(onehot * logits, axis=-1)
    again = (
        lax.all_gather(qkv_weight, "fsdp", axis=0, tiled=True),
        lax.all_gather(query_bias, "fsdp", axis=0, tiled=True),
        lax.all_gather(value_bias, "fsdp", axis=0, tiled=True),
        lax.all_gather(out_weight, "fsdp", axis=0, tiled=True),
        lax.all_gather(out_bias, "fsdp", axis=0, tiled=True),
        lax.all_gather(first_gain, "fsdp", axis=0, tiled=True),
        lax.all_gather(first_shift, "fsdp", axis=0, tiled=True),
        lax.all_gather(inner_weight, "fsdp", axis=0, tiled=True),
        lax.all_gather(inner_bias, "fsdp", axis=0, tiled=True),
        lax.all_gather(outer_weight, "fsdp", axis=0, tiled=True),
        lax.all_gather(outer_bias, "fsdp", axis=0, tiled=True),
        lax.all_gather(second_gain, "fsdp", axis=0, tiled=True),
        lax.all_gather(second_shift, "fsdp", axis=0, tiled=True),
        lax.all_gather(pool_weight, "fsdp", axis=0, tiled=True),
        lax.all_gather(pool_bias, "fsdp", axis=0, tiled=True),
        lax.all_gather(class_weight, "fsdp", axis=0, tiled=True),
    )
    w_qkv = again[0]
    w_out = again[3]
    g_first = again[5].astype(jnp.float32)
    w_inner = again[7]
    w_outer = again[9]
    g_second = again[11].astype(jnp.float32)
    w_pool = again[13]
    w_class = again[15]
    grad_logits = (jnp.exp(logits - logsum_class) - onehot).astype(jnp.bfloat16)
    grad_class_weight = transposed_left(pooled_low, grad_logits)
    grad_class_local = column_sum(grad_logits)
    grad_pooled = transposed_right(grad_logits, w_class)
    grad_pre = (grad_pooled * (1.0 - pooled * pooled)).astype(jnp.bfloat16)
    grad_pool_weight = transposed_left(first, grad_pre)
    grad_pool_bias = column_sum(grad_pre)
    grad_first = transposed_right(grad_pre, w_pool)
    grad_layer = (cotangent.astype(jnp.float32) * valid).reshape(seqs, span, width)
    grad_layer = jnp.concatenate(
        [grad_layer[:, :1] + grad_first[:, None, :], grad_layer[:, 1:]], axis=1
    )
    grad_layer = grad_layer.reshape(rows, width)
    grad_resid_second, grad_second_gain, grad_second_shift = norm_back(
        grad_layer, unit_second, inverse_second, g_second
    )
    grad_ffn = grad_resid_second.astype(jnp.bfloat16)
    grad_outer_weight = transposed_left(act, grad_ffn)
    grad_outer_bias = column_sum(grad_ffn)
    grad_act = transposed_right(grad_ffn, w_outer)
    gelu_value, gelu_pull = jax.vjp(lambda v: jax.nn.gelu(v, approximate=False), inner)
    grad_inner = gelu_pull(grad_act)[0].astype(jnp.bfloat16)
    grad_inner_weight = transposed_left(hidden_low, grad_inner)
    grad_inner_bias = column_sum(grad_inner)
    grad_hidden = grad_resid_second + transposed_right(grad_inner, w_inner)
    grad_resid_first, grad_first_gain, grad_first_shift = norm_back(
        grad_hidden, unit_first, inverse_first, g_first
    )
    grad_attended = grad_resid_first.astype(jnp.bfloat16)
    grad_out_weight = transposed_left(context, grad_attended)
    grad_out_bias = column_sum(grad_attended)
    grad_context = (
        transposed_right(grad_attended, w_out).astype(jnp.bfloat16).reshape(seqs, span, HEADS, size)
    )
    grad_query, grad_key, grad_value = lax.map(
        attend_back, (query, key, value, keep, logsum, grad_context)
    )
    grad_query = grad_query.reshape(rows, width)
    grad_key = grad_key.reshape(rows, width)
    grad_value = grad_value.reshape(rows, width)
    grad_qkv = jnp.concatenate([grad_query, grad_key, grad_value], axis=1)
    grad_qkv_weight = transposed_left(tokens, grad_qkv)
    grad_query_bias = column_sum(grad_query)
    grad_value_bias = column_sum(grad_value)
    tokens_grad = (grad_resid_first + transposed_right(grad_qkv, w_qkv)).astype(jnp.bfloat16)
    owned = (
        lax.psum_scatter(grad_qkv_weight, "fsdp", scatter_dimension=0, tiled=True),
        lax.psum_scatter(grad_query_bias, "fsdp", scatter_dimension=0, tiled=True),
        lax.psum_scatter(grad_value_bias, "fsdp", scatter_dimension=0, tiled=True),
        lax.psum_scatter(grad_out_weight, "fsdp", scatter_dimension=0, tiled=True),
        lax.psum_scatter(grad_out_bias, "fsdp", scatter_dimension=0, tiled=True),
        lax.psum_scatter(grad_first_gain, "fsdp", scatter_dimension=0, tiled=True),
        lax.psum_scatter(grad_first_shift, "fsdp", scatter_dimension=0, tiled=True),
        lax.psum_scatter(grad_inner_weight, "fsdp", scatter_dimension=0, tiled=True),
        lax.psum_scatter(grad_inner_bias, "fsdp", scatter_dimension=0, tiled=True),
        lax.psum_scatter(grad_outer_weight, "fsdp", scatter_dimension=0, tiled=True),
        lax.psum_scatter(grad_outer_bias, "fsdp", scatter_dimension=0, tiled=True),
        lax.psum_scatter(grad_second_gain, "fsdp", scatter_dimension=0, tiled=True),
        lax.psum_scatter(grad_second_shift, "fsdp", scatter_dimension=0, tiled=True),
        lax.psum_scatter(grad_pool_weight, "fsdp", scatter_dimension=0, tiled=True),
        lax.psum_scatter(grad_pool_bias, "fsdp", scatter_dimension=0, tiled=True),
        lax.psum_scatter(grad_class_weight, "fsdp", scatter_dimension=0, tiled=True),
    )
    summed = lax.psum(
        (
            owned[0],
            owned[1],
            owned[2],
            owned[3],
            owned[4],
            owned[5],
            owned[6],
            owned[7],
            owned[8],
            owned[9],
            owned[10],
            owned[11],
            owned[12],
            owned[13],
            owned[14],
            owned[15],
        ),
        "dp",
    )
    class_bias_grad = lax.psum(grad_class_local, ("dp", "fsdp"))
    return (
        output,
        exit_loss,
        tokens_grad,
        summed[0],
        summed[1],
        summed[2],
        summed[3],
        summed[4],
        summed[5],
        summed[6],
        summed[7],
        summed[8],
        summed[9],
        summed[10],
        summed[11],
        summed[12],
        summed[13],
        summed[14],
        summed[15],
        class_bias_grad,
    )


def per_device(nz, tokens, lengths, labels, cotangent, qkv_weight, query_bias, value_bias, out_weight, out_bias,
    first_gain, first_shift, inner_weight, inner_bias, outer_weight, outer_bias, second_gain, second_shift,
    pool_weight, pool_bias, class_weight, class_bias):
    part = query_bias.shape[0]
    vectors = jnp.stack([query_bias, value_bias, out_bias, first_gain, first_shift, outer_bias, second_gain, second_shift, pool_bias]
                        + [class_weight[:, j] for j in range(class_weight.shape[1])])
    smalls = jnp.concatenate([jnp.pad(vectors, ((0, 0), (0, 128 - part))), inner_bias.reshape(-1, 128), jnp.zeros((1, 128), BF16)])
    (output, w1, w2, w3, vec, ib, qkv, context, lse, hidden_low, unit_first, act, dgelu, unit_second, inv, firsts) = forward(
        tokens, lengths, qkv_weight, out_weight, inner_weight, outer_weight, pool_weight, smalls, nz)
    seqs = lengths.shape[0]
    rows, width = tokens.shape
    ff = act.shape[1]
    span = rows // seqs
    size = width // HEADS
    classes = class_bias.shape[0]
    w_qkv = w1.reshape(width, 3 * width)
    w2 = w2.reshape(width, width + ff)
    w_out, w_inner = w2[:, :width], w2[:, width:]
    fr = ff // (2 * nz)
    w_outer = w3[:, :, :fr].reshape(ff, width)
    w_pool = w3[:, :, fr:].reshape(width, width)
    g_first, g_second, b_pool, w_class = vec[3], vec[6], vec[8], vec[9:12].T.astype(BF16)
    b_class = class_bias.astype(jnp.float32)
    unit_first, unit_second = unit_first.astype(F32), unit_second.astype(F32)
    inverse_first, inverse_second = inv[0, :, :1], inv[1, :, :1]
    position = lax.broadcasted_iota(jnp.int32, (seqs, span), 1)
    keep = position < lengths[:, None]
    valid = keep.reshape(rows, 1).astype(jnp.float32)
    query = qkv[:, :width].reshape(seqs, span, HEADS, size)
    key = qkv[:, width : 2 * width].reshape(seqs, span, HEADS, size)
    value = qkv[:, 2 * width :].reshape(seqs, span, HEADS, size)
    logsum = (lse[:, :2] / LOG2E).reshape(seqs, HEADS, span)
    first = firsts[::8].astype(BF16)
    pooled = jnp.tanh(matmul(first, w_pool) + b_pool)
    pooled_low = pooled.astype(jnp.bfloat16)
    logits = matmul(pooled_low, w_class) + b_class
    peak = jnp.max(logits, axis=-1, keepdims=True)
    logsum_class = peak + jnp.log(jnp.sum(jnp.exp(logits - peak), axis=-1, keepdims=True))
    onehot = (labels[:, None] == lax.broadcasted_iota(jnp.int32, (seqs, classes), 1)).astype(
        jnp.float32
    )
    exit_loss = logsum_class[:, 0] - jnp.sum(onehot * logits, axis=-1)
    grad_logits = (jnp.exp(logits - logsum_class) - onehot).astype(jnp.bfloat16)
    grad_class_weight = transposed_left(pooled_low, grad_logits)
    grad_class_local = column_sum(grad_logits)
    grad_pooled = transposed_right(grad_logits, w_class)
    grad_pre = (grad_pooled * (1.0 - pooled * pooled)).astype(jnp.bfloat16)
    grad_pool_weight = transposed_left(first, grad_pre)
    grad_pool_bias = column_sum(grad_pre)
    grad_first = transposed_right(grad_pre, w_pool)
    grad_layer = (cotangent.astype(jnp.float32) * valid).reshape(seqs, span, width)
    grad_layer = jnp.concatenate(
        [grad_layer[:, :1] + grad_first[:, None, :], grad_layer[:, 1:]], axis=1
    )
    grad_layer = grad_layer.reshape(rows, width)
    grad_resid_second, grad_second_gain, grad_second_shift = norm_back(
        grad_layer, unit_second, inverse_second, g_second
    )
    grad_ffn = grad_resid_second.astype(jnp.bfloat16)
    grad_outer_weight = transposed_left(act, grad_ffn)
    grad_outer_bias = column_sum(grad_ffn)
    grad_act = transposed_right(grad_ffn, w_outer)
    grad_inner = (grad_act * dgelu.astype(F32)).astype(jnp.bfloat16)
    grad_inner_weight = transposed_left(hidden_low, grad_inner)
    grad_inner_bias = column_sum(grad_inner)
    grad_hidden = grad_resid_second + transposed_right(grad_inner, w_inner)
    grad_resid_first, grad_first_gain, grad_first_shift = norm_back(
        grad_hidden, unit_first, inverse_first, g_first
    )
    grad_attended = grad_resid_first.astype(jnp.bfloat16)
    grad_out_weight = transposed_left(context, grad_attended)
    grad_out_bias = column_sum(grad_attended)
    grad_context = (
        transposed_right(grad_attended, w_out).astype(jnp.bfloat16).reshape(seqs, span, HEADS, size)
    )
    grad_query, grad_key, grad_value = lax.map(
        attend_back, (query, key, value, keep, logsum, grad_context)
    )
    grad_query = grad_query.reshape(rows, width)
    grad_key = grad_key.reshape(rows, width)
    grad_value = grad_value.reshape(rows, width)
    grad_qkv = jnp.concatenate([grad_query, grad_key, grad_value], axis=1)
    grad_qkv_weight = transposed_left(tokens, grad_qkv)
    grad_query_bias = column_sum(grad_query)
    grad_value_bias = column_sum(grad_value)
    tokens_grad = (grad_resid_first + transposed_right(grad_qkv, w_qkv)).astype(jnp.bfloat16)
    owned = (
        lax.psum_scatter(grad_qkv_weight, "fsdp", scatter_dimension=0, tiled=True),
        lax.psum_scatter(grad_query_bias, "fsdp", scatter_dimension=0, tiled=True),
        lax.psum_scatter(grad_value_bias, "fsdp", scatter_dimension=0, tiled=True),
        lax.psum_scatter(grad_out_weight, "fsdp", scatter_dimension=0, tiled=True),
        lax.psum_scatter(grad_out_bias, "fsdp", scatter_dimension=0, tiled=True),
        lax.psum_scatter(grad_first_gain, "fsdp", scatter_dimension=0, tiled=True),
        lax.psum_scatter(grad_first_shift, "fsdp", scatter_dimension=0, tiled=True),
        lax.psum_scatter(grad_inner_weight, "fsdp", scatter_dimension=0, tiled=True),
        lax.psum_scatter(grad_inner_bias, "fsdp", scatter_dimension=0, tiled=True),
        lax.psum_scatter(grad_outer_weight, "fsdp", scatter_dimension=0, tiled=True),
        lax.psum_scatter(grad_outer_bias, "fsdp", scatter_dimension=0, tiled=True),
        lax.psum_scatter(grad_second_gain, "fsdp", scatter_dimension=0, tiled=True),
        lax.psum_scatter(grad_second_shift, "fsdp", scatter_dimension=0, tiled=True),
        lax.psum_scatter(grad_pool_weight, "fsdp", scatter_dimension=0, tiled=True),
        lax.psum_scatter(grad_pool_bias, "fsdp", scatter_dimension=0, tiled=True),
        lax.psum_scatter(grad_class_weight, "fsdp", scatter_dimension=0, tiled=True),
    )
    summed = lax.psum(
        (
            owned[0],
            owned[1],
            owned[2],
            owned[3],
            owned[4],
            owned[5],
            owned[6],
            owned[7],
            owned[8],
            owned[9],
            owned[10],
            owned[11],
            owned[12],
            owned[13],
            owned[14],
            owned[15],
        ),
        "dp",
    )
    class_bias_grad = lax.psum(grad_class_local, ("dp", "fsdp"))
    return (
        output,
        exit_loss,
        tokens_grad,
        summed[0],
        summed[1],
        summed[2],
        summed[3],
        summed[4],
        summed[5],
        summed[6],
        summed[7],
        summed[8],
        summed[9],
        summed[10],
        summed[11],
        summed[12],
        summed[13],
        summed[14],
        summed[15],
        class_bias_grad,
    )


def solution(mesh):
    in_specs = (
        P(("dp", "fsdp"), None),
        P(("dp", "fsdp")),
        P(("dp", "fsdp")),
        P(("dp", "fsdp"), None),
        P("fsdp", None),
        P("fsdp"),
        P("fsdp"),
        P("fsdp", None),
        P("fsdp"),
        P("fsdp"),
        P("fsdp"),
        P("fsdp", None),
        P("fsdp"),
        P("fsdp", None),
        P("fsdp"),
        P("fsdp"),
        P("fsdp"),
        P("fsdp", None),
        P("fsdp"),
        P("fsdp", None),
        P(),
    )
    out_specs = (
        P(("dp", "fsdp"), None),
        P(("dp", "fsdp")),
        P(("dp", "fsdp"), None),
        P("fsdp", None),
        P("fsdp"),
        P("fsdp"),
        P("fsdp", None),
        P("fsdp"),
        P("fsdp"),
        P("fsdp"),
        P("fsdp", None),
        P("fsdp"),
        P("fsdp", None),
        P("fsdp"),
        P("fsdp"),
        P("fsdp"),
        P("fsdp", None),
        P("fsdp"),
        P("fsdp", None),
        P(),
    )
    sizes = dict(mesh.shape)
    fast = sizes["dp"] == 4 and sizes["fsdp"] == 8
    return jax.shard_map(
        functools.partial(per_device, sizes["fsdp"] // 2) if fast else per_device_any, mesh=mesh, in_specs=in_specs, out_specs=out_specs, check_vma=False
    )
```

```python
import functools
import math

import jax
import jax.numpy as jnp
from jax import lax
from jax.experimental import pallas as pl
from jax.experimental.pallas import tpu as pltpu
from jax.sharding import PartitionSpec as P

HEADS = 12
EPS = 1e-12
NEG = -1000000000.0
F32 = jnp.float32
BF16 = jnp.bfloat16
MESH = pl.DeviceIdType.MESH
LOG2E = math.log2(math.e)


def nn(left, right):
    return jnp.dot(left, right, preferred_element_type=F32)


def nt(left, right):
    return lax.dot_general(left, right, (((1,), (1,)), ((), ())), preferred_element_type=F32)


def tn(left, right):
    return lax.dot_general(left, right, (((0,), (0,)), ((), ())), preferred_element_type=F32)


def rowmean(value):
    return jnp.sum(value, axis=-1, keepdims=True) * (1.0 / value.shape[-1])


def here():
    d, f = lax.axis_index("dp"), lax.axis_index("fsdp")
    return d // 2, d % 2, f // 2, f % 2


def at(x, c, z, y):
    return (x * 2 + c, z * 2 + y)


def attend_forward(qkv, ctx, lse, lengths, i, span, width, size):
    pairs = width // (2 * size)
    wide = 2 * size
    s, hp = i // pairs, i % pairs
    rows = pl.ds(pl.multiple_of(s * span, span), span)

    def part(p):
        return qkv[rows, pl.ds(pl.multiple_of(p * width + hp * wide, wide), wide)]

    q, k, v = part(0), part(1), part(2)
    lane = lax.broadcasted_iota(jnp.int32, (span, wide), 1)
    slot = lax.broadcasted_iota(jnp.int32, (span, wide), 0)
    fill = jnp.where(slot < lengths[s], 0.0, NEG).astype(BF16)
    vt = v.T
    vrow = lax.broadcasted_iota(jnp.int32, (wide, span), 0)
    factor = size ** (-0.5) * LOG2E
    halves, sums = [], []
    for h in range(2):
        mine = lane < size if h == 0 else lane >= size
        other = (1 - h) * size
        qh = jnp.where(mine, q, jnp.where(lane == other, 1.0, 0.0).astype(BF16))
        kh = jnp.where(mine, k, fill)
        scores = nt(kh, qh)
        top = jnp.max(scores, axis=0, keepdims=True)
        e = jnp.exp2((scores - top) * factor).astype(BF16)
        vmine = vrow < size if h == 0 else vrow >= size
        vh = jnp.where(vmine, vt, jnp.ones_like(vt))
        o = nn(vh, e)
        total = o[other : other + 1, :]
        halves.append(o[h * size : (h + 1) * size, :] / total)
        sums.append(top * factor + jnp.log2(total))
    ct = jnp.concatenate(halves, axis=0)
    ctx[rows, pl.ds(pl.multiple_of(hp * wide, wide), wide)] = ct.T.astype(BF16)
    lse[i] = jnp.concatenate(sums + [jnp.zeros((6, span), F32)], axis=0)


class Gather:
    def __init__(self, buf, send, recv, split):
        self.buf, self.send, self.recv = buf, send, recv
        self.nz, _, self.r, self.cols = buf.shape
        self.x, self.c, self.z, self.y = here()
        self.half = self.cols // 2
        self.split = split
        self.base = {"z": 0}
        total = 0
        for kind, count in (("z", self.nz), ("xo", self.nz), ("ya1", self.nz), ("ya2", self.nz), ("xa", self.nz), ("co", self.nz), ("cx", self.nz)):
            self.base[kind] = total
            total += count

    def region(self, kind, k, sender):
        x, c, z, y = sender
        zk = lax.rem(self.z + self.nz - k, self.nz)
        if kind == "z":
            zk = z
        row = pl.ds(pl.multiple_of(x * (self.r // 2), 16), self.r // 2)
        every = pl.ds(0, self.r)
        c0 = c * self.half
        first = pl.ds(pl.multiple_of(c0, 128), self.split)
        second = pl.ds(pl.multiple_of(c0 + self.split, 128), self.half - self.split)
        both = pl.ds(pl.multiple_of(c0, 128), self.half)
        yy, rr, cc = {
            "z": (y, row, both),
            "xo": (y, row, both),
            "ya1": (y, every, first),
            "ya2": (y, row, second),
            "xa": (1 - y, row, second),
            "co": (y, every, both),
            "cx": (1 - y, every, both),
        }[kind]
        return self.buf.at[zk, yy, rr, cc]

    def peer(self, kind, k):
        x, c, z, y = self.x, self.c, self.z, self.y
        if kind == "z":
            return x, c, lax.rem(z + k, self.nz), y
        if kind in ("xo", "xa"):
            return 1 - x, c, z, y
        if kind in ("ya1", "ya2"):
            return x, c, z, 1 - y
        return x, 1 - c, z, y

    def copy(self, kind, k, incoming):
        me = (self.x, self.c, self.z, self.y)
        peer = self.peer(kind, k)
        sender = me
        if incoming:
            sender = (self.x, self.c, lax.rem(self.z + self.nz - k, self.nz), self.y) if kind == "z" else peer
        ref = self.region(kind, k, sender)
        n = self.base[kind] + k
        return pltpu.make_async_remote_copy(
            src_ref=ref, dst_ref=ref, send_sem=self.send.at[n], recv_sem=self.recv.at[n], device_id=at(*peer), device_id_type=MESH
        )

    def go(self, kind, k):
        self.copy(kind, k, False).start()

    def got(self, kind, k):
        self.copy(kind, k, True).wait_recv()

    def start_z(self):
        for k in range(1, self.nz):
            self.go("z", k)

    def steps(self):
        out = []
        ks = range(1, self.nz)

        def s0():
            self.go("ya1", 0)
            self.go("ya2", 0)

        out.append(s0)

        def s1(k):
            self.got("z", k)
            self.go("xo", k)
            self.go("ya2", k)

        for k in ks:
            out.append(functools.partial(s1, k))

        def s2():
            self.got("ya2", 0)
            self.go("xa", 0)

        out.append(s2)

        def s3(k):
            self.got("xo", k)
            self.go("ya1", k)
            self.go("co", k)
            self.got("ya2", k)
            self.go("xa", k)

        for k in ks:
            out.append(functools.partial(s3, k))

        def s4(k):
            self.got("ya1", k)
            self.got("xa", k)
            self.go("cx", k)

        for k in range(self.nz):
            out.append(functools.partial(s4, k))
        return out

    def finish(self):
        for k in range(1, self.nz):
            self.got("co", k)
        for k in range(self.nz):
            self.got("cx", k)

    def drain(self):
        for kind in ("z", "xo", "ya1", "ya2", "xa", "co", "cx"):
            for k in range(self.nz):
                if k == 0 and kind in ("z", "xo", "co"):
                    continue
                self.copy(kind, k, False).wait_send()


def gelu_both(value):
    cdf = 0.5 + 0.5 * lax.erf(value * (0.5**0.5))
    bell = jnp.exp2(value * value * (-0.5 * LOG2E)) * (1.0 / math.sqrt(2.0 * math.pi))
    return value * cdf, cdf + value * bell


def place(sm, f, part, width):
    row = lax.broadcasted_iota(jnp.int32, (128, width), 0)
    col = lax.broadcasted_iota(jnp.int32, (128, width), 1)
    return jnp.where((col == row + f * part) & (row < part), 1.0, 0.0).astype(BF16)


def forward_kernel(comm, tokens_h, lengths, wqkv_h, wout_h, winner_h, wouter_h, wpool_h, smalls_h,
                   out_h, w1_h, w2_h, w3_h, vec_o, ib_o, qkv_h, ctx_h, lse_o, hid_h, u1_h, act_h, dg_h, u2_h, inv_o, first_o,
                   tokens, w1, w2, w3, sm, qkv, ctx, hid, hidlow, u1, act, dg, u2, outv,
                   loc, s_sm, r_sm, s1, r1, s2, r2, s3, r3):
    x, c, z, y = here() if comm else (0, 0, 0, 0)
    nz = w1.shape[0]
    rows, width = tokens.shape
    span = rows // lengths.shape[0]
    ff = act.shape[1]
    size = width // HEADS
    pairs = HEADS // 2
    d3 = 3 * width
    fr = wouter_h.shape[0] if comm else w3.shape[2] - w1.shape[2]

    if comm:
        barrier = pltpu.get_barrier_semaphore()
        peers = [(x, c, lax.rem(z + k, nz), yy) for k in range(1, nz) for yy in (y, 1 - y)]
        peers += [(x, c, z, 1 - y), (1 - x, c, z, y), (x, 1 - c, z, y)]
        local = []

        def bring(n, src, dst):
            copy = pltpu.make_async_copy(src, dst, loc.at[n])
            copy.start()
            local.append(copy)

        f_me = z * 2 + y
        bring(0, wqkv_h, w1.at[z, y])
        bring(1, smalls_h, sm.at[f_me])
        bring(2, wout_h, w2.at[z, y, :, pl.ds(0, width)])
        bring(3, winner_h, w2.at[z, y, :, pl.ds(width, ff)])
        bring(4, wouter_h, w3.at[z, y, pl.ds(0, fr)])
        bring(5, wpool_h, w3.at[z, y, pl.ds(fr, wpool_h.shape[0])])
        bring(6, tokens_h, tokens)
        for p in peers:
            pl.semaphore_signal(barrier, inc=1, device_id=at(*p), device_id_type=MESH)
        pl.semaphore_wait(barrier, len(peers))
        g1 = Gather(w1, s1, r1, 512)
        g2 = Gather(w2, s2, r2, 640)
        g3 = Gather(w3, s3, r3, 128)
        local[0].wait()
        g1.start_z()
        local[1].wait()
        others = [p for p in peers[:-2]]

        def small(n, slot):
            px, pc, pz, py = others[n]
            return pltpu.make_async_remote_copy(
                src_ref=sm.at[slot], dst_ref=sm.at[slot], send_sem=s_sm.at[n], recv_sem=r_sm.at[n], device_id=at(px, pc, pz, py), device_id_type=MESH
            )

        for n in range(len(others)):
            small(n, f_me).start()
        todo = g1.steps()
        for n, step in enumerate(todo):
            step()
            if n == 4:
                local[2].wait()
                local[3].wait()
                g2.start_z()
        local[4].wait()
        local[5].wait()
        g3.start_z()
        for n in range(len(others)):
            if n < 2 * (nz - 1):
                k, same = n // 2 + 1, n % 2 == 0
                slot = lax.rem(z + nz - k, nz) * 2 + (y if same else 1 - y)
            else:
                slot = z * 2 + 1 - y
            small(n, slot).wait_recv()
        local[6].wait()
        g1.finish()
        steps2, steps3 = g2.steps(), g3.steps()
    else:
        steps2, steps3 = [], []
        for n, (a, b) in enumerate(((tokens_h, tokens), (w1_h, w1), (w2_h, w2), (w3_h, w3), (smalls_h, sm))):
            cp = pltpu.make_async_copy(a, b, loc.at[n])
            cp.start()
            cp.wait()

    nf = nz * 2
    part = width // nf
    vec = jnp.zeros((sm.shape[1], width), F32)
    for f in range(nf):
        vec += nn(sm[f], place(None, f, part, width))
    vec_o[...] = vec
    ibs = []
    for f in range(nf):
        piece = sm[f].astype(F32)
        for j in range(ff // nf // 128):
            ibs.append(piece[12 + j : 13 + j, :])
    ib_o[...] = jnp.broadcast_to(jnp.concatenate(ibs, axis=1), ib_o.shape)

    out_copies = []

    def save(src, dst):
        cp = pltpu.make_async_copy(src, dst, loc.at[8 + len(out_copies)])
        cp.start()
        out_copies.append(cp)

    if comm:
        save(w1, w1_h)

    tile = rows // nz
    zero_row = jnp.zeros((1, width), F32)
    biases = (vec_o[0:1, :], zero_row, vec_o[1:2, :])

    def project(i, _):
        r = pl.ds(pl.multiple_of(i * tile, tile), tile)
        t = tokens[r, :]
        for p in range(3):
            w = w1[:, :, :, p * width : (p + 1) * width].reshape(width, width)
            qkv[r, p * width : (p + 1) * width] = (nn(t, w) + biases[p]).astype(BF16)
        for n, step in enumerate(steps2[:4]):
            pl.when(i == n)(step)
        return 0

    lax.fori_loop(0, rows // tile, project, 0)
    save(qkv, qkv_h)

    def attention(i, _):
        attend_forward(qkv, ctx, lse_o, lengths, i, span, width, size)
        for n, step in enumerate(steps2[4:]):
            pl.when(i == n)(step)
        for n, step in enumerate(steps3[:4]):
            pl.when(i == n + 8)(step)
        return 0

    lax.fori_loop(0, (rows // span) * pairs, attention, 0)
    save(ctx, ctx_h)
    if comm:
        g2.finish()
        save(w2, w2_h)

    b_out, g_first, s_first, b_outer, g_second, s_second = (vec_o[n : n + 1, :] for n in range(2, 8))

    def stage_one(i, _):
        r = pl.ds(pl.multiple_of(i * tile, tile), tile)
        w = w2[:, :, :, :width].reshape(width, width)
        resid = tokens[r, :].astype(F32) + (nn(ctx[r, :], w) + b_out)
        centred = resid - rowmean(resid)
        inv = lax.rsqrt(rowmean(centred * centred) + EPS)
        unit = centred * inv
        u1[r, :] = unit.astype(BF16)
        inv_o[0, r, :] = jnp.broadcast_to(inv, (tile, 128))
        h = unit * g_first + s_first
        hid[r, :] = h
        low = h.astype(BF16)
        hidlow[r, :] = low
        for b in range(ff // width):
            cols = pl.ds(b * width, width)
            w = w2[:, :, :, (b + 1) * width : (b + 2) * width].reshape(width, width)
            a, g = gelu_both(nn(low, w) + ib_o[0:1, b * width : (b + 1) * width])
            act[r, cols] = a.astype(BF16)
            dg[i, :, :, b * width : (b + 1) * width] = g.astype(BF16).reshape(2, tile // 2, width)
        for n in range(rows // tile):
            for step in steps3[4 + 2 * n : 6 + 2 * n]:
                pl.when(i == n)(step)
        return 0

    lax.fori_loop(0, rows // tile, stage_one, 0)
    save(u1, u1_h)
    save(hidlow, hid_h)
    save(act, act_h)
    save(dg, dg_h)
    if comm:
        g3.finish()
        save(w3, w3_h)

    def stage_two(i, _):
        r = pl.ds(pl.multiple_of(i * tile, tile), tile)
        w = w3[:, :, :fr, :].reshape(ff, width)
        resid = hid[r, :] + (nn(act[r, :], w) + b_outer)
        centred = resid - rowmean(resid)
        inv = lax.rsqrt(rowmean(centred * centred) + EPS)
        unit = centred * inv
        u2[r, :] = unit.astype(BF16)
        inv_o[1, r, :] = jnp.broadcast_to(inv, (tile, 128))
        layer = unit * g_second + s_second
        each = span // tile
        s, j = i // each, i % each

        @pl.when(j == 0)
        def _():
            first_o[pl.ds(pl.multiple_of(s * 8, 8), 8), :] = layer[0:8, :]

        slot = lax.broadcasted_iota(jnp.int32, (tile, width), 0) + j * tile
        outv[r, :] = jnp.where(slot < lengths[s], layer, 0.0).astype(BF16)
        return 0

    lax.fori_loop(0, rows // tile, stage_two, 0)
    save(u2, u2_h)
    save(outv, out_h)
    for cp in out_copies:
        cp.wait()
    if comm:
        for n in range(len(others)):
            small(n, f_me).wait_send()
        for g in (g1, g2, g3):
            g.drain()


def forward(tokens, lengths, wqkv, wout, winner, wouter, wpool, smalls, nz, gathered=None):
    rows, width = tokens.shape
    comm = gathered is None
    span = rows // lengths.shape[0]
    nf = nz * 2
    ff = winner.shape[1] if comm else gathered[1].shape[3] - width
    part = width // nf
    fpart = ff // nf
    any_, vm, smem = (pl.BlockSpec(memory_space=m) for m in (pl.ANY, pltpu.VMEM, pltpu.SMEM))
    S = jax.ShapeDtypeStruct
    pairs = HEADS // 2
    outs = [
        (S((rows, width), BF16), any_),
        (S((nz, 2, part, 3 * width), BF16), any_),
        (S((nz, 2, part, width + ff), BF16), any_),
        (S((nz, 2, fpart + part, width), BF16), any_),
        (S((16, width), F32), vm),
        (S((8, ff), F32), vm),
        (S((rows, 3 * width), BF16), any_),
        (S((rows, width), BF16), any_),
        (S(((rows // span) * pairs, 8, span), F32), vm),
        (S((rows, width), BF16), any_),
        (S((rows, width), BF16), any_),
        (S((rows, ff), BF16), any_),
        (S((nz, 2, rows // (2 * nz), ff), BF16), any_),
        (S((rows, width), BF16), any_),
        (S((2, rows, 128), F32), vm),
        (S((8 * (rows // span), width), F32), vm),
    ]
    V = pltpu.VMEM
    D = pltpu.SemaphoreType.DMA
    scratch = [
        V((rows, width), BF16),
        V((nz, 2, part, 3 * width), BF16),
        V((nz, 2, part, width + ff), BF16),
        V((nz, 2, fpart + part, width), BF16),
        V((nf, 16, 128), BF16),
        V((rows, 3 * width), BF16),
        V((rows, width), BF16),
        V((rows, width), F32),
        V((rows, width), BF16),
        V((rows, width), BF16),
        V((rows, ff), BF16),
        V((nz, 2, rows // (2 * nz), ff), BF16),
        V((rows, width), BF16),
        V((rows, width), BF16),
        D((24,)), D((nf,)), D((nf,)),
        D((7 * nz,)), D((7 * nz,)), D((7 * nz,)), D((7 * nz,)), D((7 * nz,)), D((7 * nz,)),
    ]
    kern = functools.partial(forward_kernel, comm)
    params = pltpu.CompilerParams(vmem_limit_bytes=60 * 2**20, has_side_effects=True, **({"collective_id": 0} if comm else {}))
    flops = 2 * rows * width * (4 * width + 2 * ff)
    cost = pl.CostEstimate(flops=flops, bytes_accessed=10**7, transcendentals=0)
    if comm:
        args = (tokens, lengths, wqkv, wout, winner, wouter, wpool, smalls)
        return pl.pallas_call(kern, out_shape=[o[0] for o in outs], out_specs=[o[1] for o in outs],
                              in_specs=[any_, smem] + [any_] * 6, scratch_shapes=scratch, compiler_params=params, cost_estimate=cost)(*args)

    def solo(tokens_h, lengths, w1_h, w2_h, w3_h, smalls_h, *rest):
        o = rest[: len(outs)]
        forward_kernel(False, tokens_h, lengths, None, None, None, None, None, smalls_h, o[0], w1_h, w2_h, w3_h, *o[4:], *rest[len(outs):])

    return pl.pallas_call(solo, out_shape=[o[0] for o in outs], out_specs=[o[1] for o in outs],
                          in_specs=[any_, smem] + [any_] * 4, scratch_shapes=scratch, compiler_params=params, cost_estimate=cost)(
        tokens, lengths, *gathered, smalls)


def attend_backward(kv, gctx, lse, lengths, s, hp, span, width, size):
    wide = 2 * size
    pairs = width // wide
    rows = pl.ds(pl.multiple_of(s * span, span), span)

    def cols(p):
        return pl.ds(pl.multiple_of(p * width + hp * wide, wide), wide)

    q, k, v = (kv[rows, cols(p)] for p in range(3))
    g = gctx[rows, cols(0)]
    logs = lse[s * pairs + hp]
    lane = lax.broadcasted_iota(jnp.int32, (span, wide), 1)
    slot = lax.broadcasted_iota(jnp.int32, (span, wide), 0)
    fill = jnp.where(slot < lengths[s], 0.0, NEG).astype(BF16)
    scale = size ** (-0.5)
    factor = scale * LOG2E
    kt = k.T
    gqs, gks, gvs = [], [], []
    for h in range(2):
        mine = lane < size if h == 0 else lane >= size
        other = (1 - h) * size
        qh = jnp.where(mine, q, jnp.where(lane == other, 1.0, 0.0).astype(BF16))
        kh = jnp.where(mine, k, fill)
        vh = jnp.where(mine, v, jnp.zeros_like(v))
        p = jnp.exp2(nt(kh, qh) * factor - logs[h : h + 1, :])
        gvs.append(nn(p.astype(BF16), g))
        gp = nt(vh, g)
        delta = jnp.sum(gp * p, axis=0, keepdims=True)
        gs = (p * (gp - delta)).astype(BF16)
        gks.append(nn(gs, q))
        gqs.append(nn(kt, gs)[h * size : (h + 1) * size, :])
    kv[rows, cols(0)] = (jnp.concatenate(gqs, axis=0).T * scale).astype(BF16)
    kv[rows, cols(1)] = (jnp.where(lane < size, gks[0], gks[1]) * scale).astype(BF16)
    kv[rows, cols(2)] = jnp.where(lane < size, gvs[0], gvs[1]).astype(BF16)


class Spread:
    def __init__(self, buf, send, recv):
        self.buf, self.send, self.recv = buf, send, recv
        self.nz = buf.shape[3]
        self.me = here()

    def copy(self, n, incoming):
        x, c, z, y = self.me
        nz = self.nz
        if n < nz - 1:
            k = n + 1
            peer = (x, c, lax.rem(z + k, nz), y)
            ref = self.buf.at[x, c, y, lax.rem(z + nz - k, nz) if incoming else z]
        elif n == nz - 1:
            peer = (x, c, z, 1 - y)
            ref = self.buf.at[x, c, 1 - y if incoming else y]
        elif n == nz:
            peer = (1 - x, c, z, y)
            ref = self.buf.at[1 - x if incoming else x, c]
        else:
            peer = (x, 1 - c, z, y)
            ref = self.buf.at[:, 1 - c if incoming else c]
        return pltpu.make_async_remote_copy(
            src_ref=ref, dst_ref=ref, send_sem=self.send.at[n], recv_sem=self.recv.at[n], device_id=at(*peer), device_id_type=MESH
        )

    def step(self, j):
        nz = self.nz
        if j == 0:
            for n in range(nz - 1):
                self.copy(n, False).start()
            return
        if j == 1:
            for n in range(nz - 1):
                self.copy(n, True).wait_recv()
        else:
            self.copy(nz + j - 3, True).wait_recv()
        if j < 4:
            self.copy(nz + j - 2, False).start()

    def drain(self):
        for n in range(self.nz + 2):
            self.copy(n, False).wait_send()


class Scatter:
    def __init__(self, refs, out, send, recv):
        self.g, self.r1, self.ry1, self.rx1, self.rx2, self.ry2, self.rz = refs
        self.out, self.send, self.recv = out, send, recv
        self.nz, _, self.r, self.cols = self.g.shape
        self.x, self.c, self.z, self.y = here()
        half = self.cols // 2
        a1 = self.ry1.shape[-1]
        r2 = self.r // 2
        self.rows = pl.ds(pl.multiple_of(self.x * r2, 16), r2)
        self.rows_o = pl.ds(pl.multiple_of((1 - self.x) * r2, 16), r2)
        self.mine = pl.ds(pl.multiple_of(self.c * half, 128), half)
        self.theirs = pl.ds(pl.multiple_of((1 - self.c) * half, 128), half)
        self.a1 = pl.ds(pl.multiple_of(self.c * half, 128), a1)
        self.a2 = pl.ds(pl.multiple_of(self.c * half + a1, 128), half - a1)

    def copy(self, n):
        x, c, z, y = self.x, self.c, self.z, self.y
        g, out = self.g, self.out
        core, xn, yn = (x, 1 - c, z, y), (1 - x, c, z, y), (x, c, z, 1 - y)
        if n == 0:
            src, dst, peer = g.at[:, :, :, self.theirs], self.r1, core
        elif n == 1:
            src, dst, peer = g.at[:, 1 - y, :, self.a1], self.ry1, yn
        elif n == 2:
            src, dst, peer = g.at[:, :, self.rows_o, self.a2], self.rx2, xn
        elif n == 3:
            src, dst, peer = g.at[:, y, self.rows_o, self.a1], self.rx1, xn
        elif n == 4:
            src, dst, peer = g.at[:, 1 - y, self.rows, self.a2], self.ry2, yn
        elif n < 4 + self.nz:
            k = n - 4
            zk = lax.rem(z + k, self.nz)
            src, dst, peer = g.at[zk, y, self.rows, self.mine], self.rz.at[k - 1], (x, c, zk, y)
        elif n == 4 + self.nz:
            src = dst = out.at[self.rows, self.mine]
            peer = xn
        else:
            src = dst = out.at[:, self.mine]
            peer = core
        return pltpu.make_async_remote_copy(
            src_ref=src, dst_ref=dst, send_sem=self.send.at[n], recv_sem=self.recv.at[n], device_id=at(*peer), device_id_type=MESH
        )

    def got(self, n):
        if n < 4 + self.nz:
            self.copy(n).wait_recv()
            return
        if n == 4 + self.nz:
            ref, peer = self.out.at[self.rows_o, self.mine], (1 - self.x, self.c, self.z, self.y)
        else:
            ref, peer = self.out.at[:, self.theirs], (self.x, 1 - self.c, self.z, self.y)
        pltpu.make_async_remote_copy(
            src_ref=ref, dst_ref=ref, send_sem=self.send.at[n], recv_sem=self.recv.at[n], device_id=at(*peer), device_id_type=MESH
        ).wait_recv()

    def step(self, j):
        g, y, nz = self.g, self.y, self.nz
        last = 4 + nz
        if j == 0:
            self.copy(0).start()
        elif j == 1:
            self.got(0)

            def add(i, _):
                for yy in range(2):
                    g[i, yy, :, self.mine] = g[i, yy, :, self.mine] + self.r1[i, yy]
                return 0

            lax.fori_loop(0, nz, add, 0)
            self.copy(1).start()
            self.copy(2).start()
        elif j == 2:
            self.got(1)

            def add(i, _):
                g[i, y, :, self.a1] = g[i, y, :, self.a1] + self.ry1[i]
                return 0

            lax.fori_loop(0, nz, add, 0)
            self.copy(3).start()
            self.got(2)

            def add(i, _):
                for yy in range(2):
                    g[i, yy, self.rows, self.a2] = g[i, yy, self.rows, self.a2] + self.rx2[i, yy]
                return 0

            lax.fori_loop(0, nz, add, 0)
            self.copy(4).start()
        elif j == 3:
            self.got(3)
            self.got(4)

            def add(i, _):
                g[i, y, self.rows, self.a1] = g[i, y, self.rows, self.a1] + self.rx1[i]
                g[i, y, self.rows, self.a2] = g[i, y, self.rows, self.a2] + self.ry2[i]
                return 0

            lax.fori_loop(0, nz, add, 0)
            for k in range(1, nz):
                self.copy(4 + k).start()
        elif j == 4:
            total = g[self.z, y, self.rows, self.mine].astype(F32)
            for k in range(1, nz):
                self.got(4 + k)
                total += self.rz[k - 1].astype(F32)
            self.out[self.rows, self.mine] = total.astype(BF16)
            self.copy(last).start()
        elif j == 5:
            self.got(last)
            self.copy(last + 1).start()
        else:
            self.got(last + 1)

    def drain(self):
        for n in range(6 + self.nz):
            self.copy(n).wait_send()


def backward_kernel(comm, lengths, labels, cb, vec, lse, first, inv_h, cot_h, tok_h, w1_h, w2_h, w3_h, qkv_h, ctx_h, hid_h, u1_h, act_h, dg_h, u2_h,
                    loss_o, own_o, ib_o, pool_o, class_o, wo_o, wi_o, wu_o, wq_o, tg_h,
                    A, D, w2, w3, cot, u2, u1, hid, gffn, gr, inv, acc, gfirst,
                    G, R1, Ry1, Rx1, Rx2, Ry2, Rz, early, late, loc, free, s_rs, r_rs, s_sp, r_sp):
    x, c, z, y = here() if comm else (0, 0, 0, 0)
    rows, width = cot.shape
    seqs = lengths.shape[0]
    span = rows // seqs
    ff = A.shape[1]
    size = width // HEADS
    nz = D.shape[0]
    tile = rows // nz
    nb = ff // width
    part = width // (2 * nz)
    fr = ff // (2 * nz)
    loads = {}

    def load(name, src, dst):
        cp = pltpu.make_async_copy(src, dst, loc.at[len(loads)])
        cp.start()
        loads[name] = cp

    load("cot", cot_h, cot)
    load("u2", u2_h, u2)
    load("inv2", inv_h.at[1], inv)
    load("w3", w3_h, w3)
    load("act", act_h, A)
    load("dg", dg_h, D)
    load("hid", hid_h, hid)
    load("w2", w2_h, w2)
    load("u1", u1_h, u1)

    if comm:
        barrier = pltpu.get_barrier_semaphore()
        peers = [(x, c, lax.rem(z + k, nz), y) for k in range(1, nz)]
        peers += [(x, c, z, 1 - y), (1 - x, c, z, y), (x, 1 - c, z, y)]
        for p in peers:
            pl.semaphore_signal(barrier, inc=1, device_id=at(*p), device_id_type=MESH)
        pl.semaphore_wait(barrier, len(peers))

        def outer_out(b):
            return wu_o.at[pl.ds(pl.multiple_of(b * part, 16), part), :]

        def inner_out(b):
            return wi_o.at[:, pl.ds(pl.multiple_of(b * width, 128), width)]

        def block(n, out):
            return Scatter([G.at[n], R1.at[n], Ry1.at[n], Rx1.at[n], Rx2.at[n], Ry2.at[n], Rz.at[n]], out, s_rs.at[n], r_rs.at[n])

        def late_block(q):
            n = 2 * nb + q
            h, t, e, hr = width // 2, width // 3, width // 6, part // 2
            refs = [
                D.at[:, :, pl.ds(0, part), pl.ds(q * width, width)],
                w2.at[:, :, :, pl.ds(q * h, h)],
                w2.at[:, 0, :, pl.ds(2 * width + q * t, t)],
                w2.at[:, 1, pl.ds(0, hr), pl.ds(2 * width + q * t, t)],
                w2.at[:, :, pl.ds(0, hr), pl.ds(2 * width + 4 * t + q * e, e)],
                w2.at[:, 1, pl.ds(hr, hr), pl.ds(2 * width + q * e, e)],
                w2.at[pl.ds(0, nz - 1), q // 2, pl.ds(hr, hr), pl.ds(2 * width + 4 * t + (q % 2) * h, h)],
            ]
            return Scatter(refs, wo_o if q == 0 else wq_o.at[q - 1], s_rs.at[n], r_rs.at[n])

        def each(first_block, count, make, j):
            def body(b, _):
                block(first_block + b, make(b)).step(j)
                return 0

            lax.fori_loop(0, count, body, 0)

        early_ag = Spread(early, s_sp.at[0], r_sp.at[0])
        late_ag = Spread(late, s_sp.at[1], r_sp.at[1])

        def step(name, j):
            if name == "outer":
                each(0, nb, outer_out, j)
            elif name == "inner0":
                each(nb, nb // 2, inner_out, j)
            elif name == "inner1":
                each(nb + nb // 2, nb // 2, lambda b: inner_out(b + nb // 2), j)
            elif name == "out":
                late_block(0).step(j)
            elif name == "early":
                early_ag.step(j)
            elif name == "late":
                late_ag.step(j)
            else:
                late_block(name + 1).step(j)
    else:
        def step(name, j):
            pass

    def steps(*pairs):
        for name, j in pairs:
            step(name, j)

    def hooks(i, table):
        for n, pairs in enumerate(table):
            if pairs and comm:
                pl.when(i == n)(functools.partial(steps, *pairs))

    acc[...] = jnp.zeros_like(acc)

    loads["w3"].wait()
    lane = lax.broadcasted_iota(jnp.int32, (8 * seqs, 128), 1)
    row = lax.broadcasted_iota(jnp.int32, (8 * seqs, 128), 0)
    live = (lane >= 1) & (lane < 4)
    w_pool = w3[:, :, fr:, :].reshape(width, width)
    first_low = first[...].astype(BF16)
    pooled = jnp.tanh(nn(first_low, w_pool) + vec[8:9, :])
    pooled_low = pooled.astype(BF16)
    heads = jnp.concatenate([vec[8:16, :], jnp.zeros((120, width), F32)], axis=0).astype(BF16)
    logits = nt(pooled_low, heads) + cb[0:1, :]
    peak = jnp.max(jnp.where(live, logits, -3.0e38), axis=-1, keepdims=True)
    mass = jnp.where(live, jnp.exp(logits - peak), 0.0)
    logsum = peak + jnp.log(jnp.sum(mass, axis=-1, keepdims=True))
    label = jnp.full((8 * seqs, 128), labels[0])
    for s in range(1, seqs):
        label = jnp.where(row >= 8 * s, labels[s], label)
    onehot = jnp.where(lane == label + 1, 1.0, 0.0)
    loss_o[...] = jnp.broadcast_to(logsum - jnp.sum(onehot * logits, axis=-1, keepdims=True), loss_o.shape)
    g_logits = jnp.where(live & (row % 8 == 0), jnp.exp(logits - logsum) - onehot, 0.0).astype(BF16)
    g_pre = (nn(g_logits, heads) * (1.0 - pooled * pooled)).astype(BF16)
    gfirst[...] = nt(g_pre, w_pool)

    loads["cot"].wait()
    loads["u2"].wait()
    loads["inv2"].wait()
    gain2, gain1 = vec[6:7, :], vec[3:4, :]

    def colsum(v):
        return jnp.sum(v, axis=0, keepdims=True)

    per = span // tile

    def second_norm(i, _):
        r = pl.ds(pl.multiple_of(i * tile, tile), tile)
        s, j = i // per, i % per
        slot = lax.broadcasted_iota(jnp.int32, (tile, width), 0) + j * tile
        gl = jnp.where(slot < lengths[s], cot[r, :].astype(F32), 0.0)
        head = gfirst[pl.ds(pl.multiple_of(8 * s, 8), 8), :] * jnp.where(j == 0, 1.0, 0.0)
        gl = gl + jnp.concatenate([head, jnp.zeros((tile - 8, width), F32)], axis=0)
        u = u2[r, :].astype(F32)
        a = gl * gain2
        iv = inv[r, :]
        g2 = (a - rowmean(a) - u * rowmean(a * u)) * iv[:, :1]
        gr[r, :] = g2
        low = g2.astype(BF16)
        gffn[r, :] = low
        acc[3:4, :] += colsum(low.astype(F32))
        acc[4:5, :] += colsum(gl * u)
        acc[5:6, :] += colsum(gl)
        return 0

    lax.fori_loop(0, rows // tile, second_norm, 0)
    load("tok", tok_h, u2)
    load("inv1", inv_h.at[0], inv)

    loads["act"].wait()

    def outer_grad(f, _):
        part_of = tn(A[:, pl.ds(pl.multiple_of(f * fr, 128), fr)], gffn[...]).astype(BF16)
        for b in range(nb):
            G[b, f // 2, f % 2] = part_of[b * part : (b + 1) * part, :]
        return 0

    lax.fori_loop(0, 2 * nz, outer_grad, 0)
    load("qkv", qkv_h, A.at[:, pl.ds(0, 3 * width)])
    load("ctx", ctx_h, A.at[:, pl.ds(3 * width, width)])
    steps(("outer", 0))

    loads["dg"].wait()

    def inner_back(i, _):
        r = pl.ds(pl.multiple_of(i * tile, tile), tile)
        for b in range(nb):
            cols = slice(b * width, (b + 1) * width)
            w = w3[b, :, :fr, :].reshape(width, width)
            g = nt(gffn[r, :], w) * D[i, :, :, cols].reshape(tile, width).astype(F32)
            low = g.astype(BF16)
            D[i, :, :, cols] = low.reshape(2, tile // 2, width)
            acc[6 + b : 7 + b, :] += colsum(low.astype(F32))
        hooks(i, [[], [], [("outer", 1)]])
        return 0

    lax.fori_loop(0, rows // tile, inner_back, 0)
    for p in range(3):
        load(("w1", p), w1_h.at[:, :, :, pl.ds(p * width, width)], w3.at[:, :, pl.ds(p * part, part), :])

    loads["hid"].wait()

    def inner_grad(b, _):
        cols = pl.ds(pl.multiple_of(b * width, width), width)
        for m in range(2):
            h = width // 2
            got = tn(hid[:, m * h : (m + 1) * h], D[:, :, :, cols].reshape(rows, width)).astype(BF16)
            G[nb + b, m * nz // 2 : (m + 1) * nz // 2] = got.reshape(nz // 2, 2, part, width)
        hooks(b, [[], [("inner0", 0), ("outer", 2)], [], [("inner1", 0), ("inner0", 1)]])
        return 0

    lax.fori_loop(0, nb, inner_grad, 0)

    loads["w2"].wait()
    loads["u1"].wait()
    loads["inv1"].wait()

    def first_norm(i, _):
        r = pl.ds(pl.multiple_of(i * tile, tile), tile)
        gh = gr[r, :]
        for b in range(nb):
            w = w2[:, :, :, (b + 1) * width : (b + 2) * width].reshape(width, width)
            gh += nt(D[i, :, :, b * width : (b + 1) * width].reshape(tile, width), w)
        u = u1[r, :].astype(F32)
        a = gh * gain1
        iv = inv[r, :]
        g1 = (a - rowmean(a) - u * rowmean(a * u)) * iv[:, :1]
        gr[r, :] = g1
        low = g1.astype(BF16)
        cot[r, :] = low
        acc[0:1, :] += colsum(low.astype(F32))
        acc[1:2, :] += colsum(gh * u)
        acc[2:3, :] += colsum(gh)
        w = w2[:, :, :, :width].reshape(width, width)
        gffn[r, :] = nt(low, w).astype(BF16)
        hooks(i, [[("outer", 3)], [("inner1", 1)], [("inner0", 2)], [("outer", 4)]])
        return 0

    lax.fori_loop(0, rows // tile, first_norm, 0)
    if comm:
        for p in peers:
            pl.semaphore_signal(free, inc=1, device_id=at(*p), device_id_type=MESH)
        pay = jnp.concatenate(
            [acc[0:10, :]]
            + [first_low[8 * s : 8 * s + 1, :].astype(F32) for s in range(seqs)]
            + [g_pre[8 * s : 8 * s + 1, :].astype(F32) for s in range(seqs)]
            + [pooled_low[8 * s : 8 * s + 1, :].astype(F32) for s in range(seqs)],
            axis=0,
        )
        early[x, c, y, z] = pay.astype(BF16)

    loads["ctx"].wait()
    loads["qkv"].wait()
    for m in range(2):
        h = width // 2
        got = tn(A[:, 3 * width + m * h : 3 * width + (m + 1) * h], cot[...]).astype(BF16)
        D[m * nz // 2 : (m + 1) * nz // 2, :, :part, :width] = got.reshape(nz // 2, 2, part, width)
    if comm:
        pl.semaphore_wait(free, len(peers))
    steps(("out", 0), ("early", 0), ("inner1", 2), ("inner0", 3))

    loads["tok"].wait()
    groups = 3
    pairs = HEADS // 2
    gp = pairs // groups
    wide = gp * 2 * size
    tables = [
        [[("out", 1)], [("inner0", 4), ("early", 1)], [("inner1", 3), ("out", 2)], [("inner1", 4), ("early", 2)]],
        [[(0, 1), ("early", 3)], [("out", 3)], [(0, 2)], [("out", 4), ("early", 4)]],
        [[(1, 1), (0, 3)], [("outer", 5), ("inner0", 5)], [(1, 2), (0, 4)], [("inner1", 5), ("out", 5)]],
    ]
    for q in range(groups):
        def attention(i, _):
            attend_backward(A, gffn, lse, lengths, i // gp, q * gp + i % gp, span, width, size)
            hooks(i, tables[q])
            return 0

        lax.fori_loop(0, seqs * gp, attention, 0)
        for p in range(3):
            block_of = A[:, p * width + q * wide : p * width + (q + 1) * wide]
            got = tn(u2[...], block_of).astype(BF16)
            D[:, :, :part, (q + 1) * width + p * wide : (q + 1) * width + (p + 1) * wide] = got.reshape(nz, 2, part, wide)
            if p != 1:
                acc[10 + p // 2 : 11 + p // 2, q * wide : (q + 1) * wide] = colsum(block_of.astype(F32))
        steps((q, 0))
    if comm:
        tilerows = [acc[10 + n : 11 + n, j * 128 : (j + 1) * 128] for n in range(2) for j in range(width // 128)]
        tilerows += [g_logits[8 * s : 8 * s + 1, :].astype(F32) for s in range(seqs)]
        tilerows.append(jnp.zeros((16 - len(tilerows), 128), F32))
        late[x, c, y, z] = jnp.concatenate(tilerows, axis=0).astype(BF16)
    steps(("late", 0))

    for p in range(3):
        loads[("w1", p)].wait()

    def input_grad(i, _):
        r = pl.ds(pl.multiple_of(i * tile, tile), tile)
        g = gr[r, :]
        for p in range(3):
            w = w3[:, :, p * part : (p + 1) * part, :].reshape(width, width)
            g += nt(A[r, p * width : (p + 1) * width], w)
        cot[r, :] = g.astype(BF16)
        hooks(i, [[(2, 1), (1, 3), ("late", 1)], [(2, 2), ("late", 2), (1, 4)], [(0, 5), ("late", 3), (2, 3)], [(2, 4), (1, 5), ("late", 4)]])
        return 0

    lax.fori_loop(0, rows // tile, input_grad, 0)
    back = pltpu.make_async_copy(cot, tg_h, loc.at[len(loads)])
    back.start()
    if comm:
        n = 4 * 2 * nz
        def slot_of(i):
            return (i // (4 * nz), i // (2 * nz) % 2, i // nz % 2, i % nz)

        total = lax.fori_loop(0, n, lambda i, t: t + early[slot_of(i)].astype(F32), jnp.zeros((16, width), F32))
        lates = late[...].reshape(n, 16, 128)
        lsum = jnp.sum(lates.astype(F32), axis=0)
        six = width // 128
        qb = jnp.concatenate([lsum[j : j + 1, :] for j in range(six)], axis=1)
        vb = jnp.concatenate([lsum[six + j : six + j + 1, :] for j in range(six)], axis=1)
        r16 = lax.broadcasted_iota(jnp.int32, (16, width), 0)
        total = jnp.where(r16 == 10, qb, jnp.where(r16 == 11, vb, total))
        f = z * 2 + y
        src = lax.broadcasted_iota(jnp.int32, (width, 128), 0)
        dst = lax.broadcasted_iota(jnp.int32, (width, 128), 1)
        pick = jnp.where((src == dst + f * part) & (dst < part), 1.0, 0.0).astype(BF16)
        src = lax.broadcasted_iota(jnp.int32, (width, fr), 0)
        dst = lax.broadcasted_iota(jnp.int32, (width, fr), 1)
        pick_ff = jnp.where(src == dst + y * fr, 1.0, 0.0).astype(BF16)
        high = total.astype(BF16)
        rest = (total - high.astype(F32)).astype(BF16)
        own = nn(high, pick) + nn(rest, pick)
        wide_own = nn(high, pick_ff) + nn(rest, pick_ff)
        r16f = lax.broadcasted_iota(jnp.int32, (16, fr), 0)
        ib_o[...] = jnp.broadcast_to(colsum(jnp.where(r16f == 6 + z, wide_own, 0.0)), ib_o.shape)
        flat = early[...].reshape(n * 16, width)
        chosen = nn(flat, pick)
        rid = lax.broadcasted_iota(jnp.int32, (n * 16, 128), 0) % 16
        firsts = pltpu.roll(jnp.where((rid >= 10) & (rid < 10 + seqs), chosen, 0.0), seqs, 0).astype(BF16)
        pool_o[...] = tn(firsts, flat)
        pooleds = pltpu.roll(jnp.where(rid >= 10 + 2 * seqs, chosen, 0.0), n * 16 - seqs, 0).astype(BF16)
        class_o[...] = tn(pooleds, lates.reshape(n * 16, 128))
        middle = (rid >= 10 + seqs) & (rid < 10 + 2 * seqs)
        pb = colsum(jnp.where(middle, chosen, 0.0))
        cbg = colsum(jnp.where(middle, lates.reshape(n * 16, 128).astype(F32), 0.0))
        r16s = lax.broadcasted_iota(jnp.int32, (16, 128), 0)
        own_o[...] = jnp.where(r16s == 12, pb, jnp.where(r16s == 13, cbg, own))
        steps((2, 5), ("outer", 6), ("inner0", 6), ("inner1", 6), ("out", 6), (0, 6), (1, 6), (2, 6))
        early_ag.drain()
        late_ag.drain()

        def finish(b, _):
            block(b, wo_o).drain()
            return 0

        lax.fori_loop(0, 2 * nb, finish, 0)
        for q in range(groups + 1):
            late_block(q).drain()
    back.wait()


def backward(lengths, labels, cb, vec, lse, inv, first, cot, tok, w1, w2, w3, qkv, ctx, hid, u1, act, dg, u2, comm=True):
    rows, width = cot.shape
    nz = w1.shape[0]
    ff = act.shape[1]
    part = width // (2 * nz)
    fr = ff // (2 * nz)
    nb = ff // width
    seqs = lengths.shape[0]
    any_, vm, smem = (pl.BlockSpec(memory_space=m) for m in (pl.ANY, pltpu.VMEM, pltpu.SMEM))
    S = jax.ShapeDtypeStruct
    outs = [
        (S((8 * seqs, 128), F32), vm),
        (S((16, 128), F32), vm),
        (S((8, fr), F32), vm),
        (S((128, width), F32), vm),
        (S((128, 128), F32), vm),
        (S((part, width), BF16), vm),
        (S((part, ff), BF16), vm),
        (S((fr, width), BF16), vm),
        (S((3, part, width), BF16), vm),
        (S((rows, width), BF16), any_),
    ]
    V = pltpu.VMEM
    D = pltpu.SemaphoreType.DMA
    n = 2 * nb
    half, third = width // 2, width // 3
    scratch = [
        V((rows, ff), BF16),
        V(dg.shape, BF16),
        V((nz, 2, part, width + ff), BF16),
        V((nz, 2, fr + part, width), BF16),
        V((rows, width), BF16),
        V((rows, width), BF16),
        V((rows, width), BF16),
        V((rows, width), BF16),
        V((rows, width), BF16),
        V((rows, width), F32),
        V((rows, 128), F32),
        V((16, width), F32),
        V((8 * seqs, width), F32),
        V((n, nz, 2, part, width), BF16),
        V((n, nz, 2, part, half), BF16),
        V((n, nz, part, third), BF16),
        V((n, nz, part // 2, third), BF16),
        V((n, nz, 2, part // 2, third // 2), BF16),
        V((n, nz, part // 2, third // 2), BF16),
        V((n, nz - 1, part // 2, half), BF16),
        V((2, 2, 2, nz, 16, width), BF16),
        V((2, 2, 2, nz, 16, 128), BF16),
        D((24,)),
        pltpu.SemaphoreType.REGULAR,
        D((n + 4, nz + 6)), D((n + 4, nz + 6)), D((2, nz + 2)), D((2, nz + 2)),
    ]
    params = pltpu.CompilerParams(vmem_limit_bytes=63 * 2**20, has_side_effects=True, **({"collective_id": 1} if comm else {}))
    cost = pl.CostEstimate(flops=4 * rows * width * (4 * width + 2 * ff), bytes_accessed=10**7, transcendentals=0)
    return pl.pallas_call(
        functools.partial(backward_kernel, comm), out_shape=[o[0] for o in outs], out_specs=[o[1] for o in outs],
        in_specs=[smem, smem] + [vm] * 4 + [any_] * 13, scratch_shapes=scratch, compiler_params=params, cost_estimate=cost,
    )(lengths, labels, cb, vec, lse, first, inv, cot, tok, w1, w2, w3, qkv, ctx, hid, u1, act, dg, u2)


def normalize(value, gain, shift):
    mean = jnp.mean(value, axis=-1, keepdims=True)
    centred = value - mean
    inverse = lax.rsqrt(jnp.mean(centred * centred, axis=-1, keepdims=True) + EPS)
    unit = centred * inverse
    return (unit * gain + shift, unit, inverse)


def norm_back(grad, unit, inverse, gain):
    scaled = grad * gain
    inner = (
        scaled
        - jnp.mean(scaled, axis=-1, keepdims=True)
        - unit * jnp.mean(scaled * unit, axis=-1, keepdims=True)
    )
    return (inner * inverse, jnp.sum(grad * unit, axis=0), jnp.sum(grad, axis=0))


def matmul(left, right):
    return jnp.dot(left, right, preferred_element_type=jnp.float32)


def transposed_left(left, right):
    return lax.dot_general(
        left, right, (((0,), (0,)), ((), ())), preferred_element_type=jnp.float32
    )


def transposed_right(left, right):
    return lax.dot_general(
        left, right, (((1,), (1,)), ((), ())), preferred_element_type=jnp.float32
    )


def column_sum(values):
    return jnp.sum(values.astype(jnp.float32), axis=0)


def attend(block):
    query, key, value, keep = block
    scale = query.shape[-1] ** (-0.5)
    scores = jnp.einsum("qhd,khd->hqk", query, key, preferred_element_type=jnp.float32) * scale
    scores = jnp.where(keep[None, None, :], scores, NEG)
    top = jnp.max(scores, axis=-1, keepdims=True)
    total = jnp.sum(jnp.exp(scores - top), axis=-1, keepdims=True)
    logsum = top + jnp.log(total)
    probs = jnp.exp(scores - logsum).astype(jnp.bfloat16)
    context = jnp.einsum("hqk,khd->qhd", probs, value, preferred_element_type=jnp.float32)
    return (context.astype(jnp.bfloat16), logsum[:, :, 0])


def attend_back(block):
    query, key, value, keep, logsum, grad_context = block
    scale = query.shape[-1] ** (-0.5)
    scores = jnp.einsum("qhd,khd->hqk", query, key, preferred_element_type=jnp.float32) * scale
    scores = jnp.where(keep[None, None, :], scores, NEG)
    probs = jnp.exp(scores - logsum[:, :, None])
    grad_value = jnp.einsum(
        "hqk,qhd->khd", probs.astype(jnp.bfloat16), grad_context, preferred_element_type=jnp.float32
    )
    grad_probs = jnp.einsum("qhd,khd->hqk", grad_context, value, preferred_element_type=jnp.float32)
    delta = jnp.sum(grad_probs * probs, axis=-1, keepdims=True)
    grad_scores = (probs * (grad_probs - delta)).astype(jnp.bfloat16)
    grad_query = (
        jnp.einsum("hqk,khd->qhd", grad_scores, key, preferred_element_type=jnp.float32) * scale
    )
    grad_key = (
        jnp.einsum("hqk,qhd->khd", grad_scores, query, preferred_element_type=jnp.float32) * scale
    )
    return (
        grad_query.astype(jnp.bfloat16),
        grad_key.astype(jnp.bfloat16),
        grad_value.astype(jnp.bfloat16),
    )


def per_device_any(
    tokens,
    lengths,
    labels,
    cotangent,
    qkv_weight,
    query_bias,
    value_bias,
    out_weight,
    out_bias,
    first_gain,
    first_shift,
    inner_weight,
    inner_bias,
    outer_weight,
    outer_bias,
    second_gain,
    second_shift,
    pool_weight,
    pool_bias,
    class_weight,
    class_bias,
):
    full = (
        lax.all_gather(qkv_weight, "fsdp", axis=0, tiled=True),
        lax.all_gather(query_bias, "fsdp", axis=0, tiled=True),
        lax.all_gather(value_bias, "fsdp", axis=0, tiled=True),
        lax.all_gather(out_weight, "fsdp", axis=0, tiled=True),
        lax.all_gather(out_bias, "fsdp", axis=0, tiled=True),
        lax.all_gather(first_gain, "fsdp", axis=0, tiled=True),
        lax.all_gather(first_shift, "fsdp", axis=0, tiled=True),
        lax.all_gather(inner_weight, "fsdp", axis=0, tiled=True),
        lax.all_gather(inner_bias, "fsdp", axis=0, tiled=True),
        lax.all_gather(outer_weight, "fsdp", axis=0, tiled=True),
        lax.all_gather(outer_bias, "fsdp", axis=0, tiled=True),
        lax.all_gather(second_gain, "fsdp", axis=0, tiled=True),
        lax.all_gather(second_shift, "fsdp", axis=0, tiled=True),
        lax.all_gather(pool_weight, "fsdp", axis=0, tiled=True),
        lax.all_gather(pool_bias, "fsdp", axis=0, tiled=True),
        lax.all_gather(class_weight, "fsdp", axis=0, tiled=True),
    )
    (
        w_qkv,
        b_query,
        b_value,
        w_out,
        b_out,
        g_first,
        s_first,
        w_inner,
        b_inner,
        w_outer,
        b_outer,
        g_second,
        s_second,
        w_pool,
        b_pool,
        w_class,
    ) = full
    b_query = b_query.astype(jnp.float32)
    b_value = b_value.astype(jnp.float32)
    b_out = b_out.astype(jnp.float32)
    g_first = g_first.astype(jnp.float32)
    s_first = s_first.astype(jnp.float32)
    b_inner = b_inner.astype(jnp.float32)
    b_outer = b_outer.astype(jnp.float32)
    g_second = g_second.astype(jnp.float32)
    s_second = s_second.astype(jnp.float32)
    b_pool = b_pool.astype(jnp.float32)
    b_class = class_bias.astype(jnp.float32)
    seqs = lengths.shape[0]
    rows, width = tokens.shape
    span = rows // seqs
    size = width // HEADS
    classes = class_bias.shape[0]
    position = lax.broadcasted_iota(jnp.int32, (seqs, span), 1)
    keep = position < lengths[:, None]
    valid = keep.reshape(rows, 1).astype(jnp.float32)
    bias_all = jnp.concatenate([b_query, jnp.zeros_like(b_query), b_value])
    qkv = (matmul(tokens, w_qkv) + bias_all).astype(jnp.bfloat16)
    query = qkv[:, :width].reshape(seqs, span, HEADS, size)
    key = qkv[:, width : 2 * width].reshape(seqs, span, HEADS, size)
    value = qkv[:, 2 * width :].reshape(seqs, span, HEADS, size)
    context, logsum = lax.map(attend, (query, key, value, keep))
    context = context.reshape(rows, width)
    attended = matmul(context, w_out) + b_out
    hidden, unit_first, inverse_first = normalize(
        tokens.astype(jnp.float32) + attended, g_first, s_first
    )
    hidden_low = hidden.astype(jnp.bfloat16)
    inner = matmul(hidden_low, w_inner) + b_inner
    act = jax.nn.gelu(inner, approximate=False).astype(jnp.bfloat16)
    ffn = matmul(act, w_outer) + b_outer
    layer, unit_second, inverse_second = normalize(hidden + ffn, g_second, s_second)
    output = (layer * valid).astype(jnp.bfloat16)
    first = layer.reshape(seqs, span, width)[:, 0].astype(jnp.bfloat16)
    pooled = jnp.tanh(matmul(first, w_pool) + b_pool)
    pooled_low = pooled.astype(jnp.bfloat16)
    logits = matmul(pooled_low, w_class) + b_class
    peak = jnp.max(logits, axis=-1, keepdims=True)
    logsum_class = peak + jnp.log(jnp.sum(jnp.exp(logits - peak), axis=-1, keepdims=True))
    onehot = (labels[:, None] == lax.broadcasted_iota(jnp.int32, (seqs, classes), 1)).astype(
        jnp.float32
    )
    exit_loss = logsum_class[:, 0] - jnp.sum(onehot * logits, axis=-1)
    again = (
        lax.all_gather(qkv_weight, "fsdp", axis=0, tiled=True),
        lax.all_gather(query_bias, "fsdp", axis=0, tiled=True),
        lax.all_gather(value_bias, "fsdp", axis=0, tiled=True),
        lax.all_gather(out_weight, "fsdp", axis=0, tiled=True),
        lax.all_gather(out_bias, "fsdp", axis=0, tiled=True),
        lax.all_gather(first_gain, "fsdp", axis=0, tiled=True),
        lax.all_gather(first_shift, "fsdp", axis=0, tiled=True),
        lax.all_gather(inner_weight, "fsdp", axis=0, tiled=True),
        lax.all_gather(inner_bias, "fsdp", axis=0, tiled=True),
        lax.all_gather(outer_weight, "fsdp", axis=0, tiled=True),
        lax.all_gather(outer_bias, "fsdp", axis=0, tiled=True),
        lax.all_gather(second_gain, "fsdp", axis=0, tiled=True),
        lax.all_gather(second_shift, "fsdp", axis=0, tiled=True),
        lax.all_gather(pool_weight, "fsdp", axis=0, tiled=True),
        lax.all_gather(pool_bias, "fsdp", axis=0, tiled=True),
        lax.all_gather(class_weight, "fsdp", axis=0, tiled=True),
    )
    w_qkv = again[0]
    w_out = again[3]
    g_first = again[5].astype(jnp.float32)
    w_inner = again[7]
    w_outer = again[9]
    g_second = again[11].astype(jnp.float32)
    w_pool = again[13]
    w_class = again[15]
    grad_logits = (jnp.exp(logits - logsum_class) - onehot).astype(jnp.bfloat16)
    grad_class_weight = transposed_left(pooled_low, grad_logits)
    grad_class_local = column_sum(grad_logits)
    grad_pooled = transposed_right(grad_logits, w_class)
    grad_pre = (grad_pooled * (1.0 - pooled * pooled)).astype(jnp.bfloat16)
    grad_pool_weight = transposed_left(first, grad_pre)
    grad_pool_bias = column_sum(grad_pre)
    grad_first = transposed_right(grad_pre, w_pool)
    grad_layer = (cotangent.astype(jnp.float32) * valid).reshape(seqs, span, width)
    grad_layer = jnp.concatenate(
        [grad_layer[:, :1] + grad_first[:, None, :], grad_layer[:, 1:]], axis=1
    )
    grad_layer = grad_layer.reshape(rows, width)
    grad_resid_second, grad_second_gain, grad_second_shift = norm_back(
        grad_layer, unit_second, inverse_second, g_second
    )
    grad_ffn = grad_resid_second.astype(jnp.bfloat16)
    grad_outer_weight = transposed_left(act, grad_ffn)
    grad_outer_bias = column_sum(grad_ffn)
    grad_act = transposed_right(grad_ffn, w_outer)
    gelu_value, gelu_pull = jax.vjp(lambda v: jax.nn.gelu(v, approximate=False), inner)
    grad_inner = gelu_pull(grad_act)[0].astype(jnp.bfloat16)
    grad_inner_weight = transposed_left(hidden_low, grad_inner)
    grad_inner_bias = column_sum(grad_inner)
    grad_hidden = grad_resid_second + transposed_right(grad_inner, w_inner)
    grad_resid_first, grad_first_gain, grad_first_shift = norm_back(
        grad_hidden, unit_first, inverse_first, g_first
    )
    grad_attended = grad_resid_first.astype(jnp.bfloat16)
    grad_out_weight = transposed_left(context, grad_attended)
    grad_out_bias = column_sum(grad_attended)
    grad_context = (
        transposed_right(grad_attended, w_out).astype(jnp.bfloat16).reshape(seqs, span, HEADS, size)
    )
    grad_query, grad_key, grad_value = lax.map(
        attend_back, (query, key, value, keep, logsum, grad_context)
    )
    grad_query = grad_query.reshape(rows, width)
    grad_key = grad_key.reshape(rows, width)
    grad_value = grad_value.reshape(rows, width)
    grad_qkv = jnp.concatenate([grad_query, grad_key, grad_value], axis=1)
    grad_qkv_weight = transposed_left(tokens, grad_qkv)
    grad_query_bias = column_sum(grad_query)
    grad_value_bias = column_sum(grad_value)
    tokens_grad = (grad_resid_first + transposed_right(grad_qkv, w_qkv)).astype(jnp.bfloat16)
    owned = (
        lax.psum_scatter(grad_qkv_weight, "fsdp", scatter_dimension=0, tiled=True),
        lax.psum_scatter(grad_query_bias, "fsdp", scatter_dimension=0, tiled=True),
        lax.psum_scatter(grad_value_bias, "fsdp", scatter_dimension=0, tiled=True),
        lax.psum_scatter(grad_out_weight, "fsdp", scatter_dimension=0, tiled=True),
        lax.psum_scatter(grad_out_bias, "fsdp", scatter_dimension=0, tiled=True),
        lax.psum_scatter(grad_first_gain, "fsdp", scatter_dimension=0, tiled=True),
        lax.psum_scatter(grad_first_shift, "fsdp", scatter_dimension=0, tiled=True),
        lax.psum_scatter(grad_inner_weight, "fsdp", scatter_dimension=0, tiled=True),
        lax.psum_scatter(grad_inner_bias, "fsdp", scatter_dimension=0, tiled=True),
        lax.psum_scatter(grad_outer_weight, "fsdp", scatter_dimension=0, tiled=True),
        lax.psum_scatter(grad_outer_bias, "fsdp", scatter_dimension=0, tiled=True),
        lax.psum_scatter(grad_second_gain, "fsdp", scatter_dimension=0, tiled=True),
        lax.psum_scatter(grad_second_shift, "fsdp", scatter_dimension=0, tiled=True),
        lax.psum_scatter(grad_pool_weight, "fsdp", scatter_dimension=0, tiled=True),
        lax.psum_scatter(grad_pool_bias, "fsdp", scatter_dimension=0, tiled=True),
        lax.psum_scatter(grad_class_weight, "fsdp", scatter_dimension=0, tiled=True),
    )
    summed = lax.psum(
        (
            owned[0],
            owned[1],
            owned[2],
            owned[3],
            owned[4],
            owned[5],
            owned[6],
            owned[7],
            owned[8],
            owned[9],
            owned[10],
            owned[11],
            owned[12],
            owned[13],
            owned[14],
            owned[15],
        ),
        "dp",
    )
    class_bias_grad = lax.psum(grad_class_local, ("dp", "fsdp"))
    return (
        output,
        exit_loss,
        tokens_grad,
        summed[0],
        summed[1],
        summed[2],
        summed[3],
        summed[4],
        summed[5],
        summed[6],
        summed[7],
        summed[8],
        summed[9],
        summed[10],
        summed[11],
        summed[12],
        summed[13],
        summed[14],
        summed[15],
        class_bias_grad,
    )


def per_device(nz, tokens, lengths, labels, cotangent, qkv_weight, query_bias, value_bias, out_weight, out_bias,
    first_gain, first_shift, inner_weight, inner_bias, outer_weight, outer_bias, second_gain, second_shift,
    pool_weight, pool_bias, class_weight, class_bias):
    part = query_bias.shape[0]
    classes = class_bias.shape[0]
    vectors = jnp.stack([query_bias, value_bias, out_bias, first_gain, first_shift, outer_bias, second_gain, second_shift, pool_bias]
                        + [class_weight[:, j] for j in range(classes)])
    smalls = jnp.concatenate([jnp.pad(vectors, ((0, 0), (0, 128 - part))), inner_bias.reshape(-1, 128), jnp.zeros((1, 128), BF16)])
    (output, w1, w2, w3, vec, ib, qkv, context, lse, hidden_low, unit_first, act, dgelu, unit_second, inv, firsts) = forward(
        tokens, lengths, qkv_weight, out_weight, inner_weight, outer_weight, pool_weight, smalls, nz)
    cb = jnp.pad(class_bias.astype(F32)[None, :], ((0, 7), (1, 127 - classes)))
    (loss, own, ibg, poolg, classg, wo, wi, wu, wq, tokens_grad) = backward(
        lengths, labels, cb, vec, lse, inv, firsts, cotangent, tokens, w1, w2, w3, qkv, context, hidden_low, unit_first, act, dgelu, unit_second)
    wide = wq.shape[2] // 3
    qkv_grad = jnp.concatenate([wq[g, :, p * wide : (p + 1) * wide] for p in range(3) for g in range(3)], axis=1)

    def row(n):
        return own[n, :part]

    return (
        output, loss[::8, 0], tokens_grad, qkv_grad.astype(F32), row(10), row(11), wo.astype(F32), row(0), row(1), row(2),
        wi.astype(F32), ibg[0], wu.astype(F32), row(3), row(4), row(5), poolg[:part], row(12), classg[:part, 1 : 1 + classes], own[13, 1 : 1 + classes],
    )


def solution(mesh):
    in_specs = (
        P(("dp", "fsdp"), None),
        P(("dp", "fsdp")),
        P(("dp", "fsdp")),
        P(("dp", "fsdp"), None),
        P("fsdp", None),
        P("fsdp"),
        P("fsdp"),
        P("fsdp", None),
        P("fsdp"),
        P("fsdp"),
        P("fsdp"),
        P("fsdp", None),
        P("fsdp"),
        P("fsdp", None),
        P("fsdp"),
        P("fsdp"),
        P("fsdp"),
        P("fsdp", None),
        P("fsdp"),
        P("fsdp", None),
        P(),
    )
    out_specs = (
        P(("dp", "fsdp"), None),
        P(("dp", "fsdp")),
        P(("dp", "fsdp"), None),
        P("fsdp", None),
        P("fsdp"),
        P("fsdp"),
        P("fsdp", None),
        P("fsdp"),
        P("fsdp"),
        P("fsdp"),
        P("fsdp", None),
        P("fsdp"),
        P("fsdp", None),
        P("fsdp"),
        P("fsdp"),
        P("fsdp"),
        P("fsdp", None),
        P("fsdp"),
        P("fsdp", None),
        P(),
    )
    sizes = dict(mesh.shape)
    fast = sizes["dp"] == 4 and sizes["fsdp"] == 8
    return jax.shard_map(
        functools.partial(per_device, sizes["fsdp"] // 2) if fast else per_device_any, mesh=mesh, in_specs=in_specs, out_specs=out_specs, check_vma=False
    )
```

```python
import functools
import math

import jax
import jax.numpy as jnp
from jax import lax
from jax.experimental import pallas as pl
from jax.experimental.pallas import tpu as pltpu
from jax.sharding import PartitionSpec as P

HEADS = 12
DP, FSDP = "dp", "fsdp"
EPS = 1e-12
NEG = -1000000000.0
F32 = jnp.float32
BF16 = jnp.bfloat16
MESH = pl.DeviceIdType.MESH
LOG2E = math.log2(math.e)

START, NEED_QKV, PROJECT, ATTEND, NEED_OUT, NORM = 0, 10, 20, 30, 40, 41
NEED_INNER, EXPAND, NEED_OUTER, CONTRACT, NEED_POOL = 50, 60, 70, 80, 90
OUTER_GRAD, INNER_BACK, INNER_GRAD, FIRST_NORM, OUT_GRAD = 0, 1, 2, 4, 5
INPUT_GRAD, SMALL_SUMS, LAST, ATTEND_BACK, QKV_GRAD = 6, 7, 8, 10, 20

FORWARD_PLAN = {
    0: ((0, 0), (1, 0), (2, 0), (3, 0), (4, 0), (5, 0), (6, 0), (7, 0), (8, 0), (9, 0), (10, 0), (11, 0),),
    10: ((0, 1), (1, 1), (0, 2), (2, 1), (1, 2), (3, 1), (0, 3), (0, 4),),
    (20, 2): ((2, 2), (4, 1),),
    (30, 0): ((1, 3),),
    (30, 1): ((5, 1),),
    (30, 2): ((1, 4), (3, 2),),
    (30, 3): ((2, 3), (6, 1),),
    (31, 0): ((2, 4), (4, 2), (7, 1),),
    (31, 1): ((5, 2),),
    (31, 2): ((3, 3),),
    (31, 3): ((8, 1),),
    (22, 1): ((3, 4), (6, 2),),
    (32, 0): ((4, 3), (9, 1),),
    (32, 2): ((4, 4), (7, 2),),
    (32, 3): ((5, 3), (10, 1),),
    (41, 2): ((5, 4), (8, 2), (11, 1),),
    (60, 0): ((6, 3),),
    (60, 3): ((6, 4),),
    (61, 0): ((9, 2),),
    (61, 2): ((7, 3),),
    (62, 1): ((7, 4), (10, 2),),
    (63, 0): ((8, 3),),
    (63, 3): ((8, 4), (11, 2),),
    (80, 2): ((9, 3),),
    71: ((9, 4),),
    (81, 0): ((10, 3),),
    72: ((11, 3), (10, 4),),
    (82, 1): ((11, 4),),
}

BACKWARD_PLAN = {
    (0, 0): ((0, 0),),
    (0, 1): ((1, 0),),
    (0, 2): ((0, 1), (2, 0),),
    (0, 3): ((1, 1), (3, 0),),
    (1, 0): ((2, 1),),
    (1, 1): ((3, 1),),
    (1, 2): ((0, 2),),
    (2, 0): ((4, 0),),
    (2, 1): ((1, 2), (5, 0),),
    (2, 2): ((4, 1), (6, 0),),
    (2, 3): ((2, 2), (5, 1), (7, 0),),
    (4, 0): ((6, 1),),
    (4, 1): ((3, 2), (7, 1), (0, 3),),
    (4, 2): ((1, 3),),
    (4, 4): ((4, 2),),
    5: ((2, 3), (8, 0), (12, 0),),
    (10, 1): ((5, 2), (8, 1),),
    (10, 3): ((3, 3), (14, 4), (6, 2), (12, 1),),
    20: ((9, 0),),
    (11, 0): ((7, 2), (4, 3),),
    (11, 1): ((14, 5), (5, 3), (9, 1),),
    (11, 2): ((14, 6),),
    (11, 3): ((4, 4), (6, 3), (8, 2),),
    21: ((12, 2), (10, 0), (5, 4), (7, 3),),
    (12, 0): ((4, 5),),
    (12, 1): ((4, 6), (6, 4), (9, 2), (10, 1), (8, 3),),
    (12, 2): ((7, 4), (12, 3),),
    (12, 3): ((5, 5), (6, 5),),
    22: ((8, 4), (12, 4), (9, 3), (11, 0), (13, 0), (5, 6), (6, 6),),
    (6, 0): ((10, 2), (7, 5),),
    (6, 1): ((11, 1), (8, 5),),
    (6, 2): ((7, 6),),
    (6, 3): ((8, 6),),
    7: ((9, 4), (13, 1), (10, 3), (9, 5), (11, 2), (13, 2), (9, 6), (10, 4), (11, 3), (13, 3), (10, 5), (13, 4),),
    8: ((10, 6), (11, 4), (11, 5), (11, 6),),
}


def nn(left, right):
    return jnp.dot(left, right, preferred_element_type=F32)


def nt(left, right):
    return lax.dot_general(left, right, (((1,), (1,)), ((), ())), preferred_element_type=F32)


def tn(left, right):
    return lax.dot_general(left, right, (((0,), (0,)), ((), ())), preferred_element_type=F32)


def rowmean(value):
    return jnp.sum(value, axis=-1, keepdims=True) * (1.0 / value.shape[-1])


def here():
    d, f = lax.axis_index(DP), lax.axis_index(FSDP)
    return d // 2, d % 2, f // 2, f % 2


def at(x, c, z, y):
    return (x * 2 + c, z * 2 + y)


def attend_forward(qkv, ctx, lse, lengths, i, span, width, size):
    pairs = width // (2 * size)
    wide = 2 * size
    s, hp = i // pairs, i % pairs
    rows = pl.ds(pl.multiple_of(s * span, span), span)

    def part(p):
        return qkv[rows, pl.ds(pl.multiple_of(p * width + hp * wide, wide), wide)]

    q, k, v = part(0), part(1), part(2)
    lane = lax.broadcasted_iota(jnp.int32, (span, wide), 1)
    slot = lax.broadcasted_iota(jnp.int32, (span, wide), 0)
    fill = jnp.where(slot < lengths[s], 0.0, NEG).astype(BF16)
    vt = v.T
    vrow = lax.broadcasted_iota(jnp.int32, (wide, span), 0)
    factor = size ** (-0.5) * LOG2E
    halves, sums = [], []
    for h in range(2):
        mine = lane < size if h == 0 else lane >= size
        other = (1 - h) * size
        qh = jnp.where(mine, q, jnp.where(lane == other, 1.0, 0.0).astype(BF16))
        kh = jnp.where(mine, k, fill)
        scores = nt(kh, qh)
        top = jnp.max(scores, axis=0, keepdims=True)
        e = jnp.exp2((scores - top) * factor).astype(BF16)
        vmine = vrow < size if h == 0 else vrow >= size
        vh = jnp.where(vmine, vt, jnp.ones_like(vt))
        o = nn(vh, e)
        total = o[other : other + 1, :]
        halves.append(o[h * size : (h + 1) * size, :] / total)
        sums.append(top * factor + jnp.log2(total))
    ct = jnp.concatenate(halves, axis=0)
    ctx[rows, pl.ds(pl.multiple_of(hp * wide, wide), wide)] = ct.T.astype(BF16)
    lse[i] = jnp.concatenate(sums + [jnp.zeros((6, span), F32)], axis=0)


class Gather:
    def __init__(self, buf, send, recv):
        self.buf, self.send, self.recv = buf, send, recv
        self.nz, _, self.r, self.cols = buf.shape
        self.me = here()
        half = self.cols // 2
        x, c, z, y = self.me
        c0 = pl.multiple_of(c * half, 128)
        third = half // 3
        self.both = pl.ds(c0, half)
        self.first = pl.ds(c0, third)
        self.second = pl.ds(pl.multiple_of(c0 + third, 128), half - third)
        self.theirs = pl.ds(pl.multiple_of((1 - c) * half, 128), half)
        r2 = self.r // 2
        self.row = pl.ds(pl.multiple_of(x * r2, 16), r2)
        self.row_o = pl.ds(pl.multiple_of((1 - x) * r2, 16), r2)
        self.every = pl.ds(0, self.r)

    def copy(self, kind, k=0, incoming=False):
        x, c, z, y = self.me
        nz, buf = self.nz, self.buf
        zk = lax.rem(z + nz - k, nz)
        row = self.row_o if incoming else self.row
        both = self.theirs if incoming else self.both
        yo = 1 - y if incoming else y
        if kind == "z":
            ref = buf.at[zk if incoming else z, y, self.row, self.both]
            peer, n = (x, c, lax.rem(z + k, nz), y), k - 1
        elif kind == "xo":
            ref, peer, n = buf.at[zk, y, row, self.both], (1 - x, c, z, y), nz + k - 2
        elif kind == "co":
            ref, peer, n = buf.at[zk, y, self.every, both], (x, 1 - c, z, y), 2 * nz + k - 3
        elif kind == "ya1":
            ref, peer, n = buf.at[:, yo, self.every, self.first], (x, c, z, 1 - y), 3 * nz - 3
        elif kind == "ya2":
            ref, peer, n = buf.at[:, yo, self.row, self.second], (x, c, z, 1 - y), 3 * nz - 2
        elif kind == "xa":
            ref, peer, n = buf.at[:, 1 - y, row, self.second], (1 - x, c, z, y), 3 * nz - 1
        else:
            ref, peer, n = buf.at[:, 1 - y, self.every, both], (x, 1 - c, z, y), 3 * nz
        return pltpu.make_async_remote_copy(
            src_ref=ref, dst_ref=ref, send_sem=self.send.at[n], recv_sem=self.recv.at[n], device_id=at(*peer), device_id_type=MESH
        )

    def go(self, *kind):
        self.copy(*kind).start()

    def got(self, kind, k=0):
        self.copy(kind, k, True).wait_recv()

    def step(self, j):
        ks = range(1, self.nz)
        if j == 0:
            for k in ks:
                self.go("z", k)
        elif j == 1:
            for k in ks:
                self.got("z", k)
                self.go("xo", k)
            self.go("ya2")
        elif j == 2:
            for k in ks:
                self.got("xo", k)
            self.go("ya1")
            self.got("ya2")
            self.go("xa")
            for k in ks:
                self.go("co", k)
        elif j == 3:
            self.got("ya1")
            self.got("xa")
            self.go("cx")
        else:
            for k in ks:
                self.got("co", k)
            self.got("cx")

    def drain(self):
        for k in range(1, self.nz):
            for kind in ("z", "xo", "co"):
                self.copy(kind, k).wait_send()
        for kind in ("ya1", "ya2", "xa", "cx"):
            self.copy(kind).wait_send()


def gelu_both(value):
    cdf = 0.5 + 0.5 * lax.erf(value * (0.5**0.5))
    bell = jnp.exp2(value * value * (-0.5 * LOG2E)) * (1.0 / math.sqrt(2.0 * math.pi))
    return value * cdf, cdf + value * bell


def place(sm, f, part, width):
    row = lax.broadcasted_iota(jnp.int32, (128, width), 0)
    col = lax.broadcasted_iota(jnp.int32, (128, width), 1)
    return jnp.where((col == row + f * part) & (row < part), 1.0, 0.0).astype(BF16)


def forward_kernel(plan, tokens_h, lengths, wqkv_h, wout_h, winner_h, wouter_h, wpool_h, smalls_h,
                   out_h, w1_h, w2_h, wu_h, wp_h, vec_o, ib_o, qkv_h, ctx_h, lse_o, hid_h, u1_h, act_h, dg_h, u2_h, inv_o, first_o,
                   tokens, w1, w2, wu, wp, sm, qkv, ctx, hid, hidlow, u1, act, dg, u2, outv,
                   loc, s_sm, r_sm, s_g, r_g):
    comm = plan is not None
    x, c, z, y = here() if comm else (0, 0, 0, 0)
    groups, nz = w1.shape[:2]
    rows, width = tokens.shape
    seqs = lengths.shape[0]
    span = rows // seqs
    ff = act.shape[1]
    nb = ff // width
    size = width // HEADS
    pairs = HEADS // 2
    gp = pairs // groups
    wide = gp * 2 * size
    nf = nz * 2
    part = width // nf
    fr = ff // nf
    ur = wu.shape[3]
    nu = wu.shape[0]
    units = [(w1, g) for g in range(groups)] + [(w2, b) for b in range(1 + nb)] + [(wu, j) for j in range(nu)] + [(wp, 0)]

    f_me = z * 2 + y
    started = []

    def bring(src, dst):
        copy = pltpu.make_async_copy(src, dst, loc.at[len(started)])
        copy.start()
        started.append(copy)
        return copy

    if comm:
        barrier = pltpu.get_barrier_semaphore()
        peers = [(x, c, lax.rem(z + k, nz), yy) for k in range(1, nz) for yy in (y, 1 - y)]
        peers += [(x, c, z, 1 - y), (1 - x, c, z, y), (x, 1 - c, z, y)]
        for p in peers:
            pl.semaphore_signal(barrier, inc=1, device_id=at(*p), device_id_type=MESH)
        own = []
        for g in range(groups):
            own.append([bring(wqkv_h.at[:, pl.ds(p * width + g * wide, wide)], w1.at[g, z, y, :, pl.ds(p * wide, wide)]) for p in range(3)])
        smc = bring(smalls_h, sm.at[f_me])
        own.append([bring(wout_h, w2.at[0, z, y])])
        for b in range(nb):
            own.append([bring(winner_h.at[:, pl.ds(b * width, width)], w2.at[b + 1, z, y])])
        tok = bring(tokens_h, tokens)
        for j in range(fr // ur):
            own.append([bring(wouter_h.at[pl.ds(j * ur, ur)], wu.at[j, z, y])])
        own.append([bring(wpool_h, wp.at[0, z, y])])

        def unit(m):
            buf, n = units[m]
            return Gather(buf.at[n], s_g.at[m], r_g.at[m])

        def small(n, slot):
            return pltpu.make_async_remote_copy(
                src_ref=sm.at[slot], dst_ref=sm.at[slot], send_sem=s_sm.at[n], recv_sem=r_sm.at[n], device_id=at(*peers[n]), device_id_type=MESH
            )

        others = len(peers) - 2

        def smalls_sent():
            smc.wait()
            for n in range(others):
                small(n, f_me).start()

        def smalls_here():
            for n in range(others):
                if n < 2 * (nz - 1):
                    slot = lax.rem(z + nz - n // 2 - 1, nz) * 2 + (y if n % 2 == 0 else 1 - y)
                else:
                    slot = z * 2 + 1 - y
                small(n, slot).wait_recv()

        pl.semaphore_wait(barrier, len(peers))

        def hook(name, i=None):
            if i is None:
                for n, j in plan.get(name, ()):
                    if j == 0:
                        for cp in own[n]:
                            cp.wait()
                    unit(n).step(j)
                    if (n, j) == (0, 0):
                        smalls_sent()
                return
            for k in range(8):
                if (name, k) in plan:
                    pl.when(i == k)(functools.partial(hook, (name, k)))
    else:
        def hook(name, i=None):
            pass

        for a, b in ((tokens_h, tokens), (w1_h, w1), (w2_h, w2), (wu_h, wu), (wp_h, wp), (smalls_h, sm)):
            bring(a, b).wait()

    hook(START)
    if comm:
        tok.wait()
        smalls_here()
    vec = jnp.zeros((sm.shape[1], width), F32)
    for f in range(nf):
        vec += nn(sm[f], place(None, f, part, width))
    vec_o[...] = vec
    ibs = []
    for f in range(nf):
        piece = sm[f].astype(F32)
        for j in range(fr // 128):
            ibs.append(piece[12 + j : 13 + j, :])
    ib_o[...] = jnp.broadcast_to(jnp.concatenate(ibs, axis=1), ib_o.shape)

    tile = rows // nz
    steps = rows // tile

    def tiles(i):
        return pl.ds(pl.multiple_of(i * tile, tile), tile)

    def loop(count, body):
        def step(i, _):
            body(i)
            return 0

        lax.fori_loop(0, count, step, 0)

    saved = []

    def save(src, dst):
        saved.append(bring(src, dst))

    for g in range(groups):
        hook(NEED_QKV + g)
        lo = g * wide
        bias = (vec_o[0:1, lo : lo + wide], None, vec_o[1:2, lo : lo + wide])

        def project(i):
            r = tiles(i)
            got = nn(tokens[r, :], w1[g].reshape(width, 3 * wide))
            for p in range(3):
                mine = got[:, p * wide : (p + 1) * wide]
                qkv[r, p * width + lo : p * width + lo + wide] = (mine if bias[p] is None else mine + bias[p]).astype(BF16)
            hook(PROJECT + g, i)

        loop(steps, project)

        def attention(i):
            s, hp = i // gp, g * gp + i % gp
            attend_forward(qkv, ctx, lse_o, lengths, s * pairs + hp, span, width, size)
            hook(ATTEND + g, i)

        loop(seqs * gp, attention)
    if comm:
        save(w1, w1_h)
    save(qkv, qkv_h)
    save(ctx, ctx_h)

    hook(NEED_OUT)
    b_out, g_first, s_first, b_outer, g_second, s_second = (vec_o[n : n + 1, :] for n in range(2, 8))

    def norm_one(i):
        r = tiles(i)
        resid = tokens[r, :].astype(F32) + (nn(ctx[r, :], w2[0].reshape(width, width)) + b_out)
        centred = resid - rowmean(resid)
        inv = lax.rsqrt(rowmean(centred * centred) + EPS)
        unit_ = centred * inv
        u1[r, :] = unit_.astype(BF16)
        inv_o[0, r, :] = jnp.broadcast_to(inv, (tile, 128))
        h = unit_ * g_first + s_first
        hid[r, :] = h + b_outer
        hidlow[r, :] = h.astype(BF16)
        hook(NORM, i)

    loop(steps, norm_one)
    save(u1, u1_h)
    save(hidlow, hid_h)
    for b in range(nb):
        hook(NEED_INNER + b)
        cols = slice(b * width, (b + 1) * width)

        def expand(i):
            r = tiles(i)
            a, g = gelu_both(nn(hidlow[r, :], w2[b + 1].reshape(width, width)) + ib_o[0:1, cols])
            act[r, cols] = a.astype(BF16)
            dg[i, :, :, cols] = g.astype(BF16).reshape(2, tile // 2, width)
            hook(EXPAND + b, i)

        loop(steps, expand)
    if comm:
        save(w2, w2_h)
    save(act, act_h)
    save(dg, dg_h)

    for j in range(nu):
        hook(NEED_OUTER + j)

        def contract(i):
            r = tiles(i)
            a = jnp.concatenate([act[r, f * fr + j * ur : f * fr + (j + 1) * ur] for f in range(nf)], axis=1)
            resid = hid[r, :] + nn(a, wu[j].reshape(nf * ur, width))
            if j < nu - 1:
                hid[r, :] = resid
            else:
                centred = resid - rowmean(resid)
                inv = lax.rsqrt(rowmean(centred * centred) + EPS)
                unit_ = centred * inv
                u2[r, :] = unit_.astype(BF16)
                inv_o[1, r, :] = jnp.broadcast_to(inv, (tile, 128))
                layer = unit_ * g_second + s_second
                each = span // tile
                s, t = i // each, i % each

                @pl.when(t == 0)
                def _():
                    first_o[pl.ds(pl.multiple_of(s * 8, 8), 8), :] = layer[0:8, :]

                slot = lax.broadcasted_iota(jnp.int32, (tile, width), 0) + t * tile
                outv[r, :] = jnp.where(slot < lengths[s], layer, 0.0).astype(BF16)
            hook(CONTRACT + j, i)

        loop(steps, contract)
    save(u2, u2_h)
    save(outv, out_h)
    if comm:
        save(wu, wu_h)
    hook(NEED_POOL)
    if comm:
        save(wp, wp_h)
    for cp in saved:
        cp.wait()
    if comm:
        for n in range(others):
            small(n, f_me).wait_send()

        for n in range(len(units)):
            unit(n).drain()


def forward(plan, tokens, lengths, wqkv, wout, winner, wouter, wpool, smalls, nz, gathered=None):
    rows, width = tokens.shape
    comm = gathered is None
    seqs = lengths.shape[0]
    span = rows // seqs
    nf = nz * 2
    ff = winner.shape[1] if comm else (gathered[1].shape[0] - 1) * width
    part = width // nf
    ur = ff // nf // 3
    any_, vm, smem = (pl.BlockSpec(memory_space=m) for m in (pl.ANY, pltpu.VMEM, pltpu.SMEM))
    S = jax.ShapeDtypeStruct
    pairs = HEADS // 2
    weights = [(3, nz, 2, part, width), (1 + ff // width, nz, 2, part, width), (3, nz, 2, ur, width), (1, nz, 2, part, width)]
    outs = [
        (S((rows, width), BF16), any_),
        *[(S(w, BF16), any_) for w in weights],
        (S((16, width), F32), vm),
        (S((8, ff), F32), vm),
        (S((rows, 3 * width), BF16), any_),
        (S((rows, width), BF16), any_),
        (S((seqs * pairs, 8, span), F32), vm),
        (S((rows, width), BF16), any_),
        (S((rows, width), BF16), any_),
        (S((rows, ff), BF16), any_),
        (S((nz, 2, rows // (2 * nz), ff), BF16), any_),
        (S((rows, width), BF16), any_),
        (S((2, rows, 128), F32), vm),
        (S((8 * seqs, width), F32), vm),
    ]
    V = pltpu.VMEM
    D = pltpu.SemaphoreType.DMA
    units = sum(w[0] for w in weights)
    sems = 3 * nz + 1
    scratch = [
        V((rows, width), BF16),
        *[V(w, BF16) for w in weights],
        V((nf, 16, 128), BF16),
        V((rows, 3 * width), BF16),
        V((rows, width), BF16),
        V((rows, width), F32),
        V((rows, width), BF16),
        V((rows, width), BF16),
        V((rows, ff), BF16),
        V((nz, 2, rows // (2 * nz), ff), BF16),
        V((rows, width), BF16),
        V((rows, width), BF16),
        D((40,)), D((nf,)), D((nf,)),
        D((units, sems)), D((units, sems)),
    ]
    params = pltpu.CompilerParams(vmem_limit_bytes=60 * 2**20, has_side_effects=True, **({"collective_id": 0} if comm else {}))
    cost = pl.CostEstimate(flops=2 * rows * width * (4 * width + 2 * ff), bytes_accessed=10**7, transcendentals=0)
    if comm:
        return pl.pallas_call(functools.partial(forward_kernel, plan), out_shape=[o[0] for o in outs], out_specs=[o[1] for o in outs],
                              in_specs=[any_, smem] + [any_] * 6, scratch_shapes=scratch, compiler_params=params, cost_estimate=cost)(
            tokens, lengths, wqkv, wout, winner, wouter, wpool, smalls)

    def solo(tokens_h, lengths, w1_h, w2_h, wu_h, wp_h, smalls_h, *rest):
        o = rest[: len(outs)]
        forward_kernel(None, tokens_h, lengths, None, None, None, None, None, smalls_h, o[0], w1_h, w2_h, wu_h, wp_h, *o[5:], *rest[len(outs):])

    return pl.pallas_call(solo, out_shape=[o[0] for o in outs], out_specs=[o[1] for o in outs],
                          in_specs=[any_, smem] + [any_] * 5, scratch_shapes=scratch, compiler_params=params, cost_estimate=cost)(
        tokens, lengths, *gathered, smalls)


def attend_backward(kv, gctx, lse, lengths, s, hp, span, width, size):
    wide = 2 * size
    pairs = width // wide
    rows = pl.ds(pl.multiple_of(s * span, span), span)

    def cols(p):
        return pl.ds(pl.multiple_of(p * width + hp * wide, wide), wide)

    q, k, v = (kv[rows, cols(p)] for p in range(3))
    g = gctx[rows, cols(0)]
    logs = lse[s * pairs + hp]
    lane = lax.broadcasted_iota(jnp.int32, (span, wide), 1)
    slot = lax.broadcasted_iota(jnp.int32, (span, wide), 0)
    fill = jnp.where(slot < lengths[s], 0.0, NEG).astype(BF16)
    scale = size ** (-0.5)
    factor = scale * LOG2E
    kt = k.T
    gqs, gks, gvs = [], [], []
    for h in range(2):
        mine = lane < size if h == 0 else lane >= size
        other = (1 - h) * size
        qh = jnp.where(mine, q, jnp.where(lane == other, 1.0, 0.0).astype(BF16))
        kh = jnp.where(mine, k, fill)
        vh = jnp.where(mine, v, jnp.zeros_like(v))
        p = jnp.exp2(nt(kh, qh) * factor - logs[h : h + 1, :])
        gvs.append(nn(p.astype(BF16), g))
        gp = nt(vh, g)
        delta = jnp.sum(gp * p, axis=0, keepdims=True)
        gs = (p * (gp - delta)).astype(BF16)
        gks.append(nn(gs, q))
        gqs.append(nn(kt, gs)[h * size : (h + 1) * size, :])
    kv[rows, cols(0)] = (jnp.concatenate(gqs, axis=0).T * scale).astype(BF16)
    kv[rows, cols(1)] = (jnp.where(lane < size, gks[0], gks[1]) * scale).astype(BF16)
    kv[rows, cols(2)] = jnp.where(lane < size, gvs[0], gvs[1]).astype(BF16)


class Spread:
    def __init__(self, buf, send, recv):
        self.buf, self.send, self.recv = buf, send, recv
        self.nz = buf.shape[3]
        self.me = here()

    def copy(self, n, incoming):
        x, c, z, y = self.me
        nz = self.nz
        if n < nz - 1:
            k = n + 1
            peer = (x, c, lax.rem(z + k, nz), y)
            ref = self.buf.at[x, c, y, lax.rem(z + nz - k, nz) if incoming else z]
        elif n == nz - 1:
            peer = (x, c, z, 1 - y)
            ref = self.buf.at[x, c, 1 - y if incoming else y]
        elif n == nz:
            peer = (1 - x, c, z, y)
            ref = self.buf.at[1 - x if incoming else x, c]
        else:
            peer = (x, 1 - c, z, y)
            ref = self.buf.at[:, 1 - c if incoming else c]
        return pltpu.make_async_remote_copy(
            src_ref=ref, dst_ref=ref, send_sem=self.send.at[n], recv_sem=self.recv.at[n], device_id=at(*peer), device_id_type=MESH
        )

    def step(self, j):
        nz = self.nz
        if j == 0:
            for n in range(nz - 1):
                self.copy(n, False).start()
            return
        if j == 1:
            for n in range(nz - 1):
                self.copy(n, True).wait_recv()
        else:
            self.copy(nz + j - 3, True).wait_recv()
        if j < 4:
            self.copy(nz + j - 2, False).start()

    def drain(self):
        for n in range(self.nz + 2):
            self.copy(n, False).wait_send()


class Scatter:
    def __init__(self, refs, out, send, recv, ahead=None, every=None):
        self.g, self.r1, self.ry1, self.rx1, self.rx2, self.ry2, self.rz = refs
        self.out, self.send, self.recv, self.ahead, self.every = out, send, recv, ahead, every
        self.lead, _, self.r, self.cols = self.g.shape
        self.me = x, c, z, y = here()
        half = self.cols // 2
        a1 = self.ry1.shape[-1]
        r2 = self.r // 2
        self.rows = pl.ds(pl.multiple_of(x * r2, 16), r2)
        self.rows_o = pl.ds(pl.multiple_of((1 - x) * r2, 16), r2)
        self.mine = pl.ds(pl.multiple_of(c * half, 128), half)
        self.theirs = pl.ds(pl.multiple_of((1 - c) * half, 128), half)
        self.a1 = pl.ds(pl.multiple_of(c * half, 128), a1)
        self.a2 = pl.ds(pl.multiple_of(c * half + a1, 128), half - a1)

    def copy(self, n):
        x, c, z, y = self.me
        g, out, nz = self.g, self.out, self.nz()
        core, xn, yn = (x, 1 - c, z, y), (1 - x, c, z, y), (x, c, z, 1 - y)
        if n == 0:
            src, dst, peer = g.at[:, :, :, self.theirs], self.r1, core
        elif n == 1:
            src, dst, peer = g.at[:, 1 - y, :, self.a1], self.ry1, yn
        elif n == 2:
            src, dst, peer = g.at[:, :, self.rows_o, self.a2], self.rx2, xn
        elif n == 3:
            src, dst, peer = g.at[:, y, self.rows_o, self.a1], self.rx1, xn
        elif n == 4:
            src, dst, peer = g.at[:, 1 - y, self.rows, self.a2], self.ry2, yn
        elif n < 4 + nz:
            k = n - 4
            zk = lax.rem(z + k, nz)
            src = g.at[:, y, self.rows, self.mine] if self.ahead else g.at[zk, y, self.rows, self.mine]
            dst, peer = self.rz.at[k - 1], (x, c, zk, y)
        elif n == 4 + nz:
            src = dst = self.region(self.rows, self.mine)
            peer = xn
        else:
            src = dst = self.region(slice(None), self.mine)
            peer = core
        return self.remote(src, dst, n, peer)

    def nz(self):
        return self.rz.shape[0] + 1

    def region(self, rows, cols):
        return self.out.at[rows, cols] if len(self.out.shape) == 2 else self.out.at[:, rows, cols]

    def remote(self, src, dst, n, peer):
        return pltpu.make_async_remote_copy(
            src_ref=src, dst_ref=dst, send_sem=self.send.at[n], recv_sem=self.recv.at[n], device_id=at(*peer), device_id_type=MESH
        )

    def got(self, n):
        x, c, z, y = self.me
        last = 4 + self.nz()
        if self.ahead == 0 and 4 < n < last:
            k = n - 4
            send, recv = (e.at[k - 1] for e in self.every)
            Scatter([self.g, self.r1, self.ry1, self.rx1, self.rx2, self.ry2, self.rz], self.out, send, recv, k).got(n)
        elif n < last:
            self.copy(n).wait_recv()
        elif n == last:
            ref = self.region(self.rows_o, self.mine)
            self.remote(ref, ref, n, (1 - x, c, z, y)).wait_recv()
        else:
            ref = self.region(slice(None), self.theirs)
            self.remote(ref, ref, n, (x, 1 - c, z, y)).wait_recv()

    def step(self, j):
        g, y, nz, z = self.g, self.me[3], self.nz(), self.me[2]
        last = 4 + nz
        if j == 0:
            self.copy(0).start()
        elif j == 1:
            self.got(0)

            def add(i, _):
                for yy in range(2):
                    g[i, yy, :, self.mine] = g[i, yy, :, self.mine] + self.r1[i, yy]
                return 0

            lax.fori_loop(0, self.lead, add, 0)
            self.copy(1).start()
            self.copy(2).start()
        elif j == 2:
            self.got(1)

            def add(i, _):
                g[i, y, :, self.a1] = g[i, y, :, self.a1] + self.ry1[i]
                return 0

            lax.fori_loop(0, self.lead, add, 0)
            self.copy(3).start()
            self.got(2)

            def add(i, _):
                for yy in range(2):
                    g[i, yy, self.rows, self.a2] = g[i, yy, self.rows, self.a2] + self.rx2[i, yy]
                return 0

            lax.fori_loop(0, self.lead, add, 0)
            self.copy(4).start()
        elif j == 3:
            self.got(3)
            self.got(4)

            def add(i, _):
                g[i, y, self.rows, self.a1] = g[i, y, self.rows, self.a1] + self.rx1[i]
                g[i, y, self.rows, self.a2] = g[i, y, self.rows, self.a2] + self.ry2[i]
                return 0

            lax.fori_loop(0, self.lead, add, 0)
            if self.ahead is None:
                for k in range(1, nz):
                    self.copy(4 + k).start()
            elif self.ahead:
                self.copy(4 + self.ahead).start()
        elif j == 4:
            total = (g[:, y, self.rows, self.mine] if self.ahead == 0 else g[z, y, self.rows, self.mine]).astype(F32)
            for k in range(1, nz):
                self.got(4 + k)
                total += self.rz[k - 1].astype(F32)
            if self.ahead == 0:
                self.out[:, self.rows, self.mine] = total.astype(BF16)
            else:
                self.out[self.rows, self.mine] = total.astype(BF16)
            self.copy(last).start()
        elif j == 5:
            self.got(last)
            self.copy(last + 1).start()
        else:
            self.got(last + 1)

    def drain(self):
        nz = self.nz()
        for n in range(6 + nz):
            if self.ahead is None or n < 5 or n == 4 + self.ahead or (self.ahead == 0 and n >= 4 + nz):
                self.copy(n).wait_send()


def backward_kernel(plan, lengths, labels, vec, lse, first, inv_h, cot_h, tok_h, w1_h, w2_h, wu_h, wp_h, qkv_h, ctx_h, hid_h, u1_h, act_h, dg_h, u2_h,
                    loss_o, own_o, ib_o, pool_o, class_o, wo_o, wi_o, wu_o, wq_o, tg_h,
                    A, D, w2, w3, cot, u2, u1, hid, gffn, gr, inv, acc, gfirst,
                    G, R1, Ry1, Rx1, Rx2, Ry2, Rz, RzU, early, late, loc, free, s_rs, r_rs, s_sp, r_sp):
    comm = plan is not None
    x, c, z, y = here() if comm else (0, 0, 0, 0)
    rows, width = cot.shape
    seqs = lengths.shape[0]
    span = rows // seqs
    ff = A.shape[1]
    size = width // HEADS
    nz = D.shape[0]
    tile = rows // nz
    nb = ff // width
    part = width // (2 * nz)
    fr = ff // (2 * nz)
    ur = wu_h.shape[3]
    groups = w1_h.shape[0]
    loads = {}

    def load(name, src, dst):
        cp = pltpu.make_async_copy(src, dst, loc.at[len(loads)])
        cp.start()
        loads[name] = cp

    load("wp", wp_h.at[0], w3.at[:, :, pl.ds(fr, part), :])
    load("cot", cot_h, cot)
    load("u2", u2_h, u2)
    load("inv2", inv_h.at[1], inv)

    if comm:
        barrier = pltpu.get_barrier_semaphore()
        peers = [(x, c, lax.rem(z + k, nz), y) for k in range(1, nz)]
        peers += [(x, c, z, 1 - y), (1 - x, c, z, y), (x, 1 - c, z, y)]
        for p in peers:
            pl.semaphore_signal(barrier, inc=1, device_id=at(*p), device_id_type=MESH)

        def scatter(n):
            own = [r.at[n] for r in (G, R1, Ry1, Rx1, Rx2, Ry2)] if n < nz + nb else []
            if n < nz:
                return Scatter(own + [RzU], wu_o, s_rs.at[n], r_rs.at[n], (n + 1) % nz, (s_rs, r_rs))
            if n < nz + nb:
                b = n - nz
                return Scatter(own + [Rz.at[b]], wi_o.at[:, pl.ds(b * width, width)], s_rs.at[n], r_rs.at[n])
            q = n - nz - nb
            h, t, e, hr = width // 2, width // 3, width // 6, part // 2
            w = w2.at[q]
            refs = [
                D.at[:, :, pl.ds(0, part), pl.ds(q * width, width)],
                w.at[:, :, :, pl.ds(0, h)],
                w.at[:, 0, :, pl.ds(h, t)],
                w.at[:, 1, pl.ds(0, hr), pl.ds(h, t)],
                w.at[:, :, pl.ds(0, hr), pl.ds(h + t, e)],
                w.at[:, 0, pl.ds(hr, hr), pl.ds(h + t, e)],
                w.at[pl.ds(0, nz - 1), 1, pl.ds(hr, hr), pl.ds(h, h)],
            ]
            return Scatter(refs, wo_o if q == 0 else wq_o.at[q - 1], s_rs.at[n], r_rs.at[n])

        blocks = nz + nb + 1 + groups
        small = [Spread(early, s_sp.at[0], r_sp.at[0]), Spread(late, s_sp.at[1], r_sp.at[1])]

        def hook(name, i=None):
            if i is None:
                for n, j in plan.get(name, ()):
                    if n < blocks:
                        scatter(n).step(j)
                    elif n < blocks + 2:
                        small[n - blocks].step(j)
                    else:
                        scatter(nz - 1).step(j)
                return
            if isinstance(i, int):
                hook((name, i))
                return
            for k in range(8):
                if (name, k) in plan:
                    pl.when(i == k)(functools.partial(hook, (name, k)))
    else:
        def hook(name, i=None):
            pass

    acc[...] = jnp.zeros_like(acc)

    for name in ("wp", "cot", "u2", "inv2"):
        loads[name].wait()
    load("act", act_h, A)
    gain2, gain1 = vec[6:7, :], vec[3:4, :]

    def colsum(v):
        return jnp.sum(v, axis=0, keepdims=True)

    per = span // tile
    steps = rows // tile

    def second_norm(i, _):
        r = pl.ds(pl.multiple_of(i * tile, tile), tile)
        s, j = i // per, i % per
        slot = lax.broadcasted_iota(jnp.int32, (tile, width), 0) + j * tile
        gl = jnp.where(slot < lengths[s], cot[r, :].astype(F32), 0.0)
        head = gfirst[pl.ds(pl.multiple_of(8 * s, 8), 8), :] * jnp.where(j == 0, 1.0, 0.0)
        gl = gl + jnp.concatenate([head, jnp.zeros((tile - 8, width), F32)], axis=0)
        u = u2[r, :].astype(F32)
        a = gl * gain2
        g2 = (a - rowmean(a) - u * rowmean(a * u)) * inv[r, :][:, :1]
        gr[r, :] = g2
        low = g2.astype(BF16)
        gffn[r, :] = low
        tally(3, [(colsum(low.astype(F32)), colsum(gl * u), colsum(gl))])
        return 0

    def tally(first_row, parts):
        for n in range(len(parts[0])):
            acc[first_row + n : first_row + n + 1, :] += sum(p[n] for p in parts[1:]) + parts[0][n]

    lane = lax.broadcasted_iota(jnp.int32, (8 * seqs, 128), 1)
    row = lax.broadcasted_iota(jnp.int32, (8 * seqs, 128), 0)
    live = (lane >= 1) & (lane < 4)
    w_pool = w3[:, :, fr:, :].reshape(width, width)
    first_low = first[...].astype(BF16)
    pooled = jnp.tanh(nn(first_low, w_pool) + vec[8:9, :])
    pooled_low = pooled.astype(BF16)
    heads = jnp.concatenate([vec[8:16, :], jnp.zeros((120, width), F32)], axis=0).astype(BF16)
    logits = nt(pooled_low, heads) + vec[15:16, :128]
    peak = jnp.max(jnp.where(live, logits, -3.0e38), axis=-1, keepdims=True)
    mass = jnp.where(live, jnp.exp(logits - peak), 0.0)
    logsum = peak + jnp.log(jnp.sum(mass, axis=-1, keepdims=True))
    label = jnp.full((8 * seqs, 128), labels[0])
    for s in range(1, seqs):
        label = jnp.where(row >= 8 * s, labels[s], label)
    onehot = jnp.where(lane == label + 1, 1.0, 0.0)
    loss_o[...] = jnp.broadcast_to(logsum - jnp.sum(onehot * logits, axis=-1, keepdims=True), loss_o.shape)
    g_logits = jnp.where(live & (row % 8 == 0), jnp.exp(logits - logsum) - onehot, 0.0).astype(BF16)
    g_pre = (nn(g_logits, heads) * (1.0 - pooled * pooled)).astype(BF16)
    g_first = nt(g_pre, w_pool)

    gfirst[...] = g_first
    lax.fori_loop(0, steps, second_norm, 0)
    load("tok", tok_h, u2)
    load("inv1", inv_h.at[0], inv)

    loads["act"].wait()
    for j in range(fr // ur):
        load(("wu", j), wu_h.at[j], w3.at[:, :, pl.ds(j * ur, ur), :])
    load("dg", dg_h, D)
    load("hid", hid_h, hid)
    if comm:
        pl.semaphore_wait(barrier, len(peers))

    def outer_grad(k, _):
        owner = lax.rem(z + k + 1, nz)
        for yy in range(2):
            f = owner * 2 + yy
            got = tn(A[:, pl.ds(pl.multiple_of(f * fr, 128), fr)], gffn[...]).astype(BF16)
            G[k, :, yy] = got.reshape(nb, part, width)
        hook(OUTER_GRAD, k)
        return 0

    lax.fori_loop(0, nz, outer_grad, 0)
    load("qkv", qkv_h, A.at[:, pl.ds(0, 3 * width)])
    load("ctx", ctx_h, A.at[:, pl.ds(3 * width, width)])
    for j in range(fr // ur):
        loads[("wu", j)].wait()
    loads["dg"].wait()
    load("w2", w2_h, w2)
    load("u1", u1_h, u1)

    def inner_back(i, _):
        r = pl.ds(pl.multiple_of(i * tile, tile), tile)
        for b in range(nb):
            cols = slice(b * width, (b + 1) * width)
            w = w3[b, :, :fr, :].reshape(width, width)
            g = nt(gffn[r, :], w) * D[i, :, :, cols].reshape(tile, width).astype(F32)
            low = g.astype(BF16)
            D[i, :, :, cols] = low.reshape(2, tile // 2, width)
            acc[6 + b : 7 + b, :] += colsum(low.astype(F32))
        hook(INNER_BACK, i)
        return 0

    lax.fori_loop(0, rows // tile, inner_back, 0)
    for g in range(groups):
        load(("w1", g), w1_h.at[g], w3.at[:, :, pl.ds(g * part, part), :])

    loads["hid"].wait()

    def inner_grad(b, _):
        cols = pl.ds(pl.multiple_of(b * width, width), width)
        for m in range(2):
            h = width // 2
            got = tn(hid[:, m * h : (m + 1) * h], D[:, :, :, cols].reshape(rows, width)).astype(BF16)
            G[nz + b, m * nz // 2 : (m + 1) * nz // 2] = got.reshape(nz // 2, 2, part, width)
        hook(INNER_GRAD, b)
        return 0

    lax.fori_loop(0, nb, inner_grad, 0)

    loads["w2"].wait()
    loads["u1"].wait()
    loads["inv1"].wait()

    def hidden_grad(i):
        r = slice(i * tile, (i + 1) * tile)
        gh = gr[r, :]
        for b in range(nb):
            gh += nt(D[i, :, :, b * width : (b + 1) * width].reshape(tile, width), w2[b + 1].reshape(width, width))
        return gh

    def first_norm(i, gh):
        r = slice(i * tile, (i + 1) * tile)
        u = u1[r, :].astype(F32)
        a = gh * gain1
        g1 = (a - rowmean(a) - u * rowmean(a * u)) * inv[r, :][:, :1]
        low = g1.astype(BF16)
        cot[r, :] = low
        tally(0, [(colsum(low.astype(F32)), colsum(gh * u), colsum(gh))])
        gffn[r, :] = nt(low, w2[0].reshape(width, width)).astype(BF16)
        gr[r, :] = g1

    for i in range(steps + 1):
        if i < steps:
            ahead = hidden_grad(i)
        if i:
            first_norm(i - 1, behind)
        if i < steps:
            gr[i * tile : (i + 1) * tile, :] = ahead
            behind = gr[i * tile : (i + 1) * tile, :]
        hook(FIRST_NORM, i)
    if comm:
        for p in peers:
            pl.semaphore_signal(free, inc=1, device_id=at(*p), device_id_type=MESH)
        pay = jnp.concatenate(
            [acc[0:10, :]]
            + [first_low[8 * s : 8 * s + 1, :].astype(F32) for s in range(seqs)]
            + [g_pre[8 * s : 8 * s + 1, :].astype(F32) for s in range(seqs)]
            + [pooled_low[8 * s : 8 * s + 1, :].astype(F32) for s in range(seqs)],
            axis=0,
        )
        early[x, c, y, z] = pay.astype(BF16)

    loads["ctx"].wait()
    loads["qkv"].wait()
    for m in range(2):
        h = width // 2
        got = tn(A[:, 3 * width + m * h : 3 * width + (m + 1) * h], cot[...]).astype(BF16)
        D[m * nz // 2 : (m + 1) * nz // 2, :, :part, :width] = got.reshape(nz // 2, 2, part, width)
    if comm:
        pl.semaphore_wait(free, len(peers))
    hook(OUT_GRAD)

    loads["tok"].wait()
    pairs = HEADS // 2
    gp = pairs // groups
    wide = gp * 2 * size
    def finish_late():
        late_rows = [acc[10 + n : 11 + n, j * 128 : (j + 1) * 128] for n in range(2) for j in range(width // 128)]
        late_rows += [g_logits[8 * s : 8 * s + 1, :].astype(F32) for s in range(seqs)]
        late_rows.append(jnp.zeros((16 - len(late_rows), 128), F32))
        late[x, c, y, z] = jnp.concatenate(late_rows, axis=0).astype(BF16)

    for q in range(groups):
        def attention(i, _):
            attend_backward(A, gffn, lse, lengths, i // gp, q * gp + i % gp, span, width, size)
            hook(ATTEND_BACK + q, i)
            return 0

        lax.fori_loop(0, seqs * gp, attention, 0)
        for p in range(3):
            block_of = A[:, p * width + q * wide : p * width + (q + 1) * wide]
            got = tn(u2[...], block_of).astype(BF16)
            D[:, :, :part, (q + 1) * width + p * wide : (q + 1) * width + (p + 1) * wide] = got.reshape(nz, 2, part, wide)
            if p != 1:
                acc[10 + p // 2 : 11 + p // 2, q * wide : (q + 1) * wide] = colsum(block_of.astype(F32))
        if comm and q == groups - 1:
            finish_late()
        hook(QKV_GRAD + q)
    for g in range(groups):
        loads[("w1", g)].wait()

    def input_grad(i, _):
        r = pl.ds(pl.multiple_of(i * tile, tile), tile)
        total = gr[r, :]
        for g in range(groups):
            w = w3[:, :, g * part : (g + 1) * part, :].reshape(width, width)
            mine = jnp.concatenate([A[r, p * width + g * wide : p * width + (g + 1) * wide] for p in range(3)], axis=1)
            total += nt(mine, w)
        cot[r, :] = total.astype(BF16)
        hook(INPUT_GRAD, i)
        return 0

    lax.fori_loop(0, rows // tile, input_grad, 0)
    back = pltpu.make_async_copy(cot, tg_h, loc.at[len(loads)])
    back.start()
    hook(SMALL_SUMS)
    if comm:
        n = 4 * 2 * nz
        def slot_of(i):
            return (i // (4 * nz), i // (2 * nz) % 2, i // nz % 2, i % nz)

        total = lax.fori_loop(0, n, lambda i, t: t + early[slot_of(i)].astype(F32), jnp.zeros((16, width), F32))
        lates = late[...].reshape(n, 16, 128)
        lsum = jnp.sum(lates.astype(F32), axis=0)
        six = width // 128
        qb = jnp.concatenate([lsum[j : j + 1, :] for j in range(six)], axis=1)
        vb = jnp.concatenate([lsum[six + j : six + j + 1, :] for j in range(six)], axis=1)
        r16 = lax.broadcasted_iota(jnp.int32, (16, width), 0)
        total = jnp.where(r16 == 10, qb, jnp.where(r16 == 11, vb, total))
        f = z * 2 + y
        src = lax.broadcasted_iota(jnp.int32, (width, 128), 0)
        dst = lax.broadcasted_iota(jnp.int32, (width, 128), 1)
        pick = jnp.where((src == dst + f * part) & (dst < part), 1.0, 0.0).astype(BF16)
        src = lax.broadcasted_iota(jnp.int32, (width, fr), 0)
        dst = lax.broadcasted_iota(jnp.int32, (width, fr), 1)
        pick_ff = jnp.where(src == dst + y * fr, 1.0, 0.0).astype(BF16)
        high = total.astype(BF16)
        rest = (total - high.astype(F32)).astype(BF16)
        own = nn(high, pick) + nn(rest, pick)
        wide_own = nn(high, pick_ff) + nn(rest, pick_ff)
        r16f = lax.broadcasted_iota(jnp.int32, (16, fr), 0)
        ib_o[...] = jnp.broadcast_to(colsum(jnp.where(r16f == 6 + z, wide_own, 0.0)), ib_o.shape)
        flat = early[...].reshape(n * 16, width)
        chosen = nn(flat, pick)
        rid = lax.broadcasted_iota(jnp.int32, (n * 16, 128), 0) % 16
        firsts = pltpu.roll(jnp.where((rid >= 10) & (rid < 10 + seqs), chosen, 0.0), seqs, 0).astype(BF16)
        pool_o[...] = tn(firsts, flat)
        pooleds = pltpu.roll(jnp.where(rid >= 10 + 2 * seqs, chosen, 0.0), n * 16 - seqs, 0).astype(BF16)
        class_o[...] = tn(pooleds, lates.reshape(n * 16, 128))
        middle = (rid >= 10 + seqs) & (rid < 10 + 2 * seqs)
        pb = colsum(jnp.where(middle, chosen, 0.0))
        cbg = colsum(jnp.where(middle, lates.reshape(n * 16, 128).astype(F32), 0.0))
        r16s = lax.broadcasted_iota(jnp.int32, (16, 128), 0)
        own_o[...] = jnp.where(r16s == 12, pb, jnp.where(r16s == 13, cbg, own))
        hook(LAST)
        for spread in small:
            spread.drain()
        for n in range(blocks):
            scatter(n).drain()
    back.wait()


def backward(plan, lengths, labels, vec, lse, inv, first, cot, tok, w1, w2, wu, wp, qkv, ctx, hid, u1, act, dg, u2):
    rows, width = cot.shape
    nz = w1.shape[1]
    ff = act.shape[1]
    part = width // (2 * nz)
    fr = ff // (2 * nz)
    nb = ff // width
    seqs = lengths.shape[0]
    any_, vm, smem = (pl.BlockSpec(memory_space=m) for m in (pl.ANY, pltpu.VMEM, pltpu.SMEM))
    S = jax.ShapeDtypeStruct
    outs = [
        (S((8 * seqs, 128), F32), vm),
        (S((16, 128), F32), vm),
        (S((8, fr), F32), vm),
        (S((128, width), F32), vm),
        (S((128, 128), F32), vm),
        (S((part, width), BF16), vm),
        (S((part, ff), BF16), vm),
        (S((nb, part, width), BF16), vm),
        (S((3, part, width), BF16), vm),
        (S((rows, width), BF16), any_),
    ]
    V = pltpu.VMEM
    D = pltpu.SemaphoreType.DMA
    n = 2 * nb
    half, third = width // 2, width // 3
    scratch = [
        V((rows, ff), BF16),
        V(dg.shape, BF16),
        V((1 + nb, nz, 2, part, width), BF16),
        V((nz, 2, fr + part, width), BF16),
        V((rows, width), BF16),
        V((rows, width), BF16),
        V((rows, width), BF16),
        V((rows, width), BF16),
        V((rows, width), BF16),
        V((rows, width), F32),
        V((rows, 128), F32),
        V((16, width), F32),
        V((8 * seqs, width), F32),
        V((n, nz, 2, part, width), BF16),
        V((n, nz, 2, part, half), BF16),
        V((n, nz, part, third), BF16),
        V((n, nz, part // 2, third), BF16),
        V((n, nz, 2, part // 2, third // 2), BF16),
        V((n, nz, part // 2, third // 2), BF16),
        V((nb, nz - 1, part // 2, half), BF16),
        V((nz - 1, nb, part // 2, half), BF16),
        V((2, 2, 2, nz, 16, width), BF16),
        V((2, 2, 2, nz, 16, 128), BF16),
        D((24,)),
        pltpu.SemaphoreType.REGULAR,
        D((n + 4, nz + 6)), D((n + 4, nz + 6)), D((2, nz + 2)), D((2, nz + 2)),
    ]
    params = pltpu.CompilerParams(vmem_limit_bytes=63 * 2**20, has_side_effects=True, **({"collective_id": 1} if plan is not None else {}))
    cost = pl.CostEstimate(flops=4 * rows * width * (4 * width + 2 * ff), bytes_accessed=10**7, transcendentals=0)
    return pl.pallas_call(
        functools.partial(backward_kernel, plan), out_shape=[o[0] for o in outs], out_specs=[o[1] for o in outs],
        in_specs=[smem, smem] + [vm] * 3 + [any_] * 14, scratch_shapes=scratch, compiler_params=params, cost_estimate=cost,
    )(lengths, labels, vec, lse, first, inv, cot, tok, w1, w2, wu, wp, qkv, ctx, hid, u1, act, dg, u2)


def finish_kernel(output, tg, loss, own, ibg, poolg, classg, wo, wi, wu, wq,
                  output_o, loss_o, tg_o, qkv_o, qb_o, vb_o, wo_o, ob_o, g1_o, s1_o, wi_o, ib_o, wu_o, outb_o, g2_o, s2_o, pool_o, pb_o, class_o, cb_o):
    output_o[...] = output[...]
    tg_o[...] = tg[...]
    part, width = wo.shape
    groups, _, wide3 = wq.shape
    wide = wide3 // groups
    for p in range(3):
        for g in range(groups):
            qkv_o[:, p * width + g * wide : p * width + (g + 1) * wide] = wq[g, :, p * wide : (p + 1) * wide].astype(F32)
    wo_o[...] = wo[...].astype(F32)
    wi_o[...] = wi[...].astype(F32)
    wu_o[...] = wu[...].reshape(wu_o.shape).astype(F32)
    pool_o[...] = poolg[:part, :]
    for n, ref in ((10, qb_o), (11, vb_o), (0, ob_o), (1, g1_o), (2, s1_o), (3, outb_o), (4, g2_o), (5, s2_o), (12, pb_o)):
        ref[...] = own[n, :part]
    ib_o[...] = ibg[0, :]
    classes = cb_o.shape[0]
    cb_o[...] = own[13, 1 : 1 + classes]
    class_o[...] = classg[:part, 1 : 1 + classes]
    for s in range(loss_o.shape[0]):
        loss_o[s : s + 1] = loss[8 * s, 0:1]


def finish(output, tg, loss, own, ibg, poolg, classg, wo, wi, wu, wq, classes):
    part, width = wo.shape
    ff = wi.shape[1]
    S = jax.ShapeDtypeStruct
    any_, vm = (pl.BlockSpec(memory_space=m) for m in (pl.ANY, pltpu.VMEM))
    vector = S((part,), F32)
    outs = [S(output.shape, BF16), S((loss.shape[0] // 8,), F32), S(tg.shape, BF16), S((part, 3 * width), F32), vector, vector,
            S((part, width), F32), vector, vector, vector, S((part, ff), F32), S((ibg.shape[1],), F32), S((wu.shape[0] * part, width), F32),
            vector, vector, vector, S((part, width), F32), vector, S((part, classes), F32), S((classes,), F32)]
    return pl.pallas_call(
        finish_kernel, out_shape=outs, in_specs=[vm] * 11, out_specs=[vm] * 20,
        compiler_params=pltpu.CompilerParams(vmem_limit_bytes=62 * 2**20),
    )(output, tg, loss, own, ibg, poolg, classg, wo, wi, wu, wq)


def normalize(value, gain, shift):
    mean = jnp.mean(value, axis=-1, keepdims=True)
    centred = value - mean
    inverse = lax.rsqrt(jnp.mean(centred * centred, axis=-1, keepdims=True) + EPS)
    unit = centred * inverse
    return (unit * gain + shift, unit, inverse)


def norm_back(grad, unit, inverse, gain):
    scaled = grad * gain
    inner = (
        scaled
        - jnp.mean(scaled, axis=-1, keepdims=True)
        - unit * jnp.mean(scaled * unit, axis=-1, keepdims=True)
    )
    return (inner * inverse, jnp.sum(grad * unit, axis=0), jnp.sum(grad, axis=0))


def matmul(left, right):
    return jnp.dot(left, right, preferred_element_type=jnp.float32)


def transposed_left(left, right):
    return lax.dot_general(
        left, right, (((0,), (0,)), ((), ())), preferred_element_type=jnp.float32
    )


def transposed_right(left, right):
    return lax.dot_general(
        left, right, (((1,), (1,)), ((), ())), preferred_element_type=jnp.float32
    )


def column_sum(values):
    return jnp.sum(values.astype(jnp.float32), axis=0)


def attend(block):
    query, key, value, keep = block
    scale = query.shape[-1] ** (-0.5)
    scores = jnp.einsum("qhd,khd->hqk", query, key, preferred_element_type=jnp.float32) * scale
    scores = jnp.where(keep[None, None, :], scores, NEG)
    top = jnp.max(scores, axis=-1, keepdims=True)
    total = jnp.sum(jnp.exp(scores - top), axis=-1, keepdims=True)
    logsum = top + jnp.log(total)
    probs = jnp.exp(scores - logsum).astype(jnp.bfloat16)
    context = jnp.einsum("hqk,khd->qhd", probs, value, preferred_element_type=jnp.float32)
    return (context.astype(jnp.bfloat16), logsum[:, :, 0])


def attend_back(block):
    query, key, value, keep, logsum, grad_context = block
    scale = query.shape[-1] ** (-0.5)
    scores = jnp.einsum("qhd,khd->hqk", query, key, preferred_element_type=jnp.float32) * scale
    scores = jnp.where(keep[None, None, :], scores, NEG)
    probs = jnp.exp(scores - logsum[:, :, None])
    grad_value = jnp.einsum(
        "hqk,qhd->khd", probs.astype(jnp.bfloat16), grad_context, preferred_element_type=jnp.float32
    )
    grad_probs = jnp.einsum("qhd,khd->hqk", grad_context, value, preferred_element_type=jnp.float32)
    delta = jnp.sum(grad_probs * probs, axis=-1, keepdims=True)
    grad_scores = (probs * (grad_probs - delta)).astype(jnp.bfloat16)
    grad_query = (
        jnp.einsum("hqk,khd->qhd", grad_scores, key, preferred_element_type=jnp.float32) * scale
    )
    grad_key = (
        jnp.einsum("hqk,qhd->khd", grad_scores, query, preferred_element_type=jnp.float32) * scale
    )
    return (
        grad_query.astype(jnp.bfloat16),
        grad_key.astype(jnp.bfloat16),
        grad_value.astype(jnp.bfloat16),
    )


def per_device_any(
    tokens,
    lengths,
    labels,
    cotangent,
    qkv_weight,
    query_bias,
    value_bias,
    out_weight,
    out_bias,
    first_gain,
    first_shift,
    inner_weight,
    inner_bias,
    outer_weight,
    outer_bias,
    second_gain,
    second_shift,
    pool_weight,
    pool_bias,
    class_weight,
    class_bias,
):
    full = (
        lax.all_gather(qkv_weight, FSDP, axis=0, tiled=True),
        lax.all_gather(query_bias, FSDP, axis=0, tiled=True),
        lax.all_gather(value_bias, FSDP, axis=0, tiled=True),
        lax.all_gather(out_weight, FSDP, axis=0, tiled=True),
        lax.all_gather(out_bias, FSDP, axis=0, tiled=True),
        lax.all_gather(first_gain, FSDP, axis=0, tiled=True),
        lax.all_gather(first_shift, FSDP, axis=0, tiled=True),
        lax.all_gather(inner_weight, FSDP, axis=0, tiled=True),
        lax.all_gather(inner_bias, FSDP, axis=0, tiled=True),
        lax.all_gather(outer_weight, FSDP, axis=0, tiled=True),
        lax.all_gather(outer_bias, FSDP, axis=0, tiled=True),
        lax.all_gather(second_gain, FSDP, axis=0, tiled=True),
        lax.all_gather(second_shift, FSDP, axis=0, tiled=True),
        lax.all_gather(pool_weight, FSDP, axis=0, tiled=True),
        lax.all_gather(pool_bias, FSDP, axis=0, tiled=True),
        lax.all_gather(class_weight, FSDP, axis=0, tiled=True),
    )
    (
        w_qkv,
        b_query,
        b_value,
        w_out,
        b_out,
        g_first,
        s_first,
        w_inner,
        b_inner,
        w_outer,
        b_outer,
        g_second,
        s_second,
        w_pool,
        b_pool,
        w_class,
    ) = full
    b_query = b_query.astype(jnp.float32)
    b_value = b_value.astype(jnp.float32)
    b_out = b_out.astype(jnp.float32)
    g_first = g_first.astype(jnp.float32)
    s_first = s_first.astype(jnp.float32)
    b_inner = b_inner.astype(jnp.float32)
    b_outer = b_outer.astype(jnp.float32)
    g_second = g_second.astype(jnp.float32)
    s_second = s_second.astype(jnp.float32)
    b_pool = b_pool.astype(jnp.float32)
    b_class = class_bias.astype(jnp.float32)
    seqs = lengths.shape[0]
    rows, width = tokens.shape
    span = rows // seqs
    size = width // HEADS
    classes = class_bias.shape[0]
    position = lax.broadcasted_iota(jnp.int32, (seqs, span), 1)
    keep = position < lengths[:, None]
    valid = keep.reshape(rows, 1).astype(jnp.float32)
    bias_all = jnp.concatenate([b_query, jnp.zeros_like(b_query), b_value])
    qkv = (matmul(tokens, w_qkv) + bias_all).astype(jnp.bfloat16)
    query = qkv[:, :width].reshape(seqs, span, HEADS, size)
    key = qkv[:, width : 2 * width].reshape(seqs, span, HEADS, size)
    value = qkv[:, 2 * width :].reshape(seqs, span, HEADS, size)
    context, logsum = lax.map(attend, (query, key, value, keep))
    context = context.reshape(rows, width)
    attended = matmul(context, w_out) + b_out
    hidden, unit_first, inverse_first = normalize(
        tokens.astype(jnp.float32) + attended, g_first, s_first
    )
    hidden_low = hidden.astype(jnp.bfloat16)
    inner = matmul(hidden_low, w_inner) + b_inner
    act = jax.nn.gelu(inner, approximate=False).astype(jnp.bfloat16)
    ffn = matmul(act, w_outer) + b_outer
    layer, unit_second, inverse_second = normalize(hidden + ffn, g_second, s_second)
    output = (layer * valid).astype(jnp.bfloat16)
    first = layer.reshape(seqs, span, width)[:, 0].astype(jnp.bfloat16)
    pooled = jnp.tanh(matmul(first, w_pool) + b_pool)
    pooled_low = pooled.astype(jnp.bfloat16)
    logits = matmul(pooled_low, w_class) + b_class
    peak = jnp.max(logits, axis=-1, keepdims=True)
    logsum_class = peak + jnp.log(jnp.sum(jnp.exp(logits - peak), axis=-1, keepdims=True))
    onehot = (labels[:, None] == lax.broadcasted_iota(jnp.int32, (seqs, classes), 1)).astype(
        jnp.float32
    )
    exit_loss = logsum_class[:, 0] - jnp.sum(onehot * logits, axis=-1)
    again = (
        lax.all_gather(qkv_weight, FSDP, axis=0, tiled=True),
        lax.all_gather(query_bias, FSDP, axis=0, tiled=True),
        lax.all_gather(value_bias, FSDP, axis=0, tiled=True),
        lax.all_gather(out_weight, FSDP, axis=0, tiled=True),
        lax.all_gather(out_bias, FSDP, axis=0, tiled=True),
        lax.all_gather(first_gain, FSDP, axis=0, tiled=True),
        lax.all_gather(first_shift, FSDP, axis=0, tiled=True),
        lax.all_gather(inner_weight, FSDP, axis=0, tiled=True),
        lax.all_gather(inner_bias, FSDP, axis=0, tiled=True),
        lax.all_gather(outer_weight, FSDP, axis=0, tiled=True),
        lax.all_gather(outer_bias, FSDP, axis=0, tiled=True),
        lax.all_gather(second_gain, FSDP, axis=0, tiled=True),
        lax.all_gather(second_shift, FSDP, axis=0, tiled=True),
        lax.all_gather(pool_weight, FSDP, axis=0, tiled=True),
        lax.all_gather(pool_bias, FSDP, axis=0, tiled=True),
        lax.all_gather(class_weight, FSDP, axis=0, tiled=True),
    )
    w_qkv = again[0]
    w_out = again[3]
    g_first = again[5].astype(jnp.float32)
    w_inner = again[7]
    w_outer = again[9]
    g_second = again[11].astype(jnp.float32)
    w_pool = again[13]
    w_class = again[15]
    grad_logits = (jnp.exp(logits - logsum_class) - onehot).astype(jnp.bfloat16)
    grad_class_weight = transposed_left(pooled_low, grad_logits)
    grad_class_local = column_sum(grad_logits)
    grad_pooled = transposed_right(grad_logits, w_class)
    grad_pre = (grad_pooled * (1.0 - pooled * pooled)).astype(jnp.bfloat16)
    grad_pool_weight = transposed_left(first, grad_pre)
    grad_pool_bias = column_sum(grad_pre)
    grad_first = transposed_right(grad_pre, w_pool)
    grad_layer = (cotangent.astype(jnp.float32) * valid).reshape(seqs, span, width)
    grad_layer = jnp.concatenate(
        [grad_layer[:, :1] + grad_first[:, None, :], grad_layer[:, 1:]], axis=1
    )
    grad_layer = grad_layer.reshape(rows, width)
    grad_resid_second, grad_second_gain, grad_second_shift = norm_back(
        grad_layer, unit_second, inverse_second, g_second
    )
    grad_ffn = grad_resid_second.astype(jnp.bfloat16)
    grad_outer_weight = transposed_left(act, grad_ffn)
    grad_outer_bias = column_sum(grad_ffn)
    grad_act = transposed_right(grad_ffn, w_outer)
    gelu_value, gelu_pull = jax.vjp(lambda v: jax.nn.gelu(v, approximate=False), inner)
    grad_inner = gelu_pull(grad_act)[0].astype(jnp.bfloat16)
    grad_inner_weight = transposed_left(hidden_low, grad_inner)
    grad_inner_bias = column_sum(grad_inner)
    grad_hidden = grad_resid_second + transposed_right(grad_inner, w_inner)
    grad_resid_first, grad_first_gain, grad_first_shift = norm_back(
        grad_hidden, unit_first, inverse_first, g_first
    )
    grad_attended = grad_resid_first.astype(jnp.bfloat16)
    grad_out_weight = transposed_left(context, grad_attended)
    grad_out_bias = column_sum(grad_attended)
    grad_context = (
        transposed_right(grad_attended, w_out).astype(jnp.bfloat16).reshape(seqs, span, HEADS, size)
    )
    grad_query, grad_key, grad_value = lax.map(
        attend_back, (query, key, value, keep, logsum, grad_context)
    )
    grad_query = grad_query.reshape(rows, width)
    grad_key = grad_key.reshape(rows, width)
    grad_value = grad_value.reshape(rows, width)
    grad_qkv = jnp.concatenate([grad_query, grad_key, grad_value], axis=1)
    grad_qkv_weight = transposed_left(tokens, grad_qkv)
    grad_query_bias = column_sum(grad_query)
    grad_value_bias = column_sum(grad_value)
    tokens_grad = (grad_resid_first + transposed_right(grad_qkv, w_qkv)).astype(jnp.bfloat16)
    owned = (
        lax.psum_scatter(grad_qkv_weight, FSDP, scatter_dimension=0, tiled=True),
        lax.psum_scatter(grad_query_bias, FSDP, scatter_dimension=0, tiled=True),
        lax.psum_scatter(grad_value_bias, FSDP, scatter_dimension=0, tiled=True),
        lax.psum_scatter(grad_out_weight, FSDP, scatter_dimension=0, tiled=True),
        lax.psum_scatter(grad_out_bias, FSDP, scatter_dimension=0, tiled=True),
        lax.psum_scatter(grad_first_gain, FSDP, scatter_dimension=0, tiled=True),
        lax.psum_scatter(grad_first_shift, FSDP, scatter_dimension=0, tiled=True),
        lax.psum_scatter(grad_inner_weight, FSDP, scatter_dimension=0, tiled=True),
        lax.psum_scatter(grad_inner_bias, FSDP, scatter_dimension=0, tiled=True),
        lax.psum_scatter(grad_outer_weight, FSDP, scatter_dimension=0, tiled=True),
        lax.psum_scatter(grad_outer_bias, FSDP, scatter_dimension=0, tiled=True),
        lax.psum_scatter(grad_second_gain, FSDP, scatter_dimension=0, tiled=True),
        lax.psum_scatter(grad_second_shift, FSDP, scatter_dimension=0, tiled=True),
        lax.psum_scatter(grad_pool_weight, FSDP, scatter_dimension=0, tiled=True),
        lax.psum_scatter(grad_pool_bias, FSDP, scatter_dimension=0, tiled=True),
        lax.psum_scatter(grad_class_weight, FSDP, scatter_dimension=0, tiled=True),
    )
    summed = lax.psum(
        (
            owned[0],
            owned[1],
            owned[2],
            owned[3],
            owned[4],
            owned[5],
            owned[6],
            owned[7],
            owned[8],
            owned[9],
            owned[10],
            owned[11],
            owned[12],
            owned[13],
            owned[14],
            owned[15],
        ),
        DP,
    )
    class_bias_grad = lax.psum(grad_class_local, (DP, FSDP))
    return (
        output,
        exit_loss,
        tokens_grad,
        summed[0],
        summed[1],
        summed[2],
        summed[3],
        summed[4],
        summed[5],
        summed[6],
        summed[7],
        summed[8],
        summed[9],
        summed[10],
        summed[11],
        summed[12],
        summed[13],
        summed[14],
        summed[15],
        class_bias_grad,
    )


def per_device(nz, tokens, lengths, labels, cotangent, qkv_weight, query_bias, value_bias, out_weight, out_bias,
    first_gain, first_shift, inner_weight, inner_bias, outer_weight, outer_bias, second_gain, second_shift,
    pool_weight, pool_bias, class_weight, class_bias):
    part = query_bias.shape[0]
    classes = class_bias.shape[0]
    vectors = jnp.stack([query_bias, value_bias, out_bias, first_gain, first_shift, outer_bias, second_gain, second_shift, pool_bias]
                        + [class_weight[:, j] for j in range(classes)])
    smalls = jnp.concatenate([jnp.pad(vectors, ((0, 0), (0, 128 - part))), inner_bias.reshape(-1, 128), jnp.pad(class_bias[None, :], ((0, 0), (1, 127 - classes)))])
    (output, w1, w2, wu, wp, vec, ib, qkv, context, lse, hidden_low, unit_first, act, dgelu, unit_second, inv, firsts) = forward(
        FORWARD_PLAN, tokens, lengths, qkv_weight, out_weight, inner_weight, outer_weight, pool_weight, smalls, nz)
    (loss, own, ibg, poolg, classg, wo, wi, wug, wq, tokens_grad) = backward(
        BACKWARD_PLAN, lengths, labels, vec, lse, inv, firsts, cotangent, tokens, w1, w2, wu, wp, qkv, context, hidden_low, unit_first, act, dgelu, unit_second)
    return finish(output, tokens_grad, loss, own, ibg, poolg, classg, wo, wi, wug, wq, classes)


def solution(mesh):
    in_specs = (
        P((DP, FSDP), None),
        P((DP, FSDP)),
        P((DP, FSDP)),
        P((DP, FSDP), None),
        P(FSDP, None),
        P(FSDP),
        P(FSDP),
        P(FSDP, None),
        P(FSDP),
        P(FSDP),
        P(FSDP),
        P(FSDP, None),
        P(FSDP),
        P(FSDP, None),
        P(FSDP),
        P(FSDP),
        P(FSDP),
        P(FSDP, None),
        P(FSDP),
        P(FSDP, None),
        P(),
    )
    out_specs = (
        P((DP, FSDP), None),
        P((DP, FSDP)),
        P((DP, FSDP), None),
        P(FSDP, None),
        P(FSDP),
        P(FSDP),
        P(FSDP, None),
        P(FSDP),
        P(FSDP),
        P(FSDP),
        P(FSDP, None),
        P(FSDP),
        P(FSDP, None),
        P(FSDP),
        P(FSDP),
        P(FSDP),
        P(FSDP, None),
        P(FSDP),
        P(FSDP, None),
        P(),
    )
    sizes = dict(mesh.shape)
    fast = sizes[DP] == 4 and sizes[FSDP] == 8
    return jax.shard_map(
        functools.partial(per_device, sizes[FSDP] // 2) if fast else per_device_any, mesh=mesh, in_specs=in_specs, out_specs=out_specs, check_vma=False
    )
```

```python
import functools
import math

import jax
import jax.numpy as jnp
from jax import lax
from jax.experimental import pallas as pl
from jax.experimental.pallas import tpu as pltpu
from jax.sharding import PartitionSpec as P

HEADS = 12
DP, FSDP = "dp", "fsdp"
EPS = 1e-12
NEG = -1000000000.0
F32 = jnp.float32
BF16 = jnp.bfloat16
MESH = pl.DeviceIdType.MESH
LOG2E = math.log2(math.e)

START, NEED_QKV, PROJECT, ATTEND, NEED_OUT, NORM = 0, 10, 20, 30, 40, 41
NEED_INNER, EXPAND, NEED_OUTER, CONTRACT, NEED_POOL = 50, 60, 70, 80, 90
OUTER_GRAD, INNER_BACK, INNER_GRAD, FIRST_NORM, OUT_GRAD = 0, 1, 2, 4, 5
INPUT_GRAD, SMALL_SUMS, LAST, ATTEND_BACK, QKV_GRAD = 6, 7, 8, 10, 20

FINE = (0,)
SPLIT = (256, 256, 256, 256, 128, 128, 128, 128, 128, 256, 128, 256)

FORWARD_PLAN = {
    0: ((0, 0), (1, 0),),
    10: ((0, 1), (0, 2), (0, 3), (0, 4), (0, 5), (2, 0), (0, 6), (3, 0), (0, 7), (0, 8), (0, 9), (1, 1), (0, 10), (4, 0), (0, 11), (0, 12),),
    (20, 3): ((1, 2), (2, 1),),
    (30, 1): ((5, 0),),
    (30, 3): ((1, 3), (3, 1),),
    11: ((2, 2), (1, 4),),
    (21, 0): ((6, 0),),
    (21, 3): ((4, 1),),
    (31, 0): ((3, 2), (7, 0),),
    (31, 1): ((2, 3),),
    (31, 3): ((2, 4), (5, 1), (4, 2),),
    (22, 2): ((3, 3), (8, 0),),
    (32, 0): ((3, 4),),
    (32, 1): ((5, 2), (6, 1),),
    (32, 3): ((4, 3), (9, 0),),
    (41, 0): ((7, 1),),
    (41, 1): ((4, 4), (5, 3), (10, 0),),
    (41, 3): ((5, 4), (6, 2),),
    (60, 2): ((7, 2), (8, 1),),
    (61, 0): ((11, 0), (6, 3),),
    (61, 3): ((6, 4), (7, 3),),
    (62, 0): ((9, 1),),
    (62, 1): ((7, 4), (8, 2),),
    (63, 3): ((9, 2), (10, 1),),
    70: ((8, 3), (8, 4),),
    (80, 1): ((11, 1),),
    (80, 2): ((9, 3),),
    71: ((10, 2), (9, 4),),
    72: ((11, 2), (10, 3), (10, 4),),
    (82, 0): ((11, 3),),
    (82, 2): ((11, 4),),
}

BACKWARD_PLAN = {
    (0, 0): ((0, 0),),
    (0, 1): ((1, 0),),
    (0, 2): ((0, 1), (2, 0),),
    (0, 3): ((1, 1), (3, 0),),
    (1, 0): ((2, 1),),
    (1, 1): ((3, 1),),
    (1, 2): ((0, 2),),
    (2, 0): ((4, 0),),
    (2, 1): ((1, 2), (5, 0),),
    (2, 2): ((4, 1), (6, 0),),
    (2, 3): ((5, 1), (7, 0),),
    (4, 0): ((2, 2), (6, 1),),
    (4, 1): ((7, 1),),
    (4, 2): ((3, 2),),
    (4, 3): ((0, 3), (1, 3),),
    (4, 4): ((4, 2),),
    5: ((8, 0), (12, 0),),
    (10, 0): ((2, 3), (5, 2), (8, 1),),
    (10, 1): ((6, 2),),
    (10, 3): ((3, 3), (14, 4), (7, 2), (4, 3), (4, 4), (12, 1), (14, 5),),
    20: ((5, 3), (9, 0),),
    (11, 0): ((5, 4), (8, 2), (9, 1),),
    (11, 1): ((6, 3), (6, 4),),
    (11, 2): ((14, 6), (4, 5), (7, 3), (7, 4),),
    (11, 3): ((14, 7), (5, 5), (12, 2),),
    21: ((4, 6), (8, 3), (8, 4), (10, 0),),
    (12, 0): ((4, 7), (5, 6), (6, 5), (10, 1),),
    (12, 1): ((5, 7), (7, 5), (9, 2), (12, 3),),
    (12, 2): ((6, 6), (8, 5), (12, 4),),
    (12, 3): ((6, 7), (9, 3),),
    22: ((7, 6), (10, 2), (8, 6), (9, 4), (11, 0), (13, 0),),
    (6, 0): ((7, 7), (8, 7), (9, 5),),
    (6, 1): ((11, 1),),
    (6, 3): ((9, 6), (10, 3), (10, 4), (13, 1),),
    7: ((9, 7), (11, 2), (13, 2), (10, 5), (13, 3), (11, 3), (10, 6), (13, 4),),
    8: ((10, 7), (11, 4), (11, 5), (11, 6), (11, 7),),
}


def nn(left, right):
    return jnp.dot(left, right, preferred_element_type=F32)


def nt(left, right):
    return lax.dot_general(left, right, (((1,), (1,)), ((), ())), preferred_element_type=F32)


def tn(left, right):
    return lax.dot_general(left, right, (((0,), (0,)), ((), ())), preferred_element_type=F32)


def rowmean(value):
    return jnp.sum(value, axis=-1, keepdims=True) * (1.0 / value.shape[-1])


def here():
    d, f = lax.axis_index(DP), lax.axis_index(FSDP)
    return d // 2, d % 2, f // 2, f % 2


def at(x, c, z, y):
    return (x * 2 + c, z * 2 + y)


def attend_forward(qkv, ctx, lse, lengths, i, span, width, size):
    pairs = width // (2 * size)
    wide = 2 * size
    s, hp = i // pairs, i % pairs
    rows = pl.ds(pl.multiple_of(s * span, span), span)

    def part(p):
        return qkv[rows, pl.ds(pl.multiple_of(p * width + hp * wide, wide), wide)]

    q, k, v = part(0), part(1), part(2)
    lane = lax.broadcasted_iota(jnp.int32, (span, wide), 1)
    slot = lax.broadcasted_iota(jnp.int32, (span, wide), 0)
    fill = jnp.where(slot < lengths[s], 0.0, NEG).astype(BF16)
    vt = v.T
    vrow = lax.broadcasted_iota(jnp.int32, (wide, span), 0)
    factor = size ** (-0.5) * LOG2E
    halves, sums = [], []
    for h in range(2):
        mine = lane < size if h == 0 else lane >= size
        other = (1 - h) * size
        qh = jnp.where(mine, q, jnp.where(lane == other, 1.0, 0.0).astype(BF16))
        kh = jnp.where(mine, k, fill)
        scores = nt(kh, qh)
        top = jnp.max(scores, axis=0, keepdims=True)
        e = jnp.exp2((scores - top) * factor).astype(BF16)
        vmine = vrow < size if h == 0 else vrow >= size
        vh = jnp.where(vmine, vt, jnp.ones_like(vt))
        o = nn(vh, e)
        total = o[other : other + 1, :]
        halves.append(o[h * size : (h + 1) * size, :] / total)
        sums.append(top * factor + jnp.log2(total))
    ct = jnp.concatenate(halves, axis=0)
    ctx[rows, pl.ds(pl.multiple_of(hp * wide, wide), wide)] = ct.T.astype(BF16)
    lse[i] = jnp.concatenate(sums + [jnp.zeros((6, span), F32)], axis=0)


class Gather:
    def __init__(self, buf, send, recv, first, fine):
        self.buf, self.send, self.recv, self.base, self.fine = buf, send, recv, first, fine
        self.nz, _, self.r, self.cols = buf.shape
        self.me = here()
        half = self.cols // 2
        x, c, z, y = self.me
        c0 = pl.multiple_of(c * half, 128)
        third = half // 3
        self.both = pl.ds(c0, half)
        self.first = pl.ds(c0, third)
        self.second = pl.ds(pl.multiple_of(c0 + third, 128), half - third)
        self.theirs = pl.ds(pl.multiple_of((1 - c) * half, 128), half)
        r2 = self.r // 2
        self.row = pl.ds(pl.multiple_of(x * r2, 16), r2)
        self.row_o = pl.ds(pl.multiple_of((1 - x) * r2, 16), r2)
        self.every = pl.ds(0, self.r)

    def copy(self, kind, k=None, incoming=False):
        x, c, z, y = self.me
        nz, buf = self.nz, self.buf
        if k is None:
            zk = pl.ds(0, nz if kind in ("ya", "yb", "xa", "cx") else nz - 1)
        else:
            zk = lax.rem(z + nz - k, nz)
        row = self.row_o if incoming else self.row
        both = self.theirs if incoming else self.both
        yo = 1 - y if incoming else y
        if kind in ("za", "zb"):
            slot = zk if incoming or k is None else z
            ref = buf.at[slot, y, self.every, self.first] if kind == "za" else buf.at[slot, y, self.row, self.second]
            peer = (x, c, lax.rem(z + (k or 1), nz), y)
        elif kind == "xo":
            ref, peer = buf.at[zk, y, row, self.second], (1 - x, c, z, y)
        elif kind == "co":
            ref, peer = buf.at[zk, y, self.every, both], (x, 1 - c, z, y)
        elif kind == "ya":
            ref, peer = buf.at[zk, yo, self.every, self.first], (x, c, z, 1 - y)
        elif kind == "yb":
            ref, peer = buf.at[zk, yo, self.row, self.second], (x, c, z, 1 - y)
        elif kind == "xa":
            ref, peer = buf.at[zk, 1 - y, row, self.second], (1 - x, c, z, y)
        else:
            ref, peer = buf.at[zk, 1 - y, self.every, both], (x, 1 - c, z, y)
        n = ("za", "zb", "xo", "co", "ya", "yb", "xa", "cx").index(kind)
        n = self.base + (n * nz + k if self.fine else n)
        return pltpu.make_async_remote_copy(
            src_ref=ref, dst_ref=ref, send_sem=self.send.at[n], recv_sem=self.recv.at[n], device_id=at(*peer), device_id_type=MESH
        )

    def go(self, *kind):
        self.copy(*kind).start()

    def got(self, kind, k=None):
        self.copy(kind, k, True).wait_recv()

    def step(self, j):
        nz = self.nz
        ks = range(1, nz)
        if j == 0:
            for k in ks:
                self.go("zb", k)
                self.go("za", k)
            if self.fine:
                self.go("yb", 0)
                self.go("ya", 0)
        elif self.fine:
            if j < nz:
                self.got("zb", j)
                self.go("xo", j)
                self.go("yb", j)
                self.got("za", j)
                self.go("ya", j)
            elif j < 2 * nz:
                k = j - nz
                self.got("yb", k)
                self.go("xa", k)
                if k:
                    self.got("xo", k)
                    self.go("co", k)
            elif j < 3 * nz:
                k = j - 2 * nz
                self.got("ya", k)
                self.got("xa", k)
                self.go("cx", k)
            else:
                for k in range(nz):
                    if k:
                        self.got("co", k)
                    self.got("cx", k)
        elif j == 1:
            self.got("zb")
            for k in ks:
                self.go("xo", k)
            self.go("yb")
            self.got("za")
            self.go("ya")
        elif j == 2:
            self.got("yb")
            self.go("xa")
            self.got("xo")
            for k in ks:
                self.go("co", k)
        elif j == 3:
            self.got("ya")
            self.got("xa")
            self.go("cx")
        else:
            self.got("co")
            self.got("cx")

    def drain(self):
        for kind in ("za", "zb", "xo", "co", "ya", "yb", "xa", "cx"):
            for k in range(self.nz) if self.fine else (None,):
                if k != 0 or kind in ("ya", "yb", "xa", "cx"):
                    self.copy(kind, k).wait_send()


def gelu_both(value):
    cdf = 0.5 + 0.5 * lax.erf(value * (0.5**0.5))
    bell = jnp.exp2(value * value * (-0.5 * LOG2E)) * (1.0 / math.sqrt(2.0 * math.pi))
    return value * cdf, cdf + value * bell


def place(sm, f, part, width):
    row = lax.broadcasted_iota(jnp.int32, (128, width), 0)
    col = lax.broadcasted_iota(jnp.int32, (128, width), 1)
    return jnp.where((col == row + f * part) & (row < part), 1.0, 0.0).astype(BF16)


def forward_kernel(plan, tokens_h, lengths, wqkv_h, wout_h, winner_h, wouter_h, wpool_h, small_h,
                   out_h, w1_h, w2_h, wu_h, wp_h, vec_o, ib_o, qkv_h, ctx_h, lse_o, hid_h, u1_h, act_h, dg_h, u2_h, inv_o, first_o,
                   tokens, w1, w2, wu, wp, sm, qkv, ctx, hid, hidlow, u1, act, dg, u2, outv,
                   loc, s_sm, r_sm, s_g, r_g, *raw):
    comm = plan is not None
    x, c, z, y = here() if comm else (0, 0, 0, 0)
    groups, nz = w1.shape[:2]
    rows, width = tokens.shape
    seqs = lengths.shape[0]
    span = rows // seqs
    ff = act.shape[1]
    nb = ff // width
    size = width // HEADS
    pairs = HEADS // 2
    gp = pairs // groups
    wide = gp * 2 * size
    nf = nz * 2
    part = width // nf
    fr = ff // nf
    ur = wu.shape[3]
    nu = wu.shape[0]
    units = [(w1, g) for g in range(groups)] + [(w2, b) for b in range(1 + nb)] + [(wu, j) for j in range(nu)] + [(wp, 0)]

    def small_parameters():
        vec = jnp.zeros((sm.shape[1], width), F32)
        for f in range(nf):
            vec += nn(sm[f], place(None, f, part, width))
        vec_o[...] = vec
        ibs = []
        for f in range(nf):
            piece = sm[f].astype(F32)
            for j in range(fr // 128):
                ibs.append(piece[12 + j : 13 + j, :])
        ib_o[...] = jnp.broadcast_to(jnp.concatenate(ibs, axis=1), ib_o.shape)

    f_me = z * 2 + y
    started = []

    def bring(src, dst):
        copy = pltpu.make_async_copy(src, dst, loc.at[len(started)])
        copy.start()
        started.append(copy)
        return copy

    if comm:
        barrier = pltpu.get_barrier_semaphore()
        peers = [(x, c, lax.rem(z + k, nz), yy) for k in range(1, nz) for yy in (y, 1 - y)]
        peers += [(x, c, z, 1 - y), (1 - x, c, z, y), (x, 1 - c, z, y)]
        for p in peers:
            pl.semaphore_signal(barrier, inc=1, device_id=at(*p), device_id_type=MESH)
        own = []
        for g in range(groups):
            own.append([bring(wqkv_h.at[:, pl.ds(p * width + g * wide, wide)], w1.at[g, z, y, :, pl.ds(p * wide, wide)]) for p in range(3)])
        parts = [bring(src, dst) for src, dst in zip(small_h, raw)]
        own.append([bring(wout_h, w2.at[0, z, y])])
        for b in range(nb):
            own.append([bring(winner_h.at[:, pl.ds(b * width, width)], w2.at[b + 1, z, y])])
        tok = bring(tokens_h, tokens)
        for j in range(fr // ur):
            own.append([bring(wouter_h.at[pl.ds(j * ur, ur)], wu.at[j, z, y])])
        own.append([bring(wpool_h, wp.at[0, z, y])])

        def unit(m):
            buf, n = units[m]
            ahead = sum(e < m for e in FINE)
            return Gather(buf.at[n], s_g, r_g, 8 * (m + ahead * (nz - 1)), m in FINE)

        def small(n, slot):
            return pltpu.make_async_remote_copy(
                src_ref=sm.at[slot], dst_ref=sm.at[slot], send_sem=s_sm.at[n], recv_sem=r_sm.at[n], device_id=at(*peers[n]), device_id_type=MESH
            )

        others = len(peers) - 2

        def smalls_sent():
            for cp in parts:
                cp.wait()

            def lanes(v, before=0):
                v = v.astype(F32)
                v = v.reshape(1, -1) if v.ndim == 1 else v
                ends = [jnp.zeros((v.shape[0], n), F32) for n in (before, 128 - before - v.shape[1])]
                return jnp.concatenate(([ends[0]] if before else []) + [v, ends[1]], axis=1)

            *vectors, classes, wide_bias, class_bias = (r[...] for r in raw)
            wide_bias = wide_bias.astype(F32).reshape(1, fr)
            lines = [lanes(v) for v in vectors] + [lanes(classes)]
            lines += [wide_bias[:, j * 128 : (j + 1) * 128] for j in range(fr // 128)] + [lanes(class_bias, 1)]
            sm[f_me] = jnp.concatenate(lines, axis=0).astype(BF16)
            for n in range(others):
                small(n, f_me).start()

        def smalls_here():
            for n in range(others):
                if n < 2 * (nz - 1):
                    slot = lax.rem(z + nz - n // 2 - 1, nz) * 2 + (y if n % 2 == 0 else 1 - y)
                else:
                    slot = z * 2 + 1 - y
                small(n, slot).wait_recv()

        pl.semaphore_wait(barrier, len(peers))

        def hook(name, i=None):
            if i is None:
                for n, j in plan.get(name, ()):
                    if j == 0:
                        for cp in own[n]:
                            cp.wait()
                    unit(n).step(j)
                    if (n, j) == (0, 0):
                        smalls_sent()
                    if (n, j) == (0, nz):
                        smalls_here()
                        small_parameters()
                        tok.wait()
                return
            for k in range(8):
                if (name, k) in plan:
                    pl.when(i == k)(functools.partial(hook, (name, k)))
    else:
        def hook(name, i=None):
            pass

        for a, b in ((tokens_h, tokens), (w1_h, w1), (w2_h, w2), (wu_h, wu), (wp_h, wp), (small_h, sm)):
            bring(a, b).wait()
        small_parameters()

    hook(START)
    tile = rows // nz
    steps = rows // tile

    def tiles(i):
        return pl.ds(pl.multiple_of(i * tile, tile), tile)

    def loop(count, body):
        def step(i, _):
            body(i)
            return 0

        lax.fori_loop(0, count, step, 0)

    saved = []

    def save(src, dst):
        saved.append(bring(src, dst))

    for g in range(groups):
        hook(NEED_QKV + g)
        lo = g * wide
        bias = (vec_o[0:1, lo : lo + wide], None, vec_o[1:2, lo : lo + wide])

        def project(i):
            r = tiles(i)
            got = nn(tokens[r, :], w1[g].reshape(width, 3 * wide))
            for p in range(3):
                mine = got[:, p * wide : (p + 1) * wide]
                qkv[r, p * width + lo : p * width + lo + wide] = (mine if bias[p] is None else mine + bias[p]).astype(BF16)
            hook(PROJECT + g, i)

        loop(steps, project)

        def attention(i):
            s, hp = i // gp, g * gp + i % gp
            attend_forward(qkv, ctx, lse_o, lengths, s * pairs + hp, span, width, size)
            hook(ATTEND + g, i)

        loop(seqs * gp, attention)
    if comm:
        save(w1, w1_h)
    save(qkv, qkv_h)
    save(ctx, ctx_h)

    hook(NEED_OUT)
    b_out, g_first, s_first, b_outer, g_second, s_second = (vec_o[n : n + 1, :] for n in range(2, 8))

    def norm_one(i):
        r = tiles(i)
        resid = tokens[r, :].astype(F32) + (nn(ctx[r, :], w2[0].reshape(width, width)) + b_out)
        centred = resid - rowmean(resid)
        inv = lax.rsqrt(rowmean(centred * centred) + EPS)
        unit_ = centred * inv
        u1[r, :] = unit_.astype(BF16)
        inv_o[0, r, :] = jnp.broadcast_to(inv, (tile, 128))
        h = unit_ * g_first + s_first
        hid[r, :] = h + b_outer
        hidlow[r, :] = h.astype(BF16)
        hook(NORM, i)

    loop(steps, norm_one)
    save(u1, u1_h)
    save(hidlow, hid_h)
    for b in range(nb):
        hook(NEED_INNER + b)
        cols = slice(b * width, (b + 1) * width)

        def expand(i):
            r = tiles(i)
            a, g = gelu_both(nn(hidlow[r, :], w2[b + 1].reshape(width, width)) + ib_o[0:1, cols])
            act[r, cols] = a.astype(BF16)
            dg[i, :, :, cols] = g.astype(BF16).reshape(2, tile // 2, width)
            hook(EXPAND + b, i)

        loop(steps, expand)
    if comm:
        save(w2, w2_h)
    save(act, act_h)
    save(dg, dg_h)

    for j in range(nu):
        hook(NEED_OUTER + j)
        if comm:
            save(wu.at[j], wu_h.at[j])

        def contract(i):
            r = tiles(i)
            a = jnp.concatenate([act[r, f * fr + j * ur : f * fr + (j + 1) * ur] for f in range(nf)], axis=1)
            resid = hid[r, :] + nn(a, wu[j].reshape(nf * ur, width))
            if j < nu - 1:
                hid[r, :] = resid
            else:
                centred = resid - rowmean(resid)
                inv = lax.rsqrt(rowmean(centred * centred) + EPS)
                unit_ = centred * inv
                u2[r, :] = unit_.astype(BF16)
                inv_o[1, r, :] = jnp.broadcast_to(inv, (tile, 128))
                layer = unit_ * g_second + s_second
                each = span // tile
                s, t = i // each, i % each

                @pl.when(t == 0)
                def _():
                    first_o[pl.ds(pl.multiple_of(s * 8, 8), 8), :] = layer[0:8, :]

                slot = lax.broadcasted_iota(jnp.int32, (tile, width), 0) + t * tile
                outv[r, :] = jnp.where(slot < lengths[s], layer, 0.0).astype(BF16)
            hook(CONTRACT + j, i)

        loop(steps, contract)
    save(u2, u2_h)
    save(outv, out_h)
    hook(NEED_POOL)
    if comm:
        save(wp, wp_h)
    for cp in saved:
        cp.wait()
    if comm:
        for n in range(others):
            small(n, f_me).wait_send()

        for n in range(len(units)):
            unit(n).drain()


def forward(plan, tokens, lengths, wqkv, wout, winner, wouter, wpool, small, nz):
    rows, width = tokens.shape
    seqs = lengths.shape[0]
    span = rows // seqs
    nf = nz * 2
    ff = winner.shape[1]
    part = width // nf
    ur = ff // nf // 3
    any_, vm, smem = (pl.BlockSpec(memory_space=m) for m in (pl.ANY, pltpu.VMEM, pltpu.SMEM))
    S = jax.ShapeDtypeStruct
    pairs = HEADS // 2
    weights = [(3, nz, 2, part, width), (1 + ff // width, nz, 2, part, width), (3, nz, 2, ur, width), (1, nz, 2, part, width)]
    outs = [
        (S((rows, width), BF16), any_),
        *[(S(w, BF16), any_) for w in weights],
        (S((16, width), F32), vm),
        (S((8, ff), F32), vm),
        (S((rows, 3 * width), BF16), any_),
        (S((rows, width), BF16), any_),
        (S((seqs * pairs, 8, span), F32), vm),
        (S((rows, width), BF16), any_),
        (S((rows, width), BF16), any_),
        (S((rows, ff), BF16), any_),
        (S((nz, 2, rows // (2 * nz), ff), BF16), any_),
        (S((rows, width), BF16), any_),
        (S((2, rows, 128), F32), vm),
        (S((8 * seqs, width), F32), vm),
    ]
    V = pltpu.VMEM
    D = pltpu.SemaphoreType.DMA
    units = sum(w[0] for w in weights)
    sems = 8 * (units + len(FINE) * (nz - 1))
    scratch = [
        V((rows, width), BF16),
        *[V(w, BF16) for w in weights],
        V((nf, 16, 128), BF16),
        V((rows, 3 * width), BF16),
        V((rows, width), BF16),
        V((rows, width), F32),
        V((rows, width), BF16),
        V((rows, width), BF16),
        V((rows, ff), BF16),
        V((nz, 2, rows // (2 * nz), ff), BF16),
        V((rows, width), BF16),
        V((rows, width), BF16),
        D((64,)), D((nf,)), D((nf,)),
        D((sems,)), D((sems,)),
        *[V(v.shape, BF16) for v in small],
    ]
    params = pltpu.CompilerParams(vmem_limit_bytes=60 * 2**20, has_side_effects=True, collective_id=0)
    cost = pl.CostEstimate(flops=2 * rows * width * (4 * width + 2 * ff), bytes_accessed=10**7, transcendentals=0)

    def kernel(*refs):
        n = 7 + len(small)
        forward_kernel(plan, *refs[:7], refs[7:n], *refs[n:])

    return pl.pallas_call(
        kernel, out_shape=[o[0] for o in outs], out_specs=[o[1] for o in outs], in_specs=[any_, smem] + [any_] * (5 + len(small)),
        scratch_shapes=scratch, compiler_params=params, cost_estimate=cost,
    )(tokens, lengths, wqkv, wout, winner, wouter, wpool, *small)


def attend_backward(kv, gctx, lse, lengths, s, hp, span, width, size):
    wide = 2 * size
    pairs = width // wide
    rows = pl.ds(pl.multiple_of(s * span, span), span)

    def cols(p):
        return pl.ds(pl.multiple_of(p * width + hp * wide, wide), wide)

    q, k, v = (kv[rows, cols(p)] for p in range(3))
    g = gctx[rows, cols(0)]
    logs = lse[s * pairs + hp]
    lane = lax.broadcasted_iota(jnp.int32, (span, wide), 1)
    slot = lax.broadcasted_iota(jnp.int32, (span, wide), 0)
    fill = jnp.where(slot < lengths[s], 0.0, NEG).astype(BF16)
    scale = size ** (-0.5)
    factor = scale * LOG2E
    kt = k.T
    gqs, gks, gvs = [], [], []
    for h in range(2):
        mine = lane < size if h == 0 else lane >= size
        other = (1 - h) * size
        qh = jnp.where(mine, q, jnp.where(lane == other, 1.0, 0.0).astype(BF16))
        kh = jnp.where(mine, k, fill)
        vh = jnp.where(mine, v, jnp.zeros_like(v))
        p = jnp.exp2(nt(kh, qh) * factor - logs[h : h + 1, :])
        gvs.append(nn(p.astype(BF16), g))
        gp = nt(vh, g)
        delta = jnp.sum(gp * p, axis=0, keepdims=True)
        gs = (p * (gp - delta)).astype(BF16)
        gks.append(nn(gs, q))
        gqs.append(nn(kt, gs)[h * size : (h + 1) * size, :])
    kv[rows, cols(0)] = (jnp.concatenate(gqs, axis=0).T * scale).astype(BF16)
    kv[rows, cols(1)] = (jnp.where(lane < size, gks[0], gks[1]) * scale).astype(BF16)
    kv[rows, cols(2)] = jnp.where(lane < size, gvs[0], gvs[1]).astype(BF16)


class Spread:
    def __init__(self, buf, send, recv):
        self.buf, self.send, self.recv = buf, send, recv
        self.nz = buf.shape[3]
        self.me = here()

    def copy(self, n, incoming):
        x, c, z, y = self.me
        nz = self.nz
        if n < nz - 1:
            k = n + 1
            peer = (x, c, lax.rem(z + k, nz), y)
            ref = self.buf.at[x, c, y, lax.rem(z + nz - k, nz) if incoming else z]
        elif n == nz - 1:
            peer = (x, c, z, 1 - y)
            ref = self.buf.at[x, c, 1 - y if incoming else y]
        elif n == nz:
            peer = (1 - x, c, z, y)
            ref = self.buf.at[1 - x if incoming else x, c]
        else:
            peer = (x, 1 - c, z, y)
            ref = self.buf.at[:, 1 - c if incoming else c]
        return pltpu.make_async_remote_copy(
            src_ref=ref, dst_ref=ref, send_sem=self.send.at[n], recv_sem=self.recv.at[n], device_id=at(*peer), device_id_type=MESH
        )

    def step(self, j):
        nz = self.nz
        if j == 0:
            for n in range(nz - 1):
                self.copy(n, False).start()
            return
        if j == 1:
            for n in range(nz - 1):
                self.copy(n, True).wait_recv()
        else:
            self.copy(nz + j - 3, True).wait_recv()
        if j < 4:
            self.copy(nz + j - 2, False).start()

    def drain(self):
        for n in range(self.nz + 2):
            self.copy(n, False).wait_send()


class Scatter:
    def __init__(self, g, r, split, out, sems, n, ahead=None, boxes=None):
        self.g, self.split, self.out, self.n, self.ahead = g, split, out, n, ahead
        self.send, self.recv = (e.at[n] for e in sems)
        self.lead, _, rows, cols = g.shape
        self.me = x, c, z, y = here()
        h, r2 = cols // 2, rows // 2
        t, e = pl.ds(h, split), pl.ds(h + split, h - split)
        top, low = pl.ds(0, r2), pl.ds(r2, r2)
        self.r1, self.ry1, self.rx2 = r.at[:, :, :, pl.ds(0, h)], r.at[:, 0, :, t], r.at[:, :, top, e]
        self.ry2 = r.at[:, 0, low, e]
        nz = self.lead
        if ahead is None:
            self.za, self.zb = [[r.at[k, 1, q, w] for k in range(nz - 1)] for q, w in ((pl.ds(0, rows), t), (low, e))]
            self.all_za, self.all_zb = (r.at[pl.ds(0, nz - 1), 1, q, w] for q, w in ((pl.ds(0, rows), t), (low, e)))
            self.xe = r.at[nz - 1, 1, :, t]
        else:
            self.za, self.zb = [[b.at[:, 1, q, w] for b in boxes[: nz - 1]] for q, w in ((pl.ds(0, rows), t), (low, e))]
            self.xe = boxes[nz - 1].at[:, 1, :, t]
        self.all_sems = sems
        self.rows = pl.ds(pl.multiple_of(x * r2, 16), r2)
        self.rows_o = pl.ds(pl.multiple_of((1 - x) * r2, 16), r2)
        self.mine = pl.ds(pl.multiple_of(c * h, 128), h)
        self.theirs = pl.ds(pl.multiple_of((1 - c) * h, 128), h)
        self.a1 = pl.ds(pl.multiple_of(c * h, 128), split)
        self.a2 = pl.ds(pl.multiple_of(c * h + split, 128), h - split)

    def region(self, rows, cols):
        return self.out.at[rows, cols] if self.ahead is None else self.out.at[:, rows, cols]

    def remote(self, src, dst, n, peer, unit=None):
        send, recv = (self.send, self.recv) if unit is None else (e.at[unit] for e in self.all_sems)
        return pltpu.make_async_remote_copy(
            src_ref=src, dst_ref=dst, send_sem=send.at[n], recv_sem=recv.at[n], device_id=at(*peer), device_id_type=MESH
        )

    def copy(self, n):
        x, c, z, y = self.me
        g, nz = self.g, self.lead
        every = slice(None)
        core, xn, yn = (x, 1 - c, z, y), (1 - x, c, z, y), (x, c, z, 1 - y)
        if n == 0:
            return self.remote(g.at[:, :, :, self.theirs], self.r1, n, core)
        if n == 1:
            return self.remote(g.at[:, 1 - y, :, self.a1], self.ry1, n, yn)
        if n == 2:
            return self.remote(g.at[:, :, self.rows_o, self.a2], self.rx2, n, xn)
        if n == 3:
            return self.remote(g.at[:, 1 - y, self.rows, self.a2], self.ry2, n, yn)
        if n < 2 * nz + 2:
            k = (n - 4) % (nz - 1) + 1
            zk = lax.rem(z + k, nz)
            lead = zk if self.ahead is None else every
            rows, cols, to = (every, self.a1, self.za) if n < nz + 3 else (self.rows, self.a2, self.zb)
            return self.remote(g.at[lead, y, rows, cols], to[k - 1], 4 if n < nz + 3 else 5, (x, c, zk, y))
        if n == 2 * nz + 2:
            return self.remote(self.region(every, self.a1), self.xe, 6, xn)
        if n == 2 * nz + 3:
            ref = self.region(self.rows, self.a2)
            return self.remote(ref, ref, 7, xn)
        ref = self.region(every, self.mine)
        return self.remote(ref, ref, 8, core)

    def got(self, n):
        x, c, z, y = self.me
        nz = self.lead
        if 3 < n < 2 * nz + 2 and self.ahead is not None:
            k = (n - 4) % (nz - 1) + 1
            ref = (self.za if n < nz + 3 else self.zb)[k - 1]
            self.remote(ref, ref, 4 if n < nz + 3 else 5, (x, c, lax.rem(z + nz - k, nz), y), k - 1).wait_recv()
        elif n == 2 * nz + 3:
            ref = self.region(self.rows_o, self.a2)
            self.remote(ref, ref, 7, (1 - x, c, z, y)).wait_recv()
        elif n == 2 * nz + 4:
            ref = self.region(slice(None), self.theirs)
            self.remote(ref, ref, 8, (x, 1 - c, z, y)).wait_recv()
        else:
            self.copy(n).wait_recv()

    def all_along(self, first):
        x, c, z, y = self.me
        ref = self.all_za if first == 4 else self.all_zb
        return self.remote(ref, ref, 4 if first == 4 else 5, (x, c, lax.rem(z + 1, self.lead), y))

    def along_z(self, first):
        if self.ahead is None:
            for k in range(1, self.lead):
                self.copy(first + k - 1).start()
        elif self.ahead:
            self.copy(first + self.ahead - 1).start()

    def over_z(self, first, boxes, rows, cols):
        y, z = self.me[3], self.me[2]
        total = (self.g[z, y, rows, cols] if self.ahead is None else self.g[:, y, rows, cols]).astype(F32)
        if self.ahead is None:
            self.all_along(first).wait_recv()
        for k in range(1, self.lead):
            if self.ahead is not None:
                self.got(first + k - 1)
            total += boxes[k - 1][...].astype(F32)
        self.region(rows, cols)[...] = total.astype(BF16)

    def step(self, j):
        g, y, nz = self.g, self.me[3], self.lead
        last = 2 * nz + 2

        def adds(body):
            def step(i, _):
                body(i)
                return 0

            lax.fori_loop(0, nz, step, 0)

        if j == 0:
            self.copy(0).start()
        elif j == 1:
            self.got(0)

            def add(i):
                for yy in range(2):
                    g[i, yy, :, self.mine] = g[i, yy, :, self.mine] + self.r1[i, yy]

            adds(add)
            self.copy(1).start()
            self.copy(2).start()
        elif j == 2:
            self.got(2)

            def add(i):
                for yy in range(2):
                    g[i, yy, self.rows, self.a2] = g[i, yy, self.rows, self.a2] + self.rx2[i, yy]

            adds(add)
            self.copy(3).start()
            self.got(1)

            def add(i):
                g[i, y, :, self.a1] = g[i, y, :, self.a1] + self.ry1[i]

            adds(add)
            self.along_z(4)
        elif j == 3:
            self.got(3)

            def add(i):
                g[i, y, self.rows, self.a2] = g[i, y, self.rows, self.a2] + self.ry2[i]

            adds(add)
            self.along_z(nz + 3)
        elif j == 4:
            self.over_z(4, self.za, slice(None), self.a1)
            self.copy(last).start()
        elif j == 5:
            self.over_z(nz + 3, self.zb, self.rows, self.a2)
            self.copy(last + 1).start()
        elif j == 6:
            self.copy(last).wait_send()
            self.got(last)
            ref = self.region(slice(None), self.a1)
            ref[...] = ref[...] + self.xe[...]
            self.got(last + 1)
            self.copy(last + 2).start()
        else:
            self.got(last + 2)

    def drain(self):
        nz = self.lead
        for n in range(4):
            self.copy(n).wait_send()
        if self.ahead is None:
            self.all_along(4).wait_send()
            self.all_along(nz + 3).wait_send()
        elif self.ahead:
            self.copy(3 + self.ahead).wait_send()
            self.copy(nz + 2 + self.ahead).wait_send()
        if not self.ahead:
            self.copy(2 * nz + 3).wait_send()
            self.copy(2 * nz + 4).wait_send()


def backward_kernel(plan, lengths, labels, vec, lse, first, inv_h, cot_h, tok_h, w1_h, w2_h, wu_h, wp_h, qkv_h, ctx_h, hid_h, u1_h, act_h, dg_h, u2_h,
                    loss_o, own_o, ib_o, pool_o, class_o, wo_o, wi_o, wu_o, wq_o, tg_h,
                    A, D, w2, w3, cot, u2, u1, hid, gffn, gr, inv, acc, gfirst,
                    G, R, early, late, loc, free, s_rs, r_rs, s_sp, r_sp):
    comm = plan is not None
    x, c, z, y = here() if comm else (0, 0, 0, 0)
    rows, width = cot.shape
    seqs = lengths.shape[0]
    span = rows // seqs
    ff = A.shape[1]
    size = width // HEADS
    nz = D.shape[0]
    tile = rows // nz
    nb = ff // width
    part = width // (2 * nz)
    fr = ff // (2 * nz)
    ur = wu_h.shape[3]
    groups = w1_h.shape[0]
    loads = {}

    def load(name, src, dst):
        cp = pltpu.make_async_copy(src, dst, loc.at[len(loads)])
        cp.start()
        loads[name] = cp

    load("wp", wp_h.at[0], w3.at[:, :, pl.ds(fr, part), :])
    load("cot", cot_h, cot)
    load("u2", u2_h, u2)
    load("inv2", inv_h.at[1], inv)

    if comm:
        barrier = pltpu.get_barrier_semaphore()
        peers = [(x, c, lax.rem(z + k, nz), y) for k in range(1, nz)]
        peers += [(x, c, z, 1 - y), (1 - x, c, z, y), (x, 1 - c, z, y)]
        for p in peers:
            pl.semaphore_signal(barrier, inc=1, device_id=at(*p), device_id_type=MESH)

        def scatter(n):
            sems = (s_rs, r_rs)
            split = SPLIT[n]
            if n < nz:
                return Scatter(G.at[n], R.at[n], split, wu_o, sems, n, (n + 1) % nz, [R.at[k] for k in range(nz)])
            if n < nz + nb:
                b = n - nz
                return Scatter(G.at[n], R.at[n], split, wi_o.at[:, pl.ds(b * width, width)], sems, n)
            q = n - nz - nb
            return Scatter(D.at[:, :, pl.ds(0, part), pl.ds(q * width, width)], w2.at[q], split, wo_o if q == 0 else wq_o.at[q - 1], sems, n)

        blocks = nz + nb + 1 + groups
        small = [Spread(early, s_sp.at[0], r_sp.at[0]), Spread(late, s_sp.at[1], r_sp.at[1])]

        def hook(name, i=None):
            if i is None:
                for n, j in plan.get(name, ()):
                    if n < blocks:
                        scatter(n).step(j)
                    elif n < blocks + 2:
                        small[n - blocks].step(j)
                    else:
                        scatter(nz - 1).step(j)
                return
            if isinstance(i, int):
                hook((name, i))
                return
            for k in range(8):
                if (name, k) in plan:
                    pl.when(i == k)(functools.partial(hook, (name, k)))
    else:
        def hook(name, i=None):
            pass

    acc[...] = jnp.zeros_like(acc)

    loads["wp"].wait()
    load("act", act_h, A)
    gain2, gain1 = vec[6:7, :], vec[3:4, :]

    def colsum(v):
        return jnp.sum(v, axis=0, keepdims=True)

    per = span // tile
    steps = rows // tile

    def second_norm(i, _):
        r = pl.ds(pl.multiple_of(i * tile, tile), tile)
        s, j = i // per, i % per
        slot = lax.broadcasted_iota(jnp.int32, (tile, width), 0) + j * tile
        gl = jnp.where(slot < lengths[s], cot[r, :].astype(F32), 0.0)
        head = gfirst[pl.ds(pl.multiple_of(8 * s, 8), 8), :] * jnp.where(j == 0, 1.0, 0.0)
        gl = gl + jnp.concatenate([head, jnp.zeros((tile - 8, width), F32)], axis=0)
        u = u2[r, :].astype(F32)
        a = gl * gain2
        g2 = (a - rowmean(a) - u * rowmean(a * u)) * inv[r, :][:, :1]
        gr[r, :] = g2
        low = g2.astype(BF16)
        gffn[r, :] = low
        tally(3, [(colsum(low.astype(F32)), colsum(gl * u), colsum(gl))])
        return 0

    def tally(first_row, parts):
        for n in range(len(parts[0])):
            acc[first_row + n : first_row + n + 1, :] += sum(p[n] for p in parts[1:]) + parts[0][n]

    lane = lax.broadcasted_iota(jnp.int32, (8 * seqs, 128), 1)
    row = lax.broadcasted_iota(jnp.int32, (8 * seqs, 128), 0)
    live = (lane >= 1) & (lane < 4)
    w_pool = w3[:, :, fr:, :].reshape(width, width)
    first_low = first[...].astype(BF16)
    pooled = jnp.tanh(nn(first_low, w_pool) + vec[8:9, :])
    pooled_low = pooled.astype(BF16)
    heads = jnp.concatenate([vec[8:16, :], jnp.zeros((120, width), F32)], axis=0).astype(BF16)
    logits = nt(pooled_low, heads) + vec[15:16, :128]
    peak = jnp.max(jnp.where(live, logits, -3.0e38), axis=-1, keepdims=True)
    mass = jnp.where(live, jnp.exp(logits - peak), 0.0)
    logsum = peak + jnp.log(jnp.sum(mass, axis=-1, keepdims=True))
    label = jnp.full((8 * seqs, 128), labels[0])
    for s in range(1, seqs):
        label = jnp.where(row >= 8 * s, labels[s], label)
    onehot = jnp.where(lane == label + 1, 1.0, 0.0)
    loss_o[...] = jnp.broadcast_to(logsum - jnp.sum(onehot * logits, axis=-1, keepdims=True), loss_o.shape)
    g_logits = jnp.where(live & (row % 8 == 0), jnp.exp(logits - logsum) - onehot, 0.0).astype(BF16)
    g_pre = (nn(g_logits, heads) * (1.0 - pooled * pooled)).astype(BF16)
    g_first = nt(g_pre, w_pool)

    gfirst[...] = g_first
    for name in ("cot", "u2", "inv2"):
        loads[name].wait()
    lax.fori_loop(0, steps, second_norm, 0)
    load("tok", tok_h, u2)
    load("inv1", inv_h.at[0], inv)

    loads["act"].wait()
    for j in range(fr // ur):
        load(("wu", j), wu_h.at[j], w3.at[:, :, pl.ds(j * ur, ur), :])
    load("dg", dg_h, D)
    load("hid", hid_h, hid)
    if comm:
        pl.semaphore_wait(barrier, len(peers))

    def outer_grad(k, _):
        owner = lax.rem(z + k + 1, nz)
        for yy in range(2):
            f = owner * 2 + yy
            got = tn(A[:, pl.ds(pl.multiple_of(f * fr, 128), fr)], gffn[...]).astype(BF16)
            G[k, :, yy] = got.reshape(nb, part, width)
        hook(OUTER_GRAD, k)
        return 0

    lax.fori_loop(0, nz, outer_grad, 0)
    load("qkv", qkv_h, A.at[:, pl.ds(0, 3 * width)])
    load("ctx", ctx_h, A.at[:, pl.ds(3 * width, width)])
    for j in range(fr // ur):
        loads[("wu", j)].wait()
    loads["dg"].wait()
    load("w2", w2_h, w2)
    load("u1", u1_h, u1)

    def inner_back(i, _):
        r = pl.ds(pl.multiple_of(i * tile, tile), tile)
        for b in range(nb):
            cols = slice(b * width, (b + 1) * width)
            w = w3[b, :, :fr, :].reshape(width, width)
            g = nt(gffn[r, :], w) * D[i, :, :, cols].reshape(tile, width).astype(F32)
            low = g.astype(BF16)
            D[i, :, :, cols] = low.reshape(2, tile // 2, width)
            acc[6 + b : 7 + b, :] += colsum(low.astype(F32))
        hook(INNER_BACK, i)
        return 0

    lax.fori_loop(0, rows // tile, inner_back, 0)
    for g in range(groups):
        load(("w1", g), w1_h.at[g], w3.at[:, :, pl.ds(g * part, part), :])

    loads["hid"].wait()

    def inner_grad(b, _):
        cols = pl.ds(pl.multiple_of(b * width, width), width)
        for m in range(2):
            h = width // 2
            got = tn(hid[:, m * h : (m + 1) * h], D[:, :, :, cols].reshape(rows, width)).astype(BF16)
            G[nz + b, m * nz // 2 : (m + 1) * nz // 2] = got.reshape(nz // 2, 2, part, width)
        hook(INNER_GRAD, b)
        return 0

    lax.fori_loop(0, nb, inner_grad, 0)

    loads["w2"].wait()
    loads["u1"].wait()
    loads["inv1"].wait()

    def hidden_grad(i):
        r = slice(i * tile, (i + 1) * tile)
        gh = gr[r, :]
        for b in range(nb):
            gh += nt(D[i, :, :, b * width : (b + 1) * width].reshape(tile, width), w2[b + 1].reshape(width, width))
        return gh

    def first_norm(i, gh):
        r = slice(i * tile, (i + 1) * tile)
        u = u1[r, :].astype(F32)
        a = gh * gain1
        g1 = (a - rowmean(a) - u * rowmean(a * u)) * inv[r, :][:, :1]
        low = g1.astype(BF16)
        cot[r, :] = low
        tally(0, [(colsum(low.astype(F32)), colsum(gh * u), colsum(gh))])
        gffn[r, :] = nt(low, w2[0].reshape(width, width)).astype(BF16)
        gr[r, :] = g1

    for i in range(steps + 1):
        if i < steps:
            ahead = hidden_grad(i)
        if i:
            first_norm(i - 1, behind)
        if i < steps:
            gr[i * tile : (i + 1) * tile, :] = ahead
            behind = gr[i * tile : (i + 1) * tile, :]
        hook(FIRST_NORM, i)
    if comm:
        for p in peers:
            pl.semaphore_signal(free, inc=1, device_id=at(*p), device_id_type=MESH)
        pay = jnp.concatenate(
            [acc[0:10, :]]
            + [first_low[8 * s : 8 * s + 1, :].astype(F32) for s in range(seqs)]
            + [g_pre[8 * s : 8 * s + 1, :].astype(F32) for s in range(seqs)]
            + [pooled_low[8 * s : 8 * s + 1, :].astype(F32) for s in range(seqs)],
            axis=0,
        )
        early[x, c, y, z] = pay.astype(BF16)

    loads["ctx"].wait()
    loads["qkv"].wait()
    for m in range(2):
        h = width // 2
        got = tn(A[:, 3 * width + m * h : 3 * width + (m + 1) * h], cot[...]).astype(BF16)
        D[m * nz // 2 : (m + 1) * nz // 2, :, :part, :width] = got.reshape(nz // 2, 2, part, width)
    if comm:
        pl.semaphore_wait(free, len(peers))
    hook(OUT_GRAD)

    loads["tok"].wait()
    pairs = HEADS // 2
    gp = pairs // groups
    wide = gp * 2 * size
    def finish_late():
        late_rows = [acc[10 + n : 11 + n, j * 128 : (j + 1) * 128] for n in range(2) for j in range(width // 128)]
        late_rows += [g_logits[8 * s : 8 * s + 1, :].astype(F32) for s in range(seqs)]
        late_rows.append(jnp.zeros((16 - len(late_rows), 128), F32))
        late[x, c, y, z] = jnp.concatenate(late_rows, axis=0).astype(BF16)

    for q in range(groups):
        def attention(i, _):
            attend_backward(A, gffn, lse, lengths, i // gp, q * gp + i % gp, span, width, size)
            hook(ATTEND_BACK + q, i)
            return 0

        lax.fori_loop(0, seqs * gp, attention, 0)
        for p in range(3):
            block_of = A[:, p * width + q * wide : p * width + (q + 1) * wide]
            got = tn(u2[...], block_of).astype(BF16)
            D[:, :, :part, (q + 1) * width + p * wide : (q + 1) * width + (p + 1) * wide] = got.reshape(nz, 2, part, wide)
            if p != 1:
                acc[10 + p // 2 : 11 + p // 2, q * wide : (q + 1) * wide] = colsum(block_of.astype(F32))
        if comm and q == groups - 1:
            finish_late()
        hook(QKV_GRAD + q)
    for g in range(groups):
        loads[("w1", g)].wait()

    def input_grad(i, _):
        r = pl.ds(pl.multiple_of(i * tile, tile), tile)
        total = gr[r, :]
        for g in range(groups):
            w = w3[:, :, g * part : (g + 1) * part, :].reshape(width, width)
            mine = jnp.concatenate([A[r, p * width + g * wide : p * width + (g + 1) * wide] for p in range(3)], axis=1)
            total += nt(mine, w)
        cot[r, :] = total.astype(BF16)
        hook(INPUT_GRAD, i)
        return 0

    lax.fori_loop(0, rows // tile, input_grad, 0)
    back = pltpu.make_async_copy(cot, tg_h, loc.at[len(loads)])
    back.start()
    hook(SMALL_SUMS)
    if comm:
        n = 4 * 2 * nz
        def slot_of(i):
            return (i // (4 * nz), i // (2 * nz) % 2, i // nz % 2, i % nz)

        total = lax.fori_loop(0, n, lambda i, t: t + early[slot_of(i)].astype(F32), jnp.zeros((16, width), F32))
        lates = late[...].reshape(n, 16, 128)
        lsum = jnp.sum(lates.astype(F32), axis=0)
        six = width // 128
        qb = jnp.concatenate([lsum[j : j + 1, :] for j in range(six)], axis=1)
        vb = jnp.concatenate([lsum[six + j : six + j + 1, :] for j in range(six)], axis=1)
        r16 = lax.broadcasted_iota(jnp.int32, (16, width), 0)
        total = jnp.where(r16 == 10, qb, jnp.where(r16 == 11, vb, total))
        f = z * 2 + y
        src = lax.broadcasted_iota(jnp.int32, (width, 128), 0)
        dst = lax.broadcasted_iota(jnp.int32, (width, 128), 1)
        pick = jnp.where((src == dst + f * part) & (dst < part), 1.0, 0.0).astype(BF16)
        src = lax.broadcasted_iota(jnp.int32, (width, fr), 0)
        dst = lax.broadcasted_iota(jnp.int32, (width, fr), 1)
        pick_ff = jnp.where(src == dst + y * fr, 1.0, 0.0).astype(BF16)
        high = total.astype(BF16)
        rest = (total - high.astype(F32)).astype(BF16)
        own = nn(high, pick) + nn(rest, pick)
        wide_own = nn(high, pick_ff) + nn(rest, pick_ff)
        r16f = lax.broadcasted_iota(jnp.int32, (16, fr), 0)
        ib_o[...] = jnp.broadcast_to(colsum(jnp.where(r16f == 6 + z, wide_own, 0.0)), ib_o.shape)
        flat = early[...].reshape(n * 16, width)
        chosen = nn(flat, pick)
        rid = lax.broadcasted_iota(jnp.int32, (n * 16, 128), 0) % 16
        firsts = pltpu.roll(jnp.where((rid >= 10) & (rid < 10 + seqs), chosen, 0.0), seqs, 0).astype(BF16)
        pool_o[...] = tn(firsts, flat)
        pooleds = pltpu.roll(jnp.where(rid >= 10 + 2 * seqs, chosen, 0.0), n * 16 - seqs, 0).astype(BF16)
        class_o[...] = tn(lates.reshape(n * 16, 128), pooleds)
        middle = (rid >= 10 + seqs) & (rid < 10 + 2 * seqs)
        pb = colsum(jnp.where(middle, chosen, 0.0))
        cbg = colsum(jnp.where(middle, lates.reshape(n * 16, 128).astype(F32), 0.0))
        r16s = lax.broadcasted_iota(jnp.int32, (16, 128), 0)
        own_o[...] = jnp.where(r16s == 12, pb, jnp.where(r16s == 13, cbg, own))
        hook(LAST)
        for spread in small:
            spread.drain()
        for n in range(blocks):
            scatter(n).drain()
    back.wait()


def backward(plan, lengths, labels, vec, lse, inv, first, cot, tok, w1, w2, wu, wp, qkv, ctx, hid, u1, act, dg, u2):
    rows, width = cot.shape
    nz = w1.shape[1]
    ff = act.shape[1]
    part = width // (2 * nz)
    fr = ff // (2 * nz)
    nb = ff // width
    seqs = lengths.shape[0]
    any_, vm, smem = (pl.BlockSpec(memory_space=m) for m in (pl.ANY, pltpu.VMEM, pltpu.SMEM))
    S = jax.ShapeDtypeStruct
    outs = [
        (S((8 * seqs, 128), F32), vm),
        (S((16, 128), F32), vm),
        (S((8, fr), F32), vm),
        (S((128, width), F32), vm),
        (S((128, 128), F32), vm),
        (S((part, width), BF16), vm),
        (S((part, ff), BF16), vm),
        (S((nb, part, width), BF16), vm),
        (S((3, part, width), BF16), vm),
        (S((rows, width), BF16), any_),
    ]
    V = pltpu.VMEM
    D = pltpu.SemaphoreType.DMA
    n = 2 * nb
    scratch = [
        V((rows, ff), BF16),
        V(dg.shape, BF16),
        V((1 + nb, nz, 2, part, width), BF16),
        V((nz, 2, fr + part, width), BF16),
        V((rows, width), BF16),
        V((rows, width), BF16),
        V((rows, width), BF16),
        V((rows, width), BF16),
        V((rows, width), BF16),
        V((rows, width), F32),
        V((rows, 128), F32),
        V((16, width), F32),
        V((8 * seqs, width), F32),
        V((n, nz, 2, part, width), BF16),
        V((n, nz, 2, part, width), BF16),
        V((2, 2, 2, nz, 16, width), BF16),
        V((2, 2, 2, nz, 16, 128), BF16),
        D((24,)),
        pltpu.SemaphoreType.REGULAR,
        D((n + 4, 9)), D((n + 4, 9)), D((2, nz + 2)), D((2, nz + 2)),
    ]
    params = pltpu.CompilerParams(vmem_limit_bytes=63 * 2**20, has_side_effects=True, **({"collective_id": 1} if plan is not None else {}))
    cost = pl.CostEstimate(flops=4 * rows * width * (4 * width + 2 * ff), bytes_accessed=10**7, transcendentals=0)
    return pl.pallas_call(
        functools.partial(backward_kernel, plan), out_shape=[o[0] for o in outs], out_specs=[o[1] for o in outs],
        in_specs=[smem, smem] + [vm] * 3 + [any_] * 14, scratch_shapes=scratch, compiler_params=params, cost_estimate=cost,
    )(lengths, labels, vec, lse, first, inv, cot, tok, w1, w2, wu, wp, qkv, ctx, hid, u1, act, dg, u2)


def finish_kernel(output, tg, loss, own, ibg, poolg, classg, wo, wi, wu, wq,
                  output_o, loss_o, tg_o, qkv_o, qb_o, vb_o, wo_o, ob_o, g1_o, s1_o, wi_o, ib_o, wu_o, outb_o, g2_o, s2_o, pool_o, pb_o, class_o, cb_o):
    output_o[...] = output[...]
    tg_o[...] = tg[...]
    part, width = wo.shape
    groups, _, wide3 = wq.shape
    wide = wide3 // groups
    for p in range(3):
        for g in range(groups):
            qkv_o[:, p * width + g * wide : p * width + (g + 1) * wide] = wq[g, :, p * wide : (p + 1) * wide].astype(F32)
    wo_o[...] = wo[...].astype(F32)
    wi_o[...] = wi[...].astype(F32)
    wu_o[...] = wu[...].reshape(wu_o.shape).astype(F32)
    pool_o[...] = poolg[:part, :]
    for n, ref in ((10, qb_o), (11, vb_o), (0, ob_o), (1, g1_o), (2, s1_o), (3, outb_o), (4, g2_o), (5, s2_o), (12, pb_o)):
        ref[...] = own[n, :part]
    ib_o[...] = ibg[0, :]
    classes = cb_o.shape[0]
    cb_o[...] = own[13, 1 : 1 + classes]
    class_o[...] = classg[1 : 1 + classes, :part]
    for s in range(loss_o.shape[0]):
        loss_o[s : s + 1] = loss[8 * s, 0:1]


def finish(output, tg, loss, own, ibg, poolg, classg, wo, wi, wu, wq, classes):
    part, width = wo.shape
    ff = wi.shape[1]
    S = jax.ShapeDtypeStruct
    any_, vm = (pl.BlockSpec(memory_space=m) for m in (pl.ANY, pltpu.VMEM))
    vector = S((part,), F32)
    outs = [S(output.shape, BF16), S((loss.shape[0] // 8,), F32), S(tg.shape, BF16), S((part, 3 * width), F32), vector, vector,
            S((part, width), F32), vector, vector, vector, S((part, ff), F32), S((ibg.shape[1],), F32), S((wu.shape[0] * part, width), F32),
            vector, vector, vector, S((part, width), F32), vector, S((classes, part), F32), S((classes,), F32)]
    *done, classes_t, class_b = pl.pallas_call(
        finish_kernel, out_shape=outs, in_specs=[vm] * 11, out_specs=[vm] * 20,
        compiler_params=pltpu.CompilerParams(vmem_limit_bytes=62 * 2**20),
    )(output, tg, loss, own, ibg, poolg, classg, wo, wi, wu, wq)
    return (*done, classes_t.T, class_b)


def normalize(value, gain, shift):
    mean = jnp.mean(value, axis=-1, keepdims=True)
    centred = value - mean
    inverse = lax.rsqrt(jnp.mean(centred * centred, axis=-1, keepdims=True) + EPS)
    unit = centred * inverse
    return (unit * gain + shift, unit, inverse)


def norm_back(grad, unit, inverse, gain):
    scaled = grad * gain
    inner = (
        scaled
        - jnp.mean(scaled, axis=-1, keepdims=True)
        - unit * jnp.mean(scaled * unit, axis=-1, keepdims=True)
    )
    return (inner * inverse, jnp.sum(grad * unit, axis=0), jnp.sum(grad, axis=0))


def matmul(left, right):
    return jnp.dot(left, right, preferred_element_type=jnp.float32)


def transposed_left(left, right):
    return lax.dot_general(
        left, right, (((0,), (0,)), ((), ())), preferred_element_type=jnp.float32
    )


def transposed_right(left, right):
    return lax.dot_general(
        left, right, (((1,), (1,)), ((), ())), preferred_element_type=jnp.float32
    )


def column_sum(values):
    return jnp.sum(values.astype(jnp.float32), axis=0)


def attend(block):
    query, key, value, keep = block
    scale = query.shape[-1] ** (-0.5)
    scores = jnp.einsum("qhd,khd->hqk", query, key, preferred_element_type=jnp.float32) * scale
    scores = jnp.where(keep[None, None, :], scores, NEG)
    top = jnp.max(scores, axis=-1, keepdims=True)
    total = jnp.sum(jnp.exp(scores - top), axis=-1, keepdims=True)
    logsum = top + jnp.log(total)
    probs = jnp.exp(scores - logsum).astype(jnp.bfloat16)
    context = jnp.einsum("hqk,khd->qhd", probs, value, preferred_element_type=jnp.float32)
    return (context.astype(jnp.bfloat16), logsum[:, :, 0])


def attend_back(block):
    query, key, value, keep, logsum, grad_context = block
    scale = query.shape[-1] ** (-0.5)
    scores = jnp.einsum("qhd,khd->hqk", query, key, preferred_element_type=jnp.float32) * scale
    scores = jnp.where(keep[None, None, :], scores, NEG)
    probs = jnp.exp(scores - logsum[:, :, None])
    grad_value = jnp.einsum(
        "hqk,qhd->khd", probs.astype(jnp.bfloat16), grad_context, preferred_element_type=jnp.float32
    )
    grad_probs = jnp.einsum("qhd,khd->hqk", grad_context, value, preferred_element_type=jnp.float32)
    delta = jnp.sum(grad_probs * probs, axis=-1, keepdims=True)
    grad_scores = (probs * (grad_probs - delta)).astype(jnp.bfloat16)
    grad_query = (
        jnp.einsum("hqk,khd->qhd", grad_scores, key, preferred_element_type=jnp.float32) * scale
    )
    grad_key = (
        jnp.einsum("hqk,qhd->khd", grad_scores, query, preferred_element_type=jnp.float32) * scale
    )
    return (
        grad_query.astype(jnp.bfloat16),
        grad_key.astype(jnp.bfloat16),
        grad_value.astype(jnp.bfloat16),
    )


def per_device_any(
    tokens,
    lengths,
    labels,
    cotangent,
    qkv_weight,
    query_bias,
    value_bias,
    out_weight,
    out_bias,
    first_gain,
    first_shift,
    inner_weight,
    inner_bias,
    outer_weight,
    outer_bias,
    second_gain,
    second_shift,
    pool_weight,
    pool_bias,
    class_weight,
    class_bias,
):
    full = (
        lax.all_gather(qkv_weight, FSDP, axis=0, tiled=True),
        lax.all_gather(query_bias, FSDP, axis=0, tiled=True),
        lax.all_gather(value_bias, FSDP, axis=0, tiled=True),
        lax.all_gather(out_weight, FSDP, axis=0, tiled=True),
        lax.all_gather(out_bias, FSDP, axis=0, tiled=True),
        lax.all_gather(first_gain, FSDP, axis=0, tiled=True),
        lax.all_gather(first_shift, FSDP, axis=0, tiled=True),
        lax.all_gather(inner_weight, FSDP, axis=0, tiled=True),
        lax.all_gather(inner_bias, FSDP, axis=0, tiled=True),
        lax.all_gather(outer_weight, FSDP, axis=0, tiled=True),
        lax.all_gather(outer_bias, FSDP, axis=0, tiled=True),
        lax.all_gather(second_gain, FSDP, axis=0, tiled=True),
        lax.all_gather(second_shift, FSDP, axis=0, tiled=True),
        lax.all_gather(pool_weight, FSDP, axis=0, tiled=True),
        lax.all_gather(pool_bias, FSDP, axis=0, tiled=True),
        lax.all_gather(class_weight, FSDP, axis=0, tiled=True),
    )
    (
        w_qkv,
        b_query,
        b_value,
        w_out,
        b_out,
        g_first,
        s_first,
        w_inner,
        b_inner,
        w_outer,
        b_outer,
        g_second,
        s_second,
        w_pool,
        b_pool,
        w_class,
    ) = full
    b_query = b_query.astype(jnp.float32)
    b_value = b_value.astype(jnp.float32)
    b_out = b_out.astype(jnp.float32)
    g_first = g_first.astype(jnp.float32)
    s_first = s_first.astype(jnp.float32)
    b_inner = b_inner.astype(jnp.float32)
    b_outer = b_outer.astype(jnp.float32)
    g_second = g_second.astype(jnp.float32)
    s_second = s_second.astype(jnp.float32)
    b_pool = b_pool.astype(jnp.float32)
    b_class = class_bias.astype(jnp.float32)
    seqs = lengths.shape[0]
    rows, width = tokens.shape
    span = rows // seqs
    size = width // HEADS
    classes = class_bias.shape[0]
    position = lax.broadcasted_iota(jnp.int32, (seqs, span), 1)
    keep = position < lengths[:, None]
    valid = keep.reshape(rows, 1).astype(jnp.float32)
    bias_all = jnp.concatenate([b_query, jnp.zeros_like(b_query), b_value])
    qkv = (matmul(tokens, w_qkv) + bias_all).astype(jnp.bfloat16)
    query = qkv[:, :width].reshape(seqs, span, HEADS, size)
    key = qkv[:, width : 2 * width].reshape(seqs, span, HEADS, size)
    value = qkv[:, 2 * width :].reshape(seqs, span, HEADS, size)
    context, logsum = lax.map(attend, (query, key, value, keep))
    context = context.reshape(rows, width)
    attended = matmul(context, w_out) + b_out
    hidden, unit_first, inverse_first = normalize(
        tokens.astype(jnp.float32) + attended, g_first, s_first
    )
    hidden_low = hidden.astype(jnp.bfloat16)
    inner = matmul(hidden_low, w_inner) + b_inner
    act = jax.nn.gelu(inner, approximate=False).astype(jnp.bfloat16)
    ffn = matmul(act, w_outer) + b_outer
    layer, unit_second, inverse_second = normalize(hidden + ffn, g_second, s_second)
    output = (layer * valid).astype(jnp.bfloat16)
    first = layer.reshape(seqs, span, width)[:, 0].astype(jnp.bfloat16)
    pooled = jnp.tanh(matmul(first, w_pool) + b_pool)
    pooled_low = pooled.astype(jnp.bfloat16)
    logits = matmul(pooled_low, w_class) + b_class
    peak = jnp.max(logits, axis=-1, keepdims=True)
    logsum_class = peak + jnp.log(jnp.sum(jnp.exp(logits - peak), axis=-1, keepdims=True))
    onehot = (labels[:, None] == lax.broadcasted_iota(jnp.int32, (seqs, classes), 1)).astype(
        jnp.float32
    )
    exit_loss = logsum_class[:, 0] - jnp.sum(onehot * logits, axis=-1)
    again = (
        lax.all_gather(qkv_weight, FSDP, axis=0, tiled=True),
        lax.all_gather(query_bias, FSDP, axis=0, tiled=True),
        lax.all_gather(value_bias, FSDP, axis=0, tiled=True),
        lax.all_gather(out_weight, FSDP, axis=0, tiled=True),
        lax.all_gather(out_bias, FSDP, axis=0, tiled=True),
        lax.all_gather(first_gain, FSDP, axis=0, tiled=True),
        lax.all_gather(first_shift, FSDP, axis=0, tiled=True),
        lax.all_gather(inner_weight, FSDP, axis=0, tiled=True),
        lax.all_gather(inner_bias, FSDP, axis=0, tiled=True),
        lax.all_gather(outer_weight, FSDP, axis=0, tiled=True),
        lax.all_gather(outer_bias, FSDP, axis=0, tiled=True),
        lax.all_gather(second_gain, FSDP, axis=0, tiled=True),
        lax.all_gather(second_shift, FSDP, axis=0, tiled=True),
        lax.all_gather(pool_weight, FSDP, axis=0, tiled=True),
        lax.all_gather(pool_bias, FSDP, axis=0, tiled=True),
        lax.all_gather(class_weight, FSDP, axis=0, tiled=True),
    )
    w_qkv = again[0]
    w_out = again[3]
    g_first = again[5].astype(jnp.float32)
    w_inner = again[7]
    w_outer = again[9]
    g_second = again[11].astype(jnp.float32)
    w_pool = again[13]
    w_class = again[15]
    grad_logits = (jnp.exp(logits - logsum_class) - onehot).astype(jnp.bfloat16)
    grad_class_weight = transposed_left(pooled_low, grad_logits)
    grad_class_local = column_sum(grad_logits)
    grad_pooled = transposed_right(grad_logits, w_class)
    grad_pre = (grad_pooled * (1.0 - pooled * pooled)).astype(jnp.bfloat16)
    grad_pool_weight = transposed_left(first, grad_pre)
    grad_pool_bias = column_sum(grad_pre)
    grad_first = transposed_right(grad_pre, w_pool)
    grad_layer = (cotangent.astype(jnp.float32) * valid).reshape(seqs, span, width)
    grad_layer = jnp.concatenate(
        [grad_layer[:, :1] + grad_first[:, None, :], grad_layer[:, 1:]], axis=1
    )
    grad_layer = grad_layer.reshape(rows, width)
    grad_resid_second, grad_second_gain, grad_second_shift = norm_back(
        grad_layer, unit_second, inverse_second, g_second
    )
    grad_ffn = grad_resid_second.astype(jnp.bfloat16)
    grad_outer_weight = transposed_left(act, grad_ffn)
    grad_outer_bias = column_sum(grad_ffn)
    grad_act = transposed_right(grad_ffn, w_outer)
    gelu_value, gelu_pull = jax.vjp(lambda v: jax.nn.gelu(v, approximate=False), inner)
    grad_inner = gelu_pull(grad_act)[0].astype(jnp.bfloat16)
    grad_inner_weight = transposed_left(hidden_low, grad_inner)
    grad_inner_bias = column_sum(grad_inner)
    grad_hidden = grad_resid_second + transposed_right(grad_inner, w_inner)
    grad_resid_first, grad_first_gain, grad_first_shift = norm_back(
        grad_hidden, unit_first, inverse_first, g_first
    )
    grad_attended = grad_resid_first.astype(jnp.bfloat16)
    grad_out_weight = transposed_left(context, grad_attended)
    grad_out_bias = column_sum(grad_attended)
    grad_context = (
        transposed_right(grad_attended, w_out).astype(jnp.bfloat16).reshape(seqs, span, HEADS, size)
    )
    grad_query, grad_key, grad_value = lax.map(
        attend_back, (query, key, value, keep, logsum, grad_context)
    )
    grad_query = grad_query.reshape(rows, width)
    grad_key = grad_key.reshape(rows, width)
    grad_value = grad_value.reshape(rows, width)
    grad_qkv = jnp.concatenate([grad_query, grad_key, grad_value], axis=1)
    grad_qkv_weight = transposed_left(tokens, grad_qkv)
    grad_query_bias = column_sum(grad_query)
    grad_value_bias = column_sum(grad_value)
    tokens_grad = (grad_resid_first + transposed_right(grad_qkv, w_qkv)).astype(jnp.bfloat16)
    owned = (
        lax.psum_scatter(grad_qkv_weight, FSDP, scatter_dimension=0, tiled=True),
        lax.psum_scatter(grad_query_bias, FSDP, scatter_dimension=0, tiled=True),
        lax.psum_scatter(grad_value_bias, FSDP, scatter_dimension=0, tiled=True),
        lax.psum_scatter(grad_out_weight, FSDP, scatter_dimension=0, tiled=True),
        lax.psum_scatter(grad_out_bias, FSDP, scatter_dimension=0, tiled=True),
        lax.psum_scatter(grad_first_gain, FSDP, scatter_dimension=0, tiled=True),
        lax.psum_scatter(grad_first_shift, FSDP, scatter_dimension=0, tiled=True),
        lax.psum_scatter(grad_inner_weight, FSDP, scatter_dimension=0, tiled=True),
        lax.psum_scatter(grad_inner_bias, FSDP, scatter_dimension=0, tiled=True),
        lax.psum_scatter(grad_outer_weight, FSDP, scatter_dimension=0, tiled=True),
        lax.psum_scatter(grad_outer_bias, FSDP, scatter_dimension=0, tiled=True),
        lax.psum_scatter(grad_second_gain, FSDP, scatter_dimension=0, tiled=True),
        lax.psum_scatter(grad_second_shift, FSDP, scatter_dimension=0, tiled=True),
        lax.psum_scatter(grad_pool_weight, FSDP, scatter_dimension=0, tiled=True),
        lax.psum_scatter(grad_pool_bias, FSDP, scatter_dimension=0, tiled=True),
        lax.psum_scatter(grad_class_weight, FSDP, scatter_dimension=0, tiled=True),
    )
    summed = lax.psum(
        (
            owned[0],
            owned[1],
            owned[2],
            owned[3],
            owned[4],
            owned[5],
            owned[6],
            owned[7],
            owned[8],
            owned[9],
            owned[10],
            owned[11],
            owned[12],
            owned[13],
            owned[14],
            owned[15],
        ),
        DP,
    )
    class_bias_grad = lax.psum(grad_class_local, (DP, FSDP))
    return (
        output,
        exit_loss,
        tokens_grad,
        summed[0],
        summed[1],
        summed[2],
        summed[3],
        summed[4],
        summed[5],
        summed[6],
        summed[7],
        summed[8],
        summed[9],
        summed[10],
        summed[11],
        summed[12],
        summed[13],
        summed[14],
        summed[15],
        class_bias_grad,
    )


def per_device(nz, tokens, lengths, labels, cotangent, qkv_weight, query_bias, value_bias, out_weight, out_bias,
    first_gain, first_shift, inner_weight, inner_bias, outer_weight, outer_bias, second_gain, second_shift,
    pool_weight, pool_bias, class_weight, class_bias):
    classes = class_bias.shape[0]
    small = [query_bias, value_bias, out_bias, first_gain, first_shift, outer_bias, second_gain, second_shift, pool_bias, class_weight.T, inner_bias, class_bias]
    (output, w1, w2, wu, wp, vec, ib, qkv, context, lse, hidden_low, unit_first, act, dgelu, unit_second, inv, firsts) = forward(
        FORWARD_PLAN, tokens, lengths, qkv_weight, out_weight, inner_weight, outer_weight, pool_weight, small, nz)
    (loss, own, ibg, poolg, classg, wo, wi, wug, wq, tokens_grad) = backward(
        BACKWARD_PLAN, lengths, labels, vec, lse, inv, firsts, cotangent, tokens, w1, w2, wu, wp, qkv, context, hidden_low, unit_first, act, dgelu, unit_second)
    return finish(output, tokens_grad, loss, own, ibg, poolg, classg, wo, wi, wug, wq, classes)


def solution(mesh):
    in_specs = (
        P((DP, FSDP), None),
        P((DP, FSDP)),
        P((DP, FSDP)),
        P((DP, FSDP), None),
        P(FSDP, None),
        P(FSDP),
        P(FSDP),
        P(FSDP, None),
        P(FSDP),
        P(FSDP),
        P(FSDP),
        P(FSDP, None),
        P(FSDP),
        P(FSDP, None),
        P(FSDP),
        P(FSDP),
        P(FSDP),
        P(FSDP, None),
        P(FSDP),
        P(FSDP, None),
        P(),
    )
    out_specs = (
        P((DP, FSDP), None),
        P((DP, FSDP)),
        P((DP, FSDP), None),
        P(FSDP, None),
        P(FSDP),
        P(FSDP),
        P(FSDP, None),
        P(FSDP),
        P(FSDP),
        P(FSDP),
        P(FSDP, None),
        P(FSDP),
        P(FSDP, None),
        P(FSDP),
        P(FSDP),
        P(FSDP),
        P(FSDP, None),
        P(FSDP),
        P(FSDP, None),
        P(),
    )
    sizes = dict(mesh.shape)
    fast = sizes[DP] == 4 and sizes[FSDP] == 8
    return jax.shard_map(
        functools.partial(per_device, sizes[FSDP] // 2) if fast else per_device_any, mesh=mesh, in_specs=in_specs, out_specs=out_specs, check_vma=False
    )
```

```python
import functools
import math

import jax
import jax.numpy as jnp
from jax import lax
from jax.experimental import pallas as pl
from jax.experimental.pallas import tpu as pltpu
from jax.sharding import PartitionSpec as P

HEADS = 12
DP, FSDP = "dp", "fsdp"
EPS = 1e-12
NEG = -1000000000.0
F32 = jnp.float32
BF16 = jnp.bfloat16
MESH = pl.DeviceIdType.MESH
LOG2E = math.log2(math.e)

START, NEED_QKV, PROJECT, ATTEND, NEED_OUT, NORM = 0, 10, 20, 30, 40, 41
NEED_INNER, EXPAND, NEED_OUTER, CONTRACT, NEED_POOL = 50, 60, 70, 80, 90
OUTER_GRAD, INNER_BACK, INNER_GRAD, FIRST_NORM, OUT_GRAD = 0, 1, 2, 4, 5
INPUT_GRAD, SMALL_SUMS, LAST, ATTEND_BACK, QKV_GRAD = 6, 7, 8, 10, 20

FINE = (0,)
ONE_WAY = (1, 2, 3)
SPLIT = (256, 256, 256, 256, 256, 256, 256, 256, 256, 256, 256, 256)

FORWARD_PLAN = {
    0: ((0, 0), (1, 0),),
    10: ((0, 1), (0, 2), (0, 3), (0, 4), (0, 5), (2, 0), (0, 6), (3, 0), (0, 7), (1, 1), (0, 8), (0, 9), (4, 0), (0, 10), (0, 11), (0, 12),),
    (20, 0): ((2, 1),),
    (20, 3): ((1, 2), (5, 0),),
    (30, 0): ((3, 1),),
    (30, 1): ((6, 0),),
    (30, 3): ((2, 2),),
    11: ((4, 1), (1, 3), (7, 0), (1, 4),),
    (21, 1): ((3, 2),),
    (21, 3): ((5, 1),),
    (31, 0): ((8, 0),),
    (31, 1): ((2, 3),),
    (31, 2): ((4, 2),),
    (31, 3): ((2, 4), (6, 1),),
    (22, 2): ((9, 0),),
    (22, 3): ((3, 3),),
    (32, 1): ((3, 4), (5, 2), (7, 1),),
    (32, 2): ((4, 3),),
    (32, 3): ((10, 0),),
    (41, 0): ((4, 4), (6, 2),),
    (41, 2): ((5, 3), (8, 1),),
    (60, 0): ((5, 4), (7, 2), (11, 0),),
    (60, 2): ((6, 3),),
    (61, 0): ((8, 2), (6, 4), (9, 1),),
    (61, 3): ((7, 3),),
    (62, 2): ((7, 4), (8, 3), (10, 1),),
    (63, 1): ((8, 4), (9, 2),),
    (63, 3): ((11, 1),),
    (80, 2): ((10, 2),),
    71: ((9, 3), (9, 4),),
    (81, 1): ((11, 2),),
    (81, 3): ((10, 3),),
    72: ((10, 4),),
    (82, 1): ((11, 3),),
    (82, 3): ((11, 4),),
}

BACKWARD_PLAN = {
    (0, 0): ((0, 0),),
    (0, 1): ((1, 0),),
    (0, 2): ((0, 1), (2, 0),),
    (0, 3): ((1, 1), (3, 0),),
    (1, 0): ((2, 1),),
    (1, 1): ((3, 1),),
    (1, 2): ((0, 2),),
    (2, 0): ((4, 0),),
    (2, 1): ((1, 2), (5, 0),),
    (2, 2): ((4, 1), (6, 0),),
    (2, 3): ((5, 1), (7, 0),),
    (4, 0): ((2, 2), (6, 1),),
    (4, 1): ((7, 1),),
    (4, 2): ((3, 2),),
    (4, 3): ((0, 3), (1, 3),),
    5: ((8, 0), (12, 0),),
    (10, 0): ((4, 2), (8, 1),),
    (10, 2): ((2, 3), (5, 2), (12, 1),),
    20: ((9, 0),),
    (11, 0): ((6, 2),),
    (11, 1): ((9, 1),),
    (11, 2): ((3, 3), (14, 4), (7, 2), (4, 3), (4, 4),),
    (11, 3): ((14, 5),),
    21: ((10, 0),),
    (12, 0): ((5, 3), (5, 4), (8, 2), (10, 1),),
    (12, 1): ((14, 6), (6, 3), (6, 4), (4, 5), (12, 2),),
    (12, 2): ((14, 7), (5, 5),),
    (12, 3): ((4, 6), (9, 2), (7, 3), (7, 4),),
    22: ((4, 7), (6, 5), (8, 3), (8, 4), (11, 0), (13, 0),),
    (6, 0): ((5, 6), (12, 3),),
    (6, 1): ((6, 6), (5, 7), (10, 2), (11, 1),),
    (6, 2): ((6, 7), (12, 4), (9, 3), (9, 4),),
    (6, 3): ((7, 5),),
    7: ((8, 5), (10, 3), (13, 1), (7, 6), (8, 6), (7, 7), (8, 7), (11, 2), (10, 4), (13, 2), (9, 5), (10, 5), (11, 3), (13, 3), (9, 6), (10, 6), (13, 4),),
    8: ((9, 7), (10, 7), (11, 4), (11, 5), (11, 6), (11, 7),),
}


def nn(left, right):
    return jnp.dot(left, right, preferred_element_type=F32)


def nt(left, right):
    return lax.dot_general(left, right, (((1,), (1,)), ((), ())), preferred_element_type=F32)


def tn(left, right):
    return lax.dot_general(left, right, (((0,), (0,)), ((), ())), preferred_element_type=F32)


def rowmean(value):
    return jnp.sum(value, axis=-1, keepdims=True) * (1.0 / value.shape[-1])


def here():
    d, f = lax.axis_index(DP), lax.axis_index(FSDP)
    return d // 2, d % 2, f // 2, f % 2


def at(x, c, z, y):
    return (x * 2 + c, z * 2 + y)


def attend_forward(qkv, ctx, lse, lengths, i, span, width, size):
    pairs = width // (2 * size)
    wide = 2 * size
    s, hp = i // pairs, i % pairs
    rows = pl.ds(pl.multiple_of(s * span, span), span)

    def part(p):
        return qkv[rows, pl.ds(pl.multiple_of(p * width + hp * wide, wide), wide)]

    q, k, v = part(0), part(1), part(2)
    lane = lax.broadcasted_iota(jnp.int32, (span, wide), 1)
    slot = lax.broadcasted_iota(jnp.int32, (span, wide), 0)
    fill = jnp.where(slot < lengths[s], 0.0, NEG).astype(BF16)
    vt = v.T
    vrow = lax.broadcasted_iota(jnp.int32, (wide, span), 0)
    factor = size ** (-0.5) * LOG2E
    halves, sums = [], []
    for h in range(2):
        mine = lane < size if h == 0 else lane >= size
        other = (1 - h) * size
        qh = jnp.where(mine, q, jnp.where(lane == other, 1.0, 0.0).astype(BF16))
        kh = jnp.where(mine, k, fill)
        scores = nt(kh, qh)
        top = jnp.max(scores, axis=0, keepdims=True)
        e = jnp.exp2((scores - top) * factor).astype(BF16)
        vmine = vrow < size if h == 0 else vrow >= size
        vh = jnp.where(vmine, vt, jnp.ones_like(vt))
        o = nn(vh, e)
        total = o[other : other + 1, :]
        halves.append(o[h * size : (h + 1) * size, :] / total)
        sums.append(top * factor + jnp.log2(total))
    ct = jnp.concatenate(halves, axis=0)
    ctx[rows, pl.ds(pl.multiple_of(hp * wide, wide), wide)] = ct.T.astype(BF16)
    lse[i] = jnp.concatenate(sums + [jnp.zeros((6, span), F32)], axis=0)


class Gather:
    def __init__(self, buf, send, recv, first, fine, one_way):
        self.buf, self.send, self.recv, self.base, self.fine, self.one_way = buf, send, recv, first, fine, one_way
        self.nz, _, self.r, self.cols = buf.shape
        self.me = here()
        half = self.cols // 2
        x, c, z, y = self.me
        c0 = pl.multiple_of(c * half, 128)
        third = 0 if one_way else half // 3
        self.both = pl.ds(c0, half)
        self.first = pl.ds(c0, third)
        self.second = pl.ds(pl.multiple_of(c0 + third, 128), half - third)
        self.theirs = pl.ds(pl.multiple_of((1 - c) * half, 128), half)
        r2 = self.r // 2
        self.row = pl.ds(pl.multiple_of(x * r2, 16), r2)
        self.row_o = pl.ds(pl.multiple_of((1 - x) * r2, 16), r2)
        self.every = pl.ds(0, self.r)

    def copy(self, kind, k=None, incoming=False):
        x, c, z, y = self.me
        nz, buf = self.nz, self.buf
        if k is None:
            zk = pl.ds(0, nz if kind in ("ya", "yb", "xa", "cx") else nz - 1)
        else:
            zk = lax.rem(z + nz - k, nz)
        row = self.row_o if incoming else self.row
        both = self.theirs if incoming else self.both
        yo = 1 - y if incoming else y
        if kind in ("za", "zb"):
            slot = zk if incoming or k is None else z
            ref = buf.at[slot, y, self.every, self.first] if kind == "za" else buf.at[slot, y, self.row, self.second]
            peer = (x, c, lax.rem(z + (k or 1), nz), y)
        elif kind == "xo":
            ref, peer = buf.at[zk, y, row, self.second], (1 - x, c, z, y)
        elif kind == "co":
            ref, peer = buf.at[zk, y, self.every, both], (x, 1 - c, z, y)
        elif kind == "ya":
            ref, peer = buf.at[zk, yo, self.every, self.first], (x, c, z, 1 - y)
        elif kind == "yb":
            ref, peer = buf.at[zk, yo, self.row, self.second], (x, c, z, 1 - y)
        elif kind == "xa":
            ref, peer = buf.at[zk, 1 - y, row, self.second], (1 - x, c, z, y)
        else:
            ref, peer = buf.at[zk, 1 - y, self.every, both], (x, 1 - c, z, y)
        n = ("za", "zb", "xo", "co", "ya", "yb", "xa", "cx").index(kind)
        n = self.base + (n * nz + k if self.fine else n)
        return pltpu.make_async_remote_copy(
            src_ref=ref, dst_ref=ref, send_sem=self.send.at[n], recv_sem=self.recv.at[n], device_id=at(*peer), device_id_type=MESH
        )

    def go(self, *kind):
        self.copy(*kind).start()

    def got(self, kind, k=None):
        self.copy(kind, k, True).wait_recv()

    def step(self, j):
        nz = self.nz
        ks = range(1, nz)
        if j == 0:
            for k in ks:
                self.go("zb", k)
                if not self.one_way:
                    self.go("za", k)
            if self.fine:
                self.go("yb", 0)
                self.go("ya", 0)
        elif self.fine:
            if j < nz:
                self.got("zb", j)
                self.go("xo", j)
                self.go("yb", j)
                self.got("za", j)
                self.go("ya", j)
            elif j < 2 * nz:
                k = j - nz
                self.got("yb", k)
                self.go("xa", k)
                if k:
                    self.got("xo", k)
                    self.go("co", k)
            elif j < 3 * nz:
                k = j - 2 * nz
                self.got("ya", k)
                self.got("xa", k)
                self.go("cx", k)
            else:
                for k in range(nz):
                    if k:
                        self.got("co", k)
                    self.got("cx", k)
        elif j == 1:
            self.got("zb")
            for k in ks:
                self.go("xo", k)
            self.go("yb")
            if not self.one_way:
                self.got("za")
                self.go("ya")
        elif j == 2:
            self.got("yb")
            self.go("xa")
            self.got("xo")
            for k in ks:
                self.go("co", k)
        elif j == 3:
            if not self.one_way:
                self.got("ya")
            self.got("xa")
            self.go("cx")
        else:
            self.got("co")
            self.got("cx")

    def drain(self):
        for kind in ("za", "zb", "xo", "co", "ya", "yb", "xa", "cx"):
            if self.one_way and kind in ("za", "ya"):
                continue
            for k in range(self.nz) if self.fine else (None,):
                if k != 0 or kind in ("ya", "yb", "xa", "cx"):
                    self.copy(kind, k).wait_send()


def gelu_both(value):
    cdf = 0.5 + 0.5 * lax.erf(value * (0.5**0.5))
    bell = jnp.exp2(value * value * (-0.5 * LOG2E)) * (1.0 / math.sqrt(2.0 * math.pi))
    return value * cdf, cdf + value * bell


def place(sm, f, part, width):
    row = lax.broadcasted_iota(jnp.int32, (128, width), 0)
    col = lax.broadcasted_iota(jnp.int32, (128, width), 1)
    return jnp.where((col == row + f * part) & (row < part), 1.0, 0.0).astype(BF16)


def forward_kernel(plan, tokens_h, lengths, wqkv_h, wout_h, winner_h, wouter_h, wpool_h, small_h,
                   out_h, w1_h, w2_h, wu_h, wp_h, vec_o, ib_o, qkv_h, ctx_h, lse_o, hid_h, u1_h, act_h, dg_h, u2_h, inv_o, first_o,
                   tokens, w1, w2, wu, wp, sm, qkv, ctx, hid, hidlow, u1, act, dg, u2, outv,
                   loc, s_sm, r_sm, s_g, r_g, *raw):
    comm = plan is not None
    x, c, z, y = here() if comm else (0, 0, 0, 0)
    groups, nz = w1.shape[:2]
    rows, width = tokens.shape
    seqs = lengths.shape[0]
    span = rows // seqs
    ff = act.shape[1]
    nb = ff // width
    size = width // HEADS
    pairs = HEADS // 2
    gp = pairs // groups
    wide = gp * 2 * size
    nf = nz * 2
    part = width // nf
    fr = ff // nf
    ur = wu.shape[3]
    nu = wu.shape[0]
    units = [(w1, g) for g in range(groups)] + [(w2, b) for b in range(1 + nb)] + [(wu, j) for j in range(nu)] + [(wp, 0)]

    def small_parameters():
        vec = jnp.zeros((sm.shape[1], width), F32)
        for f in range(nf):
            vec += nn(sm[f], place(None, f, part, width))
        vec_o[...] = vec
        ibs = []
        for f in range(nf):
            piece = sm[f].astype(F32)
            for j in range(fr // 128):
                ibs.append(piece[12 + j : 13 + j, :])
        ib_o[...] = jnp.broadcast_to(jnp.concatenate(ibs, axis=1), ib_o.shape)

    f_me = z * 2 + y
    started = []

    def bring(src, dst):
        copy = pltpu.make_async_copy(src, dst, loc.at[len(started)])
        copy.start()
        started.append(copy)
        return copy

    if comm:
        barrier = pltpu.get_barrier_semaphore()
        peers = [(x, c, lax.rem(z + k, nz), yy) for k in range(1, nz) for yy in (y, 1 - y)]
        peers += [(x, c, z, 1 - y), (1 - x, c, z, y), (x, 1 - c, z, y)]
        for p in peers:
            pl.semaphore_signal(barrier, inc=1, device_id=at(*p), device_id_type=MESH)
        own = []
        for g in range(groups):
            own.append([bring(wqkv_h.at[:, pl.ds(p * width + g * wide, wide)], w1.at[g, z, y, :, pl.ds(p * wide, wide)]) for p in range(3)])
        parts = [bring(src, dst) for src, dst in zip(small_h, raw)]
        own.append([bring(wout_h, w2.at[0, z, y])])
        for b in range(nb):
            own.append([bring(winner_h.at[:, pl.ds(b * width, width)], w2.at[b + 1, z, y])])
        tok = bring(tokens_h, tokens)
        for j in range(fr // ur):
            own.append([bring(wouter_h.at[pl.ds(j * ur, ur)], wu.at[j, z, y])])
        own.append([bring(wpool_h, wp.at[0, z, y])])

        def unit(m):
            buf, n = units[m]
            ahead = sum(e < m for e in FINE)
            return Gather(buf.at[n], s_g, r_g, 8 * (m + ahead * (nz - 1)), m in FINE, m in ONE_WAY)

        def small(n, slot):
            return pltpu.make_async_remote_copy(
                src_ref=sm.at[slot], dst_ref=sm.at[slot], send_sem=s_sm.at[n], recv_sem=r_sm.at[n], device_id=at(*peers[n]), device_id_type=MESH
            )

        others = len(peers) - 2

        def smalls_sent():
            for cp in parts:
                cp.wait()

            def lanes(v, before=0):
                v = v.astype(F32)
                v = v.reshape(1, -1) if v.ndim == 1 else v
                ends = [jnp.zeros((v.shape[0], n), F32) for n in (before, 128 - before - v.shape[1])]
                return jnp.concatenate(([ends[0]] if before else []) + [v, ends[1]], axis=1)

            *vectors, classes, wide_bias, class_bias = (r[...] for r in raw)
            wide_bias = wide_bias.astype(F32).reshape(1, fr)
            lines = [lanes(v) for v in vectors] + [lanes(classes)]
            lines += [wide_bias[:, j * 128 : (j + 1) * 128] for j in range(fr // 128)] + [lanes(class_bias, 1)]
            sm[f_me] = jnp.concatenate(lines, axis=0).astype(BF16)
            for n in range(others):
                small(n, f_me).start()

        def smalls_here():
            for n in range(others):
                if n < 2 * (nz - 1):
                    slot = lax.rem(z + nz - n // 2 - 1, nz) * 2 + (y if n % 2 == 0 else 1 - y)
                else:
                    slot = z * 2 + 1 - y
                small(n, slot).wait_recv()

        pl.semaphore_wait(barrier, len(peers))

        def hook(name, i=None):
            if i is None:
                for n, j in plan.get(name, ()):
                    if j == 0:
                        for cp in own[n]:
                            cp.wait()
                    unit(n).step(j)
                    if (n, j) == (0, 0):
                        smalls_sent()
                    if (n, j) == (0, nz):
                        smalls_here()
                        small_parameters()
                        tok.wait()
                return
            for k in range(8):
                if (name, k) in plan:
                    pl.when(i == k)(functools.partial(hook, (name, k)))
    else:
        def hook(name, i=None):
            pass

        for a, b in ((tokens_h, tokens), (w1_h, w1), (w2_h, w2), (wu_h, wu), (wp_h, wp), (small_h, sm)):
            bring(a, b).wait()
        small_parameters()

    hook(START)
    tile = rows // nz
    steps = rows // tile

    def tiles(i):
        return pl.ds(pl.multiple_of(i * tile, tile), tile)

    def loop(count, body):
        def step(i, _):
            body(i)
            return 0

        lax.fori_loop(0, count, step, 0)

    saved = []

    def save(src, dst):
        saved.append(bring(src, dst))

    for g in range(groups):
        hook(NEED_QKV + g)
        lo = g * wide
        bias = (vec_o[0:1, lo : lo + wide], None, vec_o[1:2, lo : lo + wide])

        def project(i):
            r = tiles(i)
            got = nn(tokens[r, :], w1[g].reshape(width, 3 * wide))
            for p in range(3):
                mine = got[:, p * wide : (p + 1) * wide]
                qkv[r, p * width + lo : p * width + lo + wide] = (mine if bias[p] is None else mine + bias[p]).astype(BF16)
            hook(PROJECT + g, i)

        loop(steps, project)

        def attention(i):
            s, hp = i // gp, g * gp + i % gp
            attend_forward(qkv, ctx, lse_o, lengths, s * pairs + hp, span, width, size)
            hook(ATTEND + g, i)

        loop(seqs * gp, attention)
    if comm:
        save(w1, w1_h)
    save(qkv, qkv_h)
    save(ctx, ctx_h)

    hook(NEED_OUT)
    b_out, g_first, s_first, b_outer, g_second, s_second = (vec_o[n : n + 1, :] for n in range(2, 8))

    def norm_one(i):
        r = tiles(i)
        resid = tokens[r, :].astype(F32) + (nn(ctx[r, :], w2[0].reshape(width, width)) + b_out)
        centred = resid - rowmean(resid)
        inv = lax.rsqrt(rowmean(centred * centred) + EPS)
        unit_ = centred * inv
        u1[r, :] = unit_.astype(BF16)
        inv_o[0, r, :] = jnp.broadcast_to(inv, (tile, 128))
        h = unit_ * g_first + s_first
        hid[r, :] = h + b_outer
        hidlow[r, :] = h.astype(BF16)
        hook(NORM, i)

    loop(steps, norm_one)
    save(u1, u1_h)
    save(hidlow, hid_h)
    for b in range(nb):
        hook(NEED_INNER + b)
        cols = slice(b * width, (b + 1) * width)

        def expand(i):
            r = tiles(i)
            a, g = gelu_both(nn(hidlow[r, :], w2[b + 1].reshape(width, width)) + ib_o[0:1, cols])
            act[r, cols] = a.astype(BF16)
            dg[i, :, :, cols] = g.astype(BF16).reshape(2, tile // 2, width)
            hook(EXPAND + b, i)

        loop(steps, expand)
    if comm:
        save(w2, w2_h)
    save(act, act_h)
    save(dg, dg_h)

    for j in range(nu):
        hook(NEED_OUTER + j)
        if comm:
            save(wu.at[j], wu_h.at[j])

        def contract(i):
            r = tiles(i)
            a = jnp.concatenate([act[r, f * fr + j * ur : f * fr + (j + 1) * ur] for f in range(nf)], axis=1)
            resid = hid[r, :] + nn(a, wu[j].reshape(nf * ur, width))
            if j < nu - 1:
                hid[r, :] = resid
            else:
                centred = resid - rowmean(resid)
                inv = lax.rsqrt(rowmean(centred * centred) + EPS)
                unit_ = centred * inv
                u2[r, :] = unit_.astype(BF16)
                inv_o[1, r, :] = jnp.broadcast_to(inv, (tile, 128))
                layer = unit_ * g_second + s_second
                each = span // tile
                s, t = i // each, i % each

                @pl.when(t == 0)
                def _():
                    first_o[pl.ds(pl.multiple_of(s * 8, 8), 8), :] = layer[0:8, :]

                slot = lax.broadcasted_iota(jnp.int32, (tile, width), 0) + t * tile
                outv[r, :] = jnp.where(slot < lengths[s], layer, 0.0).astype(BF16)
            hook(CONTRACT + j, i)

        loop(steps, contract)
    save(u2, u2_h)
    save(outv, out_h)
    hook(NEED_POOL)
    if comm:
        save(wp, wp_h)
    for cp in saved:
        cp.wait()
    if comm:
        for n in range(others):
            small(n, f_me).wait_send()

        for n in range(len(units)):
            unit(n).drain()


def forward(plan, tokens, lengths, wqkv, wout, winner, wouter, wpool, small, nz):
    rows, width = tokens.shape
    seqs = lengths.shape[0]
    span = rows // seqs
    nf = nz * 2
    ff = winner.shape[1]
    part = width // nf
    ur = ff // nf // 3
    any_, vm, smem = (pl.BlockSpec(memory_space=m) for m in (pl.ANY, pltpu.VMEM, pltpu.SMEM))
    S = jax.ShapeDtypeStruct
    pairs = HEADS // 2
    weights = [(3, nz, 2, part, width), (1 + ff // width, nz, 2, part, width), (3, nz, 2, ur, width), (1, nz, 2, part, width)]
    outs = [
        (S((rows, width), BF16), any_),
        *[(S(w, BF16), any_) for w in weights],
        (S((16, width), F32), vm),
        (S((8, ff), F32), vm),
        (S((rows, 3 * width), BF16), any_),
        (S((rows, width), BF16), any_),
        (S((seqs * pairs, 8, span), F32), vm),
        (S((rows, width), BF16), any_),
        (S((rows, width), BF16), any_),
        (S((rows, ff), BF16), any_),
        (S((nz, 2, rows // (2 * nz), ff), BF16), any_),
        (S((rows, width), BF16), any_),
        (S((2, rows, 128), F32), vm),
        (S((8 * seqs, width), F32), vm),
    ]
    V = pltpu.VMEM
    D = pltpu.SemaphoreType.DMA
    units = sum(w[0] for w in weights)
    sems = 8 * (units + len(FINE) * (nz - 1))
    scratch = [
        V((rows, width), BF16),
        *[V(w, BF16) for w in weights],
        V((nf, 16, 128), BF16),
        V((rows, 3 * width), BF16),
        V((rows, width), BF16),
        V((rows, width), F32),
        V((rows, width), BF16),
        V((rows, width), BF16),
        V((rows, ff), BF16),
        V((nz, 2, rows // (2 * nz), ff), BF16),
        V((rows, width), BF16),
        V((rows, width), BF16),
        D((64,)), D((nf,)), D((nf,)),
        D((sems,)), D((sems,)),
        *[V(v.shape, BF16) for v in small],
    ]
    params = pltpu.CompilerParams(vmem_limit_bytes=60 * 2**20, has_side_effects=True, collective_id=0)
    cost = pl.CostEstimate(flops=2 * rows * width * (4 * width + 2 * ff), bytes_accessed=10**7, transcendentals=0)

    def kernel(*refs):
        n = 7 + len(small)
        forward_kernel(plan, *refs[:7], refs[7:n], *refs[n:])

    return pl.pallas_call(
        kernel, out_shape=[o[0] for o in outs], out_specs=[o[1] for o in outs], in_specs=[any_, smem] + [any_] * (5 + len(small)),
        scratch_shapes=scratch, compiler_params=params, cost_estimate=cost,
    )(tokens, lengths, wqkv, wout, winner, wouter, wpool, *small)


def attend_backward(kv, gctx, lse, lengths, s, hp, span, width, size):
    wide = 2 * size
    pairs = width // wide
    rows = pl.ds(pl.multiple_of(s * span, span), span)

    def cols(p):
        return pl.ds(pl.multiple_of(p * width + hp * wide, wide), wide)

    q, k, v = (kv[rows, cols(p)] for p in range(3))
    g = gctx[rows, cols(0)]
    logs = lse[s * pairs + hp]
    lane = lax.broadcasted_iota(jnp.int32, (span, wide), 1)
    slot = lax.broadcasted_iota(jnp.int32, (span, wide), 0)
    fill = jnp.where(slot < lengths[s], 0.0, NEG).astype(BF16)
    scale = size ** (-0.5)
    factor = scale * LOG2E
    kt = k.T
    gqs, gks, gvs = [], [], []
    for h in range(2):
        mine = lane < size if h == 0 else lane >= size
        other = (1 - h) * size
        qh = jnp.where(mine, q, jnp.where(lane == other, 1.0, 0.0).astype(BF16))
        kh = jnp.where(mine, k, fill)
        vh = jnp.where(mine, v, jnp.zeros_like(v))
        p = jnp.exp2(nt(kh, qh) * factor - logs[h : h + 1, :])
        gvs.append(nn(p.astype(BF16), g))
        gp = nt(vh, g)
        delta = jnp.sum(gp * p, axis=0, keepdims=True)
        gs = (p * (gp - delta)).astype(BF16)
        gks.append(nn(gs, q))
        gqs.append(nn(kt, gs)[h * size : (h + 1) * size, :])
    kv[rows, cols(0)] = (jnp.concatenate(gqs, axis=0).T * scale).astype(BF16)
    kv[rows, cols(1)] = (jnp.where(lane < size, gks[0], gks[1]) * scale).astype(BF16)
    kv[rows, cols(2)] = jnp.where(lane < size, gvs[0], gvs[1]).astype(BF16)


class Spread:
    def __init__(self, buf, send, recv):
        self.buf, self.send, self.recv = buf, send, recv
        self.nz = buf.shape[3]
        self.me = here()

    def copy(self, n, incoming):
        x, c, z, y = self.me
        nz = self.nz
        if n < nz - 1:
            k = n + 1
            peer = (x, c, lax.rem(z + k, nz), y)
            ref = self.buf.at[x, c, y, lax.rem(z + nz - k, nz) if incoming else z]
        elif n == nz - 1:
            peer = (x, c, z, 1 - y)
            ref = self.buf.at[x, c, 1 - y if incoming else y]
        elif n == nz:
            peer = (1 - x, c, z, y)
            ref = self.buf.at[1 - x if incoming else x, c]
        else:
            peer = (x, 1 - c, z, y)
            ref = self.buf.at[:, 1 - c if incoming else c]
        return pltpu.make_async_remote_copy(
            src_ref=ref, dst_ref=ref, send_sem=self.send.at[n], recv_sem=self.recv.at[n], device_id=at(*peer), device_id_type=MESH
        )

    def step(self, j):
        nz = self.nz
        if j == 0:
            for n in range(nz - 1):
                self.copy(n, False).start()
            return
        if j == 1:
            for n in range(nz - 1):
                self.copy(n, True).wait_recv()
        else:
            self.copy(nz + j - 3, True).wait_recv()
        if j < 4:
            self.copy(nz + j - 2, False).start()

    def drain(self):
        for n in range(self.nz + 2):
            self.copy(n, False).wait_send()


class Scatter:
    def __init__(self, g, r, split, out, sems, n, ahead=None, boxes=None):
        self.g, self.split, self.out, self.n, self.ahead = g, split, out, n, ahead
        self.send, self.recv = (e.at[n] for e in sems)
        self.lead, _, rows, cols = g.shape
        self.me = x, c, z, y = here()
        h, r2 = cols // 2, rows // 2
        t, e = pl.ds(h, split), pl.ds(h + split, h - split)
        top, low = pl.ds(0, r2), pl.ds(r2, r2)
        self.r1, self.ry1, self.rx2 = r.at[:, :, :, pl.ds(0, h)], r.at[:, 0, :, t], r.at[:, :, top, e]
        self.ry2 = r.at[:, 0, low, e]
        nz = self.lead
        if ahead is None:
            self.za, self.zb = [[r.at[k, 1, q, w] for k in range(nz - 1)] for q, w in ((pl.ds(0, rows), t), (low, e))]
            self.all_za, self.all_zb = (r.at[pl.ds(0, nz - 1), 1, q, w] for q, w in ((pl.ds(0, rows), t), (low, e)))
            self.xe = r.at[nz - 1, 1, :, t]
        else:
            self.za, self.zb = [[b.at[:, 1, q, w] for b in boxes[: nz - 1]] for q, w in ((pl.ds(0, rows), t), (low, e))]
            self.xe = boxes[nz - 1].at[:, 1, :, t]
        self.all_sems = sems
        self.rows = pl.ds(pl.multiple_of(x * r2, 16), r2)
        self.rows_o = pl.ds(pl.multiple_of((1 - x) * r2, 16), r2)
        self.mine = pl.ds(pl.multiple_of(c * h, 128), h)
        self.theirs = pl.ds(pl.multiple_of((1 - c) * h, 128), h)
        self.a1 = pl.ds(pl.multiple_of(c * h, 128), split)
        self.a2 = pl.ds(pl.multiple_of(c * h + split, 128), h - split)

    def region(self, rows, cols):
        return self.out.at[rows, cols] if self.ahead is None else self.out.at[:, rows, cols]

    def remote(self, src, dst, n, peer, unit=None):
        send, recv = (self.send, self.recv) if unit is None else (e.at[unit] for e in self.all_sems)
        return pltpu.make_async_remote_copy(
            src_ref=src, dst_ref=dst, send_sem=send.at[n], recv_sem=recv.at[n], device_id=at(*peer), device_id_type=MESH
        )

    def copy(self, n):
        x, c, z, y = self.me
        g, nz = self.g, self.lead
        every = slice(None)
        core, xn, yn = (x, 1 - c, z, y), (1 - x, c, z, y), (x, c, z, 1 - y)
        if n == 0:
            return self.remote(g.at[:, :, :, self.theirs], self.r1, n, core)
        if n == 1:
            return self.remote(g.at[:, 1 - y, :, self.a1], self.ry1, n, yn)
        if n == 2:
            return self.remote(g.at[:, :, self.rows_o, self.a2], self.rx2, n, xn)
        if n == 3:
            return self.remote(g.at[:, 1 - y, self.rows, self.a2], self.ry2, n, yn)
        if n < 2 * nz + 2:
            k = (n - 4) % (nz - 1) + 1
            zk = lax.rem(z + k, nz)
            lead = zk if self.ahead is None else every
            rows, cols, to = (every, self.a1, self.za) if n < nz + 3 else (self.rows, self.a2, self.zb)
            return self.remote(g.at[lead, y, rows, cols], to[k - 1], 4 if n < nz + 3 else 5, (x, c, zk, y))
        if n == 2 * nz + 2:
            return self.remote(self.region(every, self.a1), self.xe, 6, xn)
        if n == 2 * nz + 3:
            ref = self.region(self.rows, self.a2)
            return self.remote(ref, ref, 7, xn)
        ref = self.region(every, self.mine)
        return self.remote(ref, ref, 8, core)

    def got(self, n):
        x, c, z, y = self.me
        nz = self.lead
        if 3 < n < 2 * nz + 2 and self.ahead is not None:
            k = (n - 4) % (nz - 1) + 1
            ref = (self.za if n < nz + 3 else self.zb)[k - 1]
            self.remote(ref, ref, 4 if n < nz + 3 else 5, (x, c, lax.rem(z + nz - k, nz), y), k - 1).wait_recv()
        elif n == 2 * nz + 3:
            ref = self.region(self.rows_o, self.a2)
            self.remote(ref, ref, 7, (1 - x, c, z, y)).wait_recv()
        elif n == 2 * nz + 4:
            ref = self.region(slice(None), self.theirs)
            self.remote(ref, ref, 8, (x, 1 - c, z, y)).wait_recv()
        else:
            self.copy(n).wait_recv()

    def all_along(self, first):
        x, c, z, y = self.me
        ref = self.all_za if first == 4 else self.all_zb
        return self.remote(ref, ref, 4 if first == 4 else 5, (x, c, lax.rem(z + 1, self.lead), y))

    def along_z(self, first):
        if self.ahead is None:
            for k in range(1, self.lead):
                self.copy(first + k - 1).start()
        elif self.ahead:
            self.copy(first + self.ahead - 1).start()

    def over_z(self, first, boxes, rows, cols):
        y, z = self.me[3], self.me[2]
        total = (self.g[z, y, rows, cols] if self.ahead is None else self.g[:, y, rows, cols]).astype(F32)
        if self.ahead is None:
            self.all_along(first).wait_recv()
        for k in range(1, self.lead):
            if self.ahead is not None:
                self.got(first + k - 1)
            total += boxes[k - 1][...].astype(F32)
        self.region(rows, cols)[...] = total.astype(BF16)

    def step(self, j):
        g, y, nz = self.g, self.me[3], self.lead
        last = 2 * nz + 2

        def adds(body):
            def step(i, _):
                body(i)
                return 0

            lax.fori_loop(0, nz, step, 0)

        if j == 0:
            self.copy(0).start()
        elif j == 1:
            self.got(0)

            def add(i):
                for yy in range(2):
                    g[i, yy, :, self.mine] = g[i, yy, :, self.mine] + self.r1[i, yy]

            adds(add)
            self.copy(1).start()
            self.copy(2).start()
        elif j == 2:
            self.got(2)

            def add(i):
                for yy in range(2):
                    g[i, yy, self.rows, self.a2] = g[i, yy, self.rows, self.a2] + self.rx2[i, yy]

            adds(add)
            self.copy(3).start()
            self.got(1)

            def add(i):
                g[i, y, :, self.a1] = g[i, y, :, self.a1] + self.ry1[i]

            adds(add)
            self.along_z(4)
        elif j == 3:
            self.got(3)

            def add(i):
                g[i, y, self.rows, self.a2] = g[i, y, self.rows, self.a2] + self.ry2[i]

            adds(add)
            self.along_z(nz + 3)
        elif j == 4:
            self.over_z(4, self.za, slice(None), self.a1)
            self.copy(last).start()
        elif j == 5:
            self.over_z(nz + 3, self.zb, self.rows, self.a2)
            self.copy(last + 1).start()
        elif j == 6:
            self.copy(last).wait_send()
            self.got(last)
            ref = self.region(slice(None), self.a1)
            ref[...] = ref[...] + self.xe[...]
            self.got(last + 1)
            self.copy(last + 2).start()
        else:
            self.got(last + 2)

    def drain(self):
        nz = self.lead
        for n in range(4):
            self.copy(n).wait_send()
        if self.ahead is None:
            self.all_along(4).wait_send()
            self.all_along(nz + 3).wait_send()
        elif self.ahead:
            self.copy(3 + self.ahead).wait_send()
            self.copy(nz + 2 + self.ahead).wait_send()
        if not self.ahead:
            self.copy(2 * nz + 3).wait_send()
            self.copy(2 * nz + 4).wait_send()


def backward_kernel(plan, lengths, labels, vec, lse, first, inv_h, cot_h, tok_h, w1_h, w2_h, wu_h, wp_h, qkv_h, ctx_h, hid_h, u1_h, act_h, dg_h, u2_h,
                    loss_o, own_o, ib_o, pool_o, class_o, wo_o, wi_o, wu_o, wq_o, tg_h,
                    A, D, w2, w3, cot, u2, u1, hid, gffn, gr, inv, acc, gfirst,
                    G, R, early, late, loc, free, s_rs, r_rs, s_sp, r_sp):
    comm = plan is not None
    x, c, z, y = here() if comm else (0, 0, 0, 0)
    rows, width = cot.shape
    seqs = lengths.shape[0]
    span = rows // seqs
    ff = A.shape[1]
    size = width // HEADS
    nz = D.shape[0]
    tile = rows // nz
    nb = ff // width
    part = width // (2 * nz)
    fr = ff // (2 * nz)
    ur = wu_h.shape[3]
    groups = w1_h.shape[0]
    loads = {}

    def load(name, src, dst):
        cp = pltpu.make_async_copy(src, dst, loc.at[len(loads)])
        cp.start()
        loads[name] = cp

    load("wp", wp_h.at[0], w3.at[:, :, pl.ds(fr, part), :])
    load("cot", cot_h, cot)
    load("u2", u2_h, u2)
    load("inv2", inv_h.at[1], inv)

    if comm:
        barrier = pltpu.get_barrier_semaphore()
        peers = [(x, c, lax.rem(z + k, nz), y) for k in range(1, nz)]
        peers += [(x, c, z, 1 - y), (1 - x, c, z, y), (x, 1 - c, z, y)]
        for p in peers:
            pl.semaphore_signal(barrier, inc=1, device_id=at(*p), device_id_type=MESH)

        def scatter(n):
            sems = (s_rs, r_rs)
            split = SPLIT[n]
            if n < nz:
                return Scatter(G.at[n], R.at[n], split, wu_o, sems, n, (n + 1) % nz, [R.at[k] for k in range(nz)])
            if n < nz + nb:
                b = n - nz
                return Scatter(G.at[n], R.at[n], split, wi_o.at[:, pl.ds(b * width, width)], sems, n)
            q = n - nz - nb
            return Scatter(D.at[:, :, pl.ds(0, part), pl.ds(q * width, width)], w2.at[q], split, wo_o if q == 0 else wq_o.at[q - 1], sems, n)

        blocks = nz + nb + 1 + groups
        small = [Spread(early, s_sp.at[0], r_sp.at[0]), Spread(late, s_sp.at[1], r_sp.at[1])]

        def hook(name, i=None):
            if i is None:
                for n, j in plan.get(name, ()):
                    if n < blocks:
                        scatter(n).step(j)
                    elif n < blocks + 2:
                        small[n - blocks].step(j)
                    else:
                        scatter(nz - 1).step(j)
                return
            if isinstance(i, int):
                hook((name, i))
                return
            for k in range(8):
                if (name, k) in plan:
                    pl.when(i == k)(functools.partial(hook, (name, k)))
    else:
        def hook(name, i=None):
            pass

    acc[...] = jnp.zeros_like(acc)

    loads["wp"].wait()
    load("act", act_h, A)
    gain2, gain1 = vec[6:7, :], vec[3:4, :]

    def colsum(v):
        return jnp.sum(v, axis=0, keepdims=True)

    per = span // tile
    steps = rows // tile

    def second_norm(i, _):
        r = pl.ds(pl.multiple_of(i * tile, tile), tile)
        s, j = i // per, i % per
        slot = lax.broadcasted_iota(jnp.int32, (tile, width), 0) + j * tile
        gl = jnp.where(slot < lengths[s], cot[r, :].astype(F32), 0.0)
        head = gfirst[pl.ds(pl.multiple_of(8 * s, 8), 8), :] * jnp.where(j == 0, 1.0, 0.0)
        gl = gl + jnp.concatenate([head, jnp.zeros((tile - 8, width), F32)], axis=0)
        u = u2[r, :].astype(F32)
        a = gl * gain2
        g2 = (a - rowmean(a) - u * rowmean(a * u)) * inv[r, :][:, :1]
        gr[r, :] = g2
        low = g2.astype(BF16)
        gffn[r, :] = low
        tally(3, [(colsum(low.astype(F32)), colsum(gl * u), colsum(gl))])
        return 0

    def tally(first_row, parts):
        for n in range(len(parts[0])):
            acc[first_row + n : first_row + n + 1, :] += sum(p[n] for p in parts[1:]) + parts[0][n]

    lane = lax.broadcasted_iota(jnp.int32, (8 * seqs, 128), 1)
    row = lax.broadcasted_iota(jnp.int32, (8 * seqs, 128), 0)
    live = (lane >= 1) & (lane < 4)
    w_pool = w3[:, :, fr:, :].reshape(width, width)
    first_low = first[...].astype(BF16)
    pooled = jnp.tanh(nn(first_low, w_pool) + vec[8:9, :])
    pooled_low = pooled.astype(BF16)
    heads = jnp.concatenate([vec[8:16, :], jnp.zeros((120, width), F32)], axis=0).astype(BF16)
    logits = nt(pooled_low, heads) + vec[15:16, :128]
    peak = jnp.max(jnp.where(live, logits, -3.0e38), axis=-1, keepdims=True)
    mass = jnp.where(live, jnp.exp(logits - peak), 0.0)
    logsum = peak + jnp.log(jnp.sum(mass, axis=-1, keepdims=True))
    label = jnp.full((8 * seqs, 128), labels[0])
    for s in range(1, seqs):
        label = jnp.where(row >= 8 * s, labels[s], label)
    onehot = jnp.where(lane == label + 1, 1.0, 0.0)
    loss_o[...] = jnp.broadcast_to(logsum - jnp.sum(onehot * logits, axis=-1, keepdims=True), loss_o.shape)
    g_logits = jnp.where(live & (row % 8 == 0), jnp.exp(logits - logsum) - onehot, 0.0).astype(BF16)
    g_pre = (nn(g_logits, heads) * (1.0 - pooled * pooled)).astype(BF16)
    g_first = nt(g_pre, w_pool)

    gfirst[...] = g_first
    for name in ("cot", "u2", "inv2"):
        loads[name].wait()
    lax.fori_loop(0, steps, second_norm, 0)
    load("tok", tok_h, u2)
    load("inv1", inv_h.at[0], inv)

    loads["act"].wait()
    for j in range(fr // ur):
        load(("wu", j), wu_h.at[j], w3.at[:, :, pl.ds(j * ur, ur), :])
    load("dg", dg_h, D)
    load("hid", hid_h, hid)
    if comm:
        pl.semaphore_wait(barrier, len(peers))

    def outer_grad(k, _):
        owner = lax.rem(z + k + 1, nz)
        for yy in range(2):
            f = owner * 2 + yy
            got = tn(A[:, pl.ds(pl.multiple_of(f * fr, 128), fr)], gffn[...]).astype(BF16)
            G[k, :, yy] = got.reshape(nb, part, width)
        hook(OUTER_GRAD, k)
        return 0

    lax.fori_loop(0, nz, outer_grad, 0)
    load("qkv", qkv_h, A.at[:, pl.ds(0, 3 * width)])
    load("ctx", ctx_h, A.at[:, pl.ds(3 * width, width)])
    for j in range(fr // ur):
        loads[("wu", j)].wait()
    loads["dg"].wait()
    load("w2", w2_h, w2)
    load("u1", u1_h, u1)

    def inner_back(i, _):
        r = pl.ds(pl.multiple_of(i * tile, tile), tile)
        for b in range(nb):
            cols = slice(b * width, (b + 1) * width)
            w = w3[b, :, :fr, :].reshape(width, width)
            g = nt(gffn[r, :], w) * D[i, :, :, cols].reshape(tile, width).astype(F32)
            low = g.astype(BF16)
            D[i, :, :, cols] = low.reshape(2, tile // 2, width)
            acc[6 + b : 7 + b, :] += colsum(low.astype(F32))
        hook(INNER_BACK, i)
        return 0

    lax.fori_loop(0, rows // tile, inner_back, 0)
    for g in range(groups):
        load(("w1", g), w1_h.at[g], w3.at[:, :, pl.ds(g * part, part), :])

    loads["hid"].wait()

    def inner_grad(b, _):
        cols = pl.ds(pl.multiple_of(b * width, width), width)
        for m in range(2):
            h = width // 2
            got = tn(hid[:, m * h : (m + 1) * h], D[:, :, :, cols].reshape(rows, width)).astype(BF16)
            G[nz + b, m * nz // 2 : (m + 1) * nz // 2] = got.reshape(nz // 2, 2, part, width)
        hook(INNER_GRAD, b)
        return 0

    lax.fori_loop(0, nb, inner_grad, 0)

    loads["w2"].wait()
    loads["u1"].wait()
    loads["inv1"].wait()

    def hidden_grad(i):
        r = slice(i * tile, (i + 1) * tile)
        gh = gr[r, :]
        for b in range(nb):
            gh += nt(D[i, :, :, b * width : (b + 1) * width].reshape(tile, width), w2[b + 1].reshape(width, width))
        return gh

    def first_norm(i, gh):
        r = slice(i * tile, (i + 1) * tile)
        u = u1[r, :].astype(F32)
        a = gh * gain1
        g1 = (a - rowmean(a) - u * rowmean(a * u)) * inv[r, :][:, :1]
        low = g1.astype(BF16)
        cot[r, :] = low
        tally(0, [(colsum(low.astype(F32)), colsum(gh * u), colsum(gh))])
        gffn[r, :] = nt(low, w2[0].reshape(width, width)).astype(BF16)
        gr[r, :] = g1

    for i in range(steps + 1):
        if i < steps:
            ahead = hidden_grad(i)
        if i:
            first_norm(i - 1, behind)
        if i < steps:
            gr[i * tile : (i + 1) * tile, :] = ahead
            behind = gr[i * tile : (i + 1) * tile, :]
        hook(FIRST_NORM, i)
    if comm:
        for p in peers:
            pl.semaphore_signal(free, inc=1, device_id=at(*p), device_id_type=MESH)
        pay = jnp.concatenate(
            [acc[0:10, :]]
            + [first_low[8 * s : 8 * s + 1, :].astype(F32) for s in range(seqs)]
            + [g_pre[8 * s : 8 * s + 1, :].astype(F32) for s in range(seqs)]
            + [pooled_low[8 * s : 8 * s + 1, :].astype(F32) for s in range(seqs)],
            axis=0,
        )
        early[x, c, y, z] = pay.astype(BF16)

    loads["ctx"].wait()
    loads["qkv"].wait()
    for m in range(2):
        h = width // 2
        got = tn(A[:, 3 * width + m * h : 3 * width + (m + 1) * h], cot[...]).astype(BF16)
        D[m * nz // 2 : (m + 1) * nz // 2, :, :part, :width] = got.reshape(nz // 2, 2, part, width)
    if comm:
        pl.semaphore_wait(free, len(peers))
    hook(OUT_GRAD)

    loads["tok"].wait()
    pairs = HEADS // 2
    gp = pairs // groups
    wide = gp * 2 * size
    def finish_late():
        late_rows = [acc[10 + n : 11 + n, j * 128 : (j + 1) * 128] for n in range(2) for j in range(width // 128)]
        late_rows += [g_logits[8 * s : 8 * s + 1, :].astype(F32) for s in range(seqs)]
        late_rows.append(jnp.zeros((16 - len(late_rows), 128), F32))
        late[x, c, y, z] = jnp.concatenate(late_rows, axis=0).astype(BF16)

    for q in range(groups):
        def attention(i, _):
            attend_backward(A, gffn, lse, lengths, i // gp, q * gp + i % gp, span, width, size)
            hook(ATTEND_BACK + q, i)
            return 0

        lax.fori_loop(0, seqs * gp, attention, 0)
        for p in range(3):
            block_of = A[:, p * width + q * wide : p * width + (q + 1) * wide]
            got = tn(u2[...], block_of).astype(BF16)
            D[:, :, :part, (q + 1) * width + p * wide : (q + 1) * width + (p + 1) * wide] = got.reshape(nz, 2, part, wide)
            if p != 1:
                acc[10 + p // 2 : 11 + p // 2, q * wide : (q + 1) * wide] = colsum(block_of.astype(F32))
        if comm and q == groups - 1:
            finish_late()
        hook(QKV_GRAD + q)
    for g in range(groups):
        loads[("w1", g)].wait()

    def input_grad(i, _):
        r = pl.ds(pl.multiple_of(i * tile, tile), tile)
        total = gr[r, :]
        for g in range(groups):
            w = w3[:, :, g * part : (g + 1) * part, :].reshape(width, width)
            mine = jnp.concatenate([A[r, p * width + g * wide : p * width + (g + 1) * wide] for p in range(3)], axis=1)
            total += nt(mine, w)
        cot[r, :] = total.astype(BF16)
        hook(INPUT_GRAD, i)
        return 0

    lax.fori_loop(0, rows // tile, input_grad, 0)
    back = pltpu.make_async_copy(cot, tg_h, loc.at[len(loads)])
    back.start()
    hook(SMALL_SUMS)
    if comm:
        n = 4 * 2 * nz
        def slot_of(i):
            return (i // (4 * nz), i // (2 * nz) % 2, i // nz % 2, i % nz)

        total = lax.fori_loop(0, n, lambda i, t: t + early[slot_of(i)].astype(F32), jnp.zeros((16, width), F32))
        lates = late[...].reshape(n, 16, 128)
        lsum = jnp.sum(lates.astype(F32), axis=0)
        six = width // 128
        qb = jnp.concatenate([lsum[j : j + 1, :] for j in range(six)], axis=1)
        vb = jnp.concatenate([lsum[six + j : six + j + 1, :] for j in range(six)], axis=1)
        r16 = lax.broadcasted_iota(jnp.int32, (16, width), 0)
        total = jnp.where(r16 == 10, qb, jnp.where(r16 == 11, vb, total))
        f = z * 2 + y
        src = lax.broadcasted_iota(jnp.int32, (width, 128), 0)
        dst = lax.broadcasted_iota(jnp.int32, (width, 128), 1)
        pick = jnp.where((src == dst + f * part) & (dst < part), 1.0, 0.0).astype(BF16)
        src = lax.broadcasted_iota(jnp.int32, (width, fr), 0)
        dst = lax.broadcasted_iota(jnp.int32, (width, fr), 1)
        pick_ff = jnp.where(src == dst + y * fr, 1.0, 0.0).astype(BF16)
        high = total.astype(BF16)
        rest = (total - high.astype(F32)).astype(BF16)
        own = nn(high, pick) + nn(rest, pick)
        wide_own = nn(high, pick_ff) + nn(rest, pick_ff)
        r16f = lax.broadcasted_iota(jnp.int32, (16, fr), 0)
        ib_o[...] = jnp.broadcast_to(colsum(jnp.where(r16f == 6 + z, wide_own, 0.0)), ib_o.shape)
        flat = early[...].reshape(n * 16, width)
        chosen = nn(flat, pick)
        rid = lax.broadcasted_iota(jnp.int32, (n * 16, 128), 0) % 16
        firsts = pltpu.roll(jnp.where((rid >= 10) & (rid < 10 + seqs), chosen, 0.0), seqs, 0).astype(BF16)
        pool_o[...] = tn(firsts, flat)
        pooleds = pltpu.roll(jnp.where(rid >= 10 + 2 * seqs, chosen, 0.0), n * 16 - seqs, 0).astype(BF16)
        class_o[...] = tn(lates.reshape(n * 16, 128), pooleds)
        middle = (rid >= 10 + seqs) & (rid < 10 + 2 * seqs)
        pb = colsum(jnp.where(middle, chosen, 0.0))
        cbg = colsum(jnp.where(middle, lates.reshape(n * 16, 128).astype(F32), 0.0))
        r16s = lax.broadcasted_iota(jnp.int32, (16, 128), 0)
        own_o[...] = jnp.where(r16s == 12, pb, jnp.where(r16s == 13, cbg, own))
        hook(LAST)
        for spread in small:
            spread.drain()
        for n in range(blocks):
            scatter(n).drain()
    back.wait()


def backward(plan, lengths, labels, vec, lse, inv, first, cot, tok, w1, w2, wu, wp, qkv, ctx, hid, u1, act, dg, u2):
    rows, width = cot.shape
    nz = w1.shape[1]
    ff = act.shape[1]
    part = width // (2 * nz)
    fr = ff // (2 * nz)
    nb = ff // width
    seqs = lengths.shape[0]
    any_, vm, smem = (pl.BlockSpec(memory_space=m) for m in (pl.ANY, pltpu.VMEM, pltpu.SMEM))
    S = jax.ShapeDtypeStruct
    outs = [
        (S((8 * seqs, 128), F32), vm),
        (S((16, 128), F32), vm),
        (S((8, fr), F32), vm),
        (S((128, width), F32), vm),
        (S((128, 128), F32), vm),
        (S((part, width), BF16), vm),
        (S((part, ff), BF16), vm),
        (S((nb, part, width), BF16), vm),
        (S((3, part, width), BF16), vm),
        (S((rows, width), BF16), any_),
    ]
    V = pltpu.VMEM
    D = pltpu.SemaphoreType.DMA
    n = 2 * nb
    scratch = [
        V((rows, ff), BF16),
        V(dg.shape, BF16),
        V((1 + nb, nz, 2, part, width), BF16),
        V((nz, 2, fr + part, width), BF16),
        V((rows, width), BF16),
        V((rows, width), BF16),
        V((rows, width), BF16),
        V((rows, width), BF16),
        V((rows, width), BF16),
        V((rows, width), F32),
        V((rows, 128), F32),
        V((16, width), F32),
        V((8 * seqs, width), F32),
        V((n, nz, 2, part, width), BF16),
        V((n, nz, 2, part, width), BF16),
        V((2, 2, 2, nz, 16, width), BF16),
        V((2, 2, 2, nz, 16, 128), BF16),
        D((24,)),
        pltpu.SemaphoreType.REGULAR,
        D((n + 4, 9)), D((n + 4, 9)), D((2, nz + 2)), D((2, nz + 2)),
    ]
    params = pltpu.CompilerParams(vmem_limit_bytes=63 * 2**20, has_side_effects=True, **({"collective_id": 1} if plan is not None else {}))
    cost = pl.CostEstimate(flops=4 * rows * width * (4 * width + 2 * ff), bytes_accessed=10**7, transcendentals=0)
    return pl.pallas_call(
        functools.partial(backward_kernel, plan), out_shape=[o[0] for o in outs], out_specs=[o[1] for o in outs],
        in_specs=[smem, smem] + [vm] * 3 + [any_] * 14, scratch_shapes=scratch, compiler_params=params, cost_estimate=cost,
    )(lengths, labels, vec, lse, first, inv, cot, tok, w1, w2, wu, wp, qkv, ctx, hid, u1, act, dg, u2)


def finish_kernel(output, tg, loss, own, ibg, poolg, classg, wo, wi, wu, wq,
                  output_o, loss_o, tg_o, qkv_o, qb_o, vb_o, wo_o, ob_o, g1_o, s1_o, wi_o, ib_o, wu_o, outb_o, g2_o, s2_o, pool_o, pb_o, class_o, cb_o):
    output_o[...] = output[...]
    tg_o[...] = tg[...]
    part, width = wo.shape
    groups, _, wide3 = wq.shape
    wide = wide3 // groups
    for p in range(3):
        for g in range(groups):
            qkv_o[:, p * width + g * wide : p * width + (g + 1) * wide] = wq[g, :, p * wide : (p + 1) * wide].astype(F32)
    wo_o[...] = wo[...].astype(F32)
    wi_o[...] = wi[...].astype(F32)
    wu_o[...] = wu[...].reshape(wu_o.shape).astype(F32)
    pool_o[...] = poolg[:part, :]
    for n, ref in ((10, qb_o), (11, vb_o), (0, ob_o), (1, g1_o), (2, s1_o), (3, outb_o), (4, g2_o), (5, s2_o), (12, pb_o)):
        ref[...] = own[n, :part]
    ib_o[...] = ibg[0, :]
    classes = cb_o.shape[0]
    cb_o[...] = own[13, 1 : 1 + classes]
    class_o[...] = classg[1 : 1 + classes, :part]
    for s in range(loss_o.shape[0]):
        loss_o[s : s + 1] = loss[8 * s, 0:1]


def finish(output, tg, loss, own, ibg, poolg, classg, wo, wi, wu, wq, classes):
    part, width = wo.shape
    ff = wi.shape[1]
    S = jax.ShapeDtypeStruct
    any_, vm = (pl.BlockSpec(memory_space=m) for m in (pl.ANY, pltpu.VMEM))
    vector = S((part,), F32)
    outs = [S(output.shape, BF16), S((loss.shape[0] // 8,), F32), S(tg.shape, BF16), S((part, 3 * width), F32), vector, vector,
            S((part, width), F32), vector, vector, vector, S((part, ff), F32), S((ibg.shape[1],), F32), S((wu.shape[0] * part, width), F32),
            vector, vector, vector, S((part, width), F32), vector, S((classes, part), F32), S((classes,), F32)]
    *done, classes_t, class_b = pl.pallas_call(
        finish_kernel, out_shape=outs, in_specs=[vm] * 11, out_specs=[vm] * 20,
        compiler_params=pltpu.CompilerParams(vmem_limit_bytes=62 * 2**20),
    )(output, tg, loss, own, ibg, poolg, classg, wo, wi, wu, wq)
    return (*done, classes_t.T, class_b)


def normalize(value, gain, shift):
    mean = jnp.mean(value, axis=-1, keepdims=True)
    centred = value - mean
    inverse = lax.rsqrt(jnp.mean(centred * centred, axis=-1, keepdims=True) + EPS)
    unit = centred * inverse
    return (unit * gain + shift, unit, inverse)


def norm_back(grad, unit, inverse, gain):
    scaled = grad * gain
    inner = (
        scaled
        - jnp.mean(scaled, axis=-1, keepdims=True)
        - unit * jnp.mean(scaled * unit, axis=-1, keepdims=True)
    )
    return (inner * inverse, jnp.sum(grad * unit, axis=0), jnp.sum(grad, axis=0))


def matmul(left, right):
    return jnp.dot(left, right, preferred_element_type=jnp.float32)


def transposed_left(left, right):
    return lax.dot_general(
        left, right, (((0,), (0,)), ((), ())), preferred_element_type=jnp.float32
    )


def transposed_right(left, right):
    return lax.dot_general(
        left, right, (((1,), (1,)), ((), ())), preferred_element_type=jnp.float32
    )


def column_sum(values):
    return jnp.sum(values.astype(jnp.float32), axis=0)


def attend(block):
    query, key, value, keep = block
    scale = query.shape[-1] ** (-0.5)
    scores = jnp.einsum("qhd,khd->hqk", query, key, preferred_element_type=jnp.float32) * scale
    scores = jnp.where(keep[None, None, :], scores, NEG)
    top = jnp.max(scores, axis=-1, keepdims=True)
    total = jnp.sum(jnp.exp(scores - top), axis=-1, keepdims=True)
    logsum = top + jnp.log(total)
    probs = jnp.exp(scores - logsum).astype(jnp.bfloat16)
    context = jnp.einsum("hqk,khd->qhd", probs, value, preferred_element_type=jnp.float32)
    return (context.astype(jnp.bfloat16), logsum[:, :, 0])


def attend_back(block):
    query, key, value, keep, logsum, grad_context = block
    scale = query.shape[-1] ** (-0.5)
    scores = jnp.einsum("qhd,khd->hqk", query, key, preferred_element_type=jnp.float32) * scale
    scores = jnp.where(keep[None, None, :], scores, NEG)
    probs = jnp.exp(scores - logsum[:, :, None])
    grad_value = jnp.einsum(
        "hqk,qhd->khd", probs.astype(jnp.bfloat16), grad_context, preferred_element_type=jnp.float32
    )
    grad_probs = jnp.einsum("qhd,khd->hqk", grad_context, value, preferred_element_type=jnp.float32)
    delta = jnp.sum(grad_probs * probs, axis=-1, keepdims=True)
    grad_scores = (probs * (grad_probs - delta)).astype(jnp.bfloat16)
    grad_query = (
        jnp.einsum("hqk,khd->qhd", grad_scores, key, preferred_element_type=jnp.float32) * scale
    )
    grad_key = (
        jnp.einsum("hqk,qhd->khd", grad_scores, query, preferred_element_type=jnp.float32) * scale
    )
    return (
        grad_query.astype(jnp.bfloat16),
        grad_key.astype(jnp.bfloat16),
        grad_value.astype(jnp.bfloat16),
    )


def per_device_any(
    tokens,
    lengths,
    labels,
    cotangent,
    qkv_weight,
    query_bias,
    value_bias,
    out_weight,
    out_bias,
    first_gain,
    first_shift,
    inner_weight,
    inner_bias,
    outer_weight,
    outer_bias,
    second_gain,
    second_shift,
    pool_weight,
    pool_bias,
    class_weight,
    class_bias,
):
    full = (
        lax.all_gather(qkv_weight, FSDP, axis=0, tiled=True),
        lax.all_gather(query_bias, FSDP, axis=0, tiled=True),
        lax.all_gather(value_bias, FSDP, axis=0, tiled=True),
        lax.all_gather(out_weight, FSDP, axis=0, tiled=True),
        lax.all_gather(out_bias, FSDP, axis=0, tiled=True),
        lax.all_gather(first_gain, FSDP, axis=0, tiled=True),
        lax.all_gather(first_shift, FSDP, axis=0, tiled=True),
        lax.all_gather(inner_weight, FSDP, axis=0, tiled=True),
        lax.all_gather(inner_bias, FSDP, axis=0, tiled=True),
        lax.all_gather(outer_weight, FSDP, axis=0, tiled=True),
        lax.all_gather(outer_bias, FSDP, axis=0, tiled=True),
        lax.all_gather(second_gain, FSDP, axis=0, tiled=True),
        lax.all_gather(second_shift, FSDP, axis=0, tiled=True),
        lax.all_gather(pool_weight, FSDP, axis=0, tiled=True),
        lax.all_gather(pool_bias, FSDP, axis=0, tiled=True),
        lax.all_gather(class_weight, FSDP, axis=0, tiled=True),
    )
    (
        w_qkv,
        b_query,
        b_value,
        w_out,
        b_out,
        g_first,
        s_first,
        w_inner,
        b_inner,
        w_outer,
        b_outer,
        g_second,
        s_second,
        w_pool,
        b_pool,
        w_class,
    ) = full
    b_query = b_query.astype(jnp.float32)
    b_value = b_value.astype(jnp.float32)
    b_out = b_out.astype(jnp.float32)
    g_first = g_first.astype(jnp.float32)
    s_first = s_first.astype(jnp.float32)
    b_inner = b_inner.astype(jnp.float32)
    b_outer = b_outer.astype(jnp.float32)
    g_second = g_second.astype(jnp.float32)
    s_second = s_second.astype(jnp.float32)
    b_pool = b_pool.astype(jnp.float32)
    b_class = class_bias.astype(jnp.float32)
    seqs = lengths.shape[0]
    rows, width = tokens.shape
    span = rows // seqs
    size = width // HEADS
    classes = class_bias.shape[0]
    position = lax.broadcasted_iota(jnp.int32, (seqs, span), 1)
    keep = position < lengths[:, None]
    valid = keep.reshape(rows, 1).astype(jnp.float32)
    bias_all = jnp.concatenate([b_query, jnp.zeros_like(b_query), b_value])
    qkv = (matmul(tokens, w_qkv) + bias_all).astype(jnp.bfloat16)
    query = qkv[:, :width].reshape(seqs, span, HEADS, size)
    key = qkv[:, width : 2 * width].reshape(seqs, span, HEADS, size)
    value = qkv[:, 2 * width :].reshape(seqs, span, HEADS, size)
    context, logsum = lax.map(attend, (query, key, value, keep))
    context = context.reshape(rows, width)
    attended = matmul(context, w_out) + b_out
    hidden, unit_first, inverse_first = normalize(
        tokens.astype(jnp.float32) + attended, g_first, s_first
    )
    hidden_low = hidden.astype(jnp.bfloat16)
    inner = matmul(hidden_low, w_inner) + b_inner
    act = jax.nn.gelu(inner, approximate=False).astype(jnp.bfloat16)
    ffn = matmul(act, w_outer) + b_outer
    layer, unit_second, inverse_second = normalize(hidden + ffn, g_second, s_second)
    output = (layer * valid).astype(jnp.bfloat16)
    first = layer.reshape(seqs, span, width)[:, 0].astype(jnp.bfloat16)
    pooled = jnp.tanh(matmul(first, w_pool) + b_pool)
    pooled_low = pooled.astype(jnp.bfloat16)
    logits = matmul(pooled_low, w_class) + b_class
    peak = jnp.max(logits, axis=-1, keepdims=True)
    logsum_class = peak + jnp.log(jnp.sum(jnp.exp(logits - peak), axis=-1, keepdims=True))
    onehot = (labels[:, None] == lax.broadcasted_iota(jnp.int32, (seqs, classes), 1)).astype(
        jnp.float32
    )
    exit_loss = logsum_class[:, 0] - jnp.sum(onehot * logits, axis=-1)
    again = (
        lax.all_gather(qkv_weight, FSDP, axis=0, tiled=True),
        lax.all_gather(query_bias, FSDP, axis=0, tiled=True),
        lax.all_gather(value_bias, FSDP, axis=0, tiled=True),
        lax.all_gather(out_weight, FSDP, axis=0, tiled=True),
        lax.all_gather(out_bias, FSDP, axis=0, tiled=True),
        lax.all_gather(first_gain, FSDP, axis=0, tiled=True),
        lax.all_gather(first_shift, FSDP, axis=0, tiled=True),
        lax.all_gather(inner_weight, FSDP, axis=0, tiled=True),
        lax.all_gather(inner_bias, FSDP, axis=0, tiled=True),
        lax.all_gather(outer_weight, FSDP, axis=0, tiled=True),
        lax.all_gather(outer_bias, FSDP, axis=0, tiled=True),
        lax.all_gather(second_gain, FSDP, axis=0, tiled=True),
        lax.all_gather(second_shift, FSDP, axis=0, tiled=True),
        lax.all_gather(pool_weight, FSDP, axis=0, tiled=True),
        lax.all_gather(pool_bias, FSDP, axis=0, tiled=True),
        lax.all_gather(class_weight, FSDP, axis=0, tiled=True),
    )
    w_qkv = again[0]
    w_out = again[3]
    g_first = again[5].astype(jnp.float32)
    w_inner = again[7]
    w_outer = again[9]
    g_second = again[11].astype(jnp.float32)
    w_pool = again[13]
    w_class = again[15]
    grad_logits = (jnp.exp(logits - logsum_class) - onehot).astype(jnp.bfloat16)
    grad_class_weight = transposed_left(pooled_low, grad_logits)
    grad_class_local = column_sum(grad_logits)
    grad_pooled = transposed_right(grad_logits, w_class)
    grad_pre = (grad_pooled * (1.0 - pooled * pooled)).astype(jnp.bfloat16)
    grad_pool_weight = transposed_left(first, grad_pre)
    grad_pool_bias = column_sum(grad_pre)
    grad_first = transposed_right(grad_pre, w_pool)
    grad_layer = (cotangent.astype(jnp.float32) * valid).reshape(seqs, span, width)
    grad_layer = jnp.concatenate(
        [grad_layer[:, :1] + grad_first[:, None, :], grad_layer[:, 1:]], axis=1
    )
    grad_layer = grad_layer.reshape(rows, width)
    grad_resid_second, grad_second_gain, grad_second_shift = norm_back(
        grad_layer, unit_second, inverse_second, g_second
    )
    grad_ffn = grad_resid_second.astype(jnp.bfloat16)
    grad_outer_weight = transposed_left(act, grad_ffn)
    grad_outer_bias = column_sum(grad_ffn)
    grad_act = transposed_right(grad_ffn, w_outer)
    gelu_value, gelu_pull = jax.vjp(lambda v: jax.nn.gelu(v, approximate=False), inner)
    grad_inner = gelu_pull(grad_act)[0].astype(jnp.bfloat16)
    grad_inner_weight = transposed_left(hidden_low, grad_inner)
    grad_inner_bias = column_sum(grad_inner)
    grad_hidden = grad_resid_second + transposed_right(grad_inner, w_inner)
    grad_resid_first, grad_first_gain, grad_first_shift = norm_back(
        grad_hidden, unit_first, inverse_first, g_first
    )
    grad_attended = grad_resid_first.astype(jnp.bfloat16)
    grad_out_weight = transposed_left(context, grad_attended)
    grad_out_bias = column_sum(grad_attended)
    grad_context = (
        transposed_right(grad_attended, w_out).astype(jnp.bfloat16).reshape(seqs, span, HEADS, size)
    )
    grad_query, grad_key, grad_value = lax.map(
        attend_back, (query, key, value, keep, logsum, grad_context)
    )
    grad_query = grad_query.reshape(rows, width)
    grad_key = grad_key.reshape(rows, width)
    grad_value = grad_value.reshape(rows, width)
    grad_qkv = jnp.concatenate([grad_query, grad_key, grad_value], axis=1)
    grad_qkv_weight = transposed_left(tokens, grad_qkv)
    grad_query_bias = column_sum(grad_query)
    grad_value_bias = column_sum(grad_value)
    tokens_grad = (grad_resid_first + transposed_right(grad_qkv, w_qkv)).astype(jnp.bfloat16)
    owned = (
        lax.psum_scatter(grad_qkv_weight, FSDP, scatter_dimension=0, tiled=True),
        lax.psum_scatter(grad_query_bias, FSDP, scatter_dimension=0, tiled=True),
        lax.psum_scatter(grad_value_bias, FSDP, scatter_dimension=0, tiled=True),
        lax.psum_scatter(grad_out_weight, FSDP, scatter_dimension=0, tiled=True),
        lax.psum_scatter(grad_out_bias, FSDP, scatter_dimension=0, tiled=True),
        lax.psum_scatter(grad_first_gain, FSDP, scatter_dimension=0, tiled=True),
        lax.psum_scatter(grad_first_shift, FSDP, scatter_dimension=0, tiled=True),
        lax.psum_scatter(grad_inner_weight, FSDP, scatter_dimension=0, tiled=True),
        lax.psum_scatter(grad_inner_bias, FSDP, scatter_dimension=0, tiled=True),
        lax.psum_scatter(grad_outer_weight, FSDP, scatter_dimension=0, tiled=True),
        lax.psum_scatter(grad_outer_bias, FSDP, scatter_dimension=0, tiled=True),
        lax.psum_scatter(grad_second_gain, FSDP, scatter_dimension=0, tiled=True),
        lax.psum_scatter(grad_second_shift, FSDP, scatter_dimension=0, tiled=True),
        lax.psum_scatter(grad_pool_weight, FSDP, scatter_dimension=0, tiled=True),
        lax.psum_scatter(grad_pool_bias, FSDP, scatter_dimension=0, tiled=True),
        lax.psum_scatter(grad_class_weight, FSDP, scatter_dimension=0, tiled=True),
    )
    summed = lax.psum(
        (
            owned[0],
            owned[1],
            owned[2],
            owned[3],
            owned[4],
            owned[5],
            owned[6],
            owned[7],
            owned[8],
            owned[9],
            owned[10],
            owned[11],
            owned[12],
            owned[13],
            owned[14],
            owned[15],
        ),
        DP,
    )
    class_bias_grad = lax.psum(grad_class_local, (DP, FSDP))
    return (
        output,
        exit_loss,
        tokens_grad,
        summed[0],
        summed[1],
        summed[2],
        summed[3],
        summed[4],
        summed[5],
        summed[6],
        summed[7],
        summed[8],
        summed[9],
        summed[10],
        summed[11],
        summed[12],
        summed[13],
        summed[14],
        summed[15],
        class_bias_grad,
    )


def per_device(nz, tokens, lengths, labels, cotangent, qkv_weight, query_bias, value_bias, out_weight, out_bias,
    first_gain, first_shift, inner_weight, inner_bias, outer_weight, outer_bias, second_gain, second_shift,
    pool_weight, pool_bias, class_weight, class_bias):
    classes = class_bias.shape[0]
    small = [query_bias, value_bias, out_bias, first_gain, first_shift, outer_bias, second_gain, second_shift, pool_bias, class_weight.T, inner_bias, class_bias]
    (output, w1, w2, wu, wp, vec, ib, qkv, context, lse, hidden_low, unit_first, act, dgelu, unit_second, inv, firsts) = forward(
        FORWARD_PLAN, tokens, lengths, qkv_weight, out_weight, inner_weight, outer_weight, pool_weight, small, nz)
    (loss, own, ibg, poolg, classg, wo, wi, wug, wq, tokens_grad) = backward(
        BACKWARD_PLAN, lengths, labels, vec, lse, inv, firsts, cotangent, tokens, w1, w2, wu, wp, qkv, context, hidden_low, unit_first, act, dgelu, unit_second)
    return finish(output, tokens_grad, loss, own, ibg, poolg, classg, wo, wi, wug, wq, classes)


def solution(mesh):
    in_specs = (
        P((DP, FSDP), None),
        P((DP, FSDP)),
        P((DP, FSDP)),
        P((DP, FSDP), None),
        P(FSDP, None),
        P(FSDP),
        P(FSDP),
        P(FSDP, None),
        P(FSDP),
        P(FSDP),
        P(FSDP),
        P(FSDP, None),
        P(FSDP),
        P(FSDP, None),
        P(FSDP),
        P(FSDP),
        P(FSDP),
        P(FSDP, None),
        P(FSDP),
        P(FSDP, None),
        P(),
    )
    out_specs = (
        P((DP, FSDP), None),
        P((DP, FSDP)),
        P((DP, FSDP), None),
        P(FSDP, None),
        P(FSDP),
        P(FSDP),
        P(FSDP, None),
        P(FSDP),
        P(FSDP),
        P(FSDP),
        P(FSDP, None),
        P(FSDP),
        P(FSDP, None),
        P(FSDP),
        P(FSDP),
        P(FSDP),
        P(FSDP, None),
        P(FSDP),
        P(FSDP, None),
        P(),
    )
    sizes = dict(mesh.shape)
    fast = sizes[DP] == 4 and sizes[FSDP] == 8
    return jax.shard_map(
        functools.partial(per_device, sizes[FSDP] // 2) if fast else per_device_any, mesh=mesh, in_specs=in_specs, out_specs=out_specs, check_vma=False
    )
```

```python
import functools
import math

import jax
import jax.numpy as jnp
from jax import lax
from jax.experimental import pallas as pl
from jax.experimental.pallas import tpu as pltpu
from jax.sharding import PartitionSpec as P

HEADS = 12
DP, FSDP = "dp", "fsdp"
EPS = 1e-12
NEG = -1000000000.0
F32 = jnp.float32
BF16 = jnp.bfloat16
MESH = pl.DeviceIdType.MESH
LOG2E = math.log2(math.e)

START, NEED_QKV, PROJECT, ATTEND, NEED_OUT, NORM = 0, 10, 20, 30, 40, 41
NEED_INNER, EXPAND, NEED_OUTER, CONTRACT, NEED_POOL = 50, 60, 70, 80, 90
OUTER_GRAD, INNER_BACK, INNER_GRAD, FIRST_NORM, OUT_GRAD = 0, 1, 2, 4, 5
INPUT_GRAD, SMALL_SUMS, LAST, ATTEND_BACK, QKV_GRAD = 6, 7, 8, 10, 20

FINE = (0,)
ONE_WAY = (1, 2, 3)
SPLIT = (256, 256, 256, 256, 256, 256, 256, 256, 256, 256, 256, 256)

FORWARD_PLAN = {
    0: ((0, 0), (1, 0),),
    10: ((0, 1), (0, 2), (0, 3), (0, 4), (0, 5), (2, 0), (0, 6), (3, 0), (0, 7), (1, 1), (0, 8), (0, 9), (4, 0), (0, 10), (0, 11), (0, 12),),
    (20, 0): ((2, 1),),
    (20, 3): ((1, 2), (5, 0),),
    (30, 0): ((3, 1),),
    (30, 1): ((6, 0),),
    (30, 3): ((2, 2),),
    11: ((4, 1), (1, 3), (7, 0), (1, 4),),
    (21, 1): ((3, 2),),
    (21, 3): ((5, 1),),
    (31, 0): ((8, 0),),
    (31, 1): ((2, 3),),
    (31, 2): ((4, 2),),
    (31, 3): ((2, 4), (6, 1),),
    (22, 2): ((9, 0),),
    (22, 3): ((3, 3),),
    (32, 1): ((3, 4), (5, 2), (7, 1),),
    (32, 2): ((4, 3),),
    (32, 3): ((10, 0),),
    (41, 0): ((4, 4), (6, 2),),
    (41, 2): ((5, 3), (8, 1),),
    (60, 0): ((5, 4), (7, 2), (11, 0),),
    (60, 2): ((6, 3),),
    (61, 0): ((8, 2), (6, 4), (9, 1),),
    (61, 3): ((7, 3),),
    (62, 2): ((7, 4), (8, 3), (10, 1),),
    (63, 1): ((8, 4), (9, 2),),
    (63, 3): ((11, 1),),
    (80, 2): ((10, 2),),
    71: ((9, 3), (9, 4),),
    (81, 1): ((11, 2),),
    (81, 3): ((10, 3),),
    72: ((10, 4),),
    (82, 1): ((11, 3),),
    (82, 3): ((11, 4),),
}

BACKWARD_PLAN = {
    (0, 0): ((0, 0),),
    (0, 1): ((1, 0),),
    (0, 2): ((0, 1), (2, 0),),
    (0, 3): ((1, 1), (3, 0),),
    (1, 0): ((2, 1),),
    (1, 1): ((3, 1),),
    (1, 2): ((0, 2),),
    (2, 0): ((4, 0),),
    (2, 1): ((1, 2), (5, 0),),
    (2, 2): ((4, 1), (6, 0),),
    (2, 3): ((5, 1), (7, 0),),
    (4, 0): ((2, 2), (6, 1),),
    (4, 1): ((7, 1),),
    (4, 2): ((3, 2),),
    (4, 3): ((0, 3), (1, 3),),
    5: ((8, 0), (12, 0),),
    (10, 0): ((4, 2), (8, 1),),
    (10, 2): ((2, 3), (5, 2), (12, 1),),
    20: ((9, 0),),
    (11, 0): ((6, 2),),
    (11, 1): ((9, 1),),
    (11, 2): ((3, 3), (14, 4), (7, 2), (4, 3), (4, 4),),
    (11, 3): ((14, 5),),
    21: ((10, 0),),
    (12, 0): ((5, 3), (5, 4), (8, 2), (10, 1),),
    (12, 1): ((14, 6), (6, 3), (6, 4), (4, 5), (12, 2),),
    (12, 2): ((14, 7), (5, 5),),
    (12, 3): ((4, 6), (9, 2), (7, 3), (7, 4),),
    22: ((4, 7), (6, 5), (8, 3), (8, 4), (11, 0), (13, 0),),
    (6, 0): ((5, 6), (12, 3),),
    (6, 1): ((6, 6), (5, 7), (10, 2), (11, 1),),
    (6, 2): ((6, 7), (12, 4), (9, 3), (9, 4),),
    (6, 3): ((7, 5),),
    7: ((8, 5), (10, 3), (13, 1), (7, 6), (8, 6), (7, 7), (8, 7), (11, 2), (10, 4), (13, 2), (9, 5), (10, 5), (11, 3), (13, 3), (9, 6), (10, 6), (13, 4),),
    8: ((9, 7), (10, 7), (11, 4), (11, 5), (11, 6), (11, 7),),
}


def nn(left, right):
    return jnp.dot(left, right, preferred_element_type=F32)


def nt(left, right):
    return lax.dot_general(left, right, (((1,), (1,)), ((), ())), preferred_element_type=F32)


def tn(left, right):
    return lax.dot_general(left, right, (((0,), (0,)), ((), ())), preferred_element_type=F32)


def rowmean(value):
    return jnp.sum(value, axis=-1, keepdims=True) * (1.0 / value.shape[-1])


def here():
    d, f = lax.axis_index(DP), lax.axis_index(FSDP)
    return d // 2, d % 2, f // 2, f % 2


def at(x, c, z, y):
    return (x * 2 + c, z * 2 + y)


def attend_forward(qkv, ctx, lse, lengths, i, span, width, size):
    pairs = width // (2 * size)
    wide = 2 * size
    s, hp = i // pairs, i % pairs
    rows = pl.ds(pl.multiple_of(s * span, span), span)

    def part(p):
        return qkv[rows, pl.ds(pl.multiple_of(p * width + hp * wide, wide), wide)]

    q, k, v = part(0), part(1), part(2)
    lane = lax.broadcasted_iota(jnp.int32, (span, wide), 1)
    slot = lax.broadcasted_iota(jnp.int32, (span, wide), 0)
    fill = jnp.where(slot < lengths[s], 0.0, NEG).astype(BF16)
    vt = v.T
    vrow = lax.broadcasted_iota(jnp.int32, (wide, span), 0)
    factor = size ** (-0.5) * LOG2E
    halves, sums = [], []
    for h in range(2):
        mine = lane < size if h == 0 else lane >= size
        other = (1 - h) * size
        qh = jnp.where(mine, q, jnp.where(lane == other, 1.0, 0.0).astype(BF16))
        kh = jnp.where(mine, k, fill)
        scores = nt(kh, qh)
        top = jnp.max(scores, axis=0, keepdims=True)
        e = jnp.exp2((scores - top) * factor).astype(BF16)
        vmine = vrow < size if h == 0 else vrow >= size
        vh = jnp.where(vmine, vt, jnp.ones_like(vt))
        o = nn(vh, e)
        total = o[other : other + 1, :]
        halves.append(o[h * size : (h + 1) * size, :] / total)
        sums.append(top * factor + jnp.log2(total))
    ct = jnp.concatenate(halves, axis=0)
    ctx[rows, pl.ds(pl.multiple_of(hp * wide, wide), wide)] = ct.T.astype(BF16)
    lse[i] = jnp.concatenate(sums + [jnp.zeros((6, span), F32)], axis=0)


class Gather:
    def __init__(self, buf, send, recv, first, fine, one_way):
        self.buf, self.send, self.recv, self.base, self.fine, self.one_way = buf, send, recv, first, fine, one_way
        self.nz, _, self.r, self.cols = buf.shape
        self.me = here()
        half = self.cols // 2
        x, c, z, y = self.me
        c0 = pl.multiple_of(c * half, 128)
        third = 0 if one_way else half // 3
        self.both = pl.ds(c0, half)
        self.first = pl.ds(c0, third)
        self.second = pl.ds(pl.multiple_of(c0 + third, 128), half - third)
        self.theirs = pl.ds(pl.multiple_of((1 - c) * half, 128), half)
        r2 = self.r // 2
        self.row = pl.ds(pl.multiple_of(x * r2, 16), r2)
        self.row_o = pl.ds(pl.multiple_of((1 - x) * r2, 16), r2)
        self.every = pl.ds(0, self.r)

    def copy(self, kind, k=None, incoming=False):
        x, c, z, y = self.me
        nz, buf = self.nz, self.buf
        if k is None:
            zk = pl.ds(0, nz if kind in ("ya", "yb", "xa", "cx") else nz - 1)
        else:
            zk = lax.rem(z + nz - k, nz)
        row = self.row_o if incoming else self.row
        both = self.theirs if incoming else self.both
        yo = 1 - y if incoming else y
        if kind in ("za", "zb"):
            slot = zk if incoming or k is None else z
            ref = buf.at[slot, y, self.every, self.first] if kind == "za" else buf.at[slot, y, self.row, self.second]
            peer = (x, c, lax.rem(z + (k or 1), nz), y)
        elif kind == "xo":
            ref, peer = buf.at[zk, y, row, self.second], (1 - x, c, z, y)
        elif kind == "co":
            ref, peer = buf.at[zk, y, self.every, both], (x, 1 - c, z, y)
        elif kind == "ya":
            ref, peer = buf.at[zk, yo, self.every, self.first], (x, c, z, 1 - y)
        elif kind == "yb":
            ref, peer = buf.at[zk, yo, self.row, self.second], (x, c, z, 1 - y)
        elif kind == "xa":
            ref, peer = buf.at[zk, 1 - y, row, self.second], (1 - x, c, z, y)
        else:
            ref, peer = buf.at[zk, 1 - y, self.every, both], (x, 1 - c, z, y)
        n = ("za", "zb", "xo", "co", "ya", "yb", "xa", "cx").index(kind)
        n = self.base + (n * nz + k if self.fine else n)
        return pltpu.make_async_remote_copy(
            src_ref=ref, dst_ref=ref, send_sem=self.send.at[n], recv_sem=self.recv.at[n], device_id=at(*peer), device_id_type=MESH
        )

    def go(self, *kind):
        self.copy(*kind).start()

    def got(self, kind, k=None):
        self.copy(kind, k, True).wait_recv()

    def step(self, j):
        nz = self.nz
        ks = range(1, nz)
        if j == 0:
            for k in ks:
                self.go("zb", k)
                if not self.one_way:
                    self.go("za", k)
            if self.fine:
                self.go("yb", 0)
                self.go("ya", 0)
        elif self.fine:
            if j < nz:
                self.got("zb", j)
                self.go("xo", j)
                self.go("yb", j)
                self.got("za", j)
                self.go("ya", j)
            elif j < 2 * nz:
                k = j - nz
                self.got("yb", k)
                self.go("xa", k)
                if k:
                    self.got("xo", k)
                    self.go("co", k)
            elif j < 3 * nz:
                k = j - 2 * nz
                self.got("ya", k)
                self.got("xa", k)
                self.go("cx", k)
            else:
                for k in range(nz):
                    if k:
                        self.got("co", k)
                    self.got("cx", k)
        elif j == 1:
            self.got("zb")
            for k in ks:
                self.go("xo", k)
            self.go("yb")
            if not self.one_way:
                self.got("za")
                self.go("ya")
        elif j == 2:
            self.got("yb")
            self.go("xa")
            self.got("xo")
            for k in ks:
                self.go("co", k)
        elif j == 3:
            if not self.one_way:
                self.got("ya")
            self.got("xa")
            self.go("cx")
        else:
            self.got("co")
            self.got("cx")

    def drain(self):
        for kind in ("za", "zb", "xo", "co", "ya", "yb", "xa", "cx"):
            if self.one_way and kind in ("za", "ya"):
                continue
            for k in range(self.nz) if self.fine else (None,):
                if k != 0 or kind in ("ya", "yb", "xa", "cx"):
                    self.copy(kind, k).wait_send()


def gelu_both(value):
    cdf = 0.5 + 0.5 * lax.erf(value * (0.5**0.5))
    bell = jnp.exp2(value * value * (-0.5 * LOG2E)) * (1.0 / math.sqrt(2.0 * math.pi))
    return value * cdf, cdf + value * bell


def place(sm, f, part, width):
    row = lax.broadcasted_iota(jnp.int32, (128, width), 0)
    col = lax.broadcasted_iota(jnp.int32, (128, width), 1)
    return jnp.where((col == row + f * part) & (row < part), 1.0, 0.0).astype(BF16)


def forward_kernel(plan, tokens_h, lengths, wqkv_h, wout_h, winner_h, wouter_h, wpool_h, small_h,
                   out_h, w1_h, w2_h, wu_h, wp_h, vec_o, ib_o, qkv_h, ctx_h, lse_o, hid_h, u1_h, act_h, dg_h, u2_h, inv_o, first_o,
                   tokens, w1, w2, wu, wp, sm, qkv, ctx, hid, hidlow, u1, act, dg, u2, outv,
                   last_sem, loc, s_sm, r_sm, s_g, r_g, *raw):
    comm = plan is not None
    x, c, z, y = here() if comm else (0, 0, 0, 0)
    groups, nz = w1.shape[:2]
    rows, width = tokens.shape
    seqs = lengths.shape[0]
    span = rows // seqs
    ff = act.shape[1]
    nb = ff // width
    size = width // HEADS
    pairs = HEADS // 2
    gp = pairs // groups
    wide = gp * 2 * size
    nf = nz * 2
    part = width // nf
    fr = ff // nf
    ur = wu.shape[3]
    nu = wu.shape[0]
    units = [(w1, g) for g in range(groups)] + [(w2, b) for b in range(1 + nb)] + [(wu, j) for j in range(nu)] + [(wp, 0)]

    def small_parameters():
        vec = jnp.zeros((sm.shape[1], width), F32)
        for f in range(nf):
            vec += nn(sm[f], place(None, f, part, width))
        vec_o[...] = vec
        ibs = []
        for f in range(nf):
            piece = sm[f].astype(F32)
            for j in range(fr // 128):
                ibs.append(piece[12 + j : 13 + j, :])
        ib_o[...] = jnp.broadcast_to(jnp.concatenate(ibs, axis=1), ib_o.shape)

    f_me = z * 2 + y
    started = []

    def bring(src, dst):
        copy = pltpu.make_async_copy(src, dst, loc.at[len(started)])
        copy.start()
        started.append(copy)
        return copy

    if comm:
        barrier = pltpu.get_barrier_semaphore()
        peers = [(x, c, lax.rem(z + k, nz), yy) for k in range(1, nz) for yy in (y, 1 - y)]
        peers += [(x, c, z, 1 - y), (1 - x, c, z, y), (x, 1 - c, z, y)]
        for p in peers:
            pl.semaphore_signal(barrier, inc=1, device_id=at(*p), device_id_type=MESH)
        own = []
        for g in range(groups):
            own.append([bring(wqkv_h.at[:, pl.ds(p * width + g * wide, wide)], w1.at[g, z, y, :, pl.ds(p * wide, wide)]) for p in range(3)])
        parts = [bring(src, dst) for src, dst in zip(small_h, raw)]
        own.append([bring(wout_h, w2.at[0, z, y])])
        for b in range(nb):
            own.append([bring(winner_h.at[:, pl.ds(b * width, width)], w2.at[b + 1, z, y])])
        tok = bring(tokens_h, tokens)
        for j in range(fr // ur):
            own.append([bring(wouter_h.at[pl.ds(j * ur, ur)], wu.at[j, z, y])])
        own.append([bring(wpool_h, wp.at[0, z, y])])

        def unit(m):
            buf, n = units[m]
            ahead = sum(e < m for e in FINE)
            return Gather(buf.at[n], s_g, r_g, 8 * (m + ahead * (nz - 1)), m in FINE, m in ONE_WAY)

        def small(n, slot):
            return pltpu.make_async_remote_copy(
                src_ref=sm.at[slot], dst_ref=sm.at[slot], send_sem=s_sm.at[n], recv_sem=r_sm.at[n], device_id=at(*peers[n]), device_id_type=MESH
            )

        others = len(peers) - 2

        def smalls_sent():
            for cp in parts:
                cp.wait()

            def lanes(v, before=0):
                v = v.astype(F32)
                v = v.reshape(1, -1) if v.ndim == 1 else v
                ends = [jnp.zeros((v.shape[0], n), F32) for n in (before, 128 - before - v.shape[1])]
                return jnp.concatenate(([ends[0]] if before else []) + [v, ends[1]], axis=1)

            *vectors, classes, wide_bias, class_bias = (r[...] for r in raw)
            wide_bias = wide_bias.astype(F32).reshape(1, fr)
            lines = [lanes(v) for v in vectors] + [lanes(classes)]
            lines += [wide_bias[:, j * 128 : (j + 1) * 128] for j in range(fr // 128)] + [lanes(class_bias, 1)]
            sm[f_me] = jnp.concatenate(lines, axis=0).astype(BF16)
            for n in range(others):
                small(n, f_me).start()

        def smalls_here():
            for n in range(others):
                if n < 2 * (nz - 1):
                    slot = lax.rem(z + nz - n // 2 - 1, nz) * 2 + (y if n % 2 == 0 else 1 - y)
                else:
                    slot = z * 2 + 1 - y
                small(n, slot).wait_recv()

        pl.semaphore_wait(barrier, len(peers))

        def hook(name, i=None):
            if i is None:
                for n, j in plan.get(name, ()):
                    if j == 0:
                        for cp in own[n]:
                            cp.wait()
                    unit(n).step(j)
                    if (n, j) == (0, 0):
                        smalls_sent()
                    if (n, j) == (0, nz):
                        smalls_here()
                        small_parameters()
                        tok.wait()
                return
            for k in range(8):
                if (name, k) in plan:
                    pl.when(i == k)(functools.partial(hook, (name, k)))
    else:
        def hook(name, i=None):
            pass

        for a, b in ((tokens_h, tokens), (w1_h, w1), (w2_h, w2), (wu_h, wu), (wp_h, wp), (small_h, sm)):
            bring(a, b).wait()
        small_parameters()

    hook(START)
    tile = rows // nz
    steps = rows // tile

    def tiles(i):
        return pl.ds(pl.multiple_of(i * tile, tile), tile)

    def loop(count, body):
        def step(i, _):
            body(i)
            return 0

        lax.fori_loop(0, count, step, 0)

    saved = []

    def save(src, dst):
        saved.append(bring(src, dst))

    for g in range(groups):
        hook(NEED_QKV + g)
        lo = g * wide
        bias = (vec_o[0:1, lo : lo + wide], None, vec_o[1:2, lo : lo + wide])

        def project(i):
            r = tiles(i)
            got = nn(tokens[r, :], w1[g].reshape(width, 3 * wide))
            for p in range(3):
                mine = got[:, p * wide : (p + 1) * wide]
                qkv[r, p * width + lo : p * width + lo + wide] = (mine if bias[p] is None else mine + bias[p]).astype(BF16)
            hook(PROJECT + g, i)

        loop(steps, project)

        def attention(i):
            s, hp = i // gp, g * gp + i % gp
            attend_forward(qkv, ctx, lse_o, lengths, s * pairs + hp, span, width, size)
            hook(ATTEND + g, i)

        loop(seqs * gp, attention)
    if comm:
        save(w1, w1_h)
    save(qkv, qkv_h)
    save(ctx, ctx_h)

    hook(NEED_OUT)
    b_out, g_first, s_first, b_outer, g_second, s_second = (vec_o[n : n + 1, :] for n in range(2, 8))

    def norm_one(i):
        r = tiles(i)
        resid = tokens[r, :].astype(F32) + (nn(ctx[r, :], w2[0].reshape(width, width)) + b_out)
        centred = resid - rowmean(resid)
        inv = lax.rsqrt(rowmean(centred * centred) + EPS)
        unit_ = centred * inv
        u1[r, :] = unit_.astype(BF16)
        inv_o[0, r, :] = jnp.broadcast_to(inv, (tile, 128))
        h = unit_ * g_first + s_first
        hid[r, :] = h + b_outer
        hidlow[r, :] = h.astype(BF16)
        hook(NORM, i)

    loop(steps, norm_one)
    save(u1, u1_h)
    save(hidlow, hid_h)
    for b in range(nb):
        hook(NEED_INNER + b)
        cols = slice(b * width, (b + 1) * width)

        def expand(i):
            r = tiles(i)
            a, g = gelu_both(nn(hidlow[r, :], w2[b + 1].reshape(width, width)) + ib_o[0:1, cols])
            act[r, cols] = a.astype(BF16)
            dg[i, :, :, cols] = g.astype(BF16).reshape(2, tile // 2, width)
            hook(EXPAND + b, i)

        loop(steps, expand)
    if comm:
        save(w2, w2_h)
    save(act, act_h)
    save(dg, dg_h)

    def leaving(i):
        r = tiles(i)
        return [pltpu.make_async_copy(src.at[r], dst.at[r], last_sem.at[n, i]) for n, (src, dst) in enumerate(((u2, u2_h), (outv, out_h)))]

    for j in range(nu):
        hook(NEED_OUTER + j)
        if comm:
            save(wu.at[j], wu_h.at[j])

        def contract(i):
            r = tiles(i)
            a = jnp.concatenate([act[r, f * fr + j * ur : f * fr + (j + 1) * ur] for f in range(nf)], axis=1)
            resid = hid[r, :] + nn(a, wu[j].reshape(nf * ur, width))
            if j < nu - 1:
                hid[r, :] = resid
            else:
                centred = resid - rowmean(resid)
                inv = lax.rsqrt(rowmean(centred * centred) + EPS)
                unit_ = centred * inv
                u2[r, :] = unit_.astype(BF16)
                inv_o[1, r, :] = jnp.broadcast_to(inv, (tile, 128))
                layer = unit_ * g_second + s_second
                each = span // tile
                s, t = i // each, i % each

                @pl.when(t == 0)
                def _():
                    first_o[pl.ds(pl.multiple_of(s * 8, 8), 8), :] = layer[0:8, :]

                slot = lax.broadcasted_iota(jnp.int32, (tile, width), 0) + t * tile
                outv[r, :] = jnp.where(slot < lengths[s], layer, 0.0).astype(BF16)
                for cp in leaving(i):
                    cp.start()
            hook(CONTRACT + j, i)

        loop(steps, contract)
    hook(NEED_POOL)
    if comm:
        save(wp, wp_h)
    for cp in saved + [cp for i in range(steps) for cp in leaving(i)]:
        cp.wait()
    if comm:
        for n in range(others):
            small(n, f_me).wait_send()

        for n in range(len(units)):
            unit(n).drain()


def forward(plan, tokens, lengths, wqkv, wout, winner, wouter, wpool, small, nz):
    rows, width = tokens.shape
    seqs = lengths.shape[0]
    span = rows // seqs
    nf = nz * 2
    ff = winner.shape[1]
    part = width // nf
    ur = ff // nf // 3
    any_, vm, smem = (pl.BlockSpec(memory_space=m) for m in (pl.ANY, pltpu.VMEM, pltpu.SMEM))
    S = jax.ShapeDtypeStruct
    pairs = HEADS // 2
    weights = [(3, nz, 2, part, width), (1 + ff // width, nz, 2, part, width), (3, nz, 2, ur, width), (1, nz, 2, part, width)]
    outs = [
        (S((rows, width), BF16), any_),
        *[(S(w, BF16), any_) for w in weights],
        (S((16, width), F32), vm),
        (S((8, ff), F32), vm),
        (S((rows, 3 * width), BF16), any_),
        (S((rows, width), BF16), any_),
        (S((seqs * pairs, 8, span), F32), vm),
        (S((rows, width), BF16), any_),
        (S((rows, width), BF16), any_),
        (S((rows, ff), BF16), any_),
        (S((nz, 2, rows // (2 * nz), ff), BF16), any_),
        (S((rows, width), BF16), any_),
        (S((2, rows, 128), F32), vm),
        (S((8 * seqs, width), F32), vm),
    ]
    V = pltpu.VMEM
    D = pltpu.SemaphoreType.DMA
    units = sum(w[0] for w in weights)
    sems = 8 * (units + len(FINE) * (nz - 1))
    scratch = [
        V((rows, width), BF16),
        *[V(w, BF16) for w in weights],
        V((nf, 16, 128), BF16),
        V((rows, 3 * width), BF16),
        V((rows, width), BF16),
        V((rows, width), F32),
        V((rows, width), BF16),
        V((rows, width), BF16),
        V((rows, ff), BF16),
        V((nz, 2, rows // (2 * nz), ff), BF16),
        V((rows, width), BF16),
        V((rows, width), BF16),
        D((2, nz)), D((64,)), D((nf,)), D((nf,)),
        D((sems,)), D((sems,)),
        *[V(v.shape, BF16) for v in small],
    ]
    params = pltpu.CompilerParams(vmem_limit_bytes=60 * 2**20, has_side_effects=True, collective_id=0)
    cost = pl.CostEstimate(flops=2 * rows * width * (4 * width + 2 * ff), bytes_accessed=10**7, transcendentals=0)

    def kernel(*refs):
        n = 7 + len(small)
        forward_kernel(plan, *refs[:7], refs[7:n], *refs[n:])

    return pl.pallas_call(
        kernel, out_shape=[o[0] for o in outs], out_specs=[o[1] for o in outs], in_specs=[any_, smem] + [any_] * (5 + len(small)),
        scratch_shapes=scratch, compiler_params=params, cost_estimate=cost,
    )(tokens, lengths, wqkv, wout, winner, wouter, wpool, *small)


def attend_backward(kv, gctx, lse, lengths, s, hp, span, width, size):
    wide = 2 * size
    pairs = width // wide
    rows = pl.ds(pl.multiple_of(s * span, span), span)

    def cols(p):
        return pl.ds(pl.multiple_of(p * width + hp * wide, wide), wide)

    q, k, v = (kv[rows, cols(p)] for p in range(3))
    g = gctx[rows, cols(0)]
    logs = lse[s * pairs + hp]
    lane = lax.broadcasted_iota(jnp.int32, (span, wide), 1)
    slot = lax.broadcasted_iota(jnp.int32, (span, wide), 0)
    fill = jnp.where(slot < lengths[s], 0.0, NEG).astype(BF16)
    scale = size ** (-0.5)
    factor = scale * LOG2E
    kt = k.T
    gqs, gks, gvs = [], [], []
    for h in range(2):
        mine = lane < size if h == 0 else lane >= size
        other = (1 - h) * size
        qh = jnp.where(mine, q, jnp.where(lane == other, 1.0, 0.0).astype(BF16))
        kh = jnp.where(mine, k, fill)
        vh = jnp.where(mine, v, jnp.zeros_like(v))
        p = jnp.exp2(nt(kh, qh) * factor - logs[h : h + 1, :])
        gvs.append(nn(p.astype(BF16), g))
        gp = nt(vh, g)
        delta = jnp.sum(gp * p, axis=0, keepdims=True)
        gs = (p * (gp - delta)).astype(BF16)
        gks.append(nn(gs, q))
        gqs.append(nn(kt, gs)[h * size : (h + 1) * size, :])
    kv[rows, cols(0)] = (jnp.concatenate(gqs, axis=0).T * scale).astype(BF16)
    kv[rows, cols(1)] = (jnp.where(lane < size, gks[0], gks[1]) * scale).astype(BF16)
    kv[rows, cols(2)] = jnp.where(lane < size, gvs[0], gvs[1]).astype(BF16)


class Spread:
    def __init__(self, buf, send, recv):
        self.buf, self.send, self.recv = buf, send, recv
        self.nz = buf.shape[3]
        self.me = here()

    def copy(self, n, incoming):
        x, c, z, y = self.me
        nz = self.nz
        if n < nz - 1:
            k = n + 1
            peer = (x, c, lax.rem(z + k, nz), y)
            ref = self.buf.at[x, c, y, lax.rem(z + nz - k, nz) if incoming else z]
        elif n == nz - 1:
            peer = (x, c, z, 1 - y)
            ref = self.buf.at[x, c, 1 - y if incoming else y]
        elif n == nz:
            peer = (1 - x, c, z, y)
            ref = self.buf.at[1 - x if incoming else x, c]
        else:
            peer = (x, 1 - c, z, y)
            ref = self.buf.at[:, 1 - c if incoming else c]
        return pltpu.make_async_remote_copy(
            src_ref=ref, dst_ref=ref, send_sem=self.send.at[n], recv_sem=self.recv.at[n], device_id=at(*peer), device_id_type=MESH
        )

    def step(self, j):
        nz = self.nz
        if j == 0:
            for n in range(nz - 1):
                self.copy(n, False).start()
            return
        if j == 1:
            for n in range(nz - 1):
                self.copy(n, True).wait_recv()
        else:
            self.copy(nz + j - 3, True).wait_recv()
        if j < 4:
            self.copy(nz + j - 2, False).start()

    def drain(self):
        for n in range(self.nz + 2):
            self.copy(n, False).wait_send()


class Scatter:
    def __init__(self, g, r, split, out, sems, n, ahead=None, boxes=None):
        self.g, self.split, self.out, self.n, self.ahead = g, split, out, n, ahead
        self.send, self.recv = (e.at[n] for e in sems)
        self.lead, _, rows, cols = g.shape
        self.me = x, c, z, y = here()
        h, r2 = cols // 2, rows // 2
        t, e = pl.ds(h, split), pl.ds(h + split, h - split)
        top, low = pl.ds(0, r2), pl.ds(r2, r2)
        self.r1, self.ry1, self.rx2 = r.at[:, :, :, pl.ds(0, h)], r.at[:, 0, :, t], r.at[:, :, top, e]
        self.ry2 = r.at[:, 0, low, e]
        nz = self.lead
        if ahead is None:
            self.za, self.zb = [[r.at[k, 1, q, w] for k in range(nz - 1)] for q, w in ((pl.ds(0, rows), t), (low, e))]
            self.all_za, self.all_zb = (r.at[pl.ds(0, nz - 1), 1, q, w] for q, w in ((pl.ds(0, rows), t), (low, e)))
            self.xe = r.at[nz - 1, 1, :, t]
        else:
            self.za, self.zb = [[b.at[:, 1, q, w] for b in boxes[: nz - 1]] for q, w in ((pl.ds(0, rows), t), (low, e))]
            self.xe = boxes[nz - 1].at[:, 1, :, t]
        self.all_sems = sems
        self.rows = pl.ds(pl.multiple_of(x * r2, 16), r2)
        self.rows_o = pl.ds(pl.multiple_of((1 - x) * r2, 16), r2)
        self.mine = pl.ds(pl.multiple_of(c * h, 128), h)
        self.theirs = pl.ds(pl.multiple_of((1 - c) * h, 128), h)
        self.a1 = pl.ds(pl.multiple_of(c * h, 128), split)
        self.a2 = pl.ds(pl.multiple_of(c * h + split, 128), h - split)

    def region(self, rows, cols):
        return self.out.at[rows, cols] if self.ahead is None else self.out.at[:, rows, cols]

    def remote(self, src, dst, n, peer, unit=None):
        send, recv = (self.send, self.recv) if unit is None else (e.at[unit] for e in self.all_sems)
        return pltpu.make_async_remote_copy(
            src_ref=src, dst_ref=dst, send_sem=send.at[n], recv_sem=recv.at[n], device_id=at(*peer), device_id_type=MESH
        )

    def copy(self, n):
        x, c, z, y = self.me
        g, nz = self.g, self.lead
        every = slice(None)
        core, xn, yn = (x, 1 - c, z, y), (1 - x, c, z, y), (x, c, z, 1 - y)
        if n == 0:
            return self.remote(g.at[:, :, :, self.theirs], self.r1, n, core)
        if n == 1:
            return self.remote(g.at[:, 1 - y, :, self.a1], self.ry1, n, yn)
        if n == 2:
            return self.remote(g.at[:, :, self.rows_o, self.a2], self.rx2, n, xn)
        if n == 3:
            return self.remote(g.at[:, 1 - y, self.rows, self.a2], self.ry2, n, yn)
        if n < 2 * nz + 2:
            k = (n - 4) % (nz - 1) + 1
            zk = lax.rem(z + k, nz)
            lead = zk if self.ahead is None else every
            rows, cols, to = (every, self.a1, self.za) if n < nz + 3 else (self.rows, self.a2, self.zb)
            return self.remote(g.at[lead, y, rows, cols], to[k - 1], 4 if n < nz + 3 else 5, (x, c, zk, y))
        if n == 2 * nz + 2:
            return self.remote(self.region(every, self.a1), self.xe, 6, xn)
        if n == 2 * nz + 3:
            ref = self.region(self.rows, self.a2)
            return self.remote(ref, ref, 7, xn)
        ref = self.region(every, self.mine)
        return self.remote(ref, ref, 8, core)

    def got(self, n):
        x, c, z, y = self.me
        nz = self.lead
        if 3 < n < 2 * nz + 2 and self.ahead is not None:
            k = (n - 4) % (nz - 1) + 1
            ref = (self.za if n < nz + 3 else self.zb)[k - 1]
            self.remote(ref, ref, 4 if n < nz + 3 else 5, (x, c, lax.rem(z + nz - k, nz), y), k - 1).wait_recv()
        elif n == 2 * nz + 3:
            ref = self.region(self.rows_o, self.a2)
            self.remote(ref, ref, 7, (1 - x, c, z, y)).wait_recv()
        elif n == 2 * nz + 4:
            ref = self.region(slice(None), self.theirs)
            self.remote(ref, ref, 8, (x, 1 - c, z, y)).wait_recv()
        else:
            self.copy(n).wait_recv()

    def all_along(self, first):
        x, c, z, y = self.me
        ref = self.all_za if first == 4 else self.all_zb
        return self.remote(ref, ref, 4 if first == 4 else 5, (x, c, lax.rem(z + 1, self.lead), y))

    def along_z(self, first):
        if self.ahead is None:
            for k in range(1, self.lead):
                self.copy(first + k - 1).start()
        elif self.ahead:
            self.copy(first + self.ahead - 1).start()

    def over_z(self, first, boxes, rows, cols):
        y, z = self.me[3], self.me[2]
        total = (self.g[z, y, rows, cols] if self.ahead is None else self.g[:, y, rows, cols]).astype(F32)
        if self.ahead is None:
            self.all_along(first).wait_recv()
        for k in range(1, self.lead):
            if self.ahead is not None:
                self.got(first + k - 1)
            total += boxes[k - 1][...].astype(F32)
        self.region(rows, cols)[...] = total.astype(BF16)

    def step(self, j):
        g, y, nz = self.g, self.me[3], self.lead
        last = 2 * nz + 2

        def adds(body):
            def step(i, _):
                body(i)
                return 0

            lax.fori_loop(0, nz, step, 0)

        if j == 0:
            self.copy(0).start()
        elif j == 1:
            self.got(0)

            def add(i):
                for yy in range(2):
                    g[i, yy, :, self.mine] = g[i, yy, :, self.mine] + self.r1[i, yy]

            adds(add)
            self.copy(1).start()
            self.copy(2).start()
        elif j == 2:
            self.got(2)

            def add(i):
                for yy in range(2):
                    g[i, yy, self.rows, self.a2] = g[i, yy, self.rows, self.a2] + self.rx2[i, yy]

            adds(add)
            self.copy(3).start()
            self.got(1)

            def add(i):
                g[i, y, :, self.a1] = g[i, y, :, self.a1] + self.ry1[i]

            adds(add)
            self.along_z(4)
        elif j == 3:
            self.got(3)

            def add(i):
                g[i, y, self.rows, self.a2] = g[i, y, self.rows, self.a2] + self.ry2[i]

            adds(add)
            self.along_z(nz + 3)
        elif j == 4:
            self.over_z(4, self.za, slice(None), self.a1)
            self.copy(last).start()
        elif j == 5:
            self.over_z(nz + 3, self.zb, self.rows, self.a2)
            self.copy(last + 1).start()
        elif j == 6:
            self.copy(last).wait_send()
            self.got(last)
            ref = self.region(slice(None), self.a1)
            ref[...] = ref[...] + self.xe[...]
            self.got(last + 1)
            self.copy(last + 2).start()
        else:
            self.got(last + 2)

    def drain(self):
        nz = self.lead
        for n in range(4):
            self.copy(n).wait_send()
        if self.ahead is None:
            self.all_along(4).wait_send()
            self.all_along(nz + 3).wait_send()
        elif self.ahead:
            self.copy(3 + self.ahead).wait_send()
            self.copy(nz + 2 + self.ahead).wait_send()
        if not self.ahead:
            self.copy(2 * nz + 3).wait_send()
            self.copy(2 * nz + 4).wait_send()


def backward_kernel(plan, lengths, labels, vec, lse, first, inv_h, cot_h, tok_h, w1_h, w2_h, wu_h, wp_h, qkv_h, ctx_h, hid_h, u1_h, act_h, dg_h, u2_h,
                    loss_o, own_o, ib_o, pool_o, class_o, wo_o, wi_o, wu_o, wq_o, tg_h,
                    A, D, w2, w3, cot, u2, u1, hid, gffn, gr, inv, acc, gfirst,
                    G, R, early, late, loc, free, s_rs, r_rs, s_sp, r_sp):
    comm = plan is not None
    x, c, z, y = here() if comm else (0, 0, 0, 0)
    rows, width = cot.shape
    seqs = lengths.shape[0]
    span = rows // seqs
    ff = A.shape[1]
    size = width // HEADS
    nz = D.shape[0]
    tile = rows // nz
    nb = ff // width
    part = width // (2 * nz)
    fr = ff // (2 * nz)
    ur = wu_h.shape[3]
    groups = w1_h.shape[0]
    loads = {}

    def load(name, src, dst):
        cp = pltpu.make_async_copy(src, dst, loc.at[len(loads)])
        cp.start()
        loads[name] = cp

    load("wp", wp_h.at[0], w3.at[:, :, pl.ds(fr, part), :])
    load("cot", cot_h, cot)
    load("u2", u2_h, u2)
    load("inv2", inv_h.at[1], inv)

    if comm:
        barrier = pltpu.get_barrier_semaphore()
        peers = [(x, c, lax.rem(z + k, nz), y) for k in range(1, nz)]
        peers += [(x, c, z, 1 - y), (1 - x, c, z, y), (x, 1 - c, z, y)]
        for p in peers:
            pl.semaphore_signal(barrier, inc=1, device_id=at(*p), device_id_type=MESH)

        def scatter(n):
            sems = (s_rs, r_rs)
            split = SPLIT[n]
            if n < nz:
                return Scatter(G.at[n], R.at[n], split, wu_o, sems, n, (n + 1) % nz, [R.at[k] for k in range(nz)])
            if n < nz + nb:
                b = n - nz
                return Scatter(G.at[n], R.at[n], split, wi_o.at[:, pl.ds(b * width, width)], sems, n)
            q = n - nz - nb
            return Scatter(D.at[:, :, pl.ds(0, part), pl.ds(q * width, width)], w2.at[q], split, wo_o if q == 0 else wq_o.at[q - 1], sems, n)

        blocks = nz + nb + 1 + groups
        small = [Spread(early, s_sp.at[0], r_sp.at[0]), Spread(late, s_sp.at[1], r_sp.at[1])]

        def hook(name, i=None):
            if i is None:
                for n, j in plan.get(name, ()):
                    if n < blocks:
                        scatter(n).step(j)
                    elif n < blocks + 2:
                        small[n - blocks].step(j)
                    else:
                        scatter(nz - 1).step(j)
                return
            if isinstance(i, int):
                hook((name, i))
                return
            for k in range(8):
                if (name, k) in plan:
                    pl.when(i == k)(functools.partial(hook, (name, k)))
    else:
        def hook(name, i=None):
            pass

    acc[...] = jnp.zeros_like(acc)

    loads["wp"].wait()
    load("act", act_h, A)
    gain2, gain1 = vec[6:7, :], vec[3:4, :]

    def colsum(v):
        return jnp.sum(v, axis=0, keepdims=True)

    per = span // tile
    steps = rows // tile

    def second_norm(i, _):
        r = pl.ds(pl.multiple_of(i * tile, tile), tile)
        s, j = i // per, i % per
        slot = lax.broadcasted_iota(jnp.int32, (tile, width), 0) + j * tile
        gl = jnp.where(slot < lengths[s], cot[r, :].astype(F32), 0.0)
        head = gfirst[pl.ds(pl.multiple_of(8 * s, 8), 8), :] * jnp.where(j == 0, 1.0, 0.0)
        gl = gl + jnp.concatenate([head, jnp.zeros((tile - 8, width), F32)], axis=0)
        u = u2[r, :].astype(F32)
        a = gl * gain2
        g2 = (a - rowmean(a) - u * rowmean(a * u)) * inv[r, :][:, :1]
        gr[r, :] = g2
        low = g2.astype(BF16)
        gffn[r, :] = low
        tally(3, [(colsum(low.astype(F32)), colsum(gl * u), colsum(gl))])
        return 0

    def tally(first_row, parts):
        for n in range(len(parts[0])):
            acc[first_row + n : first_row + n + 1, :] += sum(p[n] for p in parts[1:]) + parts[0][n]

    lane = lax.broadcasted_iota(jnp.int32, (8 * seqs, 128), 1)
    row = lax.broadcasted_iota(jnp.int32, (8 * seqs, 128), 0)
    live = (lane >= 1) & (lane < 4)
    w_pool = w3[:, :, fr:, :].reshape(width, width)
    first_low = first[...].astype(BF16)
    pooled = jnp.tanh(nn(first_low, w_pool) + vec[8:9, :])
    pooled_low = pooled.astype(BF16)
    heads = jnp.concatenate([vec[8:16, :], jnp.zeros((120, width), F32)], axis=0).astype(BF16)
    logits = nt(pooled_low, heads) + vec[15:16, :128]
    peak = jnp.max(jnp.where(live, logits, -3.0e38), axis=-1, keepdims=True)
    mass = jnp.where(live, jnp.exp(logits - peak), 0.0)
    logsum = peak + jnp.log(jnp.sum(mass, axis=-1, keepdims=True))
    label = jnp.full((8 * seqs, 128), labels[0])
    for s in range(1, seqs):
        label = jnp.where(row >= 8 * s, labels[s], label)
    onehot = jnp.where(lane == label + 1, 1.0, 0.0)
    loss_o[...] = jnp.broadcast_to(logsum - jnp.sum(onehot * logits, axis=-1, keepdims=True), loss_o.shape)
    g_logits = jnp.where(live & (row % 8 == 0), jnp.exp(logits - logsum) - onehot, 0.0).astype(BF16)
    g_pre = (nn(g_logits, heads) * (1.0 - pooled * pooled)).astype(BF16)
    g_first = nt(g_pre, w_pool)

    gfirst[...] = g_first
    for name in ("cot", "u2", "inv2"):
        loads[name].wait()
    lax.fori_loop(0, steps, second_norm, 0)
    load("tok", tok_h, u2)
    load("inv1", inv_h.at[0], inv)

    loads["act"].wait()
    for j in range(fr // ur):
        load(("wu", j), wu_h.at[j], w3.at[:, :, pl.ds(j * ur, ur), :])
    load("dg", dg_h, D)
    load("hid", hid_h, hid)
    if comm:
        pl.semaphore_wait(barrier, len(peers))

    def outer_grad(k, _):
        owner = lax.rem(z + k + 1, nz)
        for yy in range(2):
            f = owner * 2 + yy
            got = tn(A[:, pl.ds(pl.multiple_of(f * fr, 128), fr)], gffn[...]).astype(BF16)
            G[k, :, yy] = got.reshape(nb, part, width)
        hook(OUTER_GRAD, k)
        return 0

    lax.fori_loop(0, nz, outer_grad, 0)
    load("qkv", qkv_h, A.at[:, pl.ds(0, 3 * width)])
    load("ctx", ctx_h, A.at[:, pl.ds(3 * width, width)])
    for j in range(fr // ur):
        loads[("wu", j)].wait()
    loads["dg"].wait()
    load("w2", w2_h, w2)
    load("u1", u1_h, u1)

    def inner_back(i, _):
        r = pl.ds(pl.multiple_of(i * tile, tile), tile)
        for b in range(nb):
            cols = slice(b * width, (b + 1) * width)
            w = w3[b, :, :fr, :].reshape(width, width)
            g = nt(gffn[r, :], w) * D[i, :, :, cols].reshape(tile, width).astype(F32)
            low = g.astype(BF16)
            D[i, :, :, cols] = low.reshape(2, tile // 2, width)
            acc[6 + b : 7 + b, :] += colsum(low.astype(F32))
        hook(INNER_BACK, i)
        return 0

    lax.fori_loop(0, rows // tile, inner_back, 0)
    for g in range(groups):
        load(("w1", g), w1_h.at[g], w3.at[:, :, pl.ds(g * part, part), :])

    loads["hid"].wait()

    def inner_grad(b, _):
        cols = pl.ds(pl.multiple_of(b * width, width), width)
        for m in range(2):
            h = width // 2
            got = tn(hid[:, m * h : (m + 1) * h], D[:, :, :, cols].reshape(rows, width)).astype(BF16)
            G[nz + b, m * nz // 2 : (m + 1) * nz // 2] = got.reshape(nz // 2, 2, part, width)
        hook(INNER_GRAD, b)
        return 0

    lax.fori_loop(0, nb, inner_grad, 0)

    loads["w2"].wait()
    loads["u1"].wait()
    loads["inv1"].wait()

    def hidden_grad(i):
        r = slice(i * tile, (i + 1) * tile)
        gh = gr[r, :]
        for b in range(nb):
            gh += nt(D[i, :, :, b * width : (b + 1) * width].reshape(tile, width), w2[b + 1].reshape(width, width))
        return gh

    def first_norm(i, gh):
        r = slice(i * tile, (i + 1) * tile)
        u = u1[r, :].astype(F32)
        a = gh * gain1
        g1 = (a - rowmean(a) - u * rowmean(a * u)) * inv[r, :][:, :1]
        low = g1.astype(BF16)
        cot[r, :] = low
        tally(0, [(colsum(low.astype(F32)), colsum(gh * u), colsum(gh))])
        gffn[r, :] = nt(low, w2[0].reshape(width, width)).astype(BF16)
        gr[r, :] = g1

    for i in range(steps + 1):
        if i < steps:
            ahead = hidden_grad(i)
        if i:
            first_norm(i - 1, behind)
        if i < steps:
            gr[i * tile : (i + 1) * tile, :] = ahead
            behind = gr[i * tile : (i + 1) * tile, :]
        hook(FIRST_NORM, i)
    if comm:
        for p in peers:
            pl.semaphore_signal(free, inc=1, device_id=at(*p), device_id_type=MESH)
        pay = jnp.concatenate(
            [acc[0:10, :]]
            + [first_low[8 * s : 8 * s + 1, :].astype(F32) for s in range(seqs)]
            + [g_pre[8 * s : 8 * s + 1, :].astype(F32) for s in range(seqs)]
            + [pooled_low[8 * s : 8 * s + 1, :].astype(F32) for s in range(seqs)],
            axis=0,
        )
        early[x, c, y, z] = pay.astype(BF16)

    loads["ctx"].wait()
    loads["qkv"].wait()
    for m in range(2):
        h = width // 2
        got = tn(A[:, 3 * width + m * h : 3 * width + (m + 1) * h], cot[...]).astype(BF16)
        D[m * nz // 2 : (m + 1) * nz // 2, :, :part, :width] = got.reshape(nz // 2, 2, part, width)
    if comm:
        pl.semaphore_wait(free, len(peers))
    hook(OUT_GRAD)

    loads["tok"].wait()
    pairs = HEADS // 2
    gp = pairs // groups
    wide = gp * 2 * size
    def finish_late():
        late_rows = [acc[10 + n : 11 + n, j * 128 : (j + 1) * 128] for n in range(2) for j in range(width // 128)]
        late_rows += [g_logits[8 * s : 8 * s + 1, :].astype(F32) for s in range(seqs)]
        late_rows.append(jnp.zeros((16 - len(late_rows), 128), F32))
        late[x, c, y, z] = jnp.concatenate(late_rows, axis=0).astype(BF16)

    for q in range(groups):
        def attention(i, _):
            attend_backward(A, gffn, lse, lengths, i // gp, q * gp + i % gp, span, width, size)
            hook(ATTEND_BACK + q, i)
            return 0

        lax.fori_loop(0, seqs * gp, attention, 0)
        for p in range(3):
            block_of = A[:, p * width + q * wide : p * width + (q + 1) * wide]
            got = tn(u2[...], block_of).astype(BF16)
            D[:, :, :part, (q + 1) * width + p * wide : (q + 1) * width + (p + 1) * wide] = got.reshape(nz, 2, part, wide)
            if p != 1:
                acc[10 + p // 2 : 11 + p // 2, q * wide : (q + 1) * wide] = colsum(block_of.astype(F32))
        if comm and q == groups - 1:
            finish_late()
        hook(QKV_GRAD + q)
    for g in range(groups):
        loads[("w1", g)].wait()

    def input_grad(i, _):
        r = pl.ds(pl.multiple_of(i * tile, tile), tile)
        total = gr[r, :]
        for g in range(groups):
            w = w3[:, :, g * part : (g + 1) * part, :].reshape(width, width)
            mine = jnp.concatenate([A[r, p * width + g * wide : p * width + (g + 1) * wide] for p in range(3)], axis=1)
            total += nt(mine, w)
        cot[r, :] = total.astype(BF16)
        hook(INPUT_GRAD, i)
        return 0

    lax.fori_loop(0, rows // tile, input_grad, 0)
    back = pltpu.make_async_copy(cot, tg_h, loc.at[len(loads)])
    back.start()
    hook(SMALL_SUMS)
    if comm:
        n = 4 * 2 * nz
        def slot_of(i):
            return (i // (4 * nz), i // (2 * nz) % 2, i // nz % 2, i % nz)

        total = lax.fori_loop(0, n, lambda i, t: t + early[slot_of(i)].astype(F32), jnp.zeros((16, width), F32))
        lates = late[...].reshape(n, 16, 128)
        lsum = jnp.sum(lates.astype(F32), axis=0)
        six = width // 128
        qb = jnp.concatenate([lsum[j : j + 1, :] for j in range(six)], axis=1)
        vb = jnp.concatenate([lsum[six + j : six + j + 1, :] for j in range(six)], axis=1)
        r16 = lax.broadcasted_iota(jnp.int32, (16, width), 0)
        total = jnp.where(r16 == 10, qb, jnp.where(r16 == 11, vb, total))
        f = z * 2 + y
        src = lax.broadcasted_iota(jnp.int32, (width, 128), 0)
        dst = lax.broadcasted_iota(jnp.int32, (width, 128), 1)
        pick = jnp.where((src == dst + f * part) & (dst < part), 1.0, 0.0).astype(BF16)
        src = lax.broadcasted_iota(jnp.int32, (width, fr), 0)
        dst = lax.broadcasted_iota(jnp.int32, (width, fr), 1)
        pick_ff = jnp.where(src == dst + y * fr, 1.0, 0.0).astype(BF16)
        high = total.astype(BF16)
        rest = (total - high.astype(F32)).astype(BF16)
        own = nn(high, pick) + nn(rest, pick)
        wide_own = nn(high, pick_ff) + nn(rest, pick_ff)
        r16f = lax.broadcasted_iota(jnp.int32, (16, fr), 0)
        ib_o[...] = jnp.broadcast_to(colsum(jnp.where(r16f == 6 + z, wide_own, 0.0)), ib_o.shape)
        flat = early[...].reshape(n * 16, width)
        chosen = nn(flat, pick)
        rid = lax.broadcasted_iota(jnp.int32, (n * 16, 128), 0) % 16
        firsts = pltpu.roll(jnp.where((rid >= 10) & (rid < 10 + seqs), chosen, 0.0), seqs, 0).astype(BF16)
        pool_o[...] = tn(firsts, flat)
        pooleds = pltpu.roll(jnp.where(rid >= 10 + 2 * seqs, chosen, 0.0), n * 16 - seqs, 0).astype(BF16)
        class_o[...] = tn(lates.reshape(n * 16, 128), pooleds)
        middle = (rid >= 10 + seqs) & (rid < 10 + 2 * seqs)
        pb = colsum(jnp.where(middle, chosen, 0.0))
        cbg = colsum(jnp.where(middle, lates.reshape(n * 16, 128).astype(F32), 0.0))
        r16s = lax.broadcasted_iota(jnp.int32, (16, 128), 0)
        own_o[...] = jnp.where(r16s == 12, pb, jnp.where(r16s == 13, cbg, own))
        hook(LAST)
        for spread in small:
            spread.drain()
        for n in range(blocks):
            scatter(n).drain()
    back.wait()


def backward(plan, lengths, labels, vec, lse, inv, first, cot, tok, w1, w2, wu, wp, qkv, ctx, hid, u1, act, dg, u2):
    rows, width = cot.shape
    nz = w1.shape[1]
    ff = act.shape[1]
    part = width // (2 * nz)
    fr = ff // (2 * nz)
    nb = ff // width
    seqs = lengths.shape[0]
    any_, vm, smem = (pl.BlockSpec(memory_space=m) for m in (pl.ANY, pltpu.VMEM, pltpu.SMEM))
    S = jax.ShapeDtypeStruct
    outs = [
        (S((8 * seqs, 128), F32), vm),
        (S((16, 128), F32), vm),
        (S((8, fr), F32), vm),
        (S((128, width), F32), vm),
        (S((128, 128), F32), vm),
        (S((part, width), BF16), vm),
        (S((part, ff), BF16), vm),
        (S((nb, part, width), BF16), vm),
        (S((3, part, width), BF16), vm),
        (S((rows, width), BF16), any_),
    ]
    V = pltpu.VMEM
    D = pltpu.SemaphoreType.DMA
    n = 2 * nb
    scratch = [
        V((rows, ff), BF16),
        V(dg.shape, BF16),
        V((1 + nb, nz, 2, part, width), BF16),
        V((nz, 2, fr + part, width), BF16),
        V((rows, width), BF16),
        V((rows, width), BF16),
        V((rows, width), BF16),
        V((rows, width), BF16),
        V((rows, width), BF16),
        V((rows, width), F32),
        V((rows, 128), F32),
        V((16, width), F32),
        V((8 * seqs, width), F32),
        V((n, nz, 2, part, width), BF16),
        V((n, nz, 2, part, width), BF16),
        V((2, 2, 2, nz, 16, width), BF16),
        V((2, 2, 2, nz, 16, 128), BF16),
        D((24,)),
        pltpu.SemaphoreType.REGULAR,
        D((n + 4, 9)), D((n + 4, 9)), D((2, nz + 2)), D((2, nz + 2)),
    ]
    params = pltpu.CompilerParams(vmem_limit_bytes=63 * 2**20, has_side_effects=True, **({"collective_id": 1} if plan is not None else {}))
    cost = pl.CostEstimate(flops=4 * rows * width * (4 * width + 2 * ff), bytes_accessed=10**7, transcendentals=0)
    return pl.pallas_call(
        functools.partial(backward_kernel, plan), out_shape=[o[0] for o in outs], out_specs=[o[1] for o in outs],
        in_specs=[smem, smem] + [vm] * 3 + [any_] * 14, scratch_shapes=scratch, compiler_params=params, cost_estimate=cost,
    )(lengths, labels, vec, lse, first, inv, cot, tok, w1, w2, wu, wp, qkv, ctx, hid, u1, act, dg, u2)


def finish_kernel(output, tg, loss, own, ibg, poolg, classg, wo, wi, wu, wq,
                  output_o, loss_o, tg_o, qkv_o, qb_o, vb_o, wo_o, ob_o, g1_o, s1_o, wi_o, ib_o, wu_o, outb_o, g2_o, s2_o, pool_o, pb_o, class_o, cb_o):
    output_o[...] = output[...]
    tg_o[...] = tg[...]
    part, width = wo.shape
    groups, _, wide3 = wq.shape
    wide = wide3 // groups
    for p in range(3):
        for g in range(groups):
            qkv_o[:, p * width + g * wide : p * width + (g + 1) * wide] = wq[g, :, p * wide : (p + 1) * wide].astype(F32)
    wo_o[...] = wo[...].astype(F32)
    wi_o[...] = wi[...].astype(F32)
    wu_o[...] = wu[...].reshape(wu_o.shape).astype(F32)
    pool_o[...] = poolg[:part, :]
    for n, ref in ((10, qb_o), (11, vb_o), (0, ob_o), (1, g1_o), (2, s1_o), (3, outb_o), (4, g2_o), (5, s2_o), (12, pb_o)):
        ref[...] = own[n, :part]
    ib_o[...] = ibg[0, :]
    classes = cb_o.shape[0]
    cb_o[...] = own[13, 1 : 1 + classes]
    class_o[...] = classg[1 : 1 + classes, :part]
    for s in range(loss_o.shape[0]):
        loss_o[s : s + 1] = loss[8 * s, 0:1]


def finish(output, tg, loss, own, ibg, poolg, classg, wo, wi, wu, wq, classes):
    part, width = wo.shape
    ff = wi.shape[1]
    S = jax.ShapeDtypeStruct
    any_, vm = (pl.BlockSpec(memory_space=m) for m in (pl.ANY, pltpu.VMEM))
    vector = S((part,), F32)
    outs = [S(output.shape, BF16), S((loss.shape[0] // 8,), F32), S(tg.shape, BF16), S((part, 3 * width), F32), vector, vector,
            S((part, width), F32), vector, vector, vector, S((part, ff), F32), S((ibg.shape[1],), F32), S((wu.shape[0] * part, width), F32),
            vector, vector, vector, S((part, width), F32), vector, S((classes, part), F32), S((classes,), F32)]
    *done, classes_t, class_b = pl.pallas_call(
        finish_kernel, out_shape=outs, in_specs=[vm] * 11, out_specs=[vm] * 20,
        compiler_params=pltpu.CompilerParams(vmem_limit_bytes=62 * 2**20),
    )(output, tg, loss, own, ibg, poolg, classg, wo, wi, wu, wq)
    return (*done, classes_t.T, class_b)


def normalize(value, gain, shift):
    mean = jnp.mean(value, axis=-1, keepdims=True)
    centred = value - mean
    inverse = lax.rsqrt(jnp.mean(centred * centred, axis=-1, keepdims=True) + EPS)
    unit = centred * inverse
    return (unit * gain + shift, unit, inverse)


def norm_back(grad, unit, inverse, gain):
    scaled = grad * gain
    inner = (
        scaled
        - jnp.mean(scaled, axis=-1, keepdims=True)
        - unit * jnp.mean(scaled * unit, axis=-1, keepdims=True)
    )
    return (inner * inverse, jnp.sum(grad * unit, axis=0), jnp.sum(grad, axis=0))


def matmul(left, right):
    return jnp.dot(left, right, preferred_element_type=jnp.float32)


def transposed_left(left, right):
    return lax.dot_general(
        left, right, (((0,), (0,)), ((), ())), preferred_element_type=jnp.float32
    )


def transposed_right(left, right):
    return lax.dot_general(
        left, right, (((1,), (1,)), ((), ())), preferred_element_type=jnp.float32
    )


def column_sum(values):
    return jnp.sum(values.astype(jnp.float32), axis=0)


def attend(block):
    query, key, value, keep = block
    scale = query.shape[-1] ** (-0.5)
    scores = jnp.einsum("qhd,khd->hqk", query, key, preferred_element_type=jnp.float32) * scale
    scores = jnp.where(keep[None, None, :], scores, NEG)
    top = jnp.max(scores, axis=-1, keepdims=True)
    total = jnp.sum(jnp.exp(scores - top), axis=-1, keepdims=True)
    logsum = top + jnp.log(total)
    probs = jnp.exp(scores - logsum).astype(jnp.bfloat16)
    context = jnp.einsum("hqk,khd->qhd", probs, value, preferred_element_type=jnp.float32)
    return (context.astype(jnp.bfloat16), logsum[:, :, 0])


def attend_back(block):
    query, key, value, keep, logsum, grad_context = block
    scale = query.shape[-1] ** (-0.5)
    scores = jnp.einsum("qhd,khd->hqk", query, key, preferred_element_type=jnp.float32) * scale
    scores = jnp.where(keep[None, None, :], scores, NEG)
    probs = jnp.exp(scores - logsum[:, :, None])
    grad_value = jnp.einsum(
        "hqk,qhd->khd", probs.astype(jnp.bfloat16), grad_context, preferred_element_type=jnp.float32
    )
    grad_probs = jnp.einsum("qhd,khd->hqk", grad_context, value, preferred_element_type=jnp.float32)
    delta = jnp.sum(grad_probs * probs, axis=-1, keepdims=True)
    grad_scores = (probs * (grad_probs - delta)).astype(jnp.bfloat16)
    grad_query = (
        jnp.einsum("hqk,khd->qhd", grad_scores, key, preferred_element_type=jnp.float32) * scale
    )
    grad_key = (
        jnp.einsum("hqk,qhd->khd", grad_scores, query, preferred_element_type=jnp.float32) * scale
    )
    return (
        grad_query.astype(jnp.bfloat16),
        grad_key.astype(jnp.bfloat16),
        grad_value.astype(jnp.bfloat16),
    )


def per_device_any(
    tokens,
    lengths,
    labels,
    cotangent,
    qkv_weight,
    query_bias,
    value_bias,
    out_weight,
    out_bias,
    first_gain,
    first_shift,
    inner_weight,
    inner_bias,
    outer_weight,
    outer_bias,
    second_gain,
    second_shift,
    pool_weight,
    pool_bias,
    class_weight,
    class_bias,
):
    full = (
        lax.all_gather(qkv_weight, FSDP, axis=0, tiled=True),
        lax.all_gather(query_bias, FSDP, axis=0, tiled=True),
        lax.all_gather(value_bias, FSDP, axis=0, tiled=True),
        lax.all_gather(out_weight, FSDP, axis=0, tiled=True),
        lax.all_gather(out_bias, FSDP, axis=0, tiled=True),
        lax.all_gather(first_gain, FSDP, axis=0, tiled=True),
        lax.all_gather(first_shift, FSDP, axis=0, tiled=True),
        lax.all_gather(inner_weight, FSDP, axis=0, tiled=True),
        lax.all_gather(inner_bias, FSDP, axis=0, tiled=True),
        lax.all_gather(outer_weight, FSDP, axis=0, tiled=True),
        lax.all_gather(outer_bias, FSDP, axis=0, tiled=True),
        lax.all_gather(second_gain, FSDP, axis=0, tiled=True),
        lax.all_gather(second_shift, FSDP, axis=0, tiled=True),
        lax.all_gather(pool_weight, FSDP, axis=0, tiled=True),
        lax.all_gather(pool_bias, FSDP, axis=0, tiled=True),
        lax.all_gather(class_weight, FSDP, axis=0, tiled=True),
    )
    (
        w_qkv,
        b_query,
        b_value,
        w_out,
        b_out,
        g_first,
        s_first,
        w_inner,
        b_inner,
        w_outer,
        b_outer,
        g_second,
        s_second,
        w_pool,
        b_pool,
        w_class,
    ) = full
    b_query = b_query.astype(jnp.float32)
    b_value = b_value.astype(jnp.float32)
    b_out = b_out.astype(jnp.float32)
    g_first = g_first.astype(jnp.float32)
    s_first = s_first.astype(jnp.float32)
    b_inner = b_inner.astype(jnp.float32)
    b_outer = b_outer.astype(jnp.float32)
    g_second = g_second.astype(jnp.float32)
    s_second = s_second.astype(jnp.float32)
    b_pool = b_pool.astype(jnp.float32)
    b_class = class_bias.astype(jnp.float32)
    seqs = lengths.shape[0]
    rows, width = tokens.shape
    span = rows // seqs
    size = width // HEADS
    classes = class_bias.shape[0]
    position = lax.broadcasted_iota(jnp.int32, (seqs, span), 1)
    keep = position < lengths[:, None]
    valid = keep.reshape(rows, 1).astype(jnp.float32)
    bias_all = jnp.concatenate([b_query, jnp.zeros_like(b_query), b_value])
    qkv = (matmul(tokens, w_qkv) + bias_all).astype(jnp.bfloat16)
    query = qkv[:, :width].reshape(seqs, span, HEADS, size)
    key = qkv[:, width : 2 * width].reshape(seqs, span, HEADS, size)
    value = qkv[:, 2 * width :].reshape(seqs, span, HEADS, size)
    context, logsum = lax.map(attend, (query, key, value, keep))
    context = context.reshape(rows, width)
    attended = matmul(context, w_out) + b_out
    hidden, unit_first, inverse_first = normalize(
        tokens.astype(jnp.float32) + attended, g_first, s_first
    )
    hidden_low = hidden.astype(jnp.bfloat16)
    inner = matmul(hidden_low, w_inner) + b_inner
    act = jax.nn.gelu(inner, approximate=False).astype(jnp.bfloat16)
    ffn = matmul(act, w_outer) + b_outer
    layer, unit_second, inverse_second = normalize(hidden + ffn, g_second, s_second)
    output = (layer * valid).astype(jnp.bfloat16)
    first = layer.reshape(seqs, span, width)[:, 0].astype(jnp.bfloat16)
    pooled = jnp.tanh(matmul(first, w_pool) + b_pool)
    pooled_low = pooled.astype(jnp.bfloat16)
    logits = matmul(pooled_low, w_class) + b_class
    peak = jnp.max(logits, axis=-1, keepdims=True)
    logsum_class = peak + jnp.log(jnp.sum(jnp.exp(logits - peak), axis=-1, keepdims=True))
    onehot = (labels[:, None] == lax.broadcasted_iota(jnp.int32, (seqs, classes), 1)).astype(
        jnp.float32
    )
    exit_loss = logsum_class[:, 0] - jnp.sum(onehot * logits, axis=-1)
    again = (
        lax.all_gather(qkv_weight, FSDP, axis=0, tiled=True),
        lax.all_gather(query_bias, FSDP, axis=0, tiled=True),
        lax.all_gather(value_bias, FSDP, axis=0, tiled=True),
        lax.all_gather(out_weight, FSDP, axis=0, tiled=True),
        lax.all_gather(out_bias, FSDP, axis=0, tiled=True),
        lax.all_gather(first_gain, FSDP, axis=0, tiled=True),
        lax.all_gather(first_shift, FSDP, axis=0, tiled=True),
        lax.all_gather(inner_weight, FSDP, axis=0, tiled=True),
        lax.all_gather(inner_bias, FSDP, axis=0, tiled=True),
        lax.all_gather(outer_weight, FSDP, axis=0, tiled=True),
        lax.all_gather(outer_bias, FSDP, axis=0, tiled=True),
        lax.all_gather(second_gain, FSDP, axis=0, tiled=True),
        lax.all_gather(second_shift, FSDP, axis=0, tiled=True),
        lax.all_gather(pool_weight, FSDP, axis=0, tiled=True),
        lax.all_gather(pool_bias, FSDP, axis=0, tiled=True),
        lax.all_gather(class_weight, FSDP, axis=0, tiled=True),
    )
    w_qkv = again[0]
    w_out = again[3]
    g_first = again[5].astype(jnp.float32)
    w_inner = again[7]
    w_outer = again[9]
    g_second = again[11].astype(jnp.float32)
    w_pool = again[13]
    w_class = again[15]
    grad_logits = (jnp.exp(logits - logsum_class) - onehot).astype(jnp.bfloat16)
    grad_class_weight = transposed_left(pooled_low, grad_logits)
    grad_class_local = column_sum(grad_logits)
    grad_pooled = transposed_right(grad_logits, w_class)
    grad_pre = (grad_pooled * (1.0 - pooled * pooled)).astype(jnp.bfloat16)
    grad_pool_weight = transposed_left(first, grad_pre)
    grad_pool_bias = column_sum(grad_pre)
    grad_first = transposed_right(grad_pre, w_pool)
    grad_layer = (cotangent.astype(jnp.float32) * valid).reshape(seqs, span, width)
    grad_layer = jnp.concatenate(
        [grad_layer[:, :1] + grad_first[:, None, :], grad_layer[:, 1:]], axis=1
    )
    grad_layer = grad_layer.reshape(rows, width)
    grad_resid_second, grad_second_gain, grad_second_shift = norm_back(
        grad_layer, unit_second, inverse_second, g_second
    )
    grad_ffn = grad_resid_second.astype(jnp.bfloat16)
    grad_outer_weight = transposed_left(act, grad_ffn)
    grad_outer_bias = column_sum(grad_ffn)
    grad_act = transposed_right(grad_ffn, w_outer)
    gelu_value, gelu_pull = jax.vjp(lambda v: jax.nn.gelu(v, approximate=False), inner)
    grad_inner = gelu_pull(grad_act)[0].astype(jnp.bfloat16)
    grad_inner_weight = transposed_left(hidden_low, grad_inner)
    grad_inner_bias = column_sum(grad_inner)
    grad_hidden = grad_resid_second + transposed_right(grad_inner, w_inner)
    grad_resid_first, grad_first_gain, grad_first_shift = norm_back(
        grad_hidden, unit_first, inverse_first, g_first
    )
    grad_attended = grad_resid_first.astype(jnp.bfloat16)
    grad_out_weight = transposed_left(context, grad_attended)
    grad_out_bias = column_sum(grad_attended)
    grad_context = (
        transposed_right(grad_attended, w_out).astype(jnp.bfloat16).reshape(seqs, span, HEADS, size)
    )
    grad_query, grad_key, grad_value = lax.map(
        attend_back, (query, key, value, keep, logsum, grad_context)
    )
    grad_query = grad_query.reshape(rows, width)
    grad_key = grad_key.reshape(rows, width)
    grad_value = grad_value.reshape(rows, width)
    grad_qkv = jnp.concatenate([grad_query, grad_key, grad_value], axis=1)
    grad_qkv_weight = transposed_left(tokens, grad_qkv)
    grad_query_bias = column_sum(grad_query)
    grad_value_bias = column_sum(grad_value)
    tokens_grad = (grad_resid_first + transposed_right(grad_qkv, w_qkv)).astype(jnp.bfloat16)
    owned = (
        lax.psum_scatter(grad_qkv_weight, FSDP, scatter_dimension=0, tiled=True),
        lax.psum_scatter(grad_query_bias, FSDP, scatter_dimension=0, tiled=True),
        lax.psum_scatter(grad_value_bias, FSDP, scatter_dimension=0, tiled=True),
        lax.psum_scatter(grad_out_weight, FSDP, scatter_dimension=0, tiled=True),
        lax.psum_scatter(grad_out_bias, FSDP, scatter_dimension=0, tiled=True),
        lax.psum_scatter(grad_first_gain, FSDP, scatter_dimension=0, tiled=True),
        lax.psum_scatter(grad_first_shift, FSDP, scatter_dimension=0, tiled=True),
        lax.psum_scatter(grad_inner_weight, FSDP, scatter_dimension=0, tiled=True),
        lax.psum_scatter(grad_inner_bias, FSDP, scatter_dimension=0, tiled=True),
        lax.psum_scatter(grad_outer_weight, FSDP, scatter_dimension=0, tiled=True),
        lax.psum_scatter(grad_outer_bias, FSDP, scatter_dimension=0, tiled=True),
        lax.psum_scatter(grad_second_gain, FSDP, scatter_dimension=0, tiled=True),
        lax.psum_scatter(grad_second_shift, FSDP, scatter_dimension=0, tiled=True),
        lax.psum_scatter(grad_pool_weight, FSDP, scatter_dimension=0, tiled=True),
        lax.psum_scatter(grad_pool_bias, FSDP, scatter_dimension=0, tiled=True),
        lax.psum_scatter(grad_class_weight, FSDP, scatter_dimension=0, tiled=True),
    )
    summed = lax.psum(
        (
            owned[0],
            owned[1],
            owned[2],
            owned[3],
            owned[4],
            owned[5],
            owned[6],
            owned[7],
            owned[8],
            owned[9],
            owned[10],
            owned[11],
            owned[12],
            owned[13],
            owned[14],
            owned[15],
        ),
        DP,
    )
    class_bias_grad = lax.psum(grad_class_local, (DP, FSDP))
    return (
        output,
        exit_loss,
        tokens_grad,
        summed[0],
        summed[1],
        summed[2],
        summed[3],
        summed[4],
        summed[5],
        summed[6],
        summed[7],
        summed[8],
        summed[9],
        summed[10],
        summed[11],
        summed[12],
        summed[13],
        summed[14],
        summed[15],
        class_bias_grad,
    )


def per_device(nz, tokens, lengths, labels, cotangent, qkv_weight, query_bias, value_bias, out_weight, out_bias,
    first_gain, first_shift, inner_weight, inner_bias, outer_weight, outer_bias, second_gain, second_shift,
    pool_weight, pool_bias, class_weight, class_bias):
    classes = class_bias.shape[0]
    small = [query_bias, value_bias, out_bias, first_gain, first_shift, outer_bias, second_gain, second_shift, pool_bias, class_weight.T, inner_bias, class_bias]
    (output, w1, w2, wu, wp, vec, ib, qkv, context, lse, hidden_low, unit_first, act, dgelu, unit_second, inv, firsts) = forward(
        FORWARD_PLAN, tokens, lengths, qkv_weight, out_weight, inner_weight, outer_weight, pool_weight, small, nz)
    (loss, own, ibg, poolg, classg, wo, wi, wug, wq, tokens_grad) = backward(
        BACKWARD_PLAN, lengths, labels, vec, lse, inv, firsts, cotangent, tokens, w1, w2, wu, wp, qkv, context, hidden_low, unit_first, act, dgelu, unit_second)
    return finish(output, tokens_grad, loss, own, ibg, poolg, classg, wo, wi, wug, wq, classes)


def solution(mesh):
    in_specs = (
        P((DP, FSDP), None),
        P((DP, FSDP)),
        P((DP, FSDP)),
        P((DP, FSDP), None),
        P(FSDP, None),
        P(FSDP),
        P(FSDP),
        P(FSDP, None),
        P(FSDP),
        P(FSDP),
        P(FSDP),
        P(FSDP, None),
        P(FSDP),
        P(FSDP, None),
        P(FSDP),
        P(FSDP),
        P(FSDP),
        P(FSDP, None),
        P(FSDP),
        P(FSDP, None),
        P(),
    )
    out_specs = (
        P((DP, FSDP), None),
        P((DP, FSDP)),
        P((DP, FSDP), None),
        P(FSDP, None),
        P(FSDP),
        P(FSDP),
        P(FSDP, None),
        P(FSDP),
        P(FSDP),
        P(FSDP),
        P(FSDP, None),
        P(FSDP),
        P(FSDP, None),
        P(FSDP),
        P(FSDP),
        P(FSDP),
        P(FSDP, None),
        P(FSDP),
        P(FSDP, None),
        P(),
    )
    sizes = dict(mesh.shape)
    fast = sizes[DP] == 4 and sizes[FSDP] == 8
    return jax.shard_map(
        functools.partial(per_device, sizes[FSDP] // 2) if fast else per_device_any, mesh=mesh, in_specs=in_specs, out_specs=out_specs, check_vma=False
    )
```
